32 devices in a mesh: seq: 4 (over z), fsdp: 8 (over y, x, core).
Axes of the slice: x: 2, y: 2, z: 4, core: 2. Of those that a mesh axis runs over, the one named last changes fastest.
Arguments:
- tokens: float32 [2, 8, 1024, 1024], P(None, 'fsdp', 'seq'), may hold values from -6 to 6
- cotangent: float32 [2, 8, 1024, 1024], P(None, 'fsdp', 'seq'), may hold values from -6 to 6
- doc_starts: int32 [2, 8, 8], P(None, 'fsdp'), may hold values from 0 to 1023, as said below
- qkv_weight: bfloat16 [1024, 3072], P('fsdp'), may hold values from -0.1875 to 0.1875
- out_weight: bfloat16 [1024, 1024], P('fsdp'), may hold values from -3.5 to 3.5
- in_weight: bfloat16 [1024, 5248], P('fsdp'), may hold values from -0.1875 to 0.1875
- down_weight: bfloat16 [2624, 1024], P('fsdp'), may hold values from -0.125 to 0.125
- attn_gain: bfloat16 [1024], P('fsdp'), may hold values from 0.5 to 1.5
- ffn_gain: bfloat16 [1024], P('fsdp'), may hold values from 0.5 to 1.5
Outputs:
- output: float32 [2, 8, 1024, 1024], P(None, 'fsdp', 'seq')
- tokens_grad: float32 [2, 8, 1024, 1024], P(None, 'fsdp', 'seq')
- qkv_grad: float32 [1024, 3072], P('fsdp')
- out_grad: float32 [1024, 1024], P('fsdp')
- in_grad: float32 [1024, 5248], P('fsdp')
- down_grad: float32 [2624, 1024], P('fsdp')
- attngain_grad: float32 [1024], P('fsdp')
- ffngain_grad: float32 [1024], P('fsdp')
The draws below stay inside these ranges and needn't reach their ends.
Inputs may be any that keep to these rules, and one draw needn't show every extreme that they name: `doc_starts`: in every stream the starts rise strictly from 0 and stay below 1024; one document of every stream begins within the first 256 positions and ends within the last 256 positions.
All inputs are finite; a program needn't handle non-finite values.
Results may differ from the reference program's by a relative error of at most 0.02.
Values may be sent and summed in bfloat16 or wider, within the bound.
A program may use at most 192 MiB of HBM per device.

```python
import jax
import jax.numpy as jnp
from jax import lax

D = 1024
HEADS = 16
HEAD_DIM = 64
FF = 2624
TOK = 256
MB = 2
NDOC = 8
SEQLEN = 1024
STREAMS = 8


def draw_doc_starts(key, part):
    key = jax.random.fold_in(key, 7)
    first_key, second_key, third_key = jax.random.split(key, 3)
    stride = TOK // NDOC
    shape = (MB, STREAMS, NDOC)
    order = jnp.arange(NDOC, dtype=jnp.int32)
    leading = order * stride + jax.random.randint(first_key, shape, 0, stride, dtype=jnp.int32)
    leading = jnp.where(order == 0, 0, leading)
    trailing = SEQLEN - TOK + order * stride + jax.random.randint(second_key, shape, 0, stride, dtype=jnp.int32)
    long_doc = jax.random.randint(third_key, (MB, STREAMS, 1), 1, NDOC - 1, dtype=jnp.int32)
    return jnp.where(order <= long_doc, leading, trailing).astype(jnp.int32)


def block_levels(stream_key, dims, cuts, smallest, high):
    level, own = 1.0, jax.random.fold_in(stream_key, 6)
    for dim, blocks in cuts:
        steps = jnp.exp(jax.random.uniform(jax.random.fold_in(own, dim), (blocks,), jnp.float32, smallest / len(cuts), high / len(cuts)))
        level = level * jnp.repeat(steps, dims[dim] // blocks).reshape([-1 if axis == dim else 1 for axis in range(len(dims))])
    return level


def gaussian(key, extent, width, reach, cuts=(), kind=jnp.bfloat16):
    loudness = block_levels(key, extent, cuts, -0.22, 0.18) if cuts else 1.0
    drawn = jax.random.normal(key, extent, jnp.float32) * width * loudness
    return jnp.minimum(jnp.maximum(drawn, -reach), reach).astype(kind)


def setup_inputs(seed: int = 0) -> dict:
    key_list = jax.random.split(jax.random.key(seed), 10)
    return {
        "tokens": gaussian(key_list[0], (MB, STREAMS, SEQLEN, D), 1.0, 6.0, ((1, 8), (2, 4)), jnp.float32),
        "cotangent": gaussian(key_list[1], (MB, STREAMS, SEQLEN, D), 1.0, 6.0, ((1, 8), (2, 4)), jnp.float32),
        "doc_starts": draw_doc_starts(jax.random.fold_in(key_list[9], 71), 0),
        "qkv_weight": gaussian(key_list[3], (D, 3 * D), D ** -0.5, 0.1875, ((0, 8),)),
        "out_weight": gaussian(key_list[4], (D, D), (max(1, 3 * D // SEQLEN)) ** -0.5, 3.5, ((0, 8),)),
        "in_weight": gaussian(key_list[5], (D, 2 * FF), D ** -0.5, 0.1875, ((0, 8),)),
        "down_weight": gaussian(key_list[6], (FF, D), FF ** -0.5, 0.125, ((0, 8),)),
        "attn_gain": jnp.clip(1.0 + 0.1 * jax.random.normal(key_list[7], (D,), jnp.float32), 0.5, 1.5).astype(jnp.bfloat16),
        "ffn_gain": jnp.clip(1.0 + 0.1 * jax.random.normal(key_list[8], (D,), jnp.float32), 0.5, 1.5).astype(jnp.bfloat16),
    }


@jax.custom_vjp
def low(v):
    return lax.optimization_barrier(v.astype(jnp.bfloat16)).astype(jnp.float32)

@jax.custom_vjp
def low_back(v):
    return v

def low_keep(v):
    return (low(v), None)

def low_pass(kept, grad):
    return (grad,)

def back_keep(v):
    return (v, None)

def back_low(kept, grad):
    return (low(grad),)
low.defvjp(low_keep, low_pass)
low_back.defvjp(back_keep, back_low)
EPSILON = 1e-05
ROPE_THETA = 160000.0
MASKED_SCORE = -1e+30
HIGHEST = lax.Precision.HIGHEST

def layer_norm(values, norm_gain):
    average = lax.optimization_barrier(jnp.mean(values, axis=-1, keepdims=True))
    centred = values - average
    spread = lax.optimization_barrier(jnp.mean(centred * centred, axis=-1, keepdims=True))
    return centred * lax.rsqrt(spread + EPSILON) * norm_gain

def gated_gelu(joined):
    half_width = joined.shape[-1] // 2
    return jax.nn.gelu(joined[:, :half_width], approximate=False) * joined[:, half_width:]

def rotate(values, cosine_table, sine_table):
    half_width = values.shape[-1] // 2
    turned = jnp.concatenate([-values[..., half_width:], values[..., :half_width]], axis=-1)
    return values * cosine_table + turned * sine_table

def tables(starts):
    places = jnp.arange(SEQLEN, dtype=jnp.int32)
    preceding = starts[:, None, :] <= places[None, :, None]
    segments = lax.optimization_barrier(jnp.sum(preceding.astype(jnp.int32), axis=-1)) - 1
    doc_begin = lax.optimization_barrier(jnp.max(jnp.where(preceding, starts[:, None, :], 0), axis=-1))
    offsets = (places[None, :] - doc_begin).astype(jnp.float32)
    inverse = ROPE_THETA ** (-jnp.arange(0, HEAD_DIM, 2, dtype=jnp.float32) / HEAD_DIM)
    angles = offsets[..., None] * inverse
    angles = jnp.concatenate([angles, angles], axis=-1)[:, :, None, :]
    return (jnp.cos(angles), jnp.sin(angles), segments)

def attend(pieces):
    queries, keyset, valueset, segments = pieces
    block_rows = min(512, SEQLEN)
    factor = HEAD_DIM ** (-0.5)

    def one_block(inner):
        query_rows, block_segs = inner
        scores = low_back(jnp.einsum('qhd,khd->hqk', query_rows, keyset, precision=HIGHEST) * factor)
        same_doc = (block_segs[:, None] == segments[None, :])[None]
        scores = jnp.where(same_doc, scores, MASKED_SCORE)
        row_max = lax.optimization_barrier(jnp.max(scores, axis=-1, keepdims=True))
        weights = jnp.exp(scores - row_max)
        weights = weights / lax.optimization_barrier(jnp.sum(weights, axis=-1, keepdims=True))
        return jnp.einsum('hqk,khd->qhd', low(weights), valueset, precision=HIGHEST)
    blocks = SEQLEN // block_rows
    mixture = lax.map(jax.checkpoint(one_block), (queries.reshape(blocks, block_rows, HEADS, HEAD_DIM), segments.reshape(blocks, block_rows)))
    return mixture.reshape(SEQLEN, HEADS, HEAD_DIM)

def reference(tokens, cotangent, doc_starts, qkv_weight, out_weight, in_weight, down_weight, attn_gain, ffn_gain):
    stream_count = MB * STREAMS
    cosine_table, sine_table, segments = tables(doc_starts.reshape(stream_count, NDOC))

    def forward(rows_in, weight_qkv, weight_out, weight_in, weight_down, gain_one, gain_two):
        flat_rows = rows_in.reshape(-1, D)
        normed = low(layer_norm(flat_rows, gain_one))
        joined_qkv = low_back(jnp.dot(normed, weight_qkv, precision=HIGHEST))
        shaped = joined_qkv.reshape(stream_count, SEQLEN, 3, HEADS, HEAD_DIM)
        queries = low(low_back(rotate(shaped[:, :, 0], cosine_table, sine_table)))
        keyset = low(low_back(rotate(shaped[:, :, 1], cosine_table, sine_table)))
        valueset = low(low_back(shaped[:, :, 2]))
        mixture = lax.map(attend, (queries, keyset, valueset, segments))
        mixture = low(low_back(mixture.reshape(-1, D)))
        middle = flat_rows + low_back(jnp.dot(mixture, weight_out, precision=HIGHEST))
        normed_two = low(layer_norm(middle, gain_two))
        joined = low_back(jnp.dot(normed_two, weight_in, precision=HIGHEST))
        active = low(gated_gelu(joined))
        result = middle + low_back(jnp.dot(active, weight_down, precision=HIGHEST))
        return result.reshape(rows_in.shape)
    output, backward = jax.vjp(forward, tokens.astype(jnp.float32), qkv_weight.astype(jnp.float32), out_weight.astype(jnp.float32), in_weight.astype(jnp.float32), down_weight.astype(jnp.float32), attn_gain.astype(jnp.float32), ffn_gain.astype(jnp.float32))
    gradients = backward(cotangent.astype(jnp.float32))
    return (output, gradients[0], gradients[1], gradients[2], gradients[3], gradients[4], gradients[5], gradients[6])
```

```python
from functools import partial

import jax
import jax.numpy as jnp
from jax import lax
from jax.experimental import pallas as pl
from jax.experimental.pallas import tpu as pltpu
from jax.sharding import PartitionSpec as P

HEADS = 16
HEAD_DIM = 64


EPSILON = 1e-05
ROPE_THETA = 160000.0
MASKED_SCORE = -1e30


def as_sent(x):

    def short(part):
        return part.astype(jnp.bfloat16) if part.dtype == jnp.float32 else part

    return jax.tree.map(short, x)


def layer_norm(values, norm_gain):
    average = jnp.mean(values, axis=-1, keepdims=True)
    centred = values - average
    spread = jnp.mean(centred * centred, axis=-1, keepdims=True)
    return centred * lax.rsqrt(spread + EPSILON) * norm_gain


def gated_gelu(joined):
    half_width = joined.shape[-1] // 2
    return jax.nn.gelu(joined[:, :half_width], approximate=False) * joined[:, half_width:]


def rotate(values, cosine_table, sine_table):
    half_width = values.shape[-1] // 2
    turned = jnp.concatenate([-values[..., half_width:], values[..., :half_width]], axis=-1)
    return values * cosine_table + turned * sine_table


def rope_tables(starts, places, head_width):
    preceding = starts[None, :] <= places[:, None]
    doc_begin = jnp.max(jnp.where(preceding, starts[None, :], 0), axis=-1)
    offsets = (places - doc_begin).astype(jnp.float32)
    inverse = ROPE_THETA ** (-jnp.arange(0, head_width, 2, dtype=jnp.float32) / head_width)
    angles = offsets[:, None] * inverse[None, :]
    angles = jnp.concatenate([angles, angles], axis=-1)
    return (jnp.cos(angles), jnp.sin(angles))


def segment_ids(starts, places):
    return jnp.sum((starts[None, :] <= places[:, None]).astype(jnp.int32), axis=-1) - 1


def turn_pair(pair, cosine_table, sine_table):
    shaped = pair.reshape(pair.shape[0], 2, HEADS, HEAD_DIM)
    turned = rotate(shaped, cosine_table[:, None, None, :], sine_table[:, None, None, :])
    return turned.reshape(pair.shape[0], 2 * HEADS * HEAD_DIM)


def attend_forward(queries, keys_in, values_in, segments, head_count):
    length = queries.shape[0]
    head_width = queries.shape[1] // head_count
    block_rows = min(512, length)
    blocks = length // block_rows
    keyset = keys_in.reshape(length, head_count, head_width)
    valueset = values_in.reshape(length, head_count, head_width)
    factor = head_width ** (-0.5)

    def one_block(pieces):
        query_rows, block_segs = pieces
        scores = (
            jnp.einsum("qhd,khd->hqk", query_rows, keyset, preferred_element_type=jnp.float32)
            * factor
        )
        scores = jnp.where((block_segs[:, None] == segments[None, :])[None], scores, MASKED_SCORE)
        row_max = jnp.max(scores, axis=-1, keepdims=True)
        totals = jnp.sum(jnp.exp(scores - row_max), axis=-1, keepdims=True)
        logsums = row_max + jnp.log(totals)
        weights = jnp.exp(scores - logsums).astype(jnp.bfloat16)
        mixture = jnp.einsum("hqk,khd->qhd", weights, valueset, preferred_element_type=jnp.float32)
        return (mixture, logsums)

    mixture, logsums = lax.map(
        one_block,
        (
            queries.reshape(blocks, block_rows, head_count, head_width),
            segments.reshape(blocks, block_rows),
        ),
    )
    return (mixture.reshape(length, head_count * head_width), logsums)


def attend_backward(queries, keys_in, values_in, grads_in, segments, logsums, head_count):
    length = queries.shape[0]
    head_width = queries.shape[1] // head_count
    block_rows = min(512, length)
    blocks = length // block_rows
    keyset = keys_in.reshape(length, head_count, head_width)
    valueset = values_in.reshape(length, head_count, head_width)
    factor = head_width ** (-0.5)

    def one_block(carry, pieces):
        key_grad, value_grad = carry
        query_rows, block_segs, grad_rows, block_lse = pieces
        scores = (
            jnp.einsum("qhd,khd->hqk", query_rows, keyset, preferred_element_type=jnp.float32)
            * factor
        )
        scores = jnp.where((block_segs[:, None] == segments[None, :])[None], scores, MASKED_SCORE)
        weights = jnp.exp(scores - block_lse)
        value_grad = value_grad + jnp.einsum(
            "hqk,qhd->khd",
            weights.astype(jnp.bfloat16),
            grad_rows,
            preferred_element_type=jnp.float32,
        )
        grad_weights = jnp.einsum(
            "qhd,khd->hqk", grad_rows, valueset, preferred_element_type=jnp.float32
        )
        centre = jnp.sum(weights * grad_weights, axis=-1, keepdims=True)
        grad_scores = (weights * (grad_weights - centre)).astype(jnp.bfloat16)
        query_grad = (
            jnp.einsum("hqk,khd->qhd", grad_scores, keyset, preferred_element_type=jnp.float32)
            * factor
        )
        key_grad = (
            key_grad
            + jnp.einsum(
                "hqk,qhd->khd", grad_scores, query_rows, preferred_element_type=jnp.float32
            )
            * factor
        )
        return ((key_grad, value_grad), query_grad)

    empty = jnp.zeros((length, head_count, head_width), jnp.float32)
    pieces = (
        queries.reshape(blocks, block_rows, head_count, head_width),
        segments.reshape(blocks, block_rows),
        grads_in.reshape(blocks, block_rows, head_count, head_width),
        logsums,
    )
    (key_grad, value_grad), query_grad = lax.scan(one_block, (empty, empty), pieces)
    flat_shape = (length, head_count * head_width)
    return (
        query_grad.reshape(flat_shape).astype(jnp.bfloat16),
        key_grad.reshape(flat_shape).astype(jnp.bfloat16),
        value_grad.reshape(flat_shape).astype(jnp.bfloat16),
    )


def shards(
    tokens,
    cotangent,
    doc_starts,
    qkv_weight,
    out_weight,
    in_weight,
    down_weight,
    attn_gain,
    ffn_gain,
):
    micro_count = tokens.shape[0]
    token_rows = tokens.shape[2]
    model_width = tokens.shape[3]
    seq_count = lax.axis_size("seq")
    head_count = HEADS // seq_count
    places = lax.axis_index("seq") * token_rows + jnp.arange(token_rows, dtype=jnp.int32)
    everywhere = jnp.arange(token_rows * seq_count, dtype=jnp.int32)
    outputs = []
    input_grads = []
    full_terms = None
    shard_terms = None
    for micro_step in range(micro_count):
        rows_in = tokens[micro_step, 0]
        starts = doc_starts[micro_step, 0]
        cosine_table, sine_table = rope_tables(starts, places, HEAD_DIM)
        segments = segment_ids(starts, everywhere)
        attn_set = (
            lax.all_gather(qkv_weight, "fsdp", axis=0, tiled=True),
            lax.all_gather(out_weight, "fsdp", axis=0, tiled=True),
            lax.all_gather(attn_gain, "fsdp", axis=0, tiled=True),
        )
        qkv_full, out_full, gain_one = attn_set
        normed, norm_back = jax.vjp(layer_norm, rows_in, gain_one.astype(jnp.float32))
        normed_low = normed.astype(jnp.bfloat16)
        qkv_rows = jnp.dot(normed_low, qkv_full, preferred_element_type=jnp.float32)
        turned, turn_back = jax.vjp(
            partial(turn_pair, cosine_table=cosine_table, sine_table=sine_table),
            qkv_rows[:, : 2 * model_width],
        )
        queries = turned[:, :model_width].astype(jnp.bfloat16)
        keyset = turned[:, model_width:].astype(jnp.bfloat16)
        valueset = qkv_rows[:, 2 * model_width :].astype(jnp.bfloat16)
        query_heads, key_heads, value_heads = (
            lax.all_to_all(queries, "seq", split_axis=1, concat_axis=0, tiled=True),
            lax.all_to_all(keyset, "seq", split_axis=1, concat_axis=0, tiled=True),
            lax.all_to_all(valueset, "seq", split_axis=1, concat_axis=0, tiled=True),
        )
        mixture, logsums = attend_forward(query_heads, key_heads, value_heads, segments, head_count)
        mixture_rows = lax.all_to_all(
            mixture.astype(jnp.bfloat16), "seq", split_axis=0, concat_axis=1, tiled=True
        )
        middle = rows_in + jnp.dot(mixture_rows, out_full, preferred_element_type=jnp.float32)
        ffn_set = (
            lax.all_gather(in_weight, "fsdp", axis=0, tiled=True),
            lax.all_gather(down_weight, "fsdp", axis=0, tiled=True),
            lax.all_gather(ffn_gain, "fsdp", axis=0, tiled=True),
        )
        in_full, down_full, gain_two = ffn_set
        normed_two, norm_back_two = jax.vjp(layer_norm, middle, gain_two.astype(jnp.float32))
        normed_two_low = normed_two.astype(jnp.bfloat16)
        joined = jnp.dot(normed_two_low, in_full, preferred_element_type=jnp.float32)
        active, gelu_back = jax.vjp(gated_gelu, joined)
        active_low = active.astype(jnp.bfloat16)
        outputs.append(middle + jnp.dot(active_low, down_full, preferred_element_type=jnp.float32))
        grad_out = cotangent[micro_step, 0]
        grad_low = grad_out.astype(jnp.bfloat16)
        ffn_set = (
            lax.all_gather(in_weight, "fsdp", axis=0, tiled=True),
            lax.all_gather(down_weight, "fsdp", axis=0, tiled=True),
            lax.all_gather(ffn_gain, "fsdp", axis=0, tiled=True),
        )
        in_full, down_full, gain_two = ffn_set
        down_term = jnp.dot(active_low.T, grad_low, preferred_element_type=jnp.float32)
        grad_active = jnp.dot(grad_low, down_full.T, preferred_element_type=jnp.float32)
        grad_joined = gelu_back(grad_active)[0].astype(jnp.bfloat16)
        in_term = jnp.dot(normed_two_low.T, grad_joined, preferred_element_type=jnp.float32)
        grad_normed_two = jnp.dot(grad_joined, in_full.T, preferred_element_type=jnp.float32)
        grad_middle_norm, gain_two_term = norm_back_two(grad_normed_two)
        grad_middle = grad_out + grad_middle_norm
        grad_mid_low = grad_middle.astype(jnp.bfloat16)
        attn_set = (
            lax.all_gather(qkv_weight, "fsdp", axis=0, tiled=True),
            lax.all_gather(out_weight, "fsdp", axis=0, tiled=True),
            lax.all_gather(attn_gain, "fsdp", axis=0, tiled=True),
        )
        qkv_full, out_full, gain_one = attn_set
        out_term = jnp.dot(mixture_rows.T, grad_mid_low, preferred_element_type=jnp.float32)
        grad_mixture = jnp.dot(grad_mid_low, out_full.T, preferred_element_type=jnp.float32).astype(
            jnp.bfloat16
        )
        grad_heads = lax.all_to_all(grad_mixture, "seq", split_axis=1, concat_axis=0, tiled=True)
        query_grad, key_grad, value_grad = attend_backward(
            query_heads, key_heads, value_heads, grad_heads, segments, logsums, head_count
        )
        query_back, key_back, value_back = (
            lax.all_to_all(query_grad, "seq", split_axis=0, concat_axis=1, tiled=True),
            lax.all_to_all(key_grad, "seq", split_axis=0, concat_axis=1, tiled=True),
            lax.all_to_all(value_grad, "seq", split_axis=0, concat_axis=1, tiled=True),
        )
        grad_pair = turn_back(jnp.concatenate([query_back, key_back], axis=1).astype(jnp.float32))[
            0
        ]
        grad_qkv = jnp.concatenate([grad_pair, value_back.astype(jnp.float32)], axis=1).astype(
            jnp.bfloat16
        )
        qkv_term = jnp.dot(normed_low.T, grad_qkv, preferred_element_type=jnp.float32)
        grad_normed = jnp.dot(grad_qkv, qkv_full.T, preferred_element_type=jnp.float32)
        grad_rows_norm, gain_one_term = norm_back(grad_normed)
        input_grads.append(grad_middle + grad_rows_norm)
        terms = (qkv_term, out_term, in_term, down_term, gain_one_term, gain_two_term)
        full_terms = terms if full_terms is None else jax.tree.map(jnp.add, full_terms, terms)
    shard_terms = jax.tree.map(
        lambda part: part.astype(jnp.float32),
        lax.psum_scatter(as_sent(full_terms), "fsdp", scatter_dimension=0, tiled=True),
    )
    totals = jax.tree.map(
        lambda part: part.astype(jnp.float32), lax.psum(as_sent(shard_terms), "seq")
    )
    return (
        jnp.stack(outputs)[:, None],
        jnp.stack(input_grads)[:, None],
        totals[0],
        totals[1],
        totals[2],
        totals[3],
        totals[4],
        totals[5],
    )


MESH = pl.DeviceIdType.MESH
ANY = pl.BlockSpec(memory_space=pl.ANY)
VMEM_BYTES = 60 * 2**20
BF = jnp.bfloat16
F32 = jnp.float32


def nn(a, b):
    return lax.dot_general(a, b, (((1,), (0,)), ((), ())), preferred_element_type=F32)


def nt(a, b):
    return lax.dot_general(a, b, (((1,), (1,)), ((), ())), preferred_element_type=F32)


def spot():
    z, f = lax.axis_index("seq"), lax.axis_index("fsdp")
    core = lax.rem(f, 2)
    x = lax.rem(f // 2, 2)
    y = f // 4
    return z, f, y, x, core


def remote(src, dst, send, recv, where):
    return pltpu.make_async_remote_copy(
        src_ref=src, dst_ref=dst, send_sem=send, recv_sem=recv, device_id=where, device_id_type=MESH
    )


class Rows:
    def __init__(self, z, f, core):
        base = f - core
        self.work, self.home = [], []
        for i in range(2):
            zw, cw = 2 * i + core, z // 2
            self.work.append((zw, base + cw, (zw == z) & (cw == core)))
            zh, ch = 2 * core + i, lax.rem(z, 2)
            self.home.append((zh, base + ch, (zh == z) & (ch == core)))
        self.z = z

    def greet(self, barrier):
        count = 0
        for zt, ft, same in self.work + self.home:

            @pl.when(jnp.logical_not(same))
            def _():
                pl.semaphore_signal(barrier, inc=1, device_id=(zt, ft), device_id_type=MESH)

            count = count + jnp.where(same, 0, 1)
        return count

    def start(self, src, dst, send, recv, local, out):
        places = self.work if out else self.home
        slot = lax.rem(self.z, 2) if out else self.z // 2
        for i, (zt, ft, same) in enumerate(places):

            @pl.when(same)
            def _(i=i):
                pltpu.make_async_copy(src.at[i], dst.at[slot], local).start()

            @pl.when(jnp.logical_not(same))
            def _(i=i, zt=zt, ft=ft):
                remote(src.at[i], dst.at[slot], send.at[i], recv.at[slot], (zt, ft)).start()

    def wait(self, src, dst, send, recv, local, out):
        goes, comes = (self.work, self.home) if out else (self.home, self.work)
        for i, (zt, ft, same) in enumerate(goes):

            @pl.when(same)
            def _(i=i):
                pltpu.make_async_copy(src.at[i], dst.at[i], local).wait()

            @pl.when(jnp.logical_not(same))
            def _(i=i, zt=zt, ft=ft):
                remote(src.at[i], dst.at[i], send.at[i], recv.at[i], (zt, ft)).wait_send()

        for i, (zt, ft, same) in enumerate(comes):

            @pl.when(jnp.logical_not(same))
            def _(i=i, zt=zt, ft=ft):
                remote(src.at[i], dst.at[i], send.at[i], recv.at[i], (zt, ft)).wait_recv()


def halves(width):
    cut = (width // 128 // 2) * 128
    return pl.ds(0, cut), pl.ds(cut, width - cut)


def gather_kernel(*refs):
    shards, (tok, cot, starts) = refs[:5], refs[5:8]
    wholes, (tok_o, cot_o, starts_o) = refs[8:13], refs[13:16]
    ss, rs, ls, es, er, el, ds_, dr = refs[16:]
    z, f, y, x, core = spot()
    fx, fy, fc = f + 2 - 4 * x, f + 4 - 8 * y, f + 1 - 2 * core
    fd = fx + 4 - 8 * y
    rows = Rows(z, f, core)
    barrier = pltpu.get_barrier_semaphore()
    for t in (fx, fy, fc):
        pl.semaphore_signal(barrier, inc=1, device_id=(z, t), device_id_type=MESH)
    pl.semaphore_wait(barrier, rows.greet(barrier) + 3)

    def copies(w):
        whole, shard = wholes[w], shards[w]
        first, second = halves(shard.shape[1])
        same = lambda i, cols=None: whole.at[i] if cols is None else whole.at[i, :, cols]
        plan = [
            (shard, whole.at[f], fx),
            (shard, whole.at[f], fy),
            (shard, whole.at[f], fc),
            (same(fx, first), same(fx, first), fy),
            (same(fy, second), same(fy, second), fx),
            (same(fx), same(fx), fc),
            (same(fy), same(fy), fc),
            (same(fd, first), same(fd, first), fc),
            (same(fd, second), same(fd, second), fc),
        ]
        return [
            remote(s, d, ss.at[w, k], rs.at[w, k], (z, t)) for k, (s, d, t) in enumerate(plan)
        ]

    every = [copies(w) for w in range(5)]
    info = remote(starts, starts_o.at[core], ds_.at[0], dr.at[0], (z, fc))
    info.start()
    own_info = pltpu.make_async_copy(starts, starts_o.at[core], el.at[2])
    own_info.start()
    rows.start(tok, tok_o, es.at[0], er.at[0], el.at[0], True)
    for w in range(5):
        for k in range(3):
            every[w][k].start()
        pltpu.make_async_copy(shards[w], wholes[w].at[f], ls.at[w]).start()
    rows.start(cot, cot_o, es.at[1], er.at[1], el.at[1], True)
    for w in range(5):
        every[w][0].wait_recv()
        every[w][3].start()
        every[w][5].start()
        every[w][1].wait_recv()
        every[w][4].start()
        every[w][6].start()
    for w in range(5):
        for k in (3, 4):
            every[w][k].wait_recv()
            every[w][k + 4].start()
    for w in range(5):
        for k in (2, 5, 6, 7, 8):
            every[w][k].wait_recv()
        for k in range(9):
            every[w][k].wait_send()
        pltpu.make_async_copy(shards[w], wholes[w].at[f], ls.at[w]).wait()
    rows.wait(tok, tok_o, es.at[0], er.at[0], el.at[0], True)
    rows.wait(cot, cot_o, es.at[1], er.at[1], el.at[1], True)
    info.wait()
    own_info.wait()


def gather_all(shards, tok, cot, starts):
    dma = pltpu.SemaphoreType.DMA
    out_shape = [jax.ShapeDtypeStruct((8,) + s.shape, s.dtype) for s in shards] + [
        jax.ShapeDtypeStruct(tok.shape, tok.dtype),
        jax.ShapeDtypeStruct(cot.shape, cot.dtype),
        jax.ShapeDtypeStruct((2,) + starts.shape, starts.dtype),
    ]
    return pl.pallas_call(
        gather_kernel,
        out_shape=out_shape,
        in_specs=[ANY] * 8,
        out_specs=[ANY] * 8,
        scratch_shapes=[
            dma((5, 9)), dma((5, 9)), dma((5,)), dma((2, 2)), dma((2, 2)), dma((3,)), dma((1,)), dma((1,)),
        ],
        compiler_params=pltpu.CompilerParams(collective_id=1, has_side_effects=True),
        name="gather_weights_and_rows",
    )(*shards, tok, cot, starts)


CHUNK = 768
CHUNKS = 16


def reduce_kernel(grads, out_rows, in_rows, total, out_home, in_home,
                  acc, r0, ax, ay, rx, ry, bx, by, r2x, r2y, part, zr, ztmp, zr2, fin,
                  l0, s0, q0, s1, q1, s2, q2, s3, q3, s4, q4, s5, q5, s6, q6, wsem, es, er, el):
    z, f, y, x, core = spot()
    fx, fy, fc = f + 2 - 4 * x, f + 4 - 8 * y, f + 1 - 2 * core
    rows = Rows(z, f, core)
    outer = (z == 0) | (z == 3)
    near = jnp.where(z < 2, 1 - z, 5 - z)
    across = 3 - z
    half = CHUNK // 2
    own = jnp.where(z < 2, 0, 1)
    barrier = pltpu.get_barrier_semaphore()
    for t in (fx, fy, fc):
        pl.semaphore_signal(barrier, inc=1, device_id=(z, t), device_id_type=MESH)
    pl.semaphore_signal(barrier, inc=1, device_id=(near, f), device_id_type=MESH)

    @pl.when(jnp.logical_not(outer))
    def _():
        pl.semaphore_signal(barrier, inc=1, device_id=(across, f), device_id_type=MESH)

    pl.semaphore_wait(barrier, rows.greet(barrier) + 4 + jnp.where(outer, 0, 1))
    rows.start(out_rows, out_home, es.at[0], er.at[0], el.at[0], False)
    rows.start(in_rows, in_home, es.at[1], er.at[1], el.at[1], False)

    def cols(t):
        return pl.ds(pl.multiple_of(t * CHUNK, 128), CHUNK)

    def c0(t):
        return [
            pltpu.make_async_copy(grads.at[:, core, :, cols(t)], acc.at[t], l0.at[t]),
            remote(grads.at[:, 1 - core, :, cols(t)], r0.at[t], s0.at[t], q0.at[t], (z, fc)),
        ]

    def c1(t):
        return [
            remote(ax.at[t], rx.at[t], s1.at[t, 0], q1.at[t, 0], (z, fx)),
            remote(ay.at[t], ry.at[t], s1.at[t, 1], q1.at[t, 1], (z, fy)),
        ]

    def c2(t):
        return [
            remote(bx.at[t], r2x.at[t], s2.at[t, 0], q2.at[t, 0], (z, fy)),
            remote(by.at[t], r2y.at[t], s2.at[t, 1], q2.at[t, 1], (z, fx)),
        ]

    def c3(t):
        return remote(part.at[t], zr.at[t], s3.at[t], q3.at[t], (near, f))

    def c4(t):
        return remote(ztmp.at[t], zr2.at[t], s4.at[t], q4.at[t], (across, f))

    def c5(t, h):
        return [
            remote(fin.at[t, h], fin.at[t, h], s5.at[t, 0], q5.at[t, 0], (across, f)),
            remote(fin.at[t, h], fin.at[t, h], s5.at[t, 1], q5.at[t, 1], (near, f)),
        ]

    def c6(t, h):
        return remote(fin.at[t, h], fin.at[t, h], s6.at[t], q6.at[t], (near, f))

    def up(v):
        return v.astype(F32)

    def stage(t, k, body):
        s = t - k

        @pl.when((s >= 0) & (s < CHUNKS))
        def _():
            body(s)

    def begin(t):
        for c in c0(t):
            c.start()

    def pair(t):
        for c in c0(t):
            c.wait()
        for i in range(2):
            o = 2 * i + (1 - x)
            ax[t, i] = (up(acc[t, o, :, :half]) + up(r0[t, o, :, :half])).astype(BF)
            o = 2 * (1 - y) + i
            ay[t, i] = (up(acc[t, o, :, half:]) + up(r0[t, o, :, half:])).astype(BF)
        for c in c1(t):
            c.start()

    def cross(t):
        for c in c1(t):
            c.wait()
        o = 2 * (1 - y) + x
        bx[t] = (up(acc[t, o, :, :half]) + up(r0[t, o, :, :half]) + up(rx[t, 1 - y])).astype(BF)
        o = 2 * y + (1 - x)
        by[t] = (up(acc[t, o, :, half:]) + up(r0[t, o, :, half:]) + up(ry[t, 1 - x])).astype(BF)
        for c in c2(t):
            c.start()

    def plane(t):
        for c in c2(t):
            c.wait()
        o = 2 * y + x
        part[t, 0] = (up(acc[t, o, :, :half]) + up(r0[t, o, :, :half]) + up(rx[t, y]) + up(r2x[t])).astype(BF)
        part[t, 1] = (up(acc[t, o, :, half:]) + up(r0[t, o, :, half:]) + up(ry[t, x]) + up(r2y[t])).astype(BF)

        @pl.when(outer)
        def _():
            c3(t).start()

    def meet(t):
        @pl.when(jnp.logical_not(outer))
        def _():
            c3(t).wait_recv()
            ztmp[t] = (up(part[t, 1 - own]) + up(zr[t, 1 - own])).astype(BF)
            c4(t).start()

    def sums(t):
        @pl.when(jnp.logical_not(outer))
        def _():
            c4(t).wait()
            fin[t, own] = (up(part[t, own]) + up(zr[t, own]) + up(zr2[t])).astype(BF)
            for c in c5(t, own):
                c.start()

    def spread(t):
        @pl.when(jnp.logical_not(outer))
        def _():
            c5(t, own)[0].wait_recv()
            c6(t, 1 - own).start()

    def write(t):
        return [
            pltpu.make_async_copy(fin.at[t, h], total.at[:, pl.ds(pl.multiple_of(t * CHUNK + h * half, 128), half)], wsem.at[t, h])
            for h in range(2)
        ]

    def finish(t):
        @pl.when(jnp.logical_not(outer))
        def _():
            for c in c5(t, own):
                c.wait_send()
            c6(t, 1 - own).wait_send()

        @pl.when(outer)
        def _():
            c3(t).wait_send()
            c5(t, own)[1].wait_recv()
            c6(t, 1 - own).wait_recv()

        for c in write(t):
            c.start()

    def end(t):
        for c in write(t):
            c.wait()

    def body(t, _):
        stage(t, 0, begin)
        stage(t, 1, pair)
        stage(t, 2, cross)
        stage(t, 3, plane)
        stage(t, 4, meet)
        stage(t, 5, sums)
        stage(t, 6, spread)
        stage(t, 7, finish)
        stage(t, 8, end)
        return 0

    lax.fori_loop(0, CHUNKS + 8, body, 0)
    rows.wait(out_rows, out_home, es.at[0], er.at[0], el.at[0], False)
    rows.wait(in_rows, in_home, es.at[1], er.at[1], el.at[1], False)


def reduce_all(grads, out_rows, in_rows):
    dma = pltpu.SemaphoreType.DMA
    half = CHUNK // 2
    n = CHUNKS
    r = 128

    def buf(*s):
        return pltpu.VMEM(s, BF)

    return pl.pallas_call(
        reduce_kernel,
        out_shape=[
            jax.ShapeDtypeStruct((r, n * CHUNK), BF),
            jax.ShapeDtypeStruct(out_rows.shape, BF),
            jax.ShapeDtypeStruct(in_rows.shape, BF),
        ],
        in_specs=[ANY] * 3,
        out_specs=[ANY] * 3,
        scratch_shapes=[
            buf(n, 4, r, CHUNK), buf(n, 4, r, CHUNK),
            buf(n, 2, r, half), buf(n, 2, r, half), buf(n, 2, r, half), buf(n, 2, r, half),
            buf(n, r, half), buf(n, r, half), buf(n, r, half), buf(n, r, half),
            buf(n, 2, r, half), buf(n, 2, r, half), buf(n, r, half), buf(n, r, half), buf(n, 2, r, half),
            dma((n,)), dma((n,)), dma((n,)), dma((n, 2)), dma((n, 2)), dma((n, 2)), dma((n, 2)),
            dma((n,)), dma((n,)), dma((n,)), dma((n,)), dma((n, 2)), dma((n, 2)), dma((n,)), dma((n,)),
            dma((n, 2)), dma((2, 2)), dma((2, 2)), dma((2,)),
        ],
        compiler_params=pltpu.CompilerParams(
            collective_id=2, has_side_effects=True, vmem_limit_bytes=VMEM_BYTES
        ),
        name="reduce_gradients",
    )(grads, out_rows, in_rows)


def attention_kernel(q_ref, k_ref, v_ref, bias_ref, o_ref, lse_ref):
    q = q_ref[...] * jnp.asarray(0.125, BF)
    k = k_ref[...]
    lane = lax.broadcasted_iota(jnp.int32, (1, 128), 1)
    vt = v_ref[...].T
    outs = []
    for h in range(2):
        mine = (lane < 64) if h == 0 else (lane >= 64)
        scores = nt(k, jnp.where(mine, q, jnp.zeros_like(q))) + bias_ref[...]
        top = jnp.max(scores, axis=0, keepdims=True)
        p = jnp.exp(scores - top)
        total = jnp.sum(p, axis=0, keepdims=True)
        outs.append(nn(vt, p.astype(BF)) / total)
        lse_ref[0, h : h + 1, :] = top + jnp.log(total)
    o_ref[...] = jnp.concatenate([outs[0][:64], outs[1][64:]], axis=0).T.astype(BF)


def attention_back_kernel(q_ref, k_ref, v_ref, bias_ref, o_ref, do_ref, lse_ref, dq_ref, dk_ref, dv_ref):
    q = q_ref[...] * jnp.asarray(0.125, BF)
    k, v, do = k_ref[...], v_ref[...], do_ref[...]
    lane = lax.broadcasted_iota(jnp.int32, (1, 128), 1)
    kt = k.T
    products = (o_ref[...].astype(F32) * do.astype(F32)).T
    none = jnp.zeros_like(q)
    dqs, dks, dvs = [], [], []
    for h in range(2):
        mine = (lane < 64) if h == 0 else (lane >= 64)
        centre = jnp.sum(products[64 * h : 64 * h + 64], axis=0, keepdims=True)
        p = jnp.exp(nt(k, jnp.where(mine, q, none)) + bias_ref[...] - lse_ref[0, h : h + 1, :])
        dvs.append(nn(p.astype(BF), do))
        ds = (p * (nt(v, jnp.where(mine, do, none)) - centre)).astype(BF)
        dks.append(nn(ds, q))
        dqs.append(nn(kt, ds))
    dq = jnp.concatenate([dqs[0][:64], dqs[1][64:]], axis=0).T
    dq_ref[...] = (dq * 0.125).astype(BF)
    dk_ref[...] = jnp.where(lane < 64, dks[0], dks[1]).astype(BF)
    dv_ref[...] = jnp.where(lane < 64, dvs[0], dvs[1]).astype(BF)


def attention(q, k, v, bias):
    rows, keys = q.shape[0], k.shape[0]
    narrow = pl.BlockSpec((rows, 128), lambda i: (0, i))
    long = pl.BlockSpec((keys, 128), lambda i: (0, i))
    return pl.pallas_call(
        attention_kernel,
        grid=(q.shape[1] // 128,),
        in_specs=[narrow, long, long, pl.BlockSpec((keys, rows), lambda i: (0, 0))],
        out_specs=[narrow, pl.BlockSpec((1, 2, rows), lambda i: (i, 0, 0))],
        out_shape=[
            jax.ShapeDtypeStruct(q.shape, BF),
            jax.ShapeDtypeStruct((q.shape[1] // 128, 2, rows), F32),
        ],
        compiler_params=pltpu.CompilerParams(vmem_limit_bytes=VMEM_BYTES),
        name="attention",
    )(q, k, v, bias)


def attention_back(q, k, v, bias, o, do, lse):
    rows, keys = q.shape[0], k.shape[0]
    narrow = pl.BlockSpec((rows, 128), lambda i: (0, i))
    long = pl.BlockSpec((keys, 128), lambda i: (0, i))
    return pl.pallas_call(
        attention_back_kernel,
        grid=(q.shape[1] // 128,),
        in_specs=[narrow, long, long, pl.BlockSpec((keys, rows), lambda i: (0, 0)), narrow, narrow,
                  pl.BlockSpec((1, 2, rows), lambda i: (i, 0, 0))],
        out_specs=[narrow, long, long],
        out_shape=[jax.ShapeDtypeStruct(q.shape, BF)] + [jax.ShapeDtypeStruct(k.shape, BF)] * 2,
        compiler_params=pltpu.CompilerParams(vmem_limit_bytes=VMEM_BYTES),
        name="attention_back",
    )(q, k, v, bias, o, do, lse)


def turn_rows(values, cosine, sine, back):
    shaped = values.reshape(values.shape[0], -1, HEAD_DIM)
    if back:
        g = shaped * sine
        half = HEAD_DIM // 2
        turned = jnp.concatenate([g[..., half:], -g[..., :half]], axis=-1)
        return (shaped * cosine + turned).reshape(values.shape)
    return rotate(shaped, cosine, sine).reshape(values.shape)


def swap(value):
    return lax.ppermute(value, "fsdp", [(i, i ^ 1) for i in range(lax.axis_size("fsdp"))])


def chip_streams(tokens, cotangent, doc_starts, qkv_weight, out_weight, in_weight, down_weight, attn_gain, ffn_gain):
    z, core = lax.axis_index("seq"), lax.axis_index("fsdp") % 2
    wide = tokens.shape[3]
    gains = jnp.concatenate([attn_gain, ffn_gain])[None] + jnp.zeros((16, 1), BF)
    starts = jnp.zeros((8, 128), jnp.int32).at[:2, :8].set(doc_starts[:, 0])
    shards_in = (gains, qkv_weight, out_weight, in_weight, down_weight)
    gains_f, qkv_f, out_f, in_f, down_f, tok_r, cot_r, starts_r = gather_all(
        shards_in, tokens[:, 0].astype(BF), cotangent[:, 0].astype(BF), starts
    )
    gain_one = gains_f[:, 0, :128].reshape(wide).astype(F32)
    gain_two = gains_f[:, 0, 128:].reshape(wide).astype(F32)
    qkv_full, out_full, in_full, down_full = (
        w.reshape(-1, w.shape[-1]) for w in (qkv_f, out_f, in_f, down_f)
    )
    rows_in = tok_r.reshape(-1, wide).astype(F32)
    grad_low = cot_r.reshape(-1, wide)
    grad_out = grad_low.astype(F32)
    count = rows_in.shape[0]
    mine = starts_r[z % 2, z // 2, :8]
    here = core * count + jnp.arange(count, dtype=jnp.int32)
    there = (1 - core) * count + jnp.arange(count, dtype=jnp.int32)
    cosine, sine = (t[:, None, :] for t in rope_tables(mine, here, HEAD_DIM))
    seg_here, seg_there = segment_ids(mine, here), segment_ids(mine, there)
    bias = jnp.where(
        jnp.concatenate([seg_here, seg_there])[:, None] == seg_here[None, :], 0.0, MASKED_SCORE
    ).astype(F32)

    normed, norm_back = jax.vjp(layer_norm, rows_in, gain_one)
    normed_low = normed.astype(BF)
    qkv = nn(normed_low, qkv_full)
    q = turn_rows(qkv[:, :wide], cosine, sine, False).astype(BF)
    k = turn_rows(qkv[:, wide : 2 * wide], cosine, sine, False).astype(BF)
    v = qkv[:, 2 * wide :].astype(BF)
    k_all = jnp.concatenate([k, swap(k)])
    v_all = jnp.concatenate([v, swap(v)])
    mixture, lse = attention(q, k_all, v_all, bias)
    middle = rows_in + nn(mixture, out_full)
    normed_two, norm_back_two = jax.vjp(layer_norm, middle, gain_two)
    normed_two_low = normed_two.astype(BF)
    joined = nn(normed_two_low, in_full)
    active, gelu_back = jax.vjp(gated_gelu, joined)
    active_low = active.astype(BF)
    output = middle + nn(active_low, down_full)

    down_term = nn(active_low.T, grad_low)
    grad_active = nt(grad_low, down_full)
    grad_joined = gelu_back(grad_active)[0].astype(BF)
    in_term = nn(normed_two_low.T, grad_joined)
    grad_normed_two = nt(grad_joined, in_full)
    grad_middle_norm, gain_two_term = norm_back_two(grad_normed_two)
    grad_middle = grad_out + grad_middle_norm
    grad_mid_low = grad_middle.astype(BF)
    out_term = nn(mixture.T, grad_mid_low)
    grad_mixture = nt(grad_mid_low, out_full).astype(BF)
    dq, dk, dv = attention_back(q, k_all, v_all, bias, mixture, grad_mixture, lse)
    dk = (dk[:count].astype(F32) + swap(dk[count:]).astype(F32)).astype(BF).astype(F32)
    dv = (dv[:count].astype(F32) + swap(dv[count:]).astype(F32)).astype(BF)
    grad_qkv = jnp.concatenate(
        [
            turn_rows(dq.astype(F32), cosine, sine, True).astype(BF),
            turn_rows(dk, cosine, sine, True).astype(BF),
            dv,
        ],
        axis=1,
    )
    qkv_term = nn(normed_low.T, grad_qkv)
    grad_normed = nt(grad_qkv, qkv_full)
    grad_rows, gain_one_term = norm_back(grad_normed)
    tokens_grad = grad_middle + grad_rows

    gain_terms = jnp.concatenate(
        [gain_one_term.reshape(8, 1, 128), gain_two_term.reshape(8, 1, 128)], axis=2
    )
    parts = [
        qkv_term.reshape(8, 128, -1).astype(BF),
        out_term.reshape(8, 128, -1).astype(BF),
        in_term.reshape(8, 128, -1).astype(BF),
        down_term.reshape(8, 128, -1).astype(BF),
        (gain_terms + jnp.zeros((1, 128, 1))).astype(BF),
    ]
    used = sum(p.shape[2] for p in parts)
    parts.append(jnp.zeros((8, 128, CHUNK * CHUNKS - used), BF))
    grads = jnp.concatenate(parts, axis=2).reshape(4, 2, 128, CHUNK * CHUNKS)
    total, out_home, in_home = reduce_all(
        grads, output.astype(BF).reshape(2, -1, wide), tokens_grad.astype(BF).reshape(2, -1, wide)
    )
    total = total.astype(F32)
    a, b, c, d = 3 * wide, 4 * wide, 4 * wide + in_weight.shape[1], used - 256
    return (
        out_home[:, None].astype(F32),
        in_home[:, None].astype(F32),
        total[:, :a],
        total[:, a:b],
        total[:, b:c],
        total[:, c:d].reshape(down_weight.shape),
        total[0, d : d + 128],
        total[0, d + 128 : d + 256],
    )


def solution(mesh):
    whole_chips = dict(mesh.shape) == {"seq": 4, "fsdp": 8}
    return jax.shard_map(
        chip_streams if whole_chips else shards,
        mesh=mesh,
        in_specs=(
            P(None, "fsdp", "seq", None),
            P(None, "fsdp", "seq", None),
            P(None, "fsdp", None),
            P("fsdp", None),
            P("fsdp", None),
            P("fsdp", None),
            P("fsdp", None),
            P("fsdp"),
            P("fsdp"),
        ),
        out_specs=(
            P(None, "fsdp", "seq", None),
            P(None, "fsdp", "seq", None),
            P("fsdp", None),
            P("fsdp", None),
            P("fsdp", None),
            P("fsdp", None),
            P("fsdp"),
            P("fsdp"),
        ),
        check_vma=False,
    )
```

```python
import functools
from functools import partial

import jax
import jax.numpy as jnp
from jax import lax
from jax.experimental import pallas as pl
from jax.experimental.pallas import tpu as pltpu
from jax.sharding import PartitionSpec as P

HEADS = 16
HEAD_DIM = 64


EPSILON = 1e-05
ROPE_THETA = 160000.0
MASKED_SCORE = -1e30


def as_sent(x):

    def short(part):
        return part.astype(jnp.bfloat16) if part.dtype == jnp.float32 else part

    return jax.tree.map(short, x)


def layer_norm(values, norm_gain):
    average = jnp.mean(values, axis=-1, keepdims=True)
    centred = values - average
    spread = jnp.mean(centred * centred, axis=-1, keepdims=True)
    return centred * lax.rsqrt(spread + EPSILON) * norm_gain


def gated_gelu(joined):
    half_width = joined.shape[-1] // 2
    return jax.nn.gelu(joined[:, :half_width], approximate=False) * joined[:, half_width:]


def rotate(values, cosine_table, sine_table):
    half_width = values.shape[-1] // 2
    turned = jnp.concatenate([-values[..., half_width:], values[..., :half_width]], axis=-1)
    return values * cosine_table + turned * sine_table


def rope_tables(starts, places, head_width):
    preceding = starts[None, :] <= places[:, None]
    doc_begin = jnp.max(jnp.where(preceding, starts[None, :], 0), axis=-1)
    offsets = (places - doc_begin).astype(jnp.float32)
    inverse = ROPE_THETA ** (-jnp.arange(0, head_width, 2, dtype=jnp.float32) / head_width)
    angles = offsets[:, None] * inverse[None, :]
    angles = jnp.concatenate([angles, angles], axis=-1)
    return (jnp.cos(angles), jnp.sin(angles))


def segment_ids(starts, places):
    return jnp.sum((starts[None, :] <= places[:, None]).astype(jnp.int32), axis=-1) - 1


def turn_pair(pair, cosine_table, sine_table):
    shaped = pair.reshape(pair.shape[0], 2, HEADS, HEAD_DIM)
    turned = rotate(shaped, cosine_table[:, None, None, :], sine_table[:, None, None, :])
    return turned.reshape(pair.shape[0], 2 * HEADS * HEAD_DIM)


def attend_forward(queries, keys_in, values_in, segments, head_count):
    length = queries.shape[0]
    head_width = queries.shape[1] // head_count
    block_rows = min(512, length)
    blocks = length // block_rows
    keyset = keys_in.reshape(length, head_count, head_width)
    valueset = values_in.reshape(length, head_count, head_width)
    factor = head_width ** (-0.5)

    def one_block(pieces):
        query_rows, block_segs = pieces
        scores = (
            jnp.einsum("qhd,khd->hqk", query_rows, keyset, preferred_element_type=jnp.float32)
            * factor
        )
        scores = jnp.where((block_segs[:, None] == segments[None, :])[None], scores, MASKED_SCORE)
        row_max = jnp.max(scores, axis=-1, keepdims=True)
        totals = jnp.sum(jnp.exp(scores - row_max), axis=-1, keepdims=True)
        logsums = row_max + jnp.log(totals)
        weights = jnp.exp(scores - logsums).astype(jnp.bfloat16)
        mixture = jnp.einsum("hqk,khd->qhd", weights, valueset, preferred_element_type=jnp.float32)
        return (mixture, logsums)

    mixture, logsums = lax.map(
        one_block,
        (
            queries.reshape(blocks, block_rows, head_count, head_width),
            segments.reshape(blocks, block_rows),
        ),
    )
    return (mixture.reshape(length, head_count * head_width), logsums)


def attend_backward(queries, keys_in, values_in, grads_in, segments, logsums, head_count):
    length = queries.shape[0]
    head_width = queries.shape[1] // head_count
    block_rows = min(512, length)
    blocks = length // block_rows
    keyset = keys_in.reshape(length, head_count, head_width)
    valueset = values_in.reshape(length, head_count, head_width)
    factor = head_width ** (-0.5)

    def one_block(carry, pieces):
        key_grad, value_grad = carry
        query_rows, block_segs, grad_rows, block_lse = pieces
        scores = (
            jnp.einsum("qhd,khd->hqk", query_rows, keyset, preferred_element_type=jnp.float32)
            * factor
        )
        scores = jnp.where((block_segs[:, None] == segments[None, :])[None], scores, MASKED_SCORE)
        weights = jnp.exp(scores - block_lse)
        value_grad = value_grad + jnp.einsum(
            "hqk,qhd->khd",
            weights.astype(jnp.bfloat16),
            grad_rows,
            preferred_element_type=jnp.float32,
        )
        grad_weights = jnp.einsum(
            "qhd,khd->hqk", grad_rows, valueset, preferred_element_type=jnp.float32
        )
        centre = jnp.sum(weights * grad_weights, axis=-1, keepdims=True)
        grad_scores = (weights * (grad_weights - centre)).astype(jnp.bfloat16)
        query_grad = (
            jnp.einsum("hqk,khd->qhd", grad_scores, keyset, preferred_element_type=jnp.float32)
            * factor
        )
        key_grad = (
            key_grad
            + jnp.einsum(
                "hqk,qhd->khd", grad_scores, query_rows, preferred_element_type=jnp.float32
            )
            * factor
        )
        return ((key_grad, value_grad), query_grad)

    empty = jnp.zeros((length, head_count, head_width), jnp.float32)
    pieces = (
        queries.reshape(blocks, block_rows, head_count, head_width),
        segments.reshape(blocks, block_rows),
        grads_in.reshape(blocks, block_rows, head_count, head_width),
        logsums,
    )
    (key_grad, value_grad), query_grad = lax.scan(one_block, (empty, empty), pieces)
    flat_shape = (length, head_count * head_width)
    return (
        query_grad.reshape(flat_shape).astype(jnp.bfloat16),
        key_grad.reshape(flat_shape).astype(jnp.bfloat16),
        value_grad.reshape(flat_shape).astype(jnp.bfloat16),
    )


def shards(
    tokens,
    cotangent,
    doc_starts,
    qkv_weight,
    out_weight,
    in_weight,
    down_weight,
    attn_gain,
    ffn_gain,
):
    micro_count = tokens.shape[0]
    token_rows = tokens.shape[2]
    model_width = tokens.shape[3]
    seq_count = lax.axis_size("seq")
    head_count = HEADS // seq_count
    places = lax.axis_index("seq") * token_rows + jnp.arange(token_rows, dtype=jnp.int32)
    everywhere = jnp.arange(token_rows * seq_count, dtype=jnp.int32)
    outputs = []
    input_grads = []
    full_terms = None
    shard_terms = None
    for micro_step in range(micro_count):
        rows_in = tokens[micro_step, 0]
        starts = doc_starts[micro_step, 0]
        cosine_table, sine_table = rope_tables(starts, places, HEAD_DIM)
        segments = segment_ids(starts, everywhere)
        attn_set = (
            lax.all_gather(qkv_weight, "fsdp", axis=0, tiled=True),
            lax.all_gather(out_weight, "fsdp", axis=0, tiled=True),
            lax.all_gather(attn_gain, "fsdp", axis=0, tiled=True),
        )
        qkv_full, out_full, gain_one = attn_set
        normed, norm_back = jax.vjp(layer_norm, rows_in, gain_one.astype(jnp.float32))
        normed_low = normed.astype(jnp.bfloat16)
        qkv_rows = jnp.dot(normed_low, qkv_full, preferred_element_type=jnp.float32)
        turned, turn_back = jax.vjp(
            partial(turn_pair, cosine_table=cosine_table, sine_table=sine_table),
            qkv_rows[:, : 2 * model_width],
        )
        queries = turned[:, :model_width].astype(jnp.bfloat16)
        keyset = turned[:, model_width:].astype(jnp.bfloat16)
        valueset = qkv_rows[:, 2 * model_width :].astype(jnp.bfloat16)
        query_heads, key_heads, value_heads = (
            lax.all_to_all(queries, "seq", split_axis=1, concat_axis=0, tiled=True),
            lax.all_to_all(keyset, "seq", split_axis=1, concat_axis=0, tiled=True),
            lax.all_to_all(valueset, "seq", split_axis=1, concat_axis=0, tiled=True),
        )
        mixture, logsums = attend_forward(query_heads, key_heads, value_heads, segments, head_count)
        mixture_rows = lax.all_to_all(
            mixture.astype(jnp.bfloat16), "seq", split_axis=0, concat_axis=1, tiled=True
        )
        middle = rows_in + jnp.dot(mixture_rows, out_full, preferred_element_type=jnp.float32)
        ffn_set = (
            lax.all_gather(in_weight, "fsdp", axis=0, tiled=True),
            lax.all_gather(down_weight, "fsdp", axis=0, tiled=True),
            lax.all_gather(ffn_gain, "fsdp", axis=0, tiled=True),
        )
        in_full, down_full, gain_two = ffn_set
        normed_two, norm_back_two = jax.vjp(layer_norm, middle, gain_two.astype(jnp.float32))
        normed_two_low = normed_two.astype(jnp.bfloat16)
        joined = jnp.dot(normed_two_low, in_full, preferred_element_type=jnp.float32)
        active, gelu_back = jax.vjp(gated_gelu, joined)
        active_low = active.astype(jnp.bfloat16)
        outputs.append(middle + jnp.dot(active_low, down_full, preferred_element_type=jnp.float32))
        grad_out = cotangent[micro_step, 0]
        grad_low = grad_out.astype(jnp.bfloat16)
        ffn_set = (
            lax.all_gather(in_weight, "fsdp", axis=0, tiled=True),
            lax.all_gather(down_weight, "fsdp", axis=0, tiled=True),
            lax.all_gather(ffn_gain, "fsdp", axis=0, tiled=True),
        )
        in_full, down_full, gain_two = ffn_set
        down_term = jnp.dot(active_low.T, grad_low, preferred_element_type=jnp.float32)
        grad_active = jnp.dot(grad_low, down_full.T, preferred_element_type=jnp.float32)
        grad_joined = gelu_back(grad_active)[0].astype(jnp.bfloat16)
        in_term = jnp.dot(normed_two_low.T, grad_joined, preferred_element_type=jnp.float32)
        grad_normed_two = jnp.dot(grad_joined, in_full.T, preferred_element_type=jnp.float32)
        grad_middle_norm, gain_two_term = norm_back_two(grad_normed_two)
        grad_middle = grad_out + grad_middle_norm
        grad_mid_low = grad_middle.astype(jnp.bfloat16)
        attn_set = (
            lax.all_gather(qkv_weight, "fsdp", axis=0, tiled=True),
            lax.all_gather(out_weight, "fsdp", axis=0, tiled=True),
            lax.all_gather(attn_gain, "fsdp", axis=0, tiled=True),
        )
        qkv_full, out_full, gain_one = attn_set
        out_term = jnp.dot(mixture_rows.T, grad_mid_low, preferred_element_type=jnp.float32)
        grad_mixture = jnp.dot(grad_mid_low, out_full.T, preferred_element_type=jnp.float32).astype(
            jnp.bfloat16
        )
        grad_heads = lax.all_to_all(grad_mixture, "seq", split_axis=1, concat_axis=0, tiled=True)
        query_grad, key_grad, value_grad = attend_backward(
            query_heads, key_heads, value_heads, grad_heads, segments, logsums, head_count
        )
        query_back, key_back, value_back = (
            lax.all_to_all(query_grad, "seq", split_axis=0, concat_axis=1, tiled=True),
            lax.all_to_all(key_grad, "seq", split_axis=0, concat_axis=1, tiled=True),
            lax.all_to_all(value_grad, "seq", split_axis=0, concat_axis=1, tiled=True),
        )
        grad_pair = turn_back(jnp.concatenate([query_back, key_back], axis=1).astype(jnp.float32))[
            0
        ]
        grad_qkv = jnp.concatenate([grad_pair, value_back.astype(jnp.float32)], axis=1).astype(
            jnp.bfloat16
        )
        qkv_term = jnp.dot(normed_low.T, grad_qkv, preferred_element_type=jnp.float32)
        grad_normed = jnp.dot(grad_qkv, qkv_full.T, preferred_element_type=jnp.float32)
        grad_rows_norm, gain_one_term = norm_back(grad_normed)
        input_grads.append(grad_middle + grad_rows_norm)
        terms = (qkv_term, out_term, in_term, down_term, gain_one_term, gain_two_term)
        full_terms = terms if full_terms is None else jax.tree.map(jnp.add, full_terms, terms)
    shard_terms = jax.tree.map(
        lambda part: part.astype(jnp.float32),
        lax.psum_scatter(as_sent(full_terms), "fsdp", scatter_dimension=0, tiled=True),
    )
    totals = jax.tree.map(
        lambda part: part.astype(jnp.float32), lax.psum(as_sent(shard_terms), "seq")
    )
    return (
        jnp.stack(outputs)[:, None],
        jnp.stack(input_grads)[:, None],
        totals[0],
        totals[1],
        totals[2],
        totals[3],
        totals[4],
        totals[5],
    )


MESH = pl.DeviceIdType.MESH
ANY = pl.BlockSpec(memory_space=pl.ANY)
VMEM_BYTES = 63 * 2**20
BF = jnp.bfloat16
F32 = jnp.float32


def nn(a, b):
    return lax.dot_general(a, b, (((1,), (0,)), ((), ())), preferred_element_type=F32)


def nt(a, b):
    return lax.dot_general(a, b, (((1,), (1,)), ((), ())), preferred_element_type=F32)


def spot():
    z, f = lax.axis_index("seq"), lax.axis_index("fsdp")
    core = lax.rem(f, 2)
    x = lax.rem(f // 2, 2)
    y = f // 4
    return z, f, y, x, core


def remote(src, dst, send, recv, where):
    return pltpu.make_async_remote_copy(
        src_ref=src, dst_ref=dst, send_sem=send, recv_sem=recv, device_id=where, device_id_type=MESH
    )


class Rows:
    def __init__(self, z, f, core):
        base = f - core
        self.work, self.home = [], []
        for i in range(2):
            zw, cw = 2 * i + core, z // 2
            self.work.append((zw, base + cw, (zw == z) & (cw == core)))
            zh, ch = 2 * core + i, lax.rem(z, 2)
            self.home.append((zh, base + ch, (zh == z) & (ch == core)))
        self.z = z

    def greet(self, barrier):
        count = 0
        for zt, ft, same in self.work + self.home:

            @pl.when(jnp.logical_not(same))
            def _():
                pl.semaphore_signal(barrier, inc=1, device_id=(zt, ft), device_id_type=MESH)

            count = count + jnp.where(same, 0, 1)
        return count

    def start(self, src, dst, send, recv, local, out, piece=slice(None)):
        places = self.work if out else self.home
        slot = lax.rem(self.z, 2) if out else self.z // 2
        for i, (zt, ft, same) in enumerate(places):

            @pl.when(same)
            def _(i=i):
                pltpu.make_async_copy(src.at[i, piece], dst.at[slot, piece], local).start()

            @pl.when(jnp.logical_not(same))
            def _(i=i, zt=zt, ft=ft):
                remote(src.at[i, piece], dst.at[slot, piece], send.at[i], recv.at[slot], (zt, ft)).start()

    def wait(self, src, dst, send, recv, local, out):
        goes, comes = (self.work, self.home) if out else (self.home, self.work)
        for i, (zt, ft, same) in enumerate(goes):

            @pl.when(same)
            def _(i=i):
                pltpu.make_async_copy(src.at[i], dst.at[i], local).wait()

            @pl.when(jnp.logical_not(same))
            def _(i=i, zt=zt, ft=ft):
                remote(src.at[i], dst.at[i], send.at[i], recv.at[i], (zt, ft)).wait_send()

        for i, (zt, ft, same) in enumerate(comes):

            @pl.when(jnp.logical_not(same))
            def _(i=i, zt=zt, ft=ft):
                remote(src.at[i], dst.at[i], send.at[i], recv.at[i], (zt, ft)).wait_recv()


def halves(width):
    cut = (width // 128 // 2) * 128
    return pl.ds(0, cut), pl.ds(cut, width - cut)


def gather_kernel(*refs):
    shards, (tok, cot, starts) = refs[:5], refs[5:8]
    wholes, (tok_o, cot_o, starts_o) = refs[8:13], refs[13:16]
    ss, rs, ls, es, er, el, ds_, dr = refs[16:24]
    held = refs[24:]
    z, f, y, x, core = spot()
    fx, fy, fc = f + 2 - 4 * x, f + 4 - 8 * y, f + 1 - 2 * core
    fd = fx + 4 - 8 * y
    rows = Rows(z, f, core)
    barrier = pltpu.get_barrier_semaphore()
    for t in (fx, fy, fc):
        pl.semaphore_signal(barrier, inc=1, device_id=(z, t), device_id_type=MESH)
    pl.semaphore_wait(barrier, rows.greet(barrier) + 3)

    def copies(w):
        whole, shard = wholes[w], shards[w]
        first, second = halves(shard.shape[1])
        same = lambda i, cols=None: whole.at[i] if cols is None else whole.at[i, :, cols]
        plan = [
            (shard, whole.at[f], fx),
            (shard, whole.at[f], fy),
            (shard, whole.at[f], fc),
            (same(fx, first), same(fx, first), fy),
            (same(fy, second), same(fy, second), fx),
            (same(fx), same(fx), fc),
            (same(fy), same(fy), fc),
            (same(fd, first), same(fd, first), fc),
            (same(fd, second), same(fd, second), fc),
        ]
        return [
            remote(s, d, ss.at[w, k], rs.at[w, k], (z, t)) for k, (s, d, t) in enumerate(plan)
        ]

    every = [copies(w) for w in range(5)]
    info = remote(starts, starts_o.at[core], ds_.at[0], dr.at[0], (z, fc))
    info.start()
    own_info = pltpu.make_async_copy(starts, starts_o.at[core], el.at[2])
    own_info.start()
    rows.start(tok, tok_o, es.at[0], er.at[0], el.at[0], True)
    for w in range(5):
        for k in range(3):
            every[w][k].start()
        pltpu.make_async_copy(shards[w], held[w], ls.at[w]).start()
    rows.start(cot, cot_o, es.at[1], er.at[1], el.at[1], True)
    for w in range(5):
        pltpu.make_async_copy(shards[w], held[w], ls.at[w]).wait()
        pltpu.make_async_copy(held[w], wholes[w].at[f], ls.at[w]).start()
    for w in range(5):
        every[w][0].wait_recv()
        every[w][3].start()
        every[w][5].start()
        every[w][1].wait_recv()
        every[w][4].start()
        every[w][6].start()
    for w in range(5):
        for k in (3, 4):
            every[w][k].wait_recv()
            every[w][k + 4].start()
    for w in range(5):
        for k in (2, 5, 6, 7, 8):
            every[w][k].wait_recv()
        for k in range(9):
            every[w][k].wait_send()
        pltpu.make_async_copy(held[w], wholes[w].at[f], ls.at[w]).wait()
    rows.wait(tok, tok_o, es.at[0], er.at[0], el.at[0], True)
    rows.wait(cot, cot_o, es.at[1], er.at[1], el.at[1], True)
    info.wait()
    own_info.wait()


def gather_all(shards, tok, cot, starts):
    dma = pltpu.SemaphoreType.DMA
    out_shape = [jax.ShapeDtypeStruct((8,) + s.shape, s.dtype) for s in shards] + [
        jax.ShapeDtypeStruct(tok.shape, tok.dtype),
        jax.ShapeDtypeStruct(cot.shape, cot.dtype),
        jax.ShapeDtypeStruct((2,) + starts.shape, starts.dtype),
    ]
    return pl.pallas_call(
        gather_kernel,
        out_shape=out_shape,
        in_specs=[ANY] * 8,
        out_specs=[ANY] * 8,
        scratch_shapes=[
            dma((5, 9)), dma((5, 9)), dma((5,)), dma((2, 2)), dma((2, 2)), dma((3,)), dma((1,)), dma((1,)),
        ]
        + [pltpu.VMEM(s.shape, s.dtype) for s in shards],
        compiler_params=pltpu.CompilerParams(collective_id=1, has_side_effects=True, vmem_limit_bytes=VMEM_BYTES),
        name="gather_weights_and_rows",
    )(*shards, tok, cot, starts)


def attention_kernel(q_ref, k_ref, v_ref, bias_ref, o_ref, lse_ref):
    q = q_ref[...] * jnp.asarray(0.125, BF)
    k = k_ref[...]
    lane = lax.broadcasted_iota(jnp.int32, (1, 128), 1)
    vt = v_ref[...].T
    outs = []
    for h in range(2):
        mine = (lane < 64) if h == 0 else (lane >= 64)
        scores = nt(k, jnp.where(mine, q, jnp.zeros_like(q))) + bias_ref[...]
        top = jnp.max(scores, axis=0, keepdims=True)
        p = jnp.exp(scores - top)
        total = jnp.sum(p, axis=0, keepdims=True)
        outs.append(nn(vt, p.astype(BF)) / total)
        lse_ref[0, h : h + 1, :] = top + jnp.log(total)
    o_ref[...] = jnp.concatenate([outs[0][:64], outs[1][64:]], axis=0).T.astype(BF)


def attention(q, k, v, bias):
    rows, keys = q.shape[0], k.shape[0]
    narrow = pl.BlockSpec((rows, 128), lambda i: (0, i))
    long = pl.BlockSpec((keys, 128), lambda i: (0, i))
    return pl.pallas_call(
        attention_kernel,
        grid=(q.shape[1] // 128,),
        in_specs=[narrow, long, long, pl.BlockSpec((keys, rows), lambda i: (0, 0))],
        out_specs=[narrow, pl.BlockSpec((1, 2, rows), lambda i: (i, 0, 0))],
        out_shape=[
            jax.ShapeDtypeStruct(q.shape, BF),
            jax.ShapeDtypeStruct((q.shape[1] // 128, 2, rows), F32),
        ],
        compiler_params=pltpu.CompilerParams(vmem_limit_bytes=VMEM_BYTES),
        name="attention",
    )(q, k, v, bias)


def turn_rows(values, cosine, sine, back):
    shaped = values.reshape(values.shape[0], -1, HEAD_DIM)
    if back:
        g = shaped * sine
        half = HEAD_DIM // 2
        turned = jnp.concatenate([g[..., half:], -g[..., :half]], axis=-1)
        return (shaped * cosine + turned).reshape(values.shape)
    return rotate(shaped, cosine, sine).reshape(values.shape)


def swap(value):
    return lax.ppermute(value, "fsdp", [(i, i ^ 1) for i in range(lax.axis_size("fsdp"))])


SQRT_HALF = 0.7071067811865476
DENSITY = 0.3989422804014327
PIECES = 8
GROUP = 384
STEPS = 7


def moments(values):
    average = jnp.mean(values, axis=-1, keepdims=True)
    centred = values - average
    spread = jnp.mean(centred * centred, axis=-1, keepdims=True)
    scale = lax.rsqrt(spread + EPSILON)
    return centred * scale, scale


def norm_back(values, gain, grads):
    unit, scale = moments(values)
    spread = grads * gain
    inner = spread - jnp.mean(spread, axis=-1, keepdims=True)
    inner = inner - unit * jnp.mean(spread * unit, axis=-1, keepdims=True)
    return inner * scale, jnp.sum(grads * unit, axis=0, keepdims=True)


def rope_back(grads, cosine, sine):
    lane = lax.broadcasted_iota(jnp.int32, (1, 128), 1)
    low = lax.rem(lane, 64) < 32
    u = grads * sine
    return grads * cosine + jnp.where(low, pltpu.roll(u, 96, 1), -pltpu.roll(u, 32, 1))


class Sums:
    KINDS = 9

    @staticmethod
    def scratch(count, slots, rows, wide):
        dma = pltpu.SemaphoreType.DMA((count, Sums.KINDS))
        shapes = [(slots, 2, 2, 2), (count, 2, 2), (count, 2), (count, 2), (count,)]
        return [pltpu.VMEM(s + (rows, wide), BF) for s in shapes] + [dma, dma]

    def __init__(self, here, count, slots, refs):
        self.here, self.count, self.slots = here, count, slots
        self.acc, self.rx, self.r2, self.zr, self.zr2, self.send, self.recv = refs

    def copy(self, t, kind):
        h = self.here
        acc = self.acc.at[lax.rem(t, self.slots)]
        plan = {
            0: lambda: (acc.at[0, :, 1 - h.x], self.rx.at[t, 0], (h.z, h.fx)),
            1: lambda: (acc.at[1, 1 - h.y], self.rx.at[t, 1], (h.z, h.fy)),
            2: lambda: (self.rx.at[t, 0, 1 - h.y], self.r2.at[t, 0], (h.z, h.fy)),
            3: lambda: (self.rx.at[t, 1, 1 - h.x], self.r2.at[t, 1], (h.z, h.fx)),
            4: lambda: (self.r2.at[t], self.zr.at[t], (h.near, h.f)),
            5: lambda: (self.zr.at[t, 1 - h.own], self.zr2.at[t], (h.across, h.f)),
            6: lambda: (self.r2.at[t, h.own], self.r2.at[t, h.own], (h.across, h.f)),
            7: lambda: (self.r2.at[t, h.own], self.zr.at[t, h.own], (h.near, h.f)),
            8: lambda: (self.r2.at[t, 1 - h.own], self.zr.at[t, 1 - h.own], (h.near, h.f)),
        }
        src, dst, where = plan[kind]()
        return remote(src, dst, self.send.at[t, kind], self.recv.at[t, kind], where)

    def begin(self, t):
        self.copy(t, 0).start()
        self.copy(t, 1).start()

    def cross(self, t):
        h, s = self.here, lax.rem(t, self.slots)
        self.copy(t, 0).wait()
        self.rx[t, 0, 1 - h.y] = added(self.rx[t, 0, 1 - h.y], self.acc[s, 0, 1 - h.y, h.x])
        self.copy(t, 2).start()
        self.copy(t, 1).wait()
        self.rx[t, 1, 1 - h.x] = added(self.rx[t, 1, 1 - h.x], self.acc[s, 1, h.y, 1 - h.x])
        self.copy(t, 3).start()

    def plane(self, t):
        h, s = self.here, lax.rem(t, self.slots)
        self.copy(t, 2).wait()
        self.r2[t, 0] = added(self.r2[t, 0], self.rx[t, 0, h.y], self.acc[s, 0, h.y, h.x])
        self.copy(t, 3).wait()
        self.r2[t, 1] = added(self.r2[t, 1], self.rx[t, 1, h.x], self.acc[s, 1, h.y, h.x])

        @pl.when(h.outer)
        def _():
            self.copy(t, 4).start()

    def meet(self, t):
        h = self.here

        @pl.when(jnp.logical_not(h.outer))
        def _():
            self.copy(t, 4).wait_recv()
            self.zr[t, 1 - h.own] = added(self.zr[t, 1 - h.own], self.r2[t, 1 - h.own])
            self.copy(t, 5).start()

    def sums(self, t):
        h = self.here

        @pl.when(jnp.logical_not(h.outer))
        def _():
            self.copy(t, 5).wait()
            self.r2[t, h.own] = added(self.r2[t, h.own], self.zr[t, h.own], self.zr2[t])
            self.copy(t, 6).start()
            self.copy(t, 7).start()

    def spread(self, t):
        @pl.when(jnp.logical_not(self.here.outer))
        def _():
            self.copy(t, 6).wait_recv()
            self.copy(t, 8).start()

    def finish(self, t):
        @pl.when(jnp.logical_not(self.here.outer))
        def _():
            self.copy(t, 6).wait_send()
            self.copy(t, 7).wait_send()
            self.copy(t, 8).wait_send()

        @pl.when(self.here.outer)
        def _():
            self.copy(t, 4).wait_send()
            self.copy(t, 7).wait_recv()
            self.copy(t, 8).wait_recv()

    def total(self, act):
        for ref, there in ((self.zr, self.here.outer), (self.r2, jnp.logical_not(self.here.outer))):
            pl.when(there)(functools.partial(act, ref))

    LATER = (("finish", 9), ("spread", 8), ("sums", 7), ("meet", 6), ("plane", 4), ("cross", 2))
    LAST = 9

    def pump(self, tick, low, high, first, last, base):
        for name, stage in self.LATER:
            if high - base - stage < first or low - base - stage >= last:
                continue
            t = tick - base - stage
            if low == high:
                getattr(self, name)(t)
            else:

                @pl.when((t >= first) & (t < last))
                def _(name=name, t=t):
                    getattr(self, name)(t)


def added(*terms):
    total = terms[0].astype(F32)
    for term in terms[1:]:
        total = total + term.astype(F32)
    return total.astype(BF)


class Halves:
    def __init__(self, ref):
        self.ref, self.at, self.size = ref, self, ref.shape[0] // 2

    def __getitem__(self, index):
        return self.ref.at[pl.ds((index[0] if isinstance(index, tuple) else index) * self.size, self.size)]


class Here:
    def __init__(self):
        self.z, self.f, self.y, self.x, self.core = spot()
        self.fx = self.f + 2 - 4 * self.x
        self.fy = self.f + 4 - 8 * self.y
        self.fc = self.f + 1 - 2 * self.core
        z = self.z
        self.outer = (z == 0) | (z == 3)
        self.near = jnp.where(z < 2, 1 - z, 5 - z)
        self.across = jnp.where(self.outer, z, 3 - z)
        self.own = jnp.where(z < 2, 0, 1)

    def greet(self, barrier, rows):
        for t in (self.fx, self.fy, self.fc):
            pl.semaphore_signal(barrier, inc=1, device_id=(self.z, t), device_id_type=MESH)
        pl.semaphore_signal(barrier, inc=1, device_id=(self.near, self.f), device_id_type=MESH)

        @pl.when(jnp.logical_not(self.outer))
        def _():
            pl.semaphore_signal(barrier, inc=1, device_id=(self.across, self.f), device_id_type=MESH)

        pl.semaphore_wait(barrier, rows.greet(barrier) + 4 + jnp.where(self.outer, 0, 1))


def lanes(start, size):
    return pl.ds(start if isinstance(start, int) else pl.multiple_of(start, 128), size)


def back_kernel(
    x2_h, mid_h, cot_h, in_h, down_h, qkv_h, out_h, q_h, k_h, v_h, mix_h, normed_h, rows_h, bias_h,
    gains, cosine, sine, lse,
    wide_o, down_o, out_o, gain_o, outh_o, inh_o,
    x2, gl, acc_f, acc_g, win, wdown, xt, xts, gj, at, glc, gm, mt, dout, bias,
    kept, dx_kv, centres, terms_one, rows_b, dx, gs, gr,
    ld, wsem, ps, pr, gjs, gjr, ats, atr, kvs, kvr, gqs, gqr, dxs, dxr, fo, es, er, el,
    *sum_refs,
):
    h = Here()
    rows = Rows(h.z, h.f, h.core)
    wide = Sums(h, 11, 4, sum_refs[0:7])
    down = Sums(h, 2, 2, sum_refs[7:14])
    outs = Sums(h, 1, 1, sum_refs[14:21])
    gain = Sums(h, 1, 1, sum_refs[21:28])
    sib = (h.z, h.fc)

    def output_piece(n):
        size = half // 2 // PIECES
        piece = pl.ds(n * size if isinstance(n, int) else pl.multiple_of(n * size, size), size)
        rows.start(rows_b, outh_o, es.at[0], er.at[0], el.at[0], False, piece)

    def advance(tick, low, high):
        wide.pump(tick, low, high, 0, STEPS, 1)
        down.pump(tick, low, high, 0, 2, 8)
        outs.pump(tick, low, high, 0, 1, 11)
        wide.pump(tick, low, high, 7, 11, 7)
        gain.pump(tick, low, high, 0, 1, 18)

    gq = gj
    last_b = Halves(dout)
    mine = dout.at[:, pl.ds(0, 512)]
    wout = at.at[pl.ds(0, 1024)]
    half = x2.shape[0]
    own_lanes = lambda i: lanes((2 * i + h.core) * 128, 128)
    sib_lanes = lambda i: lanes((2 * i + 1 - h.core) * 128, 128)

    def load(src, dst, k):
        return pltpu.make_async_copy(src, dst, ld.at[k])

    last_group = down_h.shape[0] - (STEPS - 1) * GROUP

    def weights(t, size):
        s = lax.rem(t, 2)
        return [
            pltpu.make_async_copy(in_h.at[:, :, lanes(t * 768, 768)], win.at[s], wsem.at[s, 0]),
            pltpu.make_async_copy(down_h.at[pl.ds(pl.multiple_of(t * GROUP, 16), size)], wdown.at[s, pl.ds(0, size)], wsem.at[s, 1]),
        ]

    def each(t, act):
        @pl.when(t < STEPS - 1)
        def _():
            for c in weights(t, GROUP):
                act(c)

        @pl.when(t == STEPS - 1)
        def _():
            for c in weights(t, last_group):
                act(c)

    def qkv_weights(i):
        s = lax.rem(i, 2)
        return pltpu.make_async_copy(qkv_h.at[:, :, lanes(i * 768, 768)], win.at[s], wsem.at[s, 0])

    first = [load(x2_h, x2, 0), load(cot_h, gl, 1), load(mid_h, acc_f, 2)]
    for c in first + weights(0, GROUP):
        c.start()
    h.greet(pltpu.get_barrier_semaphore(), rows)

    first[0].wait()
    first[1].wait()
    glc_send = remote(mine, glc.at[pl.ds(half, half)], ps.at[0], pr.at[0], sib)
    glc[:half] = gl[:, lanes(h.core * 512, 512)]
    mine[...] = gl[:, lanes((1 - h.core) * 512, 512)]
    glc_send.start()

    def transpose_out(src):
        for i in range(4):
            xt_rows = pl.ds(i * 128, 128)
            yield xt_rows, src[:, own_lanes(i)].T, src[:, sib_lanes(i)].T

    for at_rows, a, b in transpose_out(x2):
        xt[at_rows, :half] = a
        xts[at_rows] = b
    xt_send = remote(xts, xt.at[:, pl.ds(half, half)], ps.at[1], pr.at[1], sib)
    xt_send.start()
    first[2].wait()

    def gj_send(t):
        s = lax.rem(t, 2)
        return remote(gj.at[s, pl.ds(0, half)], gj.at[s, pl.ds(half, half)], gjs.at[s], gjr.at[s], sib)

    def at_send(t):
        r = pl.ds(pl.multiple_of(t * GROUP, 128), GROUP)
        return remote(at.at[r, pl.ds(0, half)], at.at[r, pl.ds(half, half)], ats.at[t], atr.at[t], sib)

    def feed(t, _):
        s = lax.rem(t, 2)
        advance(t, 0, STEPS)

        @pl.when(t < STEPS)
        def _():
            each(t, lambda c: c.wait())
            each(t + 1, lambda c: c.start())

            w = win[s].reshape(8 * 128, 768)
            wa, wc, wd = w[:, :GROUP], w[:, GROUP:], wdown[s]
            a, c = nn(x2[...], wa), nn(x2[...], wc)
            grad_active = nt(gl[...], wd)
            phi = 0.5 * (1.0 + lax.erf(a * SQRT_HALF))
            gate = a * phi
            slope = phi + a * (jnp.exp(-0.5 * a * a) * DENSITY)
            active = (gate * c).astype(BF)
            ga = (slope * c * grad_active).astype(BF)
            gc = (gate * grad_active).astype(BF)

            @pl.when(t >= 2)
            def _():
                gj_send(t - 2).wait_send()

            gj[s, :half, :GROUP] = ga
            gj[s, :half, GROUP:] = gc
            at[pl.ds(pl.multiple_of(t * GROUP, 128), GROUP), :half] = active.T
            at_send(t).start()
            acc_f[...] += nn(active, wd)
            back = nt(ga, wa) + nt(gc, wc)

            @pl.when(t == 0)
            def _():
                acc_g[...] = back

            @pl.when(t > 0)
            def _():
                acc_g[...] += back

        @pl.when(t == 1)
        def _():
            xt_send.wait()

        @pl.when(t >= 1)
        def _():
            u = t - 1
            gj_send(u).wait_recv()
            term = nn(xt[...], gj[lax.rem(u, 2)]).astype(BF)
            for o in range(4):
                for k in range(2):
                    wide.acc[lax.rem(u, 4), k, o // 2, o % 2] = term[o * 128 : o * 128 + 128, k * GROUP : k * GROUP + GROUP]
            wide.begin(u)

        @pl.when(t < STEPS)
        def _():
            gj_send(t).start()

        return 0

    lax.fori_loop(0, STEPS + 1, feed, 0)
    gj_send(STEPS - 2).wait_send()
    gj_send(STEPS - 1).wait_send()

    rows_b[...] = acc_f[...].astype(BF).reshape(2, half // 2, -1)
    again = [load(mid_h, acc_f, 2), load(mix_h, x2, 3), load(out_h, wout, 4), load(normed_h, x2, 0), load(bias_h, bias, 5)]
    for n in (0, 1, 4):
        again[n].start()
    for t in range(STEPS):
        at_send(t).wait()
    glc_send.wait()
    for j in range(2):
        term = nn(at[...], glc[:, j * 256 : j * 256 + 256])
        for f in range(8):
            down.acc[j, f % 2, f // 4, f // 2 % 2] = term[f * 328 : f * 328 + 336].astype(BF)
        down.begin(j)
        advance(8 + j, 8 + j, 8 + j)
    again[2].start()
    heads = [load(k_h, at.at[pl.ds(2 * half, 2 * half)], 6), load(q_h, at.at[pl.ds(4 * half, half)], 8), load(v_h, at.at[pl.ds(0, 2 * half)], 7)]
    heads[0].start()
    heads[1].start()

    again[0].wait()
    back, gain_two = norm_back(acc_f[...], gains[1:2], acc_g[...])
    grad_mid = gl[...].astype(F32) + back
    acc_f[...] = grad_mid
    gm[:half] = grad_mid.astype(BF)
    gm_send = remote(gm.at[pl.ds(0, half)], gm.at[pl.ds(half, half)], ps.at[2], pr.at[2], sib)
    gm_send.start()
    again[1].wait()
    for at_rows, a, b in transpose_out(x2):
        mt[at_rows, :half] = a
        xts[at_rows] = b
    mt_send = remote(xts, mt.at[:, pl.ds(half, half)], ps.at[3], pr.at[3], sib)
    mt_send.start()
    rows_in = load(rows_h, gl, 1)
    rows_in.start()
    output_piece(0)
    advance(10, 10, 10)
    again[2].wait()
    dout[...] = nt(gm[:half], wout[...]).astype(BF)
    heads[2].start()
    for j in range(8):
        products = (x2[:, j * 128 : j * 128 + 128].astype(F32) * dout[:, j * 128 : j * 128 + 128].astype(F32)).T
        for e in range(2):
            centres[j, e : e + 1] = jnp.sum(products[64 * e : 64 * e + 64], axis=0, keepdims=True)
    again[3].start()
    gm_send.wait()
    mt_send.wait()
    term = nn(mt[...], gm[...]).astype(BF)
    for o in range(4):
        for k in range(2):
            outs.acc[0, k, o // 2, o % 2] = term[o * 128 : o * 128 + 128, k * 512 : k * 512 + 512]
    outs.begin(0)
    again[3].wait()
    for at_rows, a, b in transpose_out(x2):
        xt[at_rows, :half] = a
        xts[at_rows] = b
    nt_send = remote(xts, xt.at[:, pl.ds(half, half)], ps.at[4], pr.at[4], sib)
    nt_send.start()
    output_piece(1)
    advance(11, 11, 11)
    again[4].wait()
    for c in heads:
        c.wait()

    lane = lax.broadcasted_iota(jnp.int32, (1, 128), 1)

    def kv_rows(s):
        return pl.ds(s * half if isinstance(s, int) else pl.multiple_of(s * half, half), half)

    def kv_send(i):
        s = lax.rem(i, 2)
        return remote(dx_kv, glc.at[kv_rows(s)], kvs.at[s], kvr.at[s], sib)

    def gq_send(i):
        s = lax.rem(i, 2)
        return remote(gq.at[s, pl.ds(0, half)], gq.at[s, pl.ds(half, half)], gqs.at[s], gqr.at[s], sib)

    def stashed(b, n, j):
        return jnp.concatenate([kept[b, pl.ds(n * 128, 128), pl.ds(m * 256 + j * 128, 128)] for m in range(4)], axis=0)

    def attend_step(i, _):
        s = lax.rem(i, 2)
        tick = 12 + i
        output_piece(i + 2)
        advance(tick, 12, 17)

        @pl.when(i < 4)
        def _():
            qkv_weights(i).start()

            @pl.when(i >= 1)
            def _():
                kv_send(i - 1).wait_send()

            for j in range(2):
                col = lanes(i * 256 + j * 128, 128)
                q = at[pl.ds(4 * half, half), col] * jnp.asarray(0.125, BF)
                v, k = at[pl.ds(0, 2 * half), col], at[pl.ds(2 * half, 2 * half), col]
                do = dout[:, col]
                kt = k.T
                none = jnp.zeros_like(q)
                dqs, dks, dvs = [], [], []
                for e in range(2):
                    part = (lane < 64) if e == 0 else (lane >= 64)
                    centre = centres[2 * i + j, e : e + 1, :]
                    p = jnp.exp(nt(k, jnp.where(part, q, none)) + bias[...].astype(F32) - lse[2 * i + j, e : e + 1, :])
                    dvs.append(nn(p.astype(BF), do))
                    ds = (p * (nt(v, jnp.where(part, do, none)) - centre)).astype(BF)
                    dks.append(nn(ds, q))
                    dqs.append(nn(kt, ds))
                c = pl.ds(j * 128, 128)
                dq = jnp.concatenate([dqs[0][:64], dqs[1][64:]], axis=0).T
                dk = jnp.where(lane < 64, dks[0], dks[1]).astype(BF)
                dv = jnp.where(lane < 64, dvs[0], dvs[1]).astype(BF)
                for n, part in enumerate(((dq * 0.125).astype(BF), dk, dv)):
                    for m in range(4):
                        kept[s, pl.ds(n * 128, 128), pl.ds(m * 256 + j * 128, 128)] = part[m * 128 : m * 128 + 128]
                dx_kv[:, pl.ds(j * 128, 128)] = dk[half:]
                dx_kv[:, pl.ds(256 + j * 128, 128)] = dv[half:]

        @pl.when((i >= 1) & (i <= 4))
        def _():
            u = i - 1
            b = lax.rem(u, 2)

            @pl.when(u >= 2)
            def _():
                gq_send(u - 2).wait_send()

            kv_send(u).wait_recv()
            for j in range(2):
                c = slice(j * 128, j * 128 + 128)
                g = stashed(b, 0, j).astype(F32)
                gq[b, :half, j * 128 : j * 128 + 128] = rope_back(g, cosine[...], sine[...]).astype(BF)
                c = slice(256 + j * 128, 256 + j * 128 + 128)
                g = added(stashed(b, 1, j), glc[kv_rows(b), j * 128 : j * 128 + 128]).astype(F32)
                gq[b, :half, c] = rope_back(g, cosine[...], sine[...]).astype(BF)
                c = slice(512 + j * 128, 512 + j * 128 + 128)
                gq[b, :half, c] = added(stashed(b, 2, j), glc[kv_rows(b), 256 + j * 128 : 256 + j * 128 + 128])
            qkv_weights(u).wait()
            back = nt(gq[b, :half], win[b].reshape(1024, 768))

            @pl.when(u == 0)
            def _():
                acc_g[...] = back

            @pl.when(u > 0)
            def _():
                acc_g[...] += back

        @pl.when(i == 2)
        def _():
            nt_send.wait()

        @pl.when(i == 5)
        def _():
            rows_in.wait()
            back, gain_one = norm_back(gl[...].astype(F32), gains[0:1], acc_g[...])
            terms_one[...] = gain_one
            dout[...] = (acc_f[...] + back).astype(BF)
            rows.start(last_b, inh_o, es.at[1], er.at[1], el.at[1], False)

        @pl.when(i >= 2)
        def _():
            u = i - 2
            gq_send(u).wait_recv()
            term = nn(xt[...], gq[lax.rem(u, 2)]).astype(BF)
            a = lax.rem(u + 7, 4)
            for o in range(4):
                for k in range(2):
                    wide.acc[a, k, o // 2, o % 2] = term[o * 128 : o * 128 + 128, k * GROUP : k * GROUP + GROUP]
            wide.begin(u + 7)

        @pl.when(i < 4)
        def _():
            kv_send(i).start()

        @pl.when((i >= 1) & (i <= 4))
        def _():
            gq_send(i - 1).start()

        return 0

    lax.fori_loop(0, 6, attend_step, 0)

    gain_one = terms_one[...]
    terms = (gain_one, gain_two)
    for k in range(2):
        for o in range(4):
            for ref, part in ((gain.acc.at[0], h.core), (gs, 1 - h.core)):
                low, high = terms[k][:, 256 * o : 256 * o + 128], terms[k][:, 256 * o + 128 : 256 * o + 256]
                value = jnp.where(part == 0, low, high)
                ref[k, o // 2, o % 2] = jnp.broadcast_to(value, (16, 128)).astype(BF)
    gs_send = remote(gs, gr, ps.at[5], pr.at[5], sib)
    gs_send.start()
    advance(18, 18, 18)
    def down_swap(act, ref):
        for j in range(2):
            act(remote(ref.at[j, 1 - h.core], dx.at[j], dxs.at[j], dxr.at[j], sib))

    down.total(functools.partial(down_swap, lambda c: c.start()))
    gs_send.wait()
    for k in range(2):
        for o in range(4):
            gain.acc[0, k, o // 2, o % 2] = added(gain.acc[0, k, o // 2, o % 2], gr[k, o // 2, o % 2])
    gain.begin(0)
    for tick in range(19, 19 + Sums.LAST):
        advance(tick, tick, tick)
    down.total(functools.partial(down_swap, lambda c: c.wait()))
    kv_send(3).wait_send()
    gq_send(2).wait_send()
    gq_send(3).wait_send()

    def write(dst, k, act, ref):
        act(pltpu.make_async_copy(ref, dst, fo.at[k]))

    def write_down(act, ref):
        for j in range(2):
            act(pltpu.make_async_copy(ref.at[j, h.core], down_o.at[h.core, j], fo.at[3 + j]))
            act(pltpu.make_async_copy(dx.at[j], down_o.at[1 - h.core, j], fo.at[5 + j]))

    for act in (lambda c: c.start(), lambda c: c.wait()):
        for k, (group, dst) in enumerate(((wide, wide_o), (outs, out_o), (gain, gain_o))):
            group.total(functools.partial(write, dst, k, act))
        down.total(functools.partial(write_down, act))
    rows.wait(rows_b, outh_o, es.at[0], er.at[0], el.at[0], False)
    rows.wait(last_b, inh_o, es.at[1], er.at[1], el.at[1], False)


def back_all(x2, middle, cot, in_f, down_f, qkv_f, out_f, q, k, v, mixture, normed, rows_in, bias, gains, cosine, sine, lse):
    dma = pltpu.SemaphoreType.DMA
    half, wide = x2.shape

    def buf(*s, kind=BF):
        return pltpu.VMEM(s, kind)

    def shape(*s):
        return jax.ShapeDtypeStruct(s, BF)

    whole = pl.BlockSpec(memory_space=pltpu.VMEM)
    sums = [(11, 4, 128, GROUP), (2, 2, 336, 256), (1, 1, 128, 512), (1, 1, 16, 128)]
    scratch = [
        buf(half, wide), buf(half, wide), buf(half, wide, kind=F32), buf(half, wide, kind=F32),
        buf(2, 8, 128, 768), buf(2, GROUP, wide), buf(half, 2 * half), buf(half, half),
        buf(2, 2 * half, 768), buf(STEPS * GROUP, 2 * half), buf(2 * half, half),
        buf(2 * half, wide), buf(half, 2 * half), buf(half, wide),
        buf(2 * half, half),
        buf(2, GROUP, wide), buf(half, 512), buf(8, 2, half, kind=F32), buf(1, wide, kind=F32),
        buf(2, half // 2, wide), buf(2, 336, 256), buf(2, 2, 2, 16, 128), buf(2, 2, 2, 16, 128),
        dma((9,)), dma((2, 2)), dma((6,)), dma((6,)), dma((2,)), dma((2,)), dma((STEPS,)), dma((STEPS,)),
        dma((2,)), dma((2,)), dma((2,)), dma((2,)), dma((2,)), dma((2,)), dma((7,)),
        dma((2, 2)), dma((2, 2)), dma((2,)),
    ]
    for s in sums:
        scratch += Sums.scratch(*s)
    return pl.pallas_call(
        back_kernel,
        out_shape=[
            shape(11, 2, 128, GROUP), shape(2, 2, 336, 256), shape(1, 2, 128, 512), shape(1, 2, 16, 128),
            shape(2, half // 2, wide), shape(2, half // 2, wide),
        ],
        in_specs=[ANY] * 14 + [whole] * 4,
        out_specs=[ANY] * 6,
        scratch_shapes=scratch,
        compiler_params=pltpu.CompilerParams(collective_id=2, has_side_effects=True, vmem_limit_bytes=VMEM_BYTES),
        name="feed_forward_and_backward",
    )(x2, middle, cot, in_f, down_f, qkv_f, out_f, q, k, v, mixture, normed, rows_in, bias, gains, cosine, sine, lse)


def chip_streams(tokens, cotangent, doc_starts, qkv_weight, out_weight, in_weight, down_weight, attn_gain, ffn_gain):
    z, core = lax.axis_index("seq"), lax.axis_index("fsdp") % 2
    wide = tokens.shape[3]
    units = down_weight.shape[0] * 8
    extra = STEPS * GROUP - units
    gains = jnp.concatenate([attn_gain, ffn_gain])[None] + jnp.zeros((16, 1), BF)
    starts = jnp.zeros((8, 128), jnp.int32).at[:2, :8].set(doc_starts[:, 0])
    in_steps = jnp.pad(in_weight.reshape(-1, 2, units), ((0, 0), (0, 0), (0, extra)))
    in_steps = in_steps.reshape(-1, 2, STEPS, GROUP).swapaxes(1, 2).reshape(-1, 2 * STEPS * GROUP)
    qkv_steps = qkv_weight.reshape(-1, 3, 4, 256).swapaxes(1, 2).reshape(qkv_weight.shape)
    shards_in = (gains, qkv_steps, out_weight, in_steps, down_weight)
    gains_f, qkv_f, out_f, in_f, down_f, tok_r, cot_r, starts_r = gather_all(
        shards_in, tokens[:, 0].astype(BF), cotangent[:, 0].astype(BF), starts
    )
    gain_one = gains_f[:, 0, :128].reshape(wide).astype(F32)
    gain_two = gains_f[:, 0, 128:].reshape(wide).astype(F32)
    rows_low = tok_r.reshape(-1, wide)
    rows_in = rows_low.astype(F32)
    grad_low = cot_r.reshape(-1, wide)
    count = rows_in.shape[0]
    mine = starts_r[z % 2, z // 2, :8]
    here = core * count + jnp.arange(count, dtype=jnp.int32)
    there = (1 - core) * count + jnp.arange(count, dtype=jnp.int32)
    tables = rope_tables(mine, here, HEAD_DIM)
    cosine, sine = (t[:, None, :] for t in tables)
    seg_here, seg_there = segment_ids(mine, here), segment_ids(mine, there)
    bias = jnp.where(
        jnp.concatenate([seg_here, seg_there])[:, None] == seg_here[None, :], 0.0, MASKED_SCORE
    ).astype(F32)

    normed_low = layer_norm(rows_in, gain_one).astype(BF)
    qkv = nn(normed_low, qkv_f.reshape(wide, -1)).reshape(count, 4, 3, 256)
    q, k, v = (qkv[:, :, i].reshape(count, wide) for i in range(3))
    q = turn_rows(q, cosine, sine, False).astype(BF)
    k = turn_rows(k, cosine, sine, False).astype(BF)
    v = v.astype(BF)
    k_all = jnp.concatenate([k, swap(k)])
    v_all = jnp.concatenate([v, swap(v)])
    mixture, lse = attention(q, k_all, v_all, bias)
    middle = rows_in + nn(mixture, out_f.reshape(wide, wide))
    normed_two_low = layer_norm(middle, gain_two).astype(BF)
    wide_t, down_t, out_t, gain_t, out_home, in_home = back_all(
        normed_two_low, middle, grad_low, in_f, down_f.reshape(units, wide), qkv_f, out_f.reshape(wide, wide), q, k_all, v_all,
        mixture, normed_low, rows_low, bias.astype(BF), jnp.stack([gain_one, gain_two]),
        jnp.tile(tables[0], (1, 2)), jnp.tile(tables[1], (1, 2)), lse,
    )
    in_t = wide_t[:STEPS].transpose(2, 1, 0, 3).reshape(128, 2, STEPS * GROUP)[:, :, :units].astype(F32)
    qkv_t = wide_t[STEPS:].astype(F32).transpose(2, 0, 1, 3).reshape(128, 4, 3, 256)
    return (
        out_home[:, None].astype(F32),
        in_home[:, None].astype(F32),
        qkv_t.swapaxes(1, 2).reshape(qkv_weight.shape),
        out_t[0].astype(F32).swapaxes(0, 1).reshape(out_weight.shape),
        in_t.reshape(in_weight.shape),
        down_t[:, :, : down_weight.shape[0]].astype(F32).transpose(2, 0, 1, 3).reshape(down_weight.shape),
        gain_t[0, 0, 0].astype(F32),
        gain_t[0, 1, 0].astype(F32),
    )


def solution(mesh):
    whole_chips = dict(mesh.shape) == {"seq": 4, "fsdp": 8}
    return jax.shard_map(
        chip_streams if whole_chips else shards,
        mesh=mesh,
        in_specs=(
            P(None, "fsdp", "seq", None),
            P(None, "fsdp", "seq", None),
            P(None, "fsdp", None),
            P("fsdp", None),
            P("fsdp", None),
            P("fsdp", None),
            P("fsdp", None),
            P("fsdp"),
            P("fsdp"),
        ),
        out_specs=(
            P(None, "fsdp", "seq", None),
            P(None, "fsdp", "seq", None),
            P("fsdp", None),
            P("fsdp", None),
            P("fsdp", None),
            P("fsdp", None),
            P("fsdp"),
            P("fsdp"),
        ),
        check_vma=False,
    )
```

```python
import functools
from functools import partial

import jax
import jax.numpy as jnp
from jax import lax
from jax.experimental import pallas as pl
from jax.experimental.pallas import tpu as pltpu
from jax.sharding import PartitionSpec as P

HEADS = 16
HEAD_DIM = 64


EPSILON = 1e-05
ROPE_THETA = 160000.0
MASKED_SCORE = -1e30


def as_sent(x):

    def short(part):
        return part.astype(jnp.bfloat16) if part.dtype == jnp.float32 else part

    return jax.tree.map(short, x)


def layer_norm(values, norm_gain):
    average = jnp.mean(values, axis=-1, keepdims=True)
    centred = values - average
    spread = jnp.mean(centred * centred, axis=-1, keepdims=True)
    return centred * lax.rsqrt(spread + EPSILON) * norm_gain


def gated_gelu(joined):
    half_width = joined.shape[-1] // 2
    return jax.nn.gelu(joined[:, :half_width], approximate=False) * joined[:, half_width:]


def rotate(values, cosine_table, sine_table):
    half_width = values.shape[-1] // 2
    turned = jnp.concatenate([-values[..., half_width:], values[..., :half_width]], axis=-1)
    return values * cosine_table + turned * sine_table


def rope_tables(starts, places, head_width):
    preceding = starts[None, :] <= places[:, None]
    doc_begin = jnp.max(jnp.where(preceding, starts[None, :], 0), axis=-1)
    offsets = (places - doc_begin).astype(jnp.float32)
    inverse = ROPE_THETA ** (-jnp.arange(0, head_width, 2, dtype=jnp.float32) / head_width)
    angles = offsets[:, None] * inverse[None, :]
    angles = jnp.concatenate([angles, angles], axis=-1)
    return (jnp.cos(angles), jnp.sin(angles))


def segment_ids(starts, places):
    return jnp.sum((starts[None, :] <= places[:, None]).astype(jnp.int32), axis=-1) - 1


def turn_pair(pair, cosine_table, sine_table):
    shaped = pair.reshape(pair.shape[0], 2, HEADS, HEAD_DIM)
    turned = rotate(shaped, cosine_table[:, None, None, :], sine_table[:, None, None, :])
    return turned.reshape(pair.shape[0], 2 * HEADS * HEAD_DIM)


def attend_forward(queries, keys_in, values_in, segments, head_count):
    length = queries.shape[0]
    head_width = queries.shape[1] // head_count
    block_rows = min(512, length)
    blocks = length // block_rows
    keyset = keys_in.reshape(length, head_count, head_width)
    valueset = values_in.reshape(length, head_count, head_width)
    factor = head_width ** (-0.5)

    def one_block(pieces):
        query_rows, block_segs = pieces
        scores = (
            jnp.einsum("qhd,khd->hqk", query_rows, keyset, preferred_element_type=jnp.float32)
            * factor
        )
        scores = jnp.where((block_segs[:, None] == segments[None, :])[None], scores, MASKED_SCORE)
        row_max = jnp.max(scores, axis=-1, keepdims=True)
        totals = jnp.sum(jnp.exp(scores - row_max), axis=-1, keepdims=True)
        logsums = row_max + jnp.log(totals)
        weights = jnp.exp(scores - logsums).astype(jnp.bfloat16)
        mixture = jnp.einsum("hqk,khd->qhd", weights, valueset, preferred_element_type=jnp.float32)
        return (mixture, logsums)

    mixture, logsums = lax.map(
        one_block,
        (
            queries.reshape(blocks, block_rows, head_count, head_width),
            segments.reshape(blocks, block_rows),
        ),
    )
    return (mixture.reshape(length, head_count * head_width), logsums)


def attend_backward(queries, keys_in, values_in, grads_in, segments, logsums, head_count):
    length = queries.shape[0]
    head_width = queries.shape[1] // head_count
    block_rows = min(512, length)
    blocks = length // block_rows
    keyset = keys_in.reshape(length, head_count, head_width)
    valueset = values_in.reshape(length, head_count, head_width)
    factor = head_width ** (-0.5)

    def one_block(carry, pieces):
        key_grad, value_grad = carry
        query_rows, block_segs, grad_rows, block_lse = pieces
        scores = (
            jnp.einsum("qhd,khd->hqk", query_rows, keyset, preferred_element_type=jnp.float32)
            * factor
        )
        scores = jnp.where((block_segs[:, None] == segments[None, :])[None], scores, MASKED_SCORE)
        weights = jnp.exp(scores - block_lse)
        value_grad = value_grad + jnp.einsum(
            "hqk,qhd->khd",
            weights.astype(jnp.bfloat16),
            grad_rows,
            preferred_element_type=jnp.float32,
        )
        grad_weights = jnp.einsum(
            "qhd,khd->hqk", grad_rows, valueset, preferred_element_type=jnp.float32
        )
        centre = jnp.sum(weights * grad_weights, axis=-1, keepdims=True)
        grad_scores = (weights * (grad_weights - centre)).astype(jnp.bfloat16)
        query_grad = (
            jnp.einsum("hqk,khd->qhd", grad_scores, keyset, preferred_element_type=jnp.float32)
            * factor
        )
        key_grad = (
            key_grad
            + jnp.einsum(
                "hqk,qhd->khd", grad_scores, query_rows, preferred_element_type=jnp.float32
            )
            * factor
        )
        return ((key_grad, value_grad), query_grad)

    empty = jnp.zeros((length, head_count, head_width), jnp.float32)
    pieces = (
        queries.reshape(blocks, block_rows, head_count, head_width),
        segments.reshape(blocks, block_rows),
        grads_in.reshape(blocks, block_rows, head_count, head_width),
        logsums,
    )
    (key_grad, value_grad), query_grad = lax.scan(one_block, (empty, empty), pieces)
    flat_shape = (length, head_count * head_width)
    return (
        query_grad.reshape(flat_shape).astype(jnp.bfloat16),
        key_grad.reshape(flat_shape).astype(jnp.bfloat16),
        value_grad.reshape(flat_shape).astype(jnp.bfloat16),
    )


def shards(
    tokens,
    cotangent,
    doc_starts,
    qkv_weight,
    out_weight,
    in_weight,
    down_weight,
    attn_gain,
    ffn_gain,
):
    micro_count = tokens.shape[0]
    token_rows = tokens.shape[2]
    model_width = tokens.shape[3]
    seq_count = lax.axis_size("seq")
    head_count = HEADS // seq_count
    places = lax.axis_index("seq") * token_rows + jnp.arange(token_rows, dtype=jnp.int32)
    everywhere = jnp.arange(token_rows * seq_count, dtype=jnp.int32)
    outputs = []
    input_grads = []
    full_terms = None
    shard_terms = None
    for micro_step in range(micro_count):
        rows_in = tokens[micro_step, 0]
        starts = doc_starts[micro_step, 0]
        cosine_table, sine_table = rope_tables(starts, places, HEAD_DIM)
        segments = segment_ids(starts, everywhere)
        attn_set = (
            lax.all_gather(qkv_weight, "fsdp", axis=0, tiled=True),
            lax.all_gather(out_weight, "fsdp", axis=0, tiled=True),
            lax.all_gather(attn_gain, "fsdp", axis=0, tiled=True),
        )
        qkv_full, out_full, gain_one = attn_set
        normed, norm_back = jax.vjp(layer_norm, rows_in, gain_one.astype(jnp.float32))
        normed_low = normed.astype(jnp.bfloat16)
        qkv_rows = jnp.dot(normed_low, qkv_full, preferred_element_type=jnp.float32)
        turned, turn_back = jax.vjp(
            partial(turn_pair, cosine_table=cosine_table, sine_table=sine_table),
            qkv_rows[:, : 2 * model_width],
        )
        queries = turned[:, :model_width].astype(jnp.bfloat16)
        keyset = turned[:, model_width:].astype(jnp.bfloat16)
        valueset = qkv_rows[:, 2 * model_width :].astype(jnp.bfloat16)
        query_heads, key_heads, value_heads = (
            lax.all_to_all(queries, "seq", split_axis=1, concat_axis=0, tiled=True),
            lax.all_to_all(keyset, "seq", split_axis=1, concat_axis=0, tiled=True),
            lax.all_to_all(valueset, "seq", split_axis=1, concat_axis=0, tiled=True),
        )
        mixture, logsums = attend_forward(query_heads, key_heads, value_heads, segments, head_count)
        mixture_rows = lax.all_to_all(
            mixture.astype(jnp.bfloat16), "seq", split_axis=0, concat_axis=1, tiled=True
        )
        middle = rows_in + jnp.dot(mixture_rows, out_full, preferred_element_type=jnp.float32)
        ffn_set = (
            lax.all_gather(in_weight, "fsdp", axis=0, tiled=True),
            lax.all_gather(down_weight, "fsdp", axis=0, tiled=True),
            lax.all_gather(ffn_gain, "fsdp", axis=0, tiled=True),
        )
        in_full, down_full, gain_two = ffn_set
        normed_two, norm_back_two = jax.vjp(layer_norm, middle, gain_two.astype(jnp.float32))
        normed_two_low = normed_two.astype(jnp.bfloat16)
        joined = jnp.dot(normed_two_low, in_full, preferred_element_type=jnp.float32)
        active, gelu_back = jax.vjp(gated_gelu, joined)
        active_low = active.astype(jnp.bfloat16)
        outputs.append(middle + jnp.dot(active_low, down_full, preferred_element_type=jnp.float32))
        grad_out = cotangent[micro_step, 0]
        grad_low = grad_out.astype(jnp.bfloat16)
        ffn_set = (
            lax.all_gather(in_weight, "fsdp", axis=0, tiled=True),
            lax.all_gather(down_weight, "fsdp", axis=0, tiled=True),
            lax.all_gather(ffn_gain, "fsdp", axis=0, tiled=True),
        )
        in_full, down_full, gain_two = ffn_set
        down_term = jnp.dot(active_low.T, grad_low, preferred_element_type=jnp.float32)
        grad_active = jnp.dot(grad_low, down_full.T, preferred_element_type=jnp.float32)
        grad_joined = gelu_back(grad_active)[0].astype(jnp.bfloat16)
        in_term = jnp.dot(normed_two_low.T, grad_joined, preferred_element_type=jnp.float32)
        grad_normed_two = jnp.dot(grad_joined, in_full.T, preferred_element_type=jnp.float32)
        grad_middle_norm, gain_two_term = norm_back_two(grad_normed_two)
        grad_middle = grad_out + grad_middle_norm
        grad_mid_low = grad_middle.astype(jnp.bfloat16)
        attn_set = (
            lax.all_gather(qkv_weight, "fsdp", axis=0, tiled=True),
            lax.all_gather(out_weight, "fsdp", axis=0, tiled=True),
            lax.all_gather(attn_gain, "fsdp", axis=0, tiled=True),
        )
        qkv_full, out_full, gain_one = attn_set
        out_term = jnp.dot(mixture_rows.T, grad_mid_low, preferred_element_type=jnp.float32)
        grad_mixture = jnp.dot(grad_mid_low, out_full.T, preferred_element_type=jnp.float32).astype(
            jnp.bfloat16
        )
        grad_heads = lax.all_to_all(grad_mixture, "seq", split_axis=1, concat_axis=0, tiled=True)
        query_grad, key_grad, value_grad = attend_backward(
            query_heads, key_heads, value_heads, grad_heads, segments, logsums, head_count
        )
        query_back, key_back, value_back = (
            lax.all_to_all(query_grad, "seq", split_axis=0, concat_axis=1, tiled=True),
            lax.all_to_all(key_grad, "seq", split_axis=0, concat_axis=1, tiled=True),
            lax.all_to_all(value_grad, "seq", split_axis=0, concat_axis=1, tiled=True),
        )
        grad_pair = turn_back(jnp.concatenate([query_back, key_back], axis=1).astype(jnp.float32))[
            0
        ]
        grad_qkv = jnp.concatenate([grad_pair, value_back.astype(jnp.float32)], axis=1).astype(
            jnp.bfloat16
        )
        qkv_term = jnp.dot(normed_low.T, grad_qkv, preferred_element_type=jnp.float32)
        grad_normed = jnp.dot(grad_qkv, qkv_full.T, preferred_element_type=jnp.float32)
        grad_rows_norm, gain_one_term = norm_back(grad_normed)
        input_grads.append(grad_middle + grad_rows_norm)
        terms = (qkv_term, out_term, in_term, down_term, gain_one_term, gain_two_term)
        full_terms = terms if full_terms is None else jax.tree.map(jnp.add, full_terms, terms)
    shard_terms = jax.tree.map(
        lambda part: part.astype(jnp.float32),
        lax.psum_scatter(as_sent(full_terms), "fsdp", scatter_dimension=0, tiled=True),
    )
    totals = jax.tree.map(
        lambda part: part.astype(jnp.float32), lax.psum(as_sent(shard_terms), "seq")
    )
    return (
        jnp.stack(outputs)[:, None],
        jnp.stack(input_grads)[:, None],
        totals[0],
        totals[1],
        totals[2],
        totals[3],
        totals[4],
        totals[5],
    )


MESH = pl.DeviceIdType.MESH
ANY = pl.BlockSpec(memory_space=pl.ANY)
VMEM_BYTES = 63 * 2**20
BF = jnp.bfloat16
F32 = jnp.float32


def nn(a, b):
    return lax.dot_general(a, b, (((1,), (0,)), ((), ())), preferred_element_type=F32)


def nt(a, b):
    return lax.dot_general(a, b, (((1,), (1,)), ((), ())), preferred_element_type=F32)


def spot():
    z, f = lax.axis_index("seq"), lax.axis_index("fsdp")
    core = lax.rem(f, 2)
    x = lax.rem(f // 2, 2)
    y = f // 4
    return z, f, y, x, core


def remote(src, dst, send, recv, where):
    return pltpu.make_async_remote_copy(
        src_ref=src, dst_ref=dst, send_sem=send, recv_sem=recv, device_id=where, device_id_type=MESH
    )


class Rows:
    def __init__(self, z, f, core):
        base = f - core
        self.work, self.home = [], []
        for i in range(2):
            zw, cw = 2 * i + core, z // 2
            self.work.append((zw, base + cw, (zw == z) & (cw == core)))
            zh, ch = 2 * core + i, lax.rem(z, 2)
            self.home.append((zh, base + ch, (zh == z) & (ch == core)))
        self.z = z

    def greet(self, barrier):
        count = 0
        for zt, ft, same in self.work + self.home:

            @pl.when(jnp.logical_not(same))
            def _():
                pl.semaphore_signal(barrier, inc=1, device_id=(zt, ft), device_id_type=MESH)

            count = count + jnp.where(same, 0, 1)
        return count

    def start(self, src, dst, send, recv, local, out, piece=slice(None)):
        places = self.work if out else self.home
        slot = lax.rem(self.z, 2) if out else self.z // 2
        for i, (zt, ft, same) in enumerate(places):

            @pl.when(same)
            def _(i=i):
                pltpu.make_async_copy(src.at[i, piece], dst.at[slot, piece], local).start()

            @pl.when(jnp.logical_not(same))
            def _(i=i, zt=zt, ft=ft):
                remote(src.at[i, piece], dst.at[slot, piece], send.at[i], recv.at[slot], (zt, ft)).start()

    def wait(self, src, dst, send, recv, local, out):
        goes, comes = (self.work, self.home) if out else (self.home, self.work)
        for i, (zt, ft, same) in enumerate(goes):

            @pl.when(same)
            def _(i=i):
                pltpu.make_async_copy(src.at[i], dst.at[i], local).wait()

            @pl.when(jnp.logical_not(same))
            def _(i=i, zt=zt, ft=ft):
                remote(src.at[i], dst.at[i], send.at[i], recv.at[i], (zt, ft)).wait_send()

        for i, (zt, ft, same) in enumerate(comes):

            @pl.when(jnp.logical_not(same))
            def _(i=i, zt=zt, ft=ft):
                remote(src.at[i], dst.at[i], send.at[i], recv.at[i], (zt, ft)).wait_recv()


def halves(width):
    cut = (width // 128 // 2) * 128
    return pl.ds(0, cut), pl.ds(cut, width - cut)


SQRT_HALF = 0.7071067811865476
DENSITY = 0.3989422804014327
PIECES = 8
GROUP = 384
STEPS = 7


def moments(values):
    average = jnp.mean(values, axis=-1, keepdims=True)
    centred = values - average
    spread = jnp.mean(centred * centred, axis=-1, keepdims=True)
    scale = lax.rsqrt(spread + EPSILON)
    return centred * scale, scale


def norm_back(values, gain, grads):
    unit, scale = moments(values)
    spread = grads * gain
    inner = spread - jnp.mean(spread, axis=-1, keepdims=True)
    inner = inner - unit * jnp.mean(spread * unit, axis=-1, keepdims=True)
    return inner * scale, jnp.sum(grads * unit, axis=0, keepdims=True)


def rope_back(grads, cosine, sine):
    lane = lax.broadcasted_iota(jnp.int32, (1, 128), 1)
    low = lax.rem(lane, 64) < 32
    u = grads * sine
    return grads * cosine + jnp.where(low, pltpu.roll(u, 96, 1), -pltpu.roll(u, 32, 1))


class Sums:
    KINDS = 9

    @staticmethod
    def scratch(count, slots, rows, wide):
        dma = pltpu.SemaphoreType.DMA((count, Sums.KINDS))
        shapes = [(slots, 2, 2, 2), (count, 2, 2), (count, 2), (count, 2), (count,)]
        return [pltpu.VMEM(s + (rows, wide), BF) for s in shapes] + [dma, dma]

    def __init__(self, here, count, slots, refs):
        self.here, self.count, self.slots = here, count, slots
        self.acc, self.rx, self.r2, self.zr, self.zr2, self.send, self.recv = refs

    def copy(self, t, kind):
        h = self.here
        acc = self.acc.at[lax.rem(t, self.slots)]
        plan = {
            0: lambda: (acc.at[0, :, 1 - h.x], self.rx.at[t, 0], (h.z, h.fx)),
            1: lambda: (acc.at[1, 1 - h.y], self.rx.at[t, 1], (h.z, h.fy)),
            2: lambda: (self.rx.at[t, 0, 1 - h.y], self.r2.at[t, 0], (h.z, h.fy)),
            3: lambda: (self.rx.at[t, 1, 1 - h.x], self.r2.at[t, 1], (h.z, h.fx)),
            4: lambda: (self.r2.at[t], self.zr.at[t], (h.near, h.f)),
            5: lambda: (self.zr.at[t, 1 - h.own], self.zr2.at[t], (h.across, h.f)),
            6: lambda: (self.r2.at[t, h.own], self.r2.at[t, h.own], (h.across, h.f)),
            7: lambda: (self.r2.at[t, h.own], self.zr.at[t, h.own], (h.near, h.f)),
            8: lambda: (self.r2.at[t, 1 - h.own], self.zr.at[t, 1 - h.own], (h.near, h.f)),
        }
        src, dst, where = plan[kind]()
        return remote(src, dst, self.send.at[t, kind], self.recv.at[t, kind], where)

    def begin(self, t):
        self.copy(t, 0).start()
        self.copy(t, 1).start()

    def cross(self, t):
        h, s = self.here, lax.rem(t, self.slots)
        self.copy(t, 0).wait()
        self.rx[t, 0, 1 - h.y] = added(self.rx[t, 0, 1 - h.y], self.acc[s, 0, 1 - h.y, h.x])
        self.copy(t, 2).start()
        self.copy(t, 1).wait()
        self.rx[t, 1, 1 - h.x] = added(self.rx[t, 1, 1 - h.x], self.acc[s, 1, h.y, 1 - h.x])
        self.copy(t, 3).start()

    def plane(self, t):
        h, s = self.here, lax.rem(t, self.slots)
        self.copy(t, 2).wait()
        self.r2[t, 0] = added(self.r2[t, 0], self.rx[t, 0, h.y], self.acc[s, 0, h.y, h.x])
        self.copy(t, 3).wait()
        self.r2[t, 1] = added(self.r2[t, 1], self.rx[t, 1, h.x], self.acc[s, 1, h.y, h.x])

        @pl.when(h.outer)
        def _():
            self.copy(t, 4).start()

    def meet(self, t):
        h = self.here

        @pl.when(jnp.logical_not(h.outer))
        def _():
            self.copy(t, 4).wait_recv()
            self.zr[t, 1 - h.own] = added(self.zr[t, 1 - h.own], self.r2[t, 1 - h.own])
            self.copy(t, 5).start()

    def sums(self, t):
        h = self.here

        @pl.when(jnp.logical_not(h.outer))
        def _():
            self.copy(t, 5).wait()
            self.r2[t, h.own] = added(self.r2[t, h.own], self.zr[t, h.own], self.zr2[t])
            self.copy(t, 6).start()
            self.copy(t, 7).start()

    def spread(self, t):
        @pl.when(jnp.logical_not(self.here.outer))
        def _():
            self.copy(t, 6).wait_recv()
            self.copy(t, 8).start()

    def finish(self, t):
        @pl.when(jnp.logical_not(self.here.outer))
        def _():
            self.copy(t, 6).wait_send()
            self.copy(t, 7).wait_send()
            self.copy(t, 8).wait_send()

        @pl.when(self.here.outer)
        def _():
            self.copy(t, 4).wait_send()
            self.copy(t, 7).wait_recv()
            self.copy(t, 8).wait_recv()

    def total(self, act):
        for ref, there in ((self.zr, self.here.outer), (self.r2, jnp.logical_not(self.here.outer))):
            pl.when(there)(functools.partial(act, ref))

    LATER = (("finish", 9), ("spread", 8), ("sums", 7), ("meet", 6), ("plane", 4), ("cross", 2))
    LAST = 9

    def pump(self, tick, low, high, first, last, base):
        for name, stage in self.LATER:
            if high - base - stage < first or low - base - stage >= last:
                continue
            t = tick - base - stage
            if low == high:
                getattr(self, name)(t)
            else:

                @pl.when((t >= first) & (t < last))
                def _(name=name, t=t):
                    getattr(self, name)(t)


def added(*terms):
    total = terms[0].astype(F32)
    for term in terms[1:]:
        total = total + term.astype(F32)
    return total.astype(BF)


class Halves:
    def __init__(self, ref):
        self.ref, self.at, self.size = ref, self, ref.shape[0] // 2

    def __getitem__(self, index):
        return self.ref.at[pl.ds((index[0] if isinstance(index, tuple) else index) * self.size, self.size)]


class Here:
    def __init__(self):
        self.z, self.f, self.y, self.x, self.core = spot()
        self.fx = self.f + 2 - 4 * self.x
        self.fy = self.f + 4 - 8 * self.y
        self.fc = self.f + 1 - 2 * self.core
        z = self.z
        self.outer = (z == 0) | (z == 3)
        self.near = jnp.where(z < 2, 1 - z, 5 - z)
        self.across = jnp.where(self.outer, z, 3 - z)
        self.own = jnp.where(z < 2, 0, 1)

    def greet(self, barrier, rows):
        for t in (self.fx, self.fy, self.fc):
            pl.semaphore_signal(barrier, inc=1, device_id=(self.z, t), device_id_type=MESH)
        pl.semaphore_signal(barrier, inc=1, device_id=(self.near, self.f), device_id_type=MESH)

        @pl.when(jnp.logical_not(self.outer))
        def _():
            pl.semaphore_signal(barrier, inc=1, device_id=(self.across, self.f), device_id_type=MESH)

        pl.semaphore_wait(barrier, rows.greet(barrier) + 4 + jnp.where(self.outer, 0, 1))


def lanes(start, size):
    return pl.ds(start if isinstance(start, int) else pl.multiple_of(start, 128), size)


def back_kernel(
    x2_h, mid_h, cot_h, in_h, down_h, qkv_h, out_h, q_h, k_h, v_h, mix_h, normed_h, rows_h, bias_h,
    gains, cosine, sine, lse,
    wide_o, down_o, out_o, gain_o, outh_o, inh_o,
    x2, gl, acc_f, acc_g, win, wdown, xt, xts, gj, at, glc, gm, mt, dout, bias,
    kept, dx_kv, centres, terms_one, rows_b, dx, gs, gr,
    ld, wsem, ps, pr, gjs, gjr, ats, atr, kvs, kvr, gqs, gqr, dxs, dxr, fo, es, er, el,
    *sum_refs,
):
    h = Here()
    rows = Rows(h.z, h.f, h.core)
    wide = Sums(h, 11, 4, sum_refs[0:7])
    down = Sums(h, 2, 2, sum_refs[7:14])
    outs = Sums(h, 1, 1, sum_refs[14:21])
    gain = Sums(h, 1, 1, sum_refs[21:28])
    sib = (h.z, h.fc)

    def output_piece(n):
        size = half // 2 // PIECES
        piece = pl.ds(n * size if isinstance(n, int) else pl.multiple_of(n * size, size), size)
        rows.start(rows_b, outh_o, es.at[0], er.at[0], el.at[0], False, piece)

    def advance(tick, low, high):
        wide.pump(tick, low, high, 0, STEPS, 1)
        down.pump(tick, low, high, 0, 2, 8)
        outs.pump(tick, low, high, 0, 1, 11)
        wide.pump(tick, low, high, 7, 11, 7)
        gain.pump(tick, low, high, 0, 1, 18)

    gq = gj
    last_b = Halves(dout)
    mine = dout.at[:, pl.ds(0, 512)]
    wout = at.at[pl.ds(0, 1024)]
    half = x2.shape[0]
    own_lanes = lambda i: lanes((2 * i + h.core) * 128, 128)
    sib_lanes = lambda i: lanes((2 * i + 1 - h.core) * 128, 128)

    def load(src, dst, k):
        return pltpu.make_async_copy(src, dst, ld.at[k])

    last_group = down_h.shape[0] - (STEPS - 1) * GROUP

    def weights(t, size):
        s = lax.rem(t, 2)
        return [
            pltpu.make_async_copy(in_h.at[:, :, lanes(t * GROUP, GROUP)], win.at[s, :, :, pl.ds(0, GROUP)], wsem.at[s, 0]),
            pltpu.make_async_copy(in_h.at[:, :, lanes((STEPS + t) * GROUP, GROUP)], win.at[s, :, :, pl.ds(GROUP, GROUP)], wsem.at[s, 2]),
            pltpu.make_async_copy(down_h.at[pl.ds(pl.multiple_of(t * GROUP, 16), size)], wdown.at[s, pl.ds(0, size)], wsem.at[s, 1]),
        ]

    def each(t, act):
        @pl.when(t < STEPS - 1)
        def _():
            for c in weights(t, GROUP):
                act(c)

        @pl.when(t == STEPS - 1)
        def _():
            for c in weights(t, last_group):
                act(c)

    def qkv_weights(i):
        s = lax.rem(i, 2)
        return [
            pltpu.make_async_copy(qkv_h.at[:, :, lanes(n * 1024 + i * 256, 256)], win.at[s, :, :, pl.ds(n * 256, 256)], wsem.at[s, n])
            for n in range(3)
        ]

    first = [load(x2_h, x2, 0), load(cot_h, gl, 1), load(mid_h, acc_f, 2)]
    for c in first + weights(0, GROUP):
        c.start()
    h.greet(pltpu.get_barrier_semaphore(), rows)

    first[0].wait()
    first[1].wait()
    glc_send = remote(mine, glc.at[pl.ds(half, half)], ps.at[0], pr.at[0], sib)
    glc[:half] = gl[:, lanes(h.core * 512, 512)]
    mine[...] = gl[:, lanes((1 - h.core) * 512, 512)]
    glc_send.start()

    def transpose_out(src):
        for i in range(4):
            xt_rows = pl.ds(i * 128, 128)
            yield xt_rows, src[:, own_lanes(i)].T, src[:, sib_lanes(i)].T

    for at_rows, a, b in transpose_out(x2):
        xt[at_rows, :half] = a
        xts[at_rows] = b
    xt_send = remote(xts, xt.at[:, pl.ds(half, half)], ps.at[1], pr.at[1], sib)
    xt_send.start()
    first[2].wait()

    def gj_send(t):
        s = lax.rem(t, 2)
        return remote(gj.at[s, pl.ds(0, half)], gj.at[s, pl.ds(half, half)], gjs.at[s], gjr.at[s], sib)

    def at_send(t):
        r = pl.ds(pl.multiple_of(t * GROUP, 128), GROUP)
        return remote(at.at[r, pl.ds(0, half)], at.at[r, pl.ds(half, half)], ats.at[t], atr.at[t], sib)

    def feed(t, _):
        s = lax.rem(t, 2)
        advance(t, 0, STEPS)

        @pl.when(t < STEPS)
        def _():
            each(t, lambda c: c.wait())
            each(t + 1, lambda c: c.start())

            w = win[s].reshape(8 * 128, 768)
            wa, wc, wd = w[:, :GROUP], w[:, GROUP:], wdown[s]
            a, c = nn(x2[...], wa), nn(x2[...], wc)
            grad_active = nt(gl[...], wd)
            phi = 0.5 * (1.0 + lax.erf(a * SQRT_HALF))
            gate = a * phi
            slope = phi + a * (jnp.exp(-0.5 * a * a) * DENSITY)
            active = (gate * c).astype(BF)
            ga = (slope * c * grad_active).astype(BF)
            gc = (gate * grad_active).astype(BF)

            @pl.when(t >= 2)
            def _():
                gj_send(t - 2).wait_send()

            gj[s, :half, :GROUP] = ga
            gj[s, :half, GROUP:] = gc
            at[pl.ds(pl.multiple_of(t * GROUP, 128), GROUP), :half] = active.T
            at_send(t).start()
            acc_f[...] += nn(active, wd)
            back = nt(ga, wa) + nt(gc, wc)

            @pl.when(t == 0)
            def _():
                acc_g[...] = back

            @pl.when(t > 0)
            def _():
                acc_g[...] += back

        @pl.when(t == 1)
        def _():
            xt_send.wait()

        @pl.when(t >= 1)
        def _():
            u = t - 1
            gj_send(u).wait_recv()
            term = nn(xt[...], gj[lax.rem(u, 2)]).astype(BF)
            for o in range(4):
                for k in range(2):
                    wide.acc[lax.rem(u, 4), k, o // 2, o % 2] = term[o * 128 : o * 128 + 128, k * GROUP : k * GROUP + GROUP]
            wide.begin(u)

        @pl.when(t < STEPS)
        def _():
            gj_send(t).start()

        return 0

    lax.fori_loop(0, STEPS + 1, feed, 0)
    gj_send(STEPS - 2).wait_send()
    gj_send(STEPS - 1).wait_send()

    rows_b[...] = acc_f[...].astype(BF).reshape(2, half // 2, -1)
    again = [load(mid_h, acc_f, 2), load(mix_h, x2, 3), load(out_h, wout, 4), load(normed_h, x2, 0), load(bias_h, bias, 5)]
    for n in (0, 1, 4):
        again[n].start()
    for t in range(STEPS):
        at_send(t).wait()
    glc_send.wait()
    for j in range(2):
        term = nn(at[...], glc[:, j * 256 : j * 256 + 256])
        for f in range(8):
            down.acc[j, f % 2, f // 4, f // 2 % 2] = term[f * 328 : f * 328 + 336].astype(BF)
        down.begin(j)
        advance(8 + j, 8 + j, 8 + j)
    again[2].start()
    heads = [load(k_h, at.at[pl.ds(2 * half, 2 * half)], 6), load(q_h, at.at[pl.ds(4 * half, half)], 8), load(v_h, at.at[pl.ds(0, 2 * half)], 7)]
    heads[0].start()
    heads[1].start()

    again[0].wait()
    back, gain_two = norm_back(acc_f[...], gains[1:2], acc_g[...])
    grad_mid = gl[...].astype(F32) + back
    acc_f[...] = grad_mid
    gm[:half] = grad_mid.astype(BF)
    gm_send = remote(gm.at[pl.ds(0, half)], gm.at[pl.ds(half, half)], ps.at[2], pr.at[2], sib)
    gm_send.start()
    again[1].wait()
    for at_rows, a, b in transpose_out(x2):
        mt[at_rows, :half] = a
        xts[at_rows] = b
    mt_send = remote(xts, mt.at[:, pl.ds(half, half)], ps.at[3], pr.at[3], sib)
    mt_send.start()
    rows_in = load(rows_h, gl, 1)
    rows_in.start()
    output_piece(0)
    advance(10, 10, 10)
    again[2].wait()
    dout[...] = nt(gm[:half], wout[...]).astype(BF)
    heads[2].start()
    for j in range(8):
        products = (x2[:, j * 128 : j * 128 + 128].astype(F32) * dout[:, j * 128 : j * 128 + 128].astype(F32)).T
        for e in range(2):
            centres[j, e : e + 1] = jnp.sum(products[64 * e : 64 * e + 64], axis=0, keepdims=True)
    again[3].start()
    gm_send.wait()
    mt_send.wait()
    term = nn(mt[...], gm[...]).astype(BF)
    for o in range(4):
        for k in range(2):
            outs.acc[0, k, o // 2, o % 2] = term[o * 128 : o * 128 + 128, k * 512 : k * 512 + 512]
    outs.begin(0)
    again[3].wait()
    for at_rows, a, b in transpose_out(x2):
        xt[at_rows, :half] = a
        xts[at_rows] = b
    nt_send = remote(xts, xt.at[:, pl.ds(half, half)], ps.at[4], pr.at[4], sib)
    nt_send.start()
    output_piece(1)
    advance(11, 11, 11)
    again[4].wait()
    for c in heads:
        c.wait()

    lane = lax.broadcasted_iota(jnp.int32, (1, 128), 1)

    def kv_rows(s):
        return pl.ds(s * half if isinstance(s, int) else pl.multiple_of(s * half, half), half)

    def kv_send(i):
        s = lax.rem(i, 2)
        return remote(dx_kv, glc.at[kv_rows(s)], kvs.at[s], kvr.at[s], sib)

    def gq_send(i):
        s = lax.rem(i, 2)
        return remote(gq.at[s, pl.ds(0, half)], gq.at[s, pl.ds(half, half)], gqs.at[s], gqr.at[s], sib)

    def stashed(b, n, j):
        return jnp.concatenate([kept[b, pl.ds(n * 128, 128), pl.ds(m * 256 + j * 128, 128)] for m in range(4)], axis=0)

    def attend_step(i, _):
        s = lax.rem(i, 2)
        tick = 12 + i
        output_piece(i + 2)
        advance(tick, 12, 17)

        @pl.when(i < 4)
        def _():
            for c in qkv_weights(i):
                c.start()

            @pl.when(i >= 1)
            def _():
                kv_send(i - 1).wait_send()

            for j in range(2):
                col = lanes(i * 256 + j * 128, 128)
                q = at[pl.ds(4 * half, half), col] * jnp.asarray(0.125, BF)
                v, k = at[pl.ds(0, 2 * half), col], at[pl.ds(2 * half, 2 * half), col]
                do = dout[:, col]
                kt = k.T
                none = jnp.zeros_like(q)
                dqs, dks, dvs = [], [], []
                for e in range(2):
                    part = (lane < 64) if e == 0 else (lane >= 64)
                    centre = centres[2 * i + j, e : e + 1, :]
                    p = jnp.exp(nt(k, jnp.where(part, q, none)) + bias[...].astype(F32) - lse[2 * i + j, e : e + 1, :])
                    dvs.append(nn(p.astype(BF), do))
                    ds = (p * (nt(v, jnp.where(part, do, none)) - centre)).astype(BF)
                    dks.append(nn(ds, q))
                    dqs.append(nn(kt, ds))
                c = pl.ds(j * 128, 128)
                dq = jnp.concatenate([dqs[0][:64], dqs[1][64:]], axis=0).T
                dk = jnp.where(lane < 64, dks[0], dks[1]).astype(BF)
                dv = jnp.where(lane < 64, dvs[0], dvs[1]).astype(BF)
                for n, part in enumerate(((dq * 0.125).astype(BF), dk, dv)):
                    for m in range(4):
                        kept[s, pl.ds(n * 128, 128), pl.ds(m * 256 + j * 128, 128)] = part[m * 128 : m * 128 + 128]
                dx_kv[:, pl.ds(j * 128, 128)] = dk[half:]
                dx_kv[:, pl.ds(256 + j * 128, 128)] = dv[half:]

        @pl.when((i >= 1) & (i <= 4))
        def _():
            u = i - 1
            b = lax.rem(u, 2)

            @pl.when(u >= 2)
            def _():
                gq_send(u - 2).wait_send()

            kv_send(u).wait_recv()
            for j in range(2):
                c = slice(j * 128, j * 128 + 128)
                g = stashed(b, 0, j).astype(F32)
                gq[b, :half, j * 128 : j * 128 + 128] = rope_back(g, cosine[...], sine[...]).astype(BF)
                c = slice(256 + j * 128, 256 + j * 128 + 128)
                g = added(stashed(b, 1, j), glc[kv_rows(b), j * 128 : j * 128 + 128]).astype(F32)
                gq[b, :half, c] = rope_back(g, cosine[...], sine[...]).astype(BF)
                c = slice(512 + j * 128, 512 + j * 128 + 128)
                gq[b, :half, c] = added(stashed(b, 2, j), glc[kv_rows(b), 256 + j * 128 : 256 + j * 128 + 128])
            for c in qkv_weights(u):
                c.wait()
            back = nt(gq[b, :half], win[b].reshape(1024, 768))

            @pl.when(u == 0)
            def _():
                acc_g[...] = back

            @pl.when(u > 0)
            def _():
                acc_g[...] += back

        @pl.when(i == 2)
        def _():
            nt_send.wait()

        @pl.when(i == 5)
        def _():
            rows_in.wait()
            back, gain_one = norm_back(gl[...].astype(F32), gains[0:1], acc_g[...])
            terms_one[...] = gain_one
            dout[...] = (acc_f[...] + back).astype(BF)
            rows.start(last_b, inh_o, es.at[1], er.at[1], el.at[1], False)

        @pl.when(i >= 2)
        def _():
            u = i - 2
            gq_send(u).wait_recv()
            term = nn(xt[...], gq[lax.rem(u, 2)]).astype(BF)
            a = lax.rem(u + 7, 4)
            for o in range(4):
                for k in range(2):
                    wide.acc[a, k, o // 2, o % 2] = term[o * 128 : o * 128 + 128, k * GROUP : k * GROUP + GROUP]
            wide.begin(u + 7)

        @pl.when(i < 4)
        def _():
            kv_send(i).start()

        @pl.when((i >= 1) & (i <= 4))
        def _():
            gq_send(i - 1).start()

        return 0

    lax.fori_loop(0, 6, attend_step, 0)

    gain_one = terms_one[...]
    terms = (gain_one, gain_two)
    for k in range(2):
        for o in range(4):
            for ref, part in ((gain.acc.at[0], h.core), (gs, 1 - h.core)):
                low, high = terms[k][:, 256 * o : 256 * o + 128], terms[k][:, 256 * o + 128 : 256 * o + 256]
                value = jnp.where(part == 0, low, high)
                ref[k, o // 2, o % 2] = jnp.broadcast_to(value, (16, 128)).astype(BF)
    gs_send = remote(gs, gr, ps.at[5], pr.at[5], sib)
    gs_send.start()
    advance(18, 18, 18)
    def down_swap(act, ref):
        for j in range(2):
            act(remote(ref.at[j, 1 - h.core], dx.at[j], dxs.at[j], dxr.at[j], sib))

    down.total(functools.partial(down_swap, lambda c: c.start()))
    gs_send.wait()
    for k in range(2):
        for o in range(4):
            gain.acc[0, k, o // 2, o % 2] = added(gain.acc[0, k, o // 2, o % 2], gr[k, o // 2, o % 2])
    gain.begin(0)
    for tick in range(19, 19 + Sums.LAST):
        advance(tick, tick, tick)
    down.total(functools.partial(down_swap, lambda c: c.wait()))
    kv_send(3).wait_send()
    gq_send(2).wait_send()
    gq_send(3).wait_send()

    def write(dst, k, act, ref):
        act(pltpu.make_async_copy(ref, dst, fo.at[k]))

    def write_down(act, ref):
        for j in range(2):
            act(pltpu.make_async_copy(ref.at[j, h.core], down_o.at[h.core, j], fo.at[3 + j]))
            act(pltpu.make_async_copy(dx.at[j], down_o.at[1 - h.core, j], fo.at[5 + j]))

    for act in (lambda c: c.start(), lambda c: c.wait()):
        for k, (group, dst) in enumerate(((wide, wide_o), (outs, out_o), (gain, gain_o))):
            group.total(functools.partial(write, dst, k, act))
        down.total(functools.partial(write_down, act))
    rows.wait(rows_b, outh_o, es.at[0], er.at[0], el.at[0], False)
    rows.wait(last_b, inh_o, es.at[1], er.at[1], el.at[1], False)


def back_all(x2, middle, cot, in_f, down_f, qkv_f, out_f, q, k, v, mixture, normed, rows_in, bias, gains, cosine, sine, lse):
    dma = pltpu.SemaphoreType.DMA
    half, wide = x2.shape

    def buf(*s, kind=BF):
        return pltpu.VMEM(s, kind)

    def shape(*s):
        return jax.ShapeDtypeStruct(s, BF)

    whole = pl.BlockSpec(memory_space=pltpu.VMEM)
    sums = [(11, 4, 128, GROUP), (2, 2, 336, 256), (1, 1, 128, 512), (1, 1, 16, 128)]
    scratch = [
        buf(half, wide), buf(half, wide), buf(half, wide, kind=F32), buf(half, wide, kind=F32),
        buf(2, 8, 128, 768), buf(2, GROUP, wide), buf(half, 2 * half), buf(half, half),
        buf(2, 2 * half, 768), buf(STEPS * GROUP, 2 * half), buf(2 * half, half),
        buf(2 * half, wide), buf(half, 2 * half), buf(half, wide),
        buf(2 * half, half),
        buf(2, GROUP, wide), buf(half, 512), buf(8, 2, half, kind=F32), buf(1, wide, kind=F32),
        buf(2, half // 2, wide), buf(2, 336, 256), buf(2, 2, 2, 16, 128), buf(2, 2, 2, 16, 128),
        dma((9,)), dma((2, 3)), dma((6,)), dma((6,)), dma((2,)), dma((2,)), dma((STEPS,)), dma((STEPS,)),
        dma((2,)), dma((2,)), dma((2,)), dma((2,)), dma((2,)), dma((2,)), dma((7,)),
        dma((2, 2)), dma((2, 2)), dma((2,)),
    ]
    for s in sums:
        scratch += Sums.scratch(*s)
    return pl.pallas_call(
        back_kernel,
        out_shape=[
            shape(11, 2, 128, GROUP), shape(2, 2, 336, 256), shape(1, 2, 128, 512), shape(1, 2, 16, 128),
            shape(2, half // 2, wide), shape(2, half // 2, wide),
        ],
        in_specs=[ANY] * 14 + [whole] * 4,
        out_specs=[ANY] * 6,
        scratch_shapes=scratch,
        compiler_params=pltpu.CompilerParams(collective_id=2, has_side_effects=True, vmem_limit_bytes=VMEM_BYTES),
        name="feed_forward_and_backward",
    )(x2, middle, cot, in_f, down_f, qkv_f, out_f, q, k, v, mixture, normed, rows_in, bias, gains, cosine, sine, lse)


def rope(values, cosine, sine):
    lane = lax.broadcasted_iota(jnp.int32, (1, 128), 1)
    turned = jnp.where(lax.rem(lane, 64) < 32, -pltpu.roll(values, 96, 1), pltpu.roll(values, 32, 1))
    return values * cosine + turned * sine


def front_kernel(
    gains_h, qkv_h, out_h, in_h, down_h, tok_h, cot_h, starts_h, inverse,
    in_o, down_o, qkv_o, out_o, cot_o, tok_o, x2_o, mid_o, q_o, k_o, v_o, mix_o, normed_o, bias_o,
    gains_o, cos_o, sin_o, lse_o,
    gains_v, qkv_v, out_v, tok_v, starts_v, held_in, held_down, mid, normed, x2, q, k, v, mix, bias,
    ss, rs, ls, es, er, el, ds_, dr, kvs, kvr, ws,
):
    h = Here()
    rows = Rows(h.z, h.f, h.core)
    z, f, core = h.z, h.f, h.core
    fx, fy, fc = h.fx, h.fy, h.fc
    fd = fx + 4 - 8 * h.y
    sib = (z, fc)
    half = normed.shape[0]
    shards = (gains_h, qkv_h, out_h, in_h, down_h)
    wholes = (gains_v, qkv_v, out_v, in_o, down_o)

    def same(whole, i, cols=None):
        return whole.at[i] if cols is None else whole.at[i, :, cols]

    def copy(w, k):
        whole, shard = wholes[w], shards[w]
        a, b = halves(shard.shape[1])
        place = {3: (fx, a), 4: (fy, b), 5: (fx, None), 6: (fy, None), 7: (fd, a), 8: (fd, b)}
        if k < 3:
            src, dst = shard, whole.at[f]
        else:
            src = dst = same(whole, *place[k])
        where = (fx, fy, fc, fy, fx, fc, fc, fc, fc)[k]
        return remote(src, dst, ss.at[w, k], rs.at[w, k], (z, where))

    def first(w):
        for k in range(3):
            copy(w, k).start()

    def second(w):
        for k in (0, 1):
            copy(w, k).wait_recv()
            copy(w, k + 3).start()
            copy(w, k + 5).start()

    def third(w):
        for k in (3, 4):
            copy(w, k).wait_recv()
            copy(w, k + 4).start()

    def rest(w):
        for k in (2, 5, 6, 7, 8):
            copy(w, k).wait_recv()

    def own(w):
        dst = {3: held_in, 4: held_down}.get(w)
        return pltpu.make_async_copy(shards[w], wholes[w].at[f] if dst is None else dst, ls.at[w])

    def own_out(w):
        return pltpu.make_async_copy({3: held_in, 4: held_down}[w], wholes[w].at[f], ls.at[w])

    for w in range(5):
        own(w).start()
    h.greet(pltpu.get_barrier_semaphore(), rows)
    info = remote(starts_h, starts_v.at[core], ds_.at[0], dr.at[0], sib)
    own_info = pltpu.make_async_copy(starts_h, starts_v.at[core], el.at[2])
    info.start()
    own_info.start()
    rows.start(tok_h, tok_v, es.at[0], er.at[0], el.at[0], True)
    for w in range(3):
        first(w)
    info.wait()
    own_info.wait()

    lane = lax.broadcasted_iota(jnp.int32, (1, 128), 1)
    begins = starts_v[lax.rem(z, 2), pl.ds(z // 2, 1), :]
    inside = lane < 8

    def documents(base):
        place = lax.broadcasted_iota(jnp.int32, (half, 128), 0) + base
        before = (begins <= place) & inside
        number = jnp.sum(jnp.where(before, 1.0, 0.0), axis=1, keepdims=True)
        begin = jnp.max(jnp.where(before, begins, 0).astype(F32), axis=1, keepdims=True)
        return place, number, begin

    place, number, begin = documents(core * half)
    angle = (place.astype(F32) - begin) * inverse[...]
    cos_o[...] = jnp.cos(angle)
    sin_o[...] = jnp.sin(angle)
    across = jnp.broadcast_to(number, (half, 128)).T[0:1, :]
    _, other, _ = documents((1 - core) * half)
    bias[:half] = jnp.where(number == across, 0.0, MASKED_SCORE).astype(BF)
    bias[half:] = jnp.where(other == across, 0.0, MASKED_SCORE).astype(BF)

    second(0)
    second(1)
    second(2)
    rows.start(cot_h, cot_o, es.at[1], er.at[1], el.at[1], True)
    own(3).wait()
    own(4).wait()
    own_out(3).start()
    own_out(4).start()
    first(3)
    first(4)
    third(0)
    rest(0)
    own(0).wait()
    for n in range(2):
        for i in range(8):
            gains_o[n : n + 1, i * 128 : i * 128 + 128] = gains_v[i, 0:1, n * 128 : n * 128 + 128].astype(F32)
    rows.wait(tok_h, tok_v, es.at[0], er.at[0], el.at[0], True)
    x = tok_v[...].reshape(half, -1).astype(F32)
    unit, _ = moments(x)
    normed[...] = (unit * gains_o[0:1]).astype(BF)
    saved = [pltpu.make_async_copy(tok_v, tok_o, ws.at[0]), pltpu.make_async_copy(normed, normed_o, ws.at[1]),
             pltpu.make_async_copy(bias, bias_o, ws.at[2])]
    for c in saved:
        c.start()
    third(1)
    rest(1)
    own(1).wait()
    saved.append(pltpu.make_async_copy(qkv_v, qkv_o, ws.at[3]))
    saved[-1].start()

    def pair_send(n, i):
        ref = (k, v)[n]
        cols = pl.ds(i * 256, 256)
        return remote(ref.at[pl.ds(0, half), cols], ref.at[pl.ds(half, half), cols], kvs.at[n, i], kvr.at[n, i], sib)

    wide = normed.shape[1]
    for n, ref in ((1, k), (2, v), (0, q)):
        for i in range(4):
            part = nn(normed[...], qkv_v[:, :, n * wide + i * 256 : n * wide + i * 256 + 256].reshape(wide, 256))
            for j in range(2):
                cols = slice(i * 256 + j * 128, i * 256 + j * 128 + 128)
                value = part[:, j * 128 : j * 128 + 128]
                value = value if n == 2 else rope(value, cos_o[...], sin_o[...])
                ref[:half, cols] = value.astype(BF)
            if n:
                pair_send(n - 1, i).start()
    third(2)
    for n in range(2):
        for i in range(4):
            pair_send(n, i).wait()
    for n, (ref, dst) in enumerate(((q, q_o), (k, k_o), (v, v_o))):
        saved.append(pltpu.make_async_copy(ref, dst, ws.at[4 + n]))
        saved[-1].start()

    def attend(i, _):
        cols = lanes(i * 128, 128)
        queries = q[:, cols] * jnp.asarray(0.125, BF)
        keys = k[:, cols]
        vt = v[:, cols].T
        outs = []
        for e in range(2):
            part = (lane < 64) if e == 0 else (lane >= 64)
            scores = nt(keys, jnp.where(part, queries, jnp.zeros_like(queries))) + bias[...].astype(F32)
            top = jnp.max(scores, axis=0, keepdims=True)
            p = jnp.exp(scores - top)
            total = jnp.sum(p, axis=0, keepdims=True)
            outs.append(nn(vt, p.astype(BF)) / total)
            lse_o[i, e : e + 1, :] = top + jnp.log(total)
        mix[:, cols] = jnp.concatenate([outs[0][:64], outs[1][64:]], axis=0).T.astype(BF)
        return 0

    lax.fori_loop(0, 8, attend, 0)
    second(3)
    rest(2)
    own(2).wait()
    saved.append(pltpu.make_async_copy(out_v, out_o, ws.at[7]))
    saved[-1].start()
    saved.append(pltpu.make_async_copy(mix, mix_o, ws.at[8]))
    saved[-1].start()
    middle = tok_v[...].reshape(half, -1).astype(F32) + nn(mix[...], out_v[...].reshape(wide, wide))
    mid[...] = middle
    unit, _ = moments(middle)
    x2[...] = (unit * gains_o[1:2]).astype(BF)
    for ref, dst in ((mid, mid_o), (x2, x2_o)):
        saved.append(pltpu.make_async_copy(ref, dst, ws.at[len(saved)]))
        saved[-1].start()
    second(4)
    third(3)
    third(4)
    rest(3)
    rest(4)
    own_out(3).wait()
    own_out(4).wait()
    for w in range(5):
        for kind in range(9):
            copy(w, kind).wait_send()
    for c in saved:
        c.wait()
    rows.wait(cot_h, cot_o, es.at[1], er.at[1], el.at[1], True)


def front_all(shards, tok, cot, starts, inverse):
    dma = pltpu.SemaphoreType.DMA
    gains, qkv, out, inw, down = shards
    half, wide = 2 * tok.shape[1], tok.shape[2]

    def shape(*s, kind=BF):
        return jax.ShapeDtypeStruct(s, kind)

    def buf(*s, kind=BF):
        return pltpu.VMEM(s, kind)

    whole = pl.BlockSpec(memory_space=pltpu.VMEM)
    return pl.pallas_call(
        front_kernel,
        out_shape=[
            shape(8, *inw.shape), shape(8, *down.shape), shape(8, *qkv.shape), shape(8, *out.shape),
            shape(*cot.shape), shape(*tok.shape), shape(half, wide), shape(half, wide, kind=F32),
            shape(half, wide), shape(2 * half, wide), shape(2 * half, wide), shape(half, wide),
            shape(half, wide), shape(2 * half, half),
            shape(2, wide, kind=F32), shape(half, 128, kind=F32), shape(half, 128, kind=F32), shape(8, 2, half, kind=F32),
        ],
        in_specs=[ANY] * 8 + [whole],
        out_specs=[ANY] * 14 + [whole] * 4,
        scratch_shapes=[
            buf(8, *gains.shape), buf(8, *qkv.shape), buf(8, *out.shape), buf(*tok.shape), buf(2, 8, 128, kind=jnp.int32),
            buf(*inw.shape), buf(*down.shape), buf(half, wide, kind=F32), buf(half, wide), buf(half, wide),
            buf(half, wide), buf(2 * half, wide), buf(2 * half, wide), buf(half, wide), buf(2 * half, half),
            dma((5, 9)), dma((5, 9)), dma((5,)), dma((2, 2)), dma((2, 2)), dma((3,)), dma((1,)), dma((1,)),
            dma((2, 4)), dma((2, 4)), dma((12,)),
        ],
        compiler_params=pltpu.CompilerParams(collective_id=1, has_side_effects=True, vmem_limit_bytes=VMEM_BYTES),
        name="gather_and_attention",
    )(*shards, tok, cot, starts, inverse)


def chip_streams(tokens, cotangent, doc_starts, qkv_weight, out_weight, in_weight, down_weight, attn_gain, ffn_gain):
    wide = tokens.shape[3]
    half = 2 * tokens.shape[2]
    units = down_weight.shape[0] * 8
    gains = jnp.concatenate([attn_gain, ffn_gain])[None] + jnp.zeros((16, 1), BF)
    starts = jnp.pad(doc_starts[:, 0], ((0, 6), (0, 120)))
    spare = jnp.zeros((in_weight.shape[0], STEPS * GROUP - units), BF)
    in_parts = jnp.concatenate([in_weight[:, :units], spare, in_weight[:, units:], spare], axis=1)
    inverse = ROPE_THETA ** (-jnp.arange(0, HEAD_DIM, 2, dtype=F32) / HEAD_DIM)
    (in_f, down_f, qkv_f, out_f, cot, rows_low, x2, middle, q, k, v, mixture, normed, bias, both_gains, cosine, sine, lse) = front_all(
        (gains, qkv_weight, out_weight, in_parts, down_weight),
        tokens[:, 0].astype(BF), cotangent[:, 0].astype(BF), starts, jnp.tile(inverse, 4)[None],
    )
    wide_t, down_t, out_t, gain_t, out_home, in_home = back_all(
        x2, middle, cot.reshape(half, wide), in_f, down_f.reshape(units, wide), qkv_f, out_f.reshape(wide, wide), q, k, v,
        mixture, normed, rows_low.reshape(half, wide), bias, both_gains, cosine, sine, lse,
    )
    in_t = wide_t[:STEPS].transpose(2, 1, 0, 3).reshape(128, 2, STEPS * GROUP)[:, :, :units].astype(F32)
    qkv_t = wide_t[STEPS:].astype(F32).transpose(2, 0, 1, 3).reshape(128, 4, 3, 256)
    return (
        out_home[:, None].astype(F32),
        in_home[:, None].astype(F32),
        qkv_t.swapaxes(1, 2).reshape(qkv_weight.shape),
        out_t[0].astype(F32).swapaxes(0, 1).reshape(out_weight.shape),
        in_t.reshape(in_weight.shape),
        down_t[:, :, : down_weight.shape[0]].astype(F32).transpose(2, 0, 1, 3).reshape(down_weight.shape),
        gain_t[0, 0, 0].astype(F32),
        gain_t[0, 1, 0].astype(F32),
    )


def solution(mesh):
    whole_chips = dict(mesh.shape) == {"seq": 4, "fsdp": 8}
    return jax.shard_map(
        chip_streams if whole_chips else shards,
        mesh=mesh,
        in_specs=(
            P(None, "fsdp", "seq", None),
            P(None, "fsdp", "seq", None),
            P(None, "fsdp", None),
            P("fsdp", None),
            P("fsdp", None),
            P("fsdp", None),
            P("fsdp", None),
            P("fsdp"),
            P("fsdp"),
        ),
        out_specs=(
            P(None, "fsdp", "seq", None),
            P(None, "fsdp", "seq", None),
            P("fsdp", None),
            P("fsdp", None),
            P("fsdp", None),
            P("fsdp", None),
            P("fsdp"),
            P("fsdp"),
        ),
        check_vma=False,
    )
```

```python
import functools
from functools import partial

import jax
import jax.numpy as jnp
from jax import lax
from jax.experimental import pallas as pl
from jax.experimental.pallas import tpu as pltpu
from jax.sharding import PartitionSpec as P

HEADS = 16
HEAD_DIM = 64


EPSILON = 1e-05
ROPE_THETA = 160000.0
MASKED_SCORE = -1e30


def as_sent(x):

    def short(part):
        return part.astype(jnp.bfloat16) if part.dtype == jnp.float32 else part

    return jax.tree.map(short, x)


def layer_norm(values, norm_gain):
    average = jnp.mean(values, axis=-1, keepdims=True)
    centred = values - average
    spread = jnp.mean(centred * centred, axis=-1, keepdims=True)
    return centred * lax.rsqrt(spread + EPSILON) * norm_gain


def gated_gelu(joined):
    half_width = joined.shape[-1] // 2
    return jax.nn.gelu(joined[:, :half_width], approximate=False) * joined[:, half_width:]


def rotate(values, cosine_table, sine_table):
    half_width = values.shape[-1] // 2
    turned = jnp.concatenate([-values[..., half_width:], values[..., :half_width]], axis=-1)
    return values * cosine_table + turned * sine_table


def rope_tables(starts, places, head_width):
    preceding = starts[None, :] <= places[:, None]
    doc_begin = jnp.max(jnp.where(preceding, starts[None, :], 0), axis=-1)
    offsets = (places - doc_begin).astype(jnp.float32)
    inverse = ROPE_THETA ** (-jnp.arange(0, head_width, 2, dtype=jnp.float32) / head_width)
    angles = offsets[:, None] * inverse[None, :]
    angles = jnp.concatenate([angles, angles], axis=-1)
    return (jnp.cos(angles), jnp.sin(angles))


def segment_ids(starts, places):
    return jnp.sum((starts[None, :] <= places[:, None]).astype(jnp.int32), axis=-1) - 1


def turn_pair(pair, cosine_table, sine_table):
    shaped = pair.reshape(pair.shape[0], 2, HEADS, HEAD_DIM)
    turned = rotate(shaped, cosine_table[:, None, None, :], sine_table[:, None, None, :])
    return turned.reshape(pair.shape[0], 2 * HEADS * HEAD_DIM)


def attend_forward(queries, keys_in, values_in, segments, head_count):
    length = queries.shape[0]
    head_width = queries.shape[1] // head_count
    block_rows = min(512, length)
    blocks = length // block_rows
    keyset = keys_in.reshape(length, head_count, head_width)
    valueset = values_in.reshape(length, head_count, head_width)
    factor = head_width ** (-0.5)

    def one_block(pieces):
        query_rows, block_segs = pieces
        scores = (
            jnp.einsum("qhd,khd->hqk", query_rows, keyset, preferred_element_type=jnp.float32)
            * factor
        )
        scores = jnp.where((block_segs[:, None] == segments[None, :])[None], scores, MASKED_SCORE)
        row_max = jnp.max(scores, axis=-1, keepdims=True)
        totals = jnp.sum(jnp.exp(scores - row_max), axis=-1, keepdims=True)
        logsums = row_max + jnp.log(totals)
        weights = jnp.exp(scores - logsums).astype(jnp.bfloat16)
        mixture = jnp.einsum("hqk,khd->qhd", weights, valueset, preferred_element_type=jnp.float32)
        return (mixture, logsums)

    mixture, logsums = lax.map(
        one_block,
        (
            queries.reshape(blocks, block_rows, head_count, head_width),
            segments.reshape(blocks, block_rows),
        ),
    )
    return (mixture.reshape(length, head_count * head_width), logsums)


def attend_backward(queries, keys_in, values_in, grads_in, segments, logsums, head_count):
    length = queries.shape[0]
    head_width = queries.shape[1] // head_count
    block_rows = min(512, length)
    blocks = length // block_rows
    keyset = keys_in.reshape(length, head_count, head_width)
    valueset = values_in.reshape(length, head_count, head_width)
    factor = head_width ** (-0.5)

    def one_block(carry, pieces):
        key_grad, value_grad = carry
        query_rows, block_segs, grad_rows, block_lse = pieces
        scores = (
            jnp.einsum("qhd,khd->hqk", query_rows, keyset, preferred_element_type=jnp.float32)
            * factor
        )
        scores = jnp.where((block_segs[:, None] == segments[None, :])[None], scores, MASKED_SCORE)
        weights = jnp.exp(scores - block_lse)
        value_grad = value_grad + jnp.einsum(
            "hqk,qhd->khd",
            weights.astype(jnp.bfloat16),
            grad_rows,
            preferred_element_type=jnp.float32,
        )
        grad_weights = jnp.einsum(
            "qhd,khd->hqk", grad_rows, valueset, preferred_element_type=jnp.float32
        )
        centre = jnp.sum(weights * grad_weights, axis=-1, keepdims=True)
        grad_scores = (weights * (grad_weights - centre)).astype(jnp.bfloat16)
        query_grad = (
            jnp.einsum("hqk,khd->qhd", grad_scores, keyset, preferred_element_type=jnp.float32)
            * factor
        )
        key_grad = (
            key_grad
            + jnp.einsum(
                "hqk,qhd->khd", grad_scores, query_rows, preferred_element_type=jnp.float32
            )
            * factor
        )
        return ((key_grad, value_grad), query_grad)

    empty = jnp.zeros((length, head_count, head_width), jnp.float32)
    pieces = (
        queries.reshape(blocks, block_rows, head_count, head_width),
        segments.reshape(blocks, block_rows),
        grads_in.reshape(blocks, block_rows, head_count, head_width),
        logsums,
    )
    (key_grad, value_grad), query_grad = lax.scan(one_block, (empty, empty), pieces)
    flat_shape = (length, head_count * head_width)
    return (
        query_grad.reshape(flat_shape).astype(jnp.bfloat16),
        key_grad.reshape(flat_shape).astype(jnp.bfloat16),
        value_grad.reshape(flat_shape).astype(jnp.bfloat16),
    )


def shards(
    tokens,
    cotangent,
    doc_starts,
    qkv_weight,
    out_weight,
    in_weight,
    down_weight,
    attn_gain,
    ffn_gain,
):
    micro_count = tokens.shape[0]
    token_rows = tokens.shape[2]
    model_width = tokens.shape[3]
    seq_count = lax.axis_size("seq")
    head_count = HEADS // seq_count
    places = lax.axis_index("seq") * token_rows + jnp.arange(token_rows, dtype=jnp.int32)
    everywhere = jnp.arange(token_rows * seq_count, dtype=jnp.int32)
    outputs = []
    input_grads = []
    full_terms = None
    shard_terms = None
    for micro_step in range(micro_count):
        rows_in = tokens[micro_step, 0]
        starts = doc_starts[micro_step, 0]
        cosine_table, sine_table = rope_tables(starts, places, HEAD_DIM)
        segments = segment_ids(starts, everywhere)
        attn_set = (
            lax.all_gather(qkv_weight, "fsdp", axis=0, tiled=True),
            lax.all_gather(out_weight, "fsdp", axis=0, tiled=True),
            lax.all_gather(attn_gain, "fsdp", axis=0, tiled=True),
        )
        qkv_full, out_full, gain_one = attn_set
        normed, norm_back = jax.vjp(layer_norm, rows_in, gain_one.astype(jnp.float32))
        normed_low = normed.astype(jnp.bfloat16)
        qkv_rows = jnp.dot(normed_low, qkv_full, preferred_element_type=jnp.float32)
        turned, turn_back = jax.vjp(
            partial(turn_pair, cosine_table=cosine_table, sine_table=sine_table),
            qkv_rows[:, : 2 * model_width],
        )
        queries = turned[:, :model_width].astype(jnp.bfloat16)
        keyset = turned[:, model_width:].astype(jnp.bfloat16)
        valueset = qkv_rows[:, 2 * model_width :].astype(jnp.bfloat16)
        query_heads, key_heads, value_heads = (
            lax.all_to_all(queries, "seq", split_axis=1, concat_axis=0, tiled=True),
            lax.all_to_all(keyset, "seq", split_axis=1, concat_axis=0, tiled=True),
            lax.all_to_all(valueset, "seq", split_axis=1, concat_axis=0, tiled=True),
        )
        mixture, logsums = attend_forward(query_heads, key_heads, value_heads, segments, head_count)
        mixture_rows = lax.all_to_all(
            mixture.astype(jnp.bfloat16), "seq", split_axis=0, concat_axis=1, tiled=True
        )
        middle = rows_in + jnp.dot(mixture_rows, out_full, preferred_element_type=jnp.float32)
        ffn_set = (
            lax.all_gather(in_weight, "fsdp", axis=0, tiled=True),
            lax.all_gather(down_weight, "fsdp", axis=0, tiled=True),
            lax.all_gather(ffn_gain, "fsdp", axis=0, tiled=True),
        )
        in_full, down_full, gain_two = ffn_set
        normed_two, norm_back_two = jax.vjp(layer_norm, middle, gain_two.astype(jnp.float32))
        normed_two_low = normed_two.astype(jnp.bfloat16)
        joined = jnp.dot(normed_two_low, in_full, preferred_element_type=jnp.float32)
        active, gelu_back = jax.vjp(gated_gelu, joined)
        active_low = active.astype(jnp.bfloat16)
        outputs.append(middle + jnp.dot(active_low, down_full, preferred_element_type=jnp.float32))
        grad_out = cotangent[micro_step, 0]
        grad_low = grad_out.astype(jnp.bfloat16)
        ffn_set = (
            lax.all_gather(in_weight, "fsdp", axis=0, tiled=True),
            lax.all_gather(down_weight, "fsdp", axis=0, tiled=True),
            lax.all_gather(ffn_gain, "fsdp", axis=0, tiled=True),
        )
        in_full, down_full, gain_two = ffn_set
        down_term = jnp.dot(active_low.T, grad_low, preferred_element_type=jnp.float32)
        grad_active = jnp.dot(grad_low, down_full.T, preferred_element_type=jnp.float32)
        grad_joined = gelu_back(grad_active)[0].astype(jnp.bfloat16)
        in_term = jnp.dot(normed_two_low.T, grad_joined, preferred_element_type=jnp.float32)
        grad_normed_two = jnp.dot(grad_joined, in_full.T, preferred_element_type=jnp.float32)
        grad_middle_norm, gain_two_term = norm_back_two(grad_normed_two)
        grad_middle = grad_out + grad_middle_norm
        grad_mid_low = grad_middle.astype(jnp.bfloat16)
        attn_set = (
            lax.all_gather(qkv_weight, "fsdp", axis=0, tiled=True),
            lax.all_gather(out_weight, "fsdp", axis=0, tiled=True),
            lax.all_gather(attn_gain, "fsdp", axis=0, tiled=True),
        )
        qkv_full, out_full, gain_one = attn_set
        out_term = jnp.dot(mixture_rows.T, grad_mid_low, preferred_element_type=jnp.float32)
        grad_mixture = jnp.dot(grad_mid_low, out_full.T, preferred_element_type=jnp.float32).astype(
            jnp.bfloat16
        )
        grad_heads = lax.all_to_all(grad_mixture, "seq", split_axis=1, concat_axis=0, tiled=True)
        query_grad, key_grad, value_grad = attend_backward(
            query_heads, key_heads, value_heads, grad_heads, segments, logsums, head_count
        )
        query_back, key_back, value_back = (
            lax.all_to_all(query_grad, "seq", split_axis=0, concat_axis=1, tiled=True),
            lax.all_to_all(key_grad, "seq", split_axis=0, concat_axis=1, tiled=True),
            lax.all_to_all(value_grad, "seq", split_axis=0, concat_axis=1, tiled=True),
        )
        grad_pair = turn_back(jnp.concatenate([query_back, key_back], axis=1).astype(jnp.float32))[
            0
        ]
        grad_qkv = jnp.concatenate([grad_pair, value_back.astype(jnp.float32)], axis=1).astype(
            jnp.bfloat16
        )
        qkv_term = jnp.dot(normed_low.T, grad_qkv, preferred_element_type=jnp.float32)
        grad_normed = jnp.dot(grad_qkv, qkv_full.T, preferred_element_type=jnp.float32)
        grad_rows_norm, gain_one_term = norm_back(grad_normed)
        input_grads.append(grad_middle + grad_rows_norm)
        terms = (qkv_term, out_term, in_term, down_term, gain_one_term, gain_two_term)
        full_terms = terms if full_terms is None else jax.tree.map(jnp.add, full_terms, terms)
    shard_terms = jax.tree.map(
        lambda part: part.astype(jnp.float32),
        lax.psum_scatter(as_sent(full_terms), "fsdp", scatter_dimension=0, tiled=True),
    )
    totals = jax.tree.map(
        lambda part: part.astype(jnp.float32), lax.psum(as_sent(shard_terms), "seq")
    )
    return (
        jnp.stack(outputs)[:, None],
        jnp.stack(input_grads)[:, None],
        totals[0],
        totals[1],
        totals[2],
        totals[3],
        totals[4],
        totals[5],
    )


MESH = pl.DeviceIdType.MESH
ANY = pl.BlockSpec(memory_space=pl.ANY)
VMEM_BYTES = 63 * 2**20
BF = jnp.bfloat16
F32 = jnp.float32


def nn(a, b):
    return lax.dot_general(a, b, (((1,), (0,)), ((), ())), preferred_element_type=F32)


def nt(a, b):
    return lax.dot_general(a, b, (((1,), (1,)), ((), ())), preferred_element_type=F32)


def spot():
    z, f = lax.axis_index("seq"), lax.axis_index("fsdp")
    core = lax.rem(f, 2)
    x = lax.rem(f // 2, 2)
    y = f // 4
    return z, f, y, x, core


def remote(src, dst, send, recv, where):
    return pltpu.make_async_remote_copy(
        src_ref=src, dst_ref=dst, send_sem=send, recv_sem=recv, device_id=where, device_id_type=MESH
    )


class Rows:
    def __init__(self, z, f, core):
        base = f - core
        self.work, self.home = [], []
        for i in range(2):
            zw, cw = 2 * i + core, z // 2
            self.work.append((zw, base + cw, (zw == z) & (cw == core)))
            zh, ch = 2 * core + i, lax.rem(z, 2)
            self.home.append((zh, base + ch, (zh == z) & (ch == core)))
        self.z = z

    def greet(self, barrier):
        count = 0
        for zt, ft, same in self.work + self.home:

            @pl.when(jnp.logical_not(same))
            def _():
                pl.semaphore_signal(barrier, inc=1, device_id=(zt, ft), device_id_type=MESH)

            count = count + jnp.where(same, 0, 1)
        return count

    def start(self, src, dst, send, recv, local, out, piece=slice(None)):
        places = self.work if out else self.home
        slot = lax.rem(self.z, 2) if out else self.z // 2
        for i, (zt, ft, same) in enumerate(places):

            @pl.when(same)
            def _(i=i):
                pltpu.make_async_copy(src.at[i, piece], dst.at[slot, piece], local).start()

            @pl.when(jnp.logical_not(same))
            def _(i=i, zt=zt, ft=ft):
                remote(src.at[i, piece], dst.at[slot, piece], send.at[i], recv.at[slot], (zt, ft)).start()

    def wait(self, src, dst, send, recv, local, out):
        goes, comes = (self.work, self.home) if out else (self.home, self.work)
        for i, (zt, ft, same) in enumerate(goes):

            @pl.when(same)
            def _(i=i):
                pltpu.make_async_copy(src.at[i], dst.at[i], local).wait()

            @pl.when(jnp.logical_not(same))
            def _(i=i, zt=zt, ft=ft):
                remote(src.at[i], dst.at[i], send.at[i], recv.at[i], (zt, ft)).wait_send()

        for i, (zt, ft, same) in enumerate(comes):

            @pl.when(jnp.logical_not(same))
            def _(i=i, zt=zt, ft=ft):
                remote(src.at[i], dst.at[i], send.at[i], recv.at[i], (zt, ft)).wait_recv()


def halves(width):
    cut = (width // 128 // 2) * 128
    return pl.ds(0, cut), pl.ds(cut, width - cut)


SQRT_HALF = 0.7071067811865476
DENSITY = 0.3989422804014327
PIECES = 8
GROUP = 384
STEPS = 7


def moments(values):
    average = jnp.mean(values, axis=-1, keepdims=True)
    centred = values - average
    spread = jnp.mean(centred * centred, axis=-1, keepdims=True)
    scale = lax.rsqrt(spread + EPSILON)
    return centred * scale, scale


def norm_back(values, gain, grads):
    unit, scale = moments(values)
    spread = grads * gain
    inner = spread - jnp.mean(spread, axis=-1, keepdims=True)
    inner = inner - unit * jnp.mean(spread * unit, axis=-1, keepdims=True)
    return inner * scale, jnp.sum(grads * unit, axis=0, keepdims=True)


def rope_back(grads, cosine, sine):
    lane = lax.broadcasted_iota(jnp.int32, (1, 128), 1)
    low = lax.rem(lane, 64) < 32
    u = grads * sine
    return grads * cosine + jnp.where(low, pltpu.roll(u, 96, 1), -pltpu.roll(u, 32, 1))


class Sums:
    KINDS = 9

    @staticmethod
    def scratch(count, slots, rows, wide):
        dma = pltpu.SemaphoreType.DMA((count, Sums.KINDS))
        shapes = [(slots, 2, 2, 2), (count, 2, 2), (count, 2), (count, 2), (count,)]
        return [pltpu.VMEM(s + (rows, wide), BF) for s in shapes] + [dma, dma]

    def __init__(self, here, count, slots, refs):
        self.here, self.count, self.slots = here, count, slots
        self.acc, self.rx, self.r2, self.zr, self.zr2, self.send, self.recv = refs

    def copy(self, t, kind):
        h = self.here
        acc = self.acc.at[lax.rem(t, self.slots)]
        plan = {
            0: lambda: (acc.at[0, :, 1 - h.x], self.rx.at[t, 0], (h.z, h.fx)),
            1: lambda: (acc.at[1, 1 - h.y], self.rx.at[t, 1], (h.z, h.fy)),
            2: lambda: (self.rx.at[t, 0, 1 - h.y], self.r2.at[t, 0], (h.z, h.fy)),
            3: lambda: (self.rx.at[t, 1, 1 - h.x], self.r2.at[t, 1], (h.z, h.fx)),
            4: lambda: (self.r2.at[t], self.zr.at[t], (h.near, h.f)),
            5: lambda: (self.zr.at[t, 1 - h.own], self.zr2.at[t], (h.across, h.f)),
            6: lambda: (self.r2.at[t, h.own], self.r2.at[t, h.own], (h.across, h.f)),
            7: lambda: (self.r2.at[t, h.own], self.zr.at[t, h.own], (h.near, h.f)),
            8: lambda: (self.r2.at[t, 1 - h.own], self.zr.at[t, 1 - h.own], (h.near, h.f)),
        }
        src, dst, where = plan[kind]()
        return remote(src, dst, self.send.at[t, kind], self.recv.at[t, kind], where)

    def begin(self, t):
        self.copy(t, 0).start()
        self.copy(t, 1).start()

    def cross(self, t):
        h, s = self.here, lax.rem(t, self.slots)
        self.copy(t, 0).wait()
        self.rx[t, 0, 1 - h.y] = added(self.rx[t, 0, 1 - h.y], self.acc[s, 0, 1 - h.y, h.x])
        self.copy(t, 2).start()
        self.copy(t, 1).wait()
        self.rx[t, 1, 1 - h.x] = added(self.rx[t, 1, 1 - h.x], self.acc[s, 1, h.y, 1 - h.x])
        self.copy(t, 3).start()

    def plane(self, t):
        h, s = self.here, lax.rem(t, self.slots)
        self.copy(t, 2).wait()
        self.r2[t, 0] = added(self.r2[t, 0], self.rx[t, 0, h.y], self.acc[s, 0, h.y, h.x])
        self.copy(t, 3).wait()
        self.r2[t, 1] = added(self.r2[t, 1], self.rx[t, 1, h.x], self.acc[s, 1, h.y, h.x])

        @pl.when(h.outer)
        def _():
            self.copy(t, 4).start()

    def meet(self, t):
        h = self.here

        @pl.when(jnp.logical_not(h.outer))
        def _():
            self.copy(t, 4).wait_recv()
            self.zr[t, 1 - h.own] = added(self.zr[t, 1 - h.own], self.r2[t, 1 - h.own])
            self.copy(t, 5).start()

    def sums(self, t):
        h = self.here

        @pl.when(jnp.logical_not(h.outer))
        def _():
            self.copy(t, 5).wait()
            self.r2[t, h.own] = added(self.r2[t, h.own], self.zr[t, h.own], self.zr2[t])
            self.copy(t, 6).start()
            self.copy(t, 7).start()

    def spread(self, t):
        @pl.when(jnp.logical_not(self.here.outer))
        def _():
            self.copy(t, 6).wait_recv()
            self.copy(t, 8).start()

    def finish(self, t):
        @pl.when(jnp.logical_not(self.here.outer))
        def _():
            self.copy(t, 6).wait_send()
            self.copy(t, 7).wait_send()
            self.copy(t, 8).wait_send()

        @pl.when(self.here.outer)
        def _():
            self.copy(t, 4).wait_send()
            self.copy(t, 7).wait_recv()
            self.copy(t, 8).wait_recv()

    def total(self, act):
        for ref, there in ((self.zr, self.here.outer), (self.r2, jnp.logical_not(self.here.outer))):
            pl.when(there)(functools.partial(act, ref))

    LATER = ("cross", "plane", "meet", "sums", "spread", "finish")

    def pump(self, tick, amid, low, high, first, last, base, steps):
        for name, step in zip(self.LATER[::-1], steps[::-1]):
            if step % 2 == amid:
                continue
            stage = (step + 1) // 2
            if high - base - stage < first or low - base - stage >= last:
                continue
            t = tick - base - stage
            if low == high:
                getattr(self, name)(t)
            else:

                @pl.when((t >= first) & (t < last))
                def _(name=name, t=t):
                    getattr(self, name)(t)


def added(*terms):
    total = terms[0].astype(F32)
    for term in terms[1:]:
        total = total + term.astype(F32)
    return total.astype(BF)


class Halves:
    def __init__(self, ref):
        self.ref, self.at, self.size = ref, self, ref.shape[0] // 2

    def __getitem__(self, index):
        return self.ref.at[pl.ds((index[0] if isinstance(index, tuple) else index) * self.size, self.size)]


class Here:
    def __init__(self):
        self.z, self.f, self.y, self.x, self.core = spot()
        self.fx = self.f + 2 - 4 * self.x
        self.fy = self.f + 4 - 8 * self.y
        self.fc = self.f + 1 - 2 * self.core
        z = self.z
        self.outer = (z == 0) | (z == 3)
        self.near = jnp.where(z < 2, 1 - z, 5 - z)
        self.across = jnp.where(self.outer, z, 3 - z)
        self.own = jnp.where(z < 2, 0, 1)

    def greet(self, barrier, rows):
        for t in (self.fx, self.fy, self.fc):
            pl.semaphore_signal(barrier, inc=1, device_id=(self.z, t), device_id_type=MESH)
        pl.semaphore_signal(barrier, inc=1, device_id=(self.near, self.f), device_id_type=MESH)

        @pl.when(jnp.logical_not(self.outer))
        def _():
            pl.semaphore_signal(barrier, inc=1, device_id=(self.across, self.f), device_id_type=MESH)

        pl.semaphore_wait(barrier, rows.greet(barrier) + 4 + jnp.where(self.outer, 0, 1))


def lanes(start, size):
    return pl.ds(start if isinstance(start, int) else pl.multiple_of(start, 128), size)


def back_kernel(
    x2_h, mid_h, cot_h, in_h, down_h, qkv_h, out_h, q_h, k_h, v_h, mix_h, normed_h, rows_h, bias_h,
    gains, cosine, sine, lse,
    in_o, qkv_o, down_o, out_o, gain_o, outh_o, inh_o,
    x2, gl, acc_f, acc_g, win, wdown, xt, xts, gj, at, glc, gm, mt, dout, bias,
    kept, dx_kv, centres, terms_one, rows_b, dx, gs, gr,
    ld, wsem, ps, pr, gjs, gjr, ats, atr, kvs, kvr, gqs, gqr, dxs, dxr, fo, es, er, el,
    *sum_refs,
):
    h = Here()
    rows = Rows(h.z, h.f, h.core)
    wide = Sums(h, 11, 4, sum_refs[0:7])
    down = Sums(h, 2, 2, sum_refs[7:14])
    outs = Sums(h, 1, 1, sum_refs[14:21])
    gain = Sums(h, 1, 1, sum_refs[21:28])
    sib = (h.z, h.fc)

    def output_piece(n):
        size = half // 2 // PIECES
        piece = pl.ds(n * size if isinstance(n, int) else pl.multiple_of(n * size, size), size)
        rows.start(rows_b, outh_o, es.at[0], er.at[0], el.at[0], False, piece)

    def advance(tick, amid, low, high):
        wide.pump(tick, amid, low, high, 0, STEPS, 1, (4, 8, 12, 14, 16, 23))
        down.pump(tick, amid, low, high, 0, 2, 8, (6, 9, 11, 13, 18, 24))
        outs.pump(tick, amid, low, high, 0, 1, 11, (5, 6, 8, 15, 20, 22))
        wide.pump(tick, amid, low, high, 7, 11, 7, (6, 8, 12, 16, 19, 24))
        gain.pump(tick, amid, low, high, 0, 1, 18, (8, 11, 14, 19, 23, 24))

    gq = gj
    last_b = Halves(dout)
    mine = dout.at[:, pl.ds(0, 512)]
    wout = at.at[pl.ds(0, 1024)]
    half = x2.shape[0]
    own_lanes = lambda i: lanes((2 * i + h.core) * 128, 128)
    sib_lanes = lambda i: lanes((2 * i + 1 - h.core) * 128, 128)

    def load(src, dst, k):
        return pltpu.make_async_copy(src, dst, ld.at[k])

    last_group = down_h.shape[0] - (STEPS - 1) * GROUP

    def weights(t, size):
        s = lax.rem(t, 2)
        return [
            pltpu.make_async_copy(in_h.at[:, :, lanes(t * GROUP, GROUP)], win.at[s, :, :, pl.ds(0, GROUP)], wsem.at[s, 0]),
            pltpu.make_async_copy(in_h.at[:, :, lanes((STEPS + t) * GROUP, GROUP)], win.at[s, :, :, pl.ds(GROUP, GROUP)], wsem.at[s, 2]),
            pltpu.make_async_copy(down_h.at[pl.ds(pl.multiple_of(t * GROUP, 16), size)], wdown.at[s, pl.ds(0, size)], wsem.at[s, 1]),
        ]

    def each(t, act):
        @pl.when(t < STEPS - 1)
        def _():
            for c in weights(t, GROUP):
                act(c)

        @pl.when(t == STEPS - 1)
        def _():
            for c in weights(t, last_group):
                act(c)

    def qkv_weights(i):
        s = lax.rem(i, 2)
        return [
            pltpu.make_async_copy(qkv_h.at[:, :, lanes(n * 1024 + i * 256, 256)], win.at[s, :, :, pl.ds(n * 256, 256)], wsem.at[s, n])
            for n in range(3)
        ]

    first = [load(x2_h, x2, 0), load(cot_h, gl, 1), load(mid_h, acc_f, 2)]
    for c in first + weights(0, GROUP):
        c.start()
    h.greet(pltpu.get_barrier_semaphore(), rows)

    first[0].wait()
    first[1].wait()
    glc_send = remote(mine, glc.at[pl.ds(half, half)], ps.at[0], pr.at[0], sib)
    glc[:half] = gl[:, lanes(h.core * 512, 512)]
    mine[...] = gl[:, lanes((1 - h.core) * 512, 512)]
    glc_send.start()

    def transpose_out(src):
        for i in range(4):
            xt_rows = pl.ds(i * 128, 128)
            yield xt_rows, src[:, own_lanes(i)].T, src[:, sib_lanes(i)].T

    for at_rows, a, b in transpose_out(x2):
        xt[at_rows, :half] = a
        xts[at_rows] = b
    xt_send = remote(xts, xt.at[:, pl.ds(half, half)], ps.at[1], pr.at[1], sib)
    xt_send.start()
    first[2].wait()

    def gj_send(t):
        s = lax.rem(t, 2)
        return remote(gj.at[s, pl.ds(0, half)], gj.at[s, pl.ds(half, half)], gjs.at[s], gjr.at[s], sib)

    def at_send(t):
        r = pl.ds(pl.multiple_of(t * GROUP, 128), GROUP)
        return remote(at.at[r, pl.ds(0, half)], at.at[r, pl.ds(half, half)], ats.at[t], atr.at[t], sib)

    def feed(t, _):
        s = lax.rem(t, 2)
        advance(t, 0, 0, STEPS)

        @pl.when(t < STEPS)
        def _():
            each(t, lambda c: c.wait())
            each(t + 1, lambda c: c.start())

            w = win[s].reshape(8 * 128, 768)
            wa, wc, wd = w[:, :GROUP], w[:, GROUP:], wdown[s]
            a, c = nn(x2[...], wa), nn(x2[...], wc)
            grad_active = nt(gl[...], wd)
            phi = 0.5 * (1.0 + lax.erf(a * SQRT_HALF))
            gate = a * phi
            slope = phi + a * (jnp.exp(-0.5 * a * a) * DENSITY)
            active = (gate * c).astype(BF)
            ga = (slope * c * grad_active).astype(BF)
            gc = (gate * grad_active).astype(BF)

            @pl.when(t >= 2)
            def _():
                gj_send(t - 2).wait_send()

            gj[s, :half, :GROUP] = ga
            gj[s, :half, GROUP:] = gc
            at[pl.ds(pl.multiple_of(t * GROUP, 128), GROUP), :half] = active.T
            at_send(t).start()
            acc_f[...] += nn(active, wd)
            back = nt(ga, wa) + nt(gc, wc)

            @pl.when(t == 0)
            def _():
                acc_g[...] = back

            @pl.when(t > 0)
            def _():
                acc_g[...] += back

        advance(t, 1, 0, STEPS)

        @pl.when(t == 1)
        def _():
            xt_send.wait()

        @pl.when(t >= 1)
        def _():
            u = t - 1
            gj_send(u).wait_recv()
            term = nn(xt[...], gj[lax.rem(u, 2)]).astype(BF)
            for o in range(4):
                for k in range(2):
                    wide.acc[lax.rem(u, 4), k, o // 2, o % 2] = term[o * 128 : o * 128 + 128, k * GROUP : k * GROUP + GROUP]
            wide.begin(u)

        @pl.when(t < STEPS)
        def _():
            gj_send(t).start()

        return 0

    lax.fori_loop(0, STEPS + 1, feed, 0)
    gj_send(STEPS - 2).wait_send()
    gj_send(STEPS - 1).wait_send()

    rows_b[...] = acc_f[...].astype(BF).reshape(2, half // 2, -1)
    again = [load(mid_h, acc_f, 2), load(mix_h, x2, 3), load(out_h, wout, 4), load(normed_h, x2, 0), load(bias_h, bias, 5)]
    for n in (0, 1, 4):
        again[n].start()
    for t in range(STEPS):
        at_send(t).wait()
    glc_send.wait()
    for j in range(2):
        advance(8 + j, 0, 8 + j, 8 + j)
        output_piece(j)
        term = nn(at[...], glc[:, j * 256 : j * 256 + 256])
        for f in range(8):
            down.acc[j, f % 2, f // 4, f // 2 % 2] = term[f * 328 : f * 328 + 336].astype(BF)
        advance(8 + j, 1, 8 + j, 8 + j)
        down.begin(j)
    again[2].start()
    heads = [load(k_h, at.at[pl.ds(2 * half, 2 * half)], 6), load(q_h, at.at[pl.ds(4 * half, half)], 8), load(v_h, at.at[pl.ds(0, 2 * half)], 7)]
    heads[0].start()
    heads[1].start()

    advance(10, 0, 10, 10)
    output_piece(2)
    again[0].wait()
    back, gain_two = norm_back(acc_f[...], gains[1:2], acc_g[...])
    grad_mid = gl[...].astype(F32) + back
    acc_f[...] = grad_mid
    gm[:half] = grad_mid.astype(BF)
    gm_send = remote(gm.at[pl.ds(0, half)], gm.at[pl.ds(half, half)], ps.at[2], pr.at[2], sib)
    gm_send.start()
    again[1].wait()
    for at_rows, a, b in transpose_out(x2):
        mt[at_rows, :half] = a
        xts[at_rows] = b
    mt_send = remote(xts, mt.at[:, pl.ds(half, half)], ps.at[3], pr.at[3], sib)
    mt_send.start()
    rows_in = load(rows_h, gl, 1)
    rows_in.start()
    advance(10, 1, 10, 10)
    again[2].wait()
    dout[...] = nt(gm[:half], wout[...]).astype(BF)
    heads[2].start()
    for j in range(8):
        products = (x2[:, j * 128 : j * 128 + 128].astype(F32) * dout[:, j * 128 : j * 128 + 128].astype(F32)).T
        for e in range(2):
            centres[j, e : e + 1] = jnp.sum(products[64 * e : 64 * e + 64], axis=0, keepdims=True)
    again[3].start()
    advance(11, 0, 11, 11)
    output_piece(3)
    gm_send.wait()
    mt_send.wait()
    term = nn(mt[...], gm[...]).astype(BF)
    for o in range(4):
        for k in range(2):
            outs.acc[0, k, o // 2, o % 2] = term[o * 128 : o * 128 + 128, k * 512 : k * 512 + 512]
    advance(11, 1, 11, 11)
    outs.begin(0)
    again[3].wait()
    for at_rows, a, b in transpose_out(x2):
        xt[at_rows, :half] = a
        xts[at_rows] = b
    nt_send = remote(xts, xt.at[:, pl.ds(half, half)], ps.at[4], pr.at[4], sib)
    nt_send.start()
    again[4].wait()
    for c in heads:
        c.wait()

    lane = lax.broadcasted_iota(jnp.int32, (1, 128), 1)

    def kv_rows(s):
        return pl.ds(s * half if isinstance(s, int) else pl.multiple_of(s * half, half), half)

    def kv_send(i):
        s = lax.rem(i, 2)
        return remote(dx_kv, glc.at[kv_rows(s)], kvs.at[s], kvr.at[s], sib)

    def gq_send(i):
        s = lax.rem(i, 2)
        return remote(gq.at[s, pl.ds(0, half)], gq.at[s, pl.ds(half, half)], gqs.at[s], gqr.at[s], sib)

    def stashed(b, n, j):
        return jnp.concatenate([kept[b, pl.ds(n * 128, 128), pl.ds(m * 256 + j * 128, 128)] for m in range(4)], axis=0)

    def attend_step(i, _):
        s = lax.rem(i, 2)
        tick = 12 + i
        advance(tick, 0, 12, 17)

        @pl.when(i < 2)
        def _():
            output_piece(4 + 2 * i)
            output_piece(5 + 2 * i)

        @pl.when(i < 4)
        def _():
            for c in qkv_weights(i):
                c.start()

            @pl.when(i >= 1)
            def _():
                kv_send(i - 1).wait_send()

            for j in range(2):
                col = lanes(i * 256 + j * 128, 128)
                q = at[pl.ds(4 * half, half), col] * jnp.asarray(0.125, BF)
                v, k = at[pl.ds(0, 2 * half), col], at[pl.ds(2 * half, 2 * half), col]
                do = dout[:, col]
                kt = k.T
                none = jnp.zeros_like(q)
                dqs, dks, dvs = [], [], []
                for e in range(2):
                    part = (lane < 64) if e == 0 else (lane >= 64)
                    centre = centres[2 * i + j, e : e + 1, :]
                    p = jnp.exp(nt(k, jnp.where(part, q, none)) + bias[...].astype(F32) - lse[2 * i + j, e : e + 1, :])
                    dvs.append(nn(p.astype(BF), do))
                    ds = (p * (nt(v, jnp.where(part, do, none)) - centre)).astype(BF)
                    dks.append(nn(ds, q))
                    dqs.append(nn(kt, ds))
                c = pl.ds(j * 128, 128)
                dq = jnp.concatenate([dqs[0][:64], dqs[1][64:]], axis=0).T
                dk = jnp.where(lane < 64, dks[0], dks[1]).astype(BF)
                dv = jnp.where(lane < 64, dvs[0], dvs[1]).astype(BF)
                for n, part in enumerate(((dq * 0.125).astype(BF), dk, dv)):
                    for m in range(4):
                        kept[s, pl.ds(n * 128, 128), pl.ds(m * 256 + j * 128, 128)] = part[m * 128 : m * 128 + 128]
                dx_kv[:, pl.ds(j * 128, 128)] = dk[half:]
                dx_kv[:, pl.ds(256 + j * 128, 128)] = dv[half:]

        advance(tick, 1, 12, 17)

        @pl.when((i >= 1) & (i <= 4))
        def _():
            u = i - 1
            b = lax.rem(u, 2)

            @pl.when(u >= 2)
            def _():
                gq_send(u - 2).wait_send()

            kv_send(u).wait_recv()
            for j in range(2):
                c = slice(j * 128, j * 128 + 128)
                g = stashed(b, 0, j).astype(F32)
                gq[b, :half, j * 128 : j * 128 + 128] = rope_back(g, cosine[...], sine[...]).astype(BF)
                c = slice(256 + j * 128, 256 + j * 128 + 128)
                g = added(stashed(b, 1, j), glc[kv_rows(b), j * 128 : j * 128 + 128]).astype(F32)
                gq[b, :half, c] = rope_back(g, cosine[...], sine[...]).astype(BF)
                c = slice(512 + j * 128, 512 + j * 128 + 128)
                gq[b, :half, c] = added(stashed(b, 2, j), glc[kv_rows(b), 256 + j * 128 : 256 + j * 128 + 128])
            for c in qkv_weights(u):
                c.wait()
            back = nt(gq[b, :half], win[b].reshape(1024, 768))

            @pl.when(u == 0)
            def _():
                acc_g[...] = back

            @pl.when(u > 0)
            def _():
                acc_g[...] += back

        @pl.when(i == 2)
        def _():
            nt_send.wait()

        @pl.when(i == 5)
        def _():
            rows_in.wait()
            back, gain_one = norm_back(gl[...].astype(F32), gains[0:1], acc_g[...])
            terms_one[...] = gain_one
            dout[...] = (acc_f[...] + back).astype(BF)
            rows.start(last_b, inh_o, es.at[1], er.at[1], el.at[1], False)

        @pl.when(i >= 2)
        def _():
            u = i - 2
            gq_send(u).wait_recv()
            term = nn(xt[...], gq[lax.rem(u, 2)]).astype(BF)
            a = lax.rem(u + 7, 4)
            for o in range(4):
                for k in range(2):
                    wide.acc[a, k, o // 2, o % 2] = term[o * 128 : o * 128 + 128, k * GROUP : k * GROUP + GROUP]
            wide.begin(u + 7)

        @pl.when(i < 4)
        def _():
            kv_send(i).start()

        @pl.when((i >= 1) & (i <= 4))
        def _():
            gq_send(i - 1).start()

        return 0

    lax.fori_loop(0, 6, attend_step, 0)

    gain_one = terms_one[...]
    terms = (gain_one, gain_two)
    for k in range(2):
        for o in range(4):
            for ref, part in ((gain.acc.at[0], h.core), (gs, 1 - h.core)):
                low, high = terms[k][:, 256 * o : 256 * o + 128], terms[k][:, 256 * o + 128 : 256 * o + 256]
                value = jnp.where(part == 0, low, high)
                ref[k, o // 2, o % 2] = jnp.broadcast_to(value, (16, 128)).astype(BF)
    gs_send = remote(gs, gr, ps.at[5], pr.at[5], sib)
    gs_send.start()
    advance(18, 0, 18, 18)
    advance(18, 1, 18, 18)
    def down_swap(act, ref):
        for j in range(2):
            act(remote(ref.at[j, 1 - h.core], dx.at[j], dxs.at[j], dxr.at[j], sib))

    gs_send.wait()
    for k in range(2):
        for o in range(4):
            gain.acc[0, k, o // 2, o % 2] = added(gain.acc[0, k, o // 2, o % 2], gr[k, o // 2, o % 2])
    gain.begin(0)
    for tick in range(19, 31):
        advance(tick, 0, tick, tick)
        advance(tick, 1, tick, tick)
        if tick == 22:
            down.total(functools.partial(down_swap, lambda c: c.start()))
    down.total(functools.partial(down_swap, lambda c: c.wait()))
    kv_send(3).wait_send()
    gq_send(2).wait_send()
    gq_send(3).wait_send()

    def write_wide(act, ref):
        for t in range(STEPS):
            for k in range(2):
                act(pltpu.make_async_copy(ref.at[t, k], in_o.at[k, :, pl.ds(t * GROUP, GROUP)], fo.at[0, 2 * t + k]))
        for i in range(4):
            parts = ((0, 0, 256, 0), (0, 256, 128, 1024), (1, 0, 128, 1152), (1, 128, 256, 2048))
            for n, (k, at_col, size, to) in enumerate(parts):
                src = ref.at[STEPS + i, k, :, pl.ds(at_col, size)]
                act(pltpu.make_async_copy(src, qkv_o.at[:, pl.ds(to + i * 256, size)], fo.at[1, 4 * i + n]))

    def write_out(act, ref):
        for k in range(2):
            act(pltpu.make_async_copy(ref.at[0, k], out_o.at[:, pl.ds(k * 512, 512)], fo.at[2, k]))

    def write_gain(act, ref):
        act(pltpu.make_async_copy(ref, gain_o, fo.at[2, 2]))

    def write_down(act, ref):
        for j in range(2):
            here, there = lanes(h.core * 512 + j * 256, 256), lanes((1 - h.core) * 512 + j * 256, 256)
            act(pltpu.make_async_copy(ref.at[j, h.core], down_o.at[:, here], fo.at[2, 3 + j]))
            act(pltpu.make_async_copy(dx.at[j], down_o.at[:, there], fo.at[2, 5 + j]))

    for act in (lambda c: c.start(), lambda c: c.wait()):
        for group, write in ((wide, write_wide), (outs, write_out), (gain, write_gain), (down, write_down)):
            group.total(functools.partial(write, act))
    rows.wait(rows_b, outh_o, es.at[0], er.at[0], el.at[0], False)
    rows.wait(last_b, inh_o, es.at[1], er.at[1], el.at[1], False)


def back_all(x2, middle, cot, in_f, down_f, qkv_f, out_f, q, k, v, mixture, normed, rows_in, bias, gains, cosine, sine, lse):
    dma = pltpu.SemaphoreType.DMA
    half, wide = x2.shape

    def buf(*s, kind=BF):
        return pltpu.VMEM(s, kind)

    def shape(*s):
        return jax.ShapeDtypeStruct(s, BF)

    whole = pl.BlockSpec(memory_space=pltpu.VMEM)
    sums = [(11, 4, 128, GROUP), (2, 2, 336, 256), (1, 1, 128, 512), (1, 1, 16, 128)]
    scratch = [
        buf(half, wide), buf(half, wide), buf(half, wide, kind=F32), buf(half, wide, kind=F32),
        buf(2, 8, 128, 768), buf(2, GROUP, wide), buf(half, 2 * half), buf(half, half),
        buf(2, 2 * half, 768), buf(STEPS * GROUP, 2 * half), buf(2 * half, half),
        buf(2 * half, wide), buf(half, 2 * half), buf(half, wide),
        buf(2 * half, half),
        buf(2, GROUP, wide), buf(half, 512), buf(8, 2, half, kind=F32), buf(1, wide, kind=F32),
        buf(2, half // 2, wide), buf(2, 336, 256), buf(2, 2, 2, 16, 128), buf(2, 2, 2, 16, 128),
        dma((9,)), dma((2, 3)), dma((6,)), dma((6,)), dma((2,)), dma((2,)), dma((STEPS,)), dma((STEPS,)),
        dma((2,)), dma((2,)), dma((2,)), dma((2,)), dma((2,)), dma((2,)), dma((3, 16)),
        dma((2, 2)), dma((2, 2)), dma((2,)),
    ]
    for s in sums:
        scratch += Sums.scratch(*s)
    return pl.pallas_call(
        back_kernel,
        out_shape=[
            shape(2, 128, STEPS * GROUP), shape(128, 3 * wide), shape(336, wide), shape(128, wide), shape(1, 2, 16, 128),
            shape(2, half // 2, wide), shape(2, half // 2, wide),
        ],
        in_specs=[ANY] * 14 + [whole] * 4,
        out_specs=[ANY] * 7,
        scratch_shapes=scratch,
        compiler_params=pltpu.CompilerParams(collective_id=2, has_side_effects=True, vmem_limit_bytes=VMEM_BYTES),
        name="feed_forward_and_backward",
    )(x2, middle, cot, in_f, down_f, qkv_f, out_f, q, k, v, mixture, normed, rows_in, bias, gains, cosine, sine, lse)


def rope(values, cosine, sine):
    lane = lax.broadcasted_iota(jnp.int32, (1, 128), 1)
    turned = jnp.where(lax.rem(lane, 64) < 32, -pltpu.roll(values, 96, 1), pltpu.roll(values, 32, 1))
    return values * cosine + turned * sine


def front_kernel(
    attn_h, ffn_h, qkv_h, out_h, in_h, down_h, tok_f, cot_f, starts_f, inverse,
    in_o, down_o, qkv_o, out_o, cot_o, tok_o, x2_o, mid_o, q_o, k_o, v_o, mix_o, normed_o, bias_o,
    gains_o, cos_o, sin_o, lse_o,
    gains_v, qkv_v, out_v, tok_v, starts_v, held_in, held_down, mid, normed, x2, q, k, v, mix, bias,
    gains_h, starts_h, tok_h, cot_h, cot_w,
    ss, rs, ls, es, er, el, ds_, dr, kvs, kvr, ws,
):
    h = Here()
    rows = Rows(h.z, h.f, h.core)
    z, f, core = h.z, h.f, h.core
    fx, fy, fc = h.fx, h.fy, h.fc
    fd = fx + 4 - 8 * h.y
    sib = (z, fc)
    half = normed.shape[0]
    shards = (gains_h, qkv_h, out_h, in_h, down_h)
    wholes = (gains_v, qkv_v, out_v, in_o, down_o)

    def same(whole, i, cols=None):
        return whole.at[i] if cols is None else whole.at[i, :, cols]

    def copy(w, k):
        whole, shard = wholes[w], shards[w]
        a, b = halves(shard.shape[1])
        place = {3: (fx, a), 4: (fy, b), 5: (fx, None), 6: (fy, None), 7: (fd, a), 8: (fd, b)}
        if k < 3:
            src, dst = shard, whole.at[f]
        else:
            src = dst = same(whole, *place[k])
        where = (fx, fy, fc, fy, fx, fc, fc, fc, fc)[k]
        return remote(src, dst, ss.at[w, k], rs.at[w, k], (z, where))

    def first(w):
        for k in range(3):
            copy(w, k).start()

    def second(w):
        for k in (0, 1):
            copy(w, k).wait_recv()
            copy(w, k + 3).start()
            copy(w, k + 5).start()

    def third(w):
        for k in (3, 4):
            copy(w, k).wait_recv()
            copy(w, k + 4).start()

    def rest(w):
        for k in (2, 5, 6, 7, 8):
            copy(w, k).wait_recv()

    def own(w):
        dst = {3: held_in, 4: held_down}.get(w)
        return pltpu.make_async_copy(shards[w], wholes[w].at[f] if dst is None else dst, ls.at[w])

    def own_out(w):
        return pltpu.make_async_copy({3: held_in, 4: held_down}[w], wholes[w].at[f], ls.at[w])

    wide_in = [
        pltpu.make_async_copy(tok_f, mid, el.at[0]),
        pltpu.make_async_copy(cot_f, cot_w, el.at[1]),
    ]
    for c in wide_in:
        c.start()
    gains_h[:, :128] = jnp.broadcast_to(attn_h[...].astype(F32), (16, 128)).astype(BF)
    gains_h[:, 128:] = jnp.broadcast_to(ffn_h[...].astype(F32), (16, 128)).astype(BF)
    starts_h[...] = jnp.zeros(starts_h.shape, jnp.int32)
    starts_h[:2, :8] = starts_f[...]
    for w in range(5):
        own(w).start()
    for c, ref, low in zip(wide_in, (mid, cot_w), (tok_h, cot_h)):
        c.wait()
        low[...] = ref[...].astype(BF)
    h.greet(pltpu.get_barrier_semaphore(), rows)
    info = remote(starts_h, starts_v.at[core], ds_.at[0], dr.at[0], sib)
    own_info = pltpu.make_async_copy(starts_h, starts_v.at[core], el.at[2])
    info.start()
    own_info.start()
    rows.start(tok_h, tok_v, es.at[0], er.at[0], el.at[0], True)
    for w in range(3):
        first(w)
    info.wait()
    own_info.wait()

    lane = lax.broadcasted_iota(jnp.int32, (1, 128), 1)
    begins = starts_v[lax.rem(z, 2), pl.ds(z // 2, 1), :]
    inside = lane < 8

    def documents(base):
        place = lax.broadcasted_iota(jnp.int32, (half, 128), 0) + base
        before = (begins <= place) & inside
        number = jnp.sum(jnp.where(before, 1.0, 0.0), axis=1, keepdims=True)
        begin = jnp.max(jnp.where(before, begins, 0).astype(F32), axis=1, keepdims=True)
        return place, number, begin

    place, number, begin = documents(core * half)
    angle = (place.astype(F32) - begin) * inverse[...]
    cos_o[...] = jnp.cos(angle)
    sin_o[...] = jnp.sin(angle)
    across = jnp.broadcast_to(number, (half, 128)).T[0:1, :]
    _, other, _ = documents((1 - core) * half)
    bias[:half] = jnp.where(number == across, 0.0, MASKED_SCORE).astype(BF)
    bias[half:] = jnp.where(other == across, 0.0, MASKED_SCORE).astype(BF)

    second(0)
    second(1)
    second(2)
    rows.start(cot_h, cot_o, es.at[1], er.at[1], el.at[1], True)
    own(3).wait()
    own(4).wait()
    own_out(3).start()
    own_out(4).start()
    first(3)
    first(4)
    third(0)
    rest(0)
    own(0).wait()
    for n in range(2):
        for i in range(8):
            gains_o[n : n + 1, i * 128 : i * 128 + 128] = gains_v[i, 0:1, n * 128 : n * 128 + 128].astype(F32)
    rows.wait(tok_h, tok_v, es.at[0], er.at[0], el.at[0], True)
    x = tok_v[...].reshape(half, -1).astype(F32)
    unit, _ = moments(x)
    normed[...] = (unit * gains_o[0:1]).astype(BF)
    saved = [pltpu.make_async_copy(tok_v, tok_o, ws.at[0]), pltpu.make_async_copy(normed, normed_o, ws.at[1]),
             pltpu.make_async_copy(bias, bias_o, ws.at[2])]
    for c in saved:
        c.start()
    third(1)
    rest(1)
    own(1).wait()
    saved.append(pltpu.make_async_copy(qkv_v, qkv_o, ws.at[3]))
    saved[-1].start()

    def pair_send(n, i):
        ref = (k, v)[n]
        cols = pl.ds(i * 256, 256)
        return remote(ref.at[pl.ds(0, half), cols], ref.at[pl.ds(half, half), cols], kvs.at[n, i], kvr.at[n, i], sib)

    wide = normed.shape[1]
    for n, ref in ((1, k), (2, v), (0, q)):
        for i in range(4):
            part = nn(normed[...], qkv_v[:, :, n * wide + i * 256 : n * wide + i * 256 + 256].reshape(wide, 256))
            for j in range(2):
                cols = slice(i * 256 + j * 128, i * 256 + j * 128 + 128)
                value = part[:, j * 128 : j * 128 + 128]
                value = value if n == 2 else rope(value, cos_o[...], sin_o[...])
                ref[:half, cols] = value.astype(BF)
            if n:
                pair_send(n - 1, i).start()
    third(2)
    for n in range(2):
        for i in range(4):
            pair_send(n, i).wait()
    for n, (ref, dst) in enumerate(((q, q_o), (k, k_o), (v, v_o))):
        saved.append(pltpu.make_async_copy(ref, dst, ws.at[4 + n]))
        saved[-1].start()

    def attend(i, _):
        cols = lanes(i * 128, 128)
        queries = q[:, cols] * jnp.asarray(0.125, BF)
        keys = k[:, cols]
        vt = v[:, cols].T
        outs = []
        for e in range(2):
            part = (lane < 64) if e == 0 else (lane >= 64)
            scores = nt(keys, jnp.where(part, queries, jnp.zeros_like(queries))) + bias[...].astype(F32)
            top = jnp.max(scores, axis=0, keepdims=True)
            p = jnp.exp(scores - top)
            total = jnp.sum(p, axis=0, keepdims=True)
            outs.append(nn(vt, p.astype(BF)) / total)
            lse_o[i, e : e + 1, :] = top + jnp.log(total)
        mix[:, cols] = jnp.concatenate([outs[0][:64], outs[1][64:]], axis=0).T.astype(BF)
        return 0

    lax.fori_loop(0, 8, attend, 0)
    second(3)
    rest(2)
    own(2).wait()
    saved.append(pltpu.make_async_copy(out_v, out_o, ws.at[7]))
    saved[-1].start()
    saved.append(pltpu.make_async_copy(mix, mix_o, ws.at[8]))
    saved[-1].start()
    middle = tok_v[...].reshape(half, -1).astype(F32) + nn(mix[...], out_v[...].reshape(wide, wide))
    mid[...] = middle.reshape(mid.shape)
    unit, _ = moments(middle)
    x2[...] = (unit * gains_o[1:2]).astype(BF)
    for ref, dst in ((mid, mid_o), (x2, x2_o)):
        saved.append(pltpu.make_async_copy(ref, dst, ws.at[len(saved)]))
        saved[-1].start()
    second(4)
    third(3)
    third(4)
    rest(3)
    rest(4)
    own_out(3).wait()
    own_out(4).wait()
    for w in range(5):
        for kind in range(9):
            copy(w, kind).wait_send()
    for c in saved:
        c.wait()
    rows.wait(cot_h, cot_o, es.at[1], er.at[1], el.at[1], True)


def front_all(attn_gain, ffn_gain, qkv, out, inw, down, tok, cot, starts, inverse):
    dma = pltpu.SemaphoreType.DMA
    half, wide = 2 * tok.shape[1], tok.shape[2]

    def shape(*s, kind=BF):
        return jax.ShapeDtypeStruct(s, kind)

    def buf(*s, kind=BF):
        return pltpu.VMEM(s, kind)

    whole = pl.BlockSpec(memory_space=pltpu.VMEM)
    return pl.pallas_call(
        front_kernel,
        out_shape=[
            shape(8, *inw.shape), shape(8, *down.shape), shape(8, *qkv.shape), shape(8, *out.shape),
            shape(*cot.shape), shape(*tok.shape), shape(half, wide), shape(*tok.shape, kind=F32),
            shape(half, wide), shape(2 * half, wide), shape(2 * half, wide), shape(half, wide),
            shape(half, wide), shape(2 * half, half),
            shape(2, wide, kind=F32), shape(half, 128, kind=F32), shape(half, 128, kind=F32), shape(8, 2, half, kind=F32),
        ],
        in_specs=[whole] * 2 + [ANY] * 6 + [whole] * 2,
        out_specs=[ANY] * 14 + [whole] * 4,
        scratch_shapes=[
            buf(8, 16, 256), buf(8, *qkv.shape), buf(8, *out.shape), buf(*tok.shape), buf(2, 8, 128, kind=jnp.int32),
            buf(*inw.shape), buf(*down.shape), buf(*tok.shape, kind=F32), buf(half, wide), buf(half, wide),
            buf(half, wide), buf(2 * half, wide), buf(2 * half, wide), buf(half, wide), buf(2 * half, half),
            buf(16, 256), pltpu.VMEM((8, 128), jnp.int32), buf(*tok.shape), buf(*cot.shape), buf(*cot.shape, kind=F32),
            dma((5, 9)), dma((5, 9)), dma((5,)), dma((2, 2)), dma((2, 2)), dma((3,)), dma((1,)), dma((1,)),
            dma((2, 4)), dma((2, 4)), dma((12,)),
        ],
        compiler_params=pltpu.CompilerParams(collective_id=1, has_side_effects=True, vmem_limit_bytes=VMEM_BYTES),
        name="gather_and_attention",
    )(attn_gain, ffn_gain, qkv, out, inw, down, tok, cot, starts, inverse)


def chip_streams(tokens, cotangent, doc_starts, qkv_weight, out_weight, in_weight, down_weight, attn_gain, ffn_gain):
    wide = tokens.shape[3]
    half = 2 * tokens.shape[2]
    units = down_weight.shape[0] * 8
    spare = jnp.zeros((in_weight.shape[0], STEPS * GROUP - units), BF)
    in_parts = jnp.concatenate([in_weight[:, :units], spare, in_weight[:, units:], spare], axis=1)
    inverse = ROPE_THETA ** (-jnp.arange(0, HEAD_DIM, 2, dtype=F32) / HEAD_DIM)
    (in_f, down_f, qkv_f, out_f, cot, rows_low, x2, middle, q, k, v, mixture, normed, bias, both_gains, cosine, sine, lse) = front_all(
        attn_gain[None], ffn_gain[None], qkv_weight, out_weight, in_parts, down_weight,
        tokens[:, 0], cotangent[:, 0], doc_starts[:, 0], jnp.tile(inverse, 4)[None],
    )
    in_t, qkv_t, down_t, out_t, gain_t, out_home, in_home = back_all(
        x2, middle.reshape(half, wide), cot.reshape(half, wide), in_f, down_f.reshape(units, wide), qkv_f, out_f.reshape(wide, wide), q, k, v,
        mixture, normed, rows_low.reshape(half, wide), bias, both_gains, cosine, sine, lse,
    )
    return (
        out_home[:, None].astype(F32),
        in_home[:, None].astype(F32),
        qkv_t.astype(F32),
        out_t.astype(F32),
        jnp.concatenate([in_t[0, :, :units], in_t[1, :, :units]], axis=1).astype(F32),
        down_t[: down_weight.shape[0]].astype(F32),
        gain_t[0, 0, 0].astype(F32),
        gain_t[0, 1, 0].astype(F32),
    )


def solution(mesh):
    whole_chips = dict(mesh.shape) == {"seq": 4, "fsdp": 8}
    return jax.shard_map(
        chip_streams if whole_chips else shards,
        mesh=mesh,
        in_specs=(
            P(None, "fsdp", "seq", None),
            P(None, "fsdp", "seq", None),
            P(None, "fsdp", None),
            P("fsdp", None),
            P("fsdp", None),
            P("fsdp", None),
            P("fsdp", None),
            P("fsdp"),
            P("fsdp"),
        ),
        out_specs=(
            P(None, "fsdp", "seq", None),
            P(None, "fsdp", "seq", None),
            P("fsdp", None),
            P("fsdp", None),
            P("fsdp", None),
            P("fsdp", None),
            P("fsdp"),
            P("fsdp"),
        ),
        check_vma=False,
    )
```

```python
import functools
from functools import partial

import jax
import jax.numpy as jnp
from jax import lax
from jax.experimental import pallas as pl
from jax.experimental.pallas import tpu as pltpu
from jax.sharding import PartitionSpec as P

HEADS = 16
HEAD_DIM = 64


EPSILON = 1e-05
ROPE_THETA = 160000.0
MASKED_SCORE = -1e30


def as_sent(x):

    def short(part):
        return part.astype(jnp.bfloat16) if part.dtype == jnp.float32 else part

    return jax.tree.map(short, x)


def layer_norm(values, norm_gain):
    average = jnp.mean(values, axis=-1, keepdims=True)
    centred = values - average
    spread = jnp.mean(centred * centred, axis=-1, keepdims=True)
    return centred * lax.rsqrt(spread + EPSILON) * norm_gain


def gated_gelu(joined):
    half_width = joined.shape[-1] // 2
    return jax.nn.gelu(joined[:, :half_width], approximate=False) * joined[:, half_width:]


def rotate(values, cosine_table, sine_table):
    half_width = values.shape[-1] // 2
    turned = jnp.concatenate([-values[..., half_width:], values[..., :half_width]], axis=-1)
    return values * cosine_table + turned * sine_table


def rope_tables(starts, places, head_width):
    preceding = starts[None, :] <= places[:, None]
    doc_begin = jnp.max(jnp.where(preceding, starts[None, :], 0), axis=-1)
    offsets = (places - doc_begin).astype(jnp.float32)
    inverse = ROPE_THETA ** (-jnp.arange(0, head_width, 2, dtype=jnp.float32) / head_width)
    angles = offsets[:, None] * inverse[None, :]
    angles = jnp.concatenate([angles, angles], axis=-1)
    return (jnp.cos(angles), jnp.sin(angles))


def segment_ids(starts, places):
    return jnp.sum((starts[None, :] <= places[:, None]).astype(jnp.int32), axis=-1) - 1


def turn_pair(pair, cosine_table, sine_table):
    shaped = pair.reshape(pair.shape[0], 2, HEADS, HEAD_DIM)
    turned = rotate(shaped, cosine_table[:, None, None, :], sine_table[:, None, None, :])
    return turned.reshape(pair.shape[0], 2 * HEADS * HEAD_DIM)


def attend_forward(queries, keys_in, values_in, segments, head_count):
    length = queries.shape[0]
    head_width = queries.shape[1] // head_count
    block_rows = min(512, length)
    blocks = length // block_rows
    keyset = keys_in.reshape(length, head_count, head_width)
    valueset = values_in.reshape(length, head_count, head_width)
    factor = head_width ** (-0.5)

    def one_block(pieces):
        query_rows, block_segs = pieces
        scores = (
            jnp.einsum("qhd,khd->hqk", query_rows, keyset, preferred_element_type=jnp.float32)
            * factor
        )
        scores = jnp.where((block_segs[:, None] == segments[None, :])[None], scores, MASKED_SCORE)
        row_max = jnp.max(scores, axis=-1, keepdims=True)
        totals = jnp.sum(jnp.exp(scores - row_max), axis=-1, keepdims=True)
        logsums = row_max + jnp.log(totals)
        weights = jnp.exp(scores - logsums).astype(jnp.bfloat16)
        mixture = jnp.einsum("hqk,khd->qhd", weights, valueset, preferred_element_type=jnp.float32)
        return (mixture, logsums)

    mixture, logsums = lax.map(
        one_block,
        (
            queries.reshape(blocks, block_rows, head_count, head_width),
            segments.reshape(blocks, block_rows),
        ),
    )
    return (mixture.reshape(length, head_count * head_width), logsums)


def attend_backward(queries, keys_in, values_in, grads_in, segments, logsums, head_count):
    length = queries.shape[0]
    head_width = queries.shape[1] // head_count
    block_rows = min(512, length)
    blocks = length // block_rows
    keyset = keys_in.reshape(length, head_count, head_width)
    valueset = values_in.reshape(length, head_count, head_width)
    factor = head_width ** (-0.5)

    def one_block(carry, pieces):
        key_grad, value_grad = carry
        query_rows, block_segs, grad_rows, block_lse = pieces
        scores = (
            jnp.einsum("qhd,khd->hqk", query_rows, keyset, preferred_element_type=jnp.float32)
            * factor
        )
        scores = jnp.where((block_segs[:, None] == segments[None, :])[None], scores, MASKED_SCORE)
        weights = jnp.exp(scores - block_lse)
        value_grad = value_grad + jnp.einsum(
            "hqk,qhd->khd",
            weights.astype(jnp.bfloat16),
            grad_rows,
            preferred_element_type=jnp.float32,
        )
        grad_weights = jnp.einsum(
            "qhd,khd->hqk", grad_rows, valueset, preferred_element_type=jnp.float32
        )
        centre = jnp.sum(weights * grad_weights, axis=-1, keepdims=True)
        grad_scores = (weights * (grad_weights - centre)).astype(jnp.bfloat16)
        query_grad = (
            jnp.einsum("hqk,khd->qhd", grad_scores, keyset, preferred_element_type=jnp.float32)
            * factor
        )
        key_grad = (
            key_grad
            + jnp.einsum(
                "hqk,qhd->khd", grad_scores, query_rows, preferred_element_type=jnp.float32
            )
            * factor
        )
        return ((key_grad, value_grad), query_grad)

    empty = jnp.zeros((length, head_count, head_width), jnp.float32)
    pieces = (
        queries.reshape(blocks, block_rows, head_count, head_width),
        segments.reshape(blocks, block_rows),
        grads_in.reshape(blocks, block_rows, head_count, head_width),
        logsums,
    )
    (key_grad, value_grad), query_grad = lax.scan(one_block, (empty, empty), pieces)
    flat_shape = (length, head_count * head_width)
    return (
        query_grad.reshape(flat_shape).astype(jnp.bfloat16),
        key_grad.reshape(flat_shape).astype(jnp.bfloat16),
        value_grad.reshape(flat_shape).astype(jnp.bfloat16),
    )


def shards(
    tokens,
    cotangent,
    doc_starts,
    qkv_weight,
    out_weight,
    in_weight,
    down_weight,
    attn_gain,
    ffn_gain,
):
    micro_count = tokens.shape[0]
    token_rows = tokens.shape[2]
    model_width = tokens.shape[3]
    seq_count = lax.axis_size("seq")
    head_count = HEADS // seq_count
    places = lax.axis_index("seq") * token_rows + jnp.arange(token_rows, dtype=jnp.int32)
    everywhere = jnp.arange(token_rows * seq_count, dtype=jnp.int32)
    outputs = []
    input_grads = []
    full_terms = None
    shard_terms = None
    for micro_step in range(micro_count):
        rows_in = tokens[micro_step, 0]
        starts = doc_starts[micro_step, 0]
        cosine_table, sine_table = rope_tables(starts, places, HEAD_DIM)
        segments = segment_ids(starts, everywhere)
        attn_set = (
            lax.all_gather(qkv_weight, "fsdp", axis=0, tiled=True),
            lax.all_gather(out_weight, "fsdp", axis=0, tiled=True),
            lax.all_gather(attn_gain, "fsdp", axis=0, tiled=True),
        )
        qkv_full, out_full, gain_one = attn_set
        normed, norm_back = jax.vjp(layer_norm, rows_in, gain_one.astype(jnp.float32))
        normed_low = normed.astype(jnp.bfloat16)
        qkv_rows = jnp.dot(normed_low, qkv_full, preferred_element_type=jnp.float32)
        turned, turn_back = jax.vjp(
            partial(turn_pair, cosine_table=cosine_table, sine_table=sine_table),
            qkv_rows[:, : 2 * model_width],
        )
        queries = turned[:, :model_width].astype(jnp.bfloat16)
        keyset = turned[:, model_width:].astype(jnp.bfloat16)
        valueset = qkv_rows[:, 2 * model_width :].astype(jnp.bfloat16)
        query_heads, key_heads, value_heads = (
            lax.all_to_all(queries, "seq", split_axis=1, concat_axis=0, tiled=True),
            lax.all_to_all(keyset, "seq", split_axis=1, concat_axis=0, tiled=True),
            lax.all_to_all(valueset, "seq", split_axis=1, concat_axis=0, tiled=True),
        )
        mixture, logsums = attend_forward(query_heads, key_heads, value_heads, segments, head_count)
        mixture_rows = lax.all_to_all(
            mixture.astype(jnp.bfloat16), "seq", split_axis=0, concat_axis=1, tiled=True
        )
        middle = rows_in + jnp.dot(mixture_rows, out_full, preferred_element_type=jnp.float32)
        ffn_set = (
            lax.all_gather(in_weight, "fsdp", axis=0, tiled=True),
            lax.all_gather(down_weight, "fsdp", axis=0, tiled=True),
            lax.all_gather(ffn_gain, "fsdp", axis=0, tiled=True),
        )
        in_full, down_full, gain_two = ffn_set
        normed_two, norm_back_two = jax.vjp(layer_norm, middle, gain_two.astype(jnp.float32))
        normed_two_low = normed_two.astype(jnp.bfloat16)
        joined = jnp.dot(normed_two_low, in_full, preferred_element_type=jnp.float32)
        active, gelu_back = jax.vjp(gated_gelu, joined)
        active_low = active.astype(jnp.bfloat16)
        outputs.append(middle + jnp.dot(active_low, down_full, preferred_element_type=jnp.float32))
        grad_out = cotangent[micro_step, 0]
        grad_low = grad_out.astype(jnp.bfloat16)
        ffn_set = (
            lax.all_gather(in_weight, "fsdp", axis=0, tiled=True),
            lax.all_gather(down_weight, "fsdp", axis=0, tiled=True),
            lax.all_gather(ffn_gain, "fsdp", axis=0, tiled=True),
        )
        in_full, down_full, gain_two = ffn_set
        down_term = jnp.dot(active_low.T, grad_low, preferred_element_type=jnp.float32)
        grad_active = jnp.dot(grad_low, down_full.T, preferred_element_type=jnp.float32)
        grad_joined = gelu_back(grad_active)[0].astype(jnp.bfloat16)
        in_term = jnp.dot(normed_two_low.T, grad_joined, preferred_element_type=jnp.float32)
        grad_normed_two = jnp.dot(grad_joined, in_full.T, preferred_element_type=jnp.float32)
        grad_middle_norm, gain_two_term = norm_back_two(grad_normed_two)
        grad_middle = grad_out + grad_middle_norm
        grad_mid_low = grad_middle.astype(jnp.bfloat16)
        attn_set = (
            lax.all_gather(qkv_weight, "fsdp", axis=0, tiled=True),
            lax.all_gather(out_weight, "fsdp", axis=0, tiled=True),
            lax.all_gather(attn_gain, "fsdp", axis=0, tiled=True),
        )
        qkv_full, out_full, gain_one = attn_set
        out_term = jnp.dot(mixture_rows.T, grad_mid_low, preferred_element_type=jnp.float32)
        grad_mixture = jnp.dot(grad_mid_low, out_full.T, preferred_element_type=jnp.float32).astype(
            jnp.bfloat16
        )
        grad_heads = lax.all_to_all(grad_mixture, "seq", split_axis=1, concat_axis=0, tiled=True)
        query_grad, key_grad, value_grad = attend_backward(
            query_heads, key_heads, value_heads, grad_heads, segments, logsums, head_count
        )
        query_back, key_back, value_back = (
            lax.all_to_all(query_grad, "seq", split_axis=0, concat_axis=1, tiled=True),
            lax.all_to_all(key_grad, "seq", split_axis=0, concat_axis=1, tiled=True),
            lax.all_to_all(value_grad, "seq", split_axis=0, concat_axis=1, tiled=True),
        )
        grad_pair = turn_back(jnp.concatenate([query_back, key_back], axis=1).astype(jnp.float32))[
            0
        ]
        grad_qkv = jnp.concatenate([grad_pair, value_back.astype(jnp.float32)], axis=1).astype(
            jnp.bfloat16
        )
        qkv_term = jnp.dot(normed_low.T, grad_qkv, preferred_element_type=jnp.float32)
        grad_normed = jnp.dot(grad_qkv, qkv_full.T, preferred_element_type=jnp.float32)
        grad_rows_norm, gain_one_term = norm_back(grad_normed)
        input_grads.append(grad_middle + grad_rows_norm)
        terms = (qkv_term, out_term, in_term, down_term, gain_one_term, gain_two_term)
        full_terms = terms if full_terms is None else jax.tree.map(jnp.add, full_terms, terms)
    shard_terms = jax.tree.map(
        lambda part: part.astype(jnp.float32),
        lax.psum_scatter(as_sent(full_terms), "fsdp", scatter_dimension=0, tiled=True),
    )
    totals = jax.tree.map(
        lambda part: part.astype(jnp.float32), lax.psum(as_sent(shard_terms), "seq")
    )
    return (
        jnp.stack(outputs)[:, None],
        jnp.stack(input_grads)[:, None],
        totals[0],
        totals[1],
        totals[2],
        totals[3],
        totals[4],
        totals[5],
    )


MESH = pl.DeviceIdType.MESH
ANY = pl.BlockSpec(memory_space=pl.ANY)
VMEM_BYTES = 127 * 2**19
BF = jnp.bfloat16
F32 = jnp.float32


def nn(a, b):
    return lax.dot_general(a, b, (((1,), (0,)), ((), ())), preferred_element_type=F32)


def nt(a, b):
    return lax.dot_general(a, b, (((1,), (1,)), ((), ())), preferred_element_type=F32)


def spot():
    z, f = lax.axis_index("seq"), lax.axis_index("fsdp")
    core = lax.rem(f, 2)
    x = lax.rem(f // 2, 2)
    y = f // 4
    return z, f, y, x, core


def remote(src, dst, send, recv, where):
    return pltpu.make_async_remote_copy(
        src_ref=src, dst_ref=dst, send_sem=send, recv_sem=recv, device_id=where, device_id_type=MESH
    )


class Rows:
    def __init__(self, z, f, core):
        base = f - core
        self.work, self.home = [], []
        for i in range(2):
            zw, cw = 2 * i + core, z // 2
            self.work.append((zw, base + cw, (zw == z) & (cw == core)))
            zh, ch = 2 * core + i, lax.rem(z, 2)
            self.home.append((zh, base + ch, (zh == z) & (ch == core)))
        self.z = z

    def greet(self, barrier):
        count = 0
        for zt, ft, same in self.work + self.home:

            @pl.when(jnp.logical_not(same))
            def _():
                pl.semaphore_signal(barrier, inc=1, device_id=(zt, ft), device_id_type=MESH)

            count = count + jnp.where(same, 0, 1)
        return count

    def start(self, src, dst, send, recv, local, out, piece=slice(None)):
        places = self.work if out else self.home
        slot = lax.rem(self.z, 2) if out else self.z // 2
        for i, (zt, ft, same) in enumerate(places):

            @pl.when(same)
            def _(i=i):
                pltpu.make_async_copy(src.at[i, piece], dst.at[slot, piece], local).start()

            @pl.when(jnp.logical_not(same))
            def _(i=i, zt=zt, ft=ft):
                remote(src.at[i, piece], dst.at[slot, piece], send.at[i], recv.at[slot], (zt, ft)).start()

    def wait(self, src, dst, send, recv, local, out):
        goes, comes = (self.work, self.home) if out else (self.home, self.work)
        for i, (zt, ft, same) in enumerate(goes):

            @pl.when(same)
            def _(i=i):
                pltpu.make_async_copy(src.at[i], dst.at[i], local).wait()

            @pl.when(jnp.logical_not(same))
            def _(i=i, zt=zt, ft=ft):
                remote(src.at[i], dst.at[i], send.at[i], recv.at[i], (zt, ft)).wait_send()

        for i, (zt, ft, same) in enumerate(comes):

            @pl.when(jnp.logical_not(same))
            def _(i=i, zt=zt, ft=ft):
                remote(src.at[i], dst.at[i], send.at[i], recv.at[i], (zt, ft)).wait_recv()


def halves(width):
    cut = (width // 128 // 2) * 128
    return pl.ds(0, cut), pl.ds(cut, width - cut)


SQRT_HALF = 0.7071067811865476
DENSITY = 0.3989422804014327
SHARD = 336
GROUP = 384
STEPS = 7


def moments(values):
    average = jnp.mean(values, axis=-1, keepdims=True)
    centred = values - average
    spread = jnp.mean(centred * centred, axis=-1, keepdims=True)
    scale = lax.rsqrt(spread + EPSILON)
    return centred * scale, scale


def norm_back(values, gain, grads):
    unit, scale = moments(values)
    spread = grads * gain
    inner = spread - jnp.mean(spread, axis=-1, keepdims=True)
    inner = inner - unit * jnp.mean(spread * unit, axis=-1, keepdims=True)
    return inner * scale, jnp.sum(grads * unit, axis=0, keepdims=True)


def rope_back(grads, cosine, sine):
    lane = lax.broadcasted_iota(jnp.int32, (1, 128), 1)
    low = lax.rem(lane, 64) < 32
    u = grads * sine
    return grads * cosine + jnp.where(low, pltpu.roll(u, 96, 1), -pltpu.roll(u, 32, 1))


class Sums:
    KINDS = 9

    @staticmethod
    def scratch(count, slots, rows, wide):
        dma = pltpu.SemaphoreType.DMA((count, Sums.KINDS))
        shapes = [(slots, 2, 2, 2), (count, 2, 2), (count, 2), (count, 2), (count,)]
        return [pltpu.VMEM(s + (rows, wide), BF) for s in shapes] + [dma, dma]

    def __init__(self, here, refs, slot):
        self.here, self.slot = here, slot
        self.acc, self.rx, self.r2, self.zr, self.zr2, self.send, self.recv = refs

    def copy(self, t, kind):
        h = self.here
        acc = self.acc.at[self.slot[t]]
        plan = {
            0: lambda: (acc.at[0, :, 1 - h.x], self.rx.at[t, 0], (h.z, h.fx)),
            1: lambda: (acc.at[1, 1 - h.y], self.rx.at[t, 1], (h.z, h.fy)),
            2: lambda: (self.rx.at[t, 0, 1 - h.y], self.r2.at[t, 0], (h.z, h.fy)),
            3: lambda: (self.rx.at[t, 1, 1 - h.x], self.r2.at[t, 1], (h.z, h.fx)),
            4: lambda: (self.r2.at[t], self.zr.at[t], (h.near, h.f)),
            5: lambda: (self.zr.at[t, 1 - h.own], self.zr2.at[t], (h.across, h.f)),
            6: lambda: (self.r2.at[t, h.own], self.r2.at[t, h.own], (h.across, h.f)),
            7: lambda: (self.r2.at[t, h.own], self.zr.at[t, h.own], (h.near, h.f)),
            8: lambda: (self.r2.at[t, 1 - h.own], self.zr.at[t, 1 - h.own], (h.near, h.f)),
        }
        src, dst, where = plan[kind]()
        return remote(src, dst, self.send.at[t, kind], self.recv.at[t, kind], where)

    def begin(self, t):
        self.copy(t, 0).start()
        self.copy(t, 1).start()

    def cross(self, t):
        h, s = self.here, self.slot[t]
        self.copy(t, 0).wait()
        self.rx[t, 0, 1 - h.y] = added(self.rx[t, 0, 1 - h.y], self.acc[s, 0, 1 - h.y, h.x])
        self.copy(t, 2).start()
        self.copy(t, 1).wait()
        self.rx[t, 1, 1 - h.x] = added(self.rx[t, 1, 1 - h.x], self.acc[s, 1, h.y, 1 - h.x])
        self.copy(t, 3).start()

    def plane(self, t):
        h, s = self.here, self.slot[t]
        self.copy(t, 2).wait()
        self.r2[t, 0] = added(self.r2[t, 0], self.rx[t, 0, h.y], self.acc[s, 0, h.y, h.x])
        self.copy(t, 3).wait()
        self.r2[t, 1] = added(self.r2[t, 1], self.rx[t, 1, h.x], self.acc[s, 1, h.y, h.x])

        @pl.when(h.outer)
        def _():
            self.copy(t, 4).start()

    def meet(self, t):
        h = self.here

        @pl.when(jnp.logical_not(h.outer))
        def _():
            self.copy(t, 4).wait_recv()
            self.zr[t, 1 - h.own] = added(self.zr[t, 1 - h.own], self.r2[t, 1 - h.own])
            self.copy(t, 5).start()

    def sums(self, t):
        h = self.here

        @pl.when(jnp.logical_not(h.outer))
        def _():
            self.copy(t, 5).wait()
            self.r2[t, h.own] = added(self.r2[t, h.own], self.zr[t, h.own], self.zr2[t])
            self.copy(t, 6).start()
            self.copy(t, 7).start()

    def spread(self, t):
        @pl.when(jnp.logical_not(self.here.outer))
        def _():
            self.copy(t, 6).wait_recv()
            self.copy(t, 8).start()

    def finish(self, t):
        @pl.when(jnp.logical_not(self.here.outer))
        def _():
            self.copy(t, 6).wait_send()
            self.copy(t, 7).wait_send()
            self.copy(t, 8).wait_send()

        @pl.when(self.here.outer)
        def _():
            self.copy(t, 4).wait_send()
            self.copy(t, 7).wait_recv()
            self.copy(t, 8).wait_recv()

    def total(self, act):
        for ref, there in ((self.zr, self.here.outer), (self.r2, jnp.logical_not(self.here.outer))):
            pl.when(there)(functools.partial(act, ref))

    LATER = ("cross", "plane", "meet", "sums", "spread", "finish")


def added(*terms):
    total = terms[0].astype(F32)
    for term in terms[1:]:
        total = total + term.astype(F32)
    return total.astype(BF)


class Halves:
    def __init__(self, ref):
        self.ref, self.at, self.size = ref, self, ref.shape[0] // 2

    def __getitem__(self, index):
        i, piece = index if isinstance(index, tuple) else (index, slice(None))
        if isinstance(piece, slice):
            return self.ref.at[pl.ds(i * self.size, self.size)]
        return self.ref.at[pl.ds(i * self.size + piece.start, piece.size)]


class Here:
    def __init__(self):
        self.z, self.f, self.y, self.x, self.core = spot()
        self.fx = self.f + 2 - 4 * self.x
        self.fy = self.f + 4 - 8 * self.y
        self.fc = self.f + 1 - 2 * self.core
        z = self.z
        self.outer = (z == 0) | (z == 3)
        self.near = jnp.where(z < 2, 1 - z, 5 - z)
        self.across = jnp.where(self.outer, z, 3 - z)
        self.own = jnp.where(z < 2, 0, 1)

    def greet(self, barrier, rows):
        for t in (self.fx, self.fy, self.fc):
            pl.semaphore_signal(barrier, inc=1, device_id=(self.z, t), device_id_type=MESH)
        pl.semaphore_signal(barrier, inc=1, device_id=(self.near, self.f), device_id_type=MESH)

        @pl.when(jnp.logical_not(self.outer))
        def _():
            pl.semaphore_signal(barrier, inc=1, device_id=(self.across, self.f), device_id_type=MESH)

        pl.semaphore_wait(barrier, rows.greet(barrier) + 4 + jnp.where(self.outer, 0, 1))


def lanes(start, size):
    return pl.ds(start if isinstance(start, int) else pl.multiple_of(start, 128), size)


PIECES = 8
WIDE_SLOTS = 3
DOWN_FIRST = 0
PLAN = (
    ("r", 0),
    ("f", ("w", 0)),
    ("f", ("w", 1)),
    ("r", 0),
    ("c", "ln2"),
    ("r", 0),
    ("f", ("d", 0)),
    ("s", ("w", 0), 0),
    ("r", 0),
    ("c", "do"),
    ("r", 0),
    ("c", "og"),
    ("s", ("w", 1), 0),
    ("b", ("o", 0)),
    ("c", "E0.0"),
    ("r", 0),
    ("c", "E0.1"),
    ("s", ("d", 0), 0),
    ("r", 0),
    ("c", "E1.0"),
    ("s", ("w", 0), 1),
    ("r", 0),
    ("c", "E1.1"),
    ("s", ("w", 1), 1),
    ("f", ("w", 2)),
    ("c", "F0"),
    ("s", ("o", 0), 0),
    ("s", ("w", 0), 2),
    ("c", "E2.0"),
    ("s", ("d", 0), 1),
    ("s", ("w", 0), 3),
    ("f", ("w", 3)),
    ("s", ("w", 1), 2),
    ("c", "E2.1"),
    ("s", ("w", 2), 0),
    ("s", ("w", 0), 4),
    ("f", ("d", 1)),
    ("s", ("o", 0), 1),
    ("s", ("w", 1), 3),
    ("s", ("d", 0), 2),
    ("c", "F1"),
    ("c", "G0"),
    ("s", ("w", 3), 0),
    ("s", ("w", 1), 4),
    ("b", ("w", 7)),
    ("c", "E3.0"),
    ("s", ("w", 2), 1),
    ("s", ("d", 0), 3),
    ("s", ("o", 0), 2),
    ("c", "E3.1"),
    ("c", "F2"),
    ("s", ("d", 1), 0),
    ("s", ("d", 0), 4),
    ("s", ("w", 2), 2),
    ("c", "G1"),
    ("s", ("w", 3), 1),
    ("b", ("w", 8)),
    ("c", "F3"),
    ("s", ("o", 0), 3),
    ("c", "G2"),
    ("s", ("w", 2), 3),
    ("b", ("w", 9)),
    ("c", "H"),
    ("s", ("w", 7), 0),
    ("s", ("o", 0), 4),
    ("s", ("w", 3), 2),
    ("c", "gains"),
    ("b", ("g", 0)),
    ("c", "G3"),
    ("s", ("d", 1), 1),
    ("s", ("w", 2), 4),
    ("r", 1),
    ("s", ("w", 8), 0),
    ("s", ("w", 3), 3),
    ("s", ("w", 9), 0),
    ("r", 1),
    ("s", ("w", 7), 1),
    ("s", ("g", 0), 0),
    ("s", ("w", 3), 4),
    ("s", ("d", 1), 2),
    ("f", ("w", 4)),
    ("s", ("w", 8), 1),
    ("f", ("w", 5)),
    ("s", ("w", 9), 1),
    ("s", ("g", 0), 1),
    ("r", 1),
    ("b", ("w", 10)),
    ("s", ("d", 0), 5),
    ("s", ("o", 0), 5),
    ("s", ("w", 0), 5),
    ("s", ("w", 1), 5),
    ("s", ("w", 2), 5),
    ("s", ("w", 3), 5),
    ("s", ("d", 1), 3),
    ("s", ("w", 7), 2),
    ("s", ("w", 4), 0),
    ("s", ("w", 8), 2),
    ("s", ("d", 1), 4),
    ("s", ("w", 5), 0),
    ("r", 1),
    ("s", ("w", 7), 3),
    ("s", ("w", 9), 2),
    ("s", ("g", 0), 2),
    ("s", ("w", 8), 3),
    ("s", ("w", 10), 0),
    ("s", ("d", 1), 5),
    ("s", ("w", 4), 1),
    ("f", ("w", 6)),
    ("s", ("w", 5), 1),
    ("s", ("w", 7), 4),
    ("s", ("w", 10), 1),
    ("s", ("w", 9), 3),
    ("s", ("g", 0), 3),
    ("s", ("w", 4), 2),
    ("s", ("w", 8), 4),
    ("r", 1),
    ("s", ("w", 9), 4),
    ("s", ("g", 0), 4),
    ("s", ("w", 5), 2),
    ("s", ("w", 4), 3),
    ("s", ("w", 7), 5),
    ("s", ("w", 6), 0),
    ("s", ("w", 10), 2),
    ("s", ("w", 5), 3),
    ("s", ("w", 4), 4),
    ("r", 1),
    ("s", ("w", 10), 3),
    ("s", ("w", 8), 5),
    ("s", ("w", 6), 1),
    ("s", ("w", 5), 4),
    ("s", ("w", 6), 2),
    ("s", ("w", 9), 5),
    ("s", ("g", 0), 5),
    ("r", 1),
    ("s", ("w", 10), 4),
    ("s", ("w", 4), 5),
    ("s", ("w", 6), 3),
    ("r", 1),
    ("s", ("w", 6), 4),
    ("s", ("w", 5), 5),
    ("s", ("w", 10), 5),
    ("s", ("w", 6), 5),
)


def split_plan():
    before, loop, after = [], {(n, m): [] for n in range(10) for m in range(3)}, []
    place = before
    for op in PLAN:
        mark = op[1] if op[0] == "c" else ""
        if mark in ("H", "G3"):
            place = after
        elif mark[:1] == "E":
            place = loop[2 * int(mark[1]) + int(mark[3]), 0]
        elif mark[:1] == "F":
            place = loop[2 * int(mark[1]) + 3, 1]
        elif mark[:1] == "G":
            place = loop[2 * int(mark[1]) + 5, 2]
        if mark[:1] not in ("E", "F", "G") or mark == "G3":
            place.append(op)
    return before, loop, after


def rope(values, cosine, sine):
    lane = lax.broadcasted_iota(jnp.int32, (1, 128), 1)
    turned = jnp.where(lax.rem(lane, 64) < 32, -pltpu.roll(values, 96, 1), pltpu.roll(values, 32, 1))
    return values * cosine + turned * sine


def front_kernel(
    attn_h, ffn_h, qkv_h, out_h, in_h, down_h, tok_f, cot_f, starts_f, inverse,
    qkv_o, out_o, cot_o, tok_o, mid_o, gn_o, ffn_o, q_o, k_o, v_o, mix_o, bias_o, xt_o, mt_o, nt_o, glc_o, gj_o, at_o,
    gains_o, cos_o, sin_o, lse_o,
    gains_v, qkv_v, out_v, in_v, down_v, tok_v, starts_v, acc_f, acc_g, gl, normed, x2, q, k, v, mix, bias,
    gains_h, starts_h, tok_h, cot_h, gj, act, mine, theirs, rows_b,
    ss, rs, ssi, rsi, ls, lsi, es, er, el, ds_, dr, kvs, kvr, ws, ts, tr, tl, gs_, gr_, gw, as_, ar_, aw,
):
    h = Here()
    rows = Rows(h.z, h.f, h.core)
    z, f, core = h.z, h.f, h.core
    fx, fy, fc = h.fx, h.fy, h.fc
    fd = fx + 4 - 8 * h.y
    sib = (z, fc)
    half, wide = normed.shape
    block = half // 2
    own_rows, sib_rows = pl.ds(0, half), pl.ds(half, half)

    shards = (gains_h, qkv_h, out_h, down_h)
    wholes = (gains_v, qkv_v, out_v, down_v)
    targets = (fx, fy, fc, fy, fx, fc, fc, fc, fc)

    def part(w, i, cols=None):
        whole = wholes[w]
        if w < 3:
            return whole.at[i] if cols is None else whole.at[i, :, cols]
        r = pl.ds(pl.multiple_of(i * SHARD, 16), SHARD)
        return whole.at[r] if cols is None else whole.at[r, cols]

    def copy(w, k):
        a, b = halves(shards[w].shape[1])
        place = {3: (fx, a), 4: (fy, b), 5: (fx,), 6: (fy,), 7: (fd, a), 8: (fd, b)}
        dst = part(w, f) if k < 3 else part(w, *place[k])
        return remote(shards[w] if k < 3 else dst, dst, ss.at[w, k], rs.at[w, k], (z, targets[k]))

    def copy_in(t, k):
        cols = lanes(t * GROUP, GROUP)
        place = {3: (fx, 0), 4: (fy, 1), 5: (fx,), 6: (fy,), 7: (fd, 0), 8: (fd, 1)}
        dst = in_v.at[t, f] if k < 3 else in_v.at[(t,) + place[k]]
        return remote(in_h.at[:, :, cols] if k < 3 else dst, dst, ssi.at[t, k], rsi.at[t, k], (z, targets[k]))

    def first(w, copy=copy):
        for k in range(3):
            copy(w, k).start()

    def second(w, copy=copy):
        for k in (0, 1):
            copy(w, k).wait_recv()
            copy(w, k + 3).start()
            copy(w, k + 5).start()

    def third(w, copy=copy):
        for k in (3, 4):
            copy(w, k).wait_recv()
            copy(w, k + 4).start()

    def rest(w, copy=copy):
        for k in (2, 5, 6, 7, 8):
            copy(w, k).wait_recv()

    def own(w):
        return pltpu.make_async_copy(shards[w], part(w, f), ls.at[w])

    def own_in(t):
        return pltpu.make_async_copy(in_h.at[:, :, lanes(t * GROUP, GROUP)], in_v.at[t, f], lsi.at[t])

    wide_in = [
        [pltpu.make_async_copy(src.at[i], ref.at[pl.ds(i * block, block)], el.at[i]) for i in range(2)]
        for src, ref in ((tok_f, acc_f), (cot_f, acc_g))
    ]
    for c in wide_in[0]:
        c.start()
    gains_h[:, :128] = jnp.broadcast_to(attn_h[...].astype(F32), (16, 128)).astype(BF)
    gains_h[:, 128:] = jnp.broadcast_to(ffn_h[...].astype(F32), (16, 128)).astype(BF)
    starts_h[...] = jnp.zeros(starts_h.shape, jnp.int32)
    starts_h[:2, :8] = starts_f[...]
    for c in wide_in[0]:
        c.wait()
    tok_h[...] = acc_f[...].astype(BF)
    for c in wide_in[1]:
        c.start()
    for w in range(4):
        own(w).start()
    for t in range(STEPS):
        own_in(t).start()
    h.greet(pltpu.get_barrier_semaphore(), rows)
    info = remote(starts_h, starts_v.at[core], ds_.at[0], dr.at[0], sib)
    own_info = pltpu.make_async_copy(starts_h, starts_v.at[core], el.at[2])
    info.start()
    own_info.start()
    rows.start(Halves(tok_h), tok_v, es.at[0], er.at[0], el.at[3], True)
    for w in range(3):
        first(w)
    for c in wide_in[1]:
        c.wait()
    cot_h[...] = acc_g[...].astype(BF)
    info.wait()
    own_info.wait()

    lane = lax.broadcasted_iota(jnp.int32, (1, 128), 1)
    begins = starts_v[lax.rem(z, 2), pl.ds(z // 2, 1), :]
    inside = lane < 8

    def documents(base):
        place = lax.broadcasted_iota(jnp.int32, (half, 128), 0) + base
        before = (begins <= place) & inside
        number = jnp.sum(jnp.where(before, 1.0, 0.0), axis=1, keepdims=True)
        begin = jnp.max(jnp.where(before, begins, 0).astype(F32), axis=1, keepdims=True)
        return place, number, begin

    place, number, begin = documents(core * half)
    angle = (place.astype(F32) - begin) * inverse[...]
    cos_o[...] = jnp.cos(angle)
    sin_o[...] = jnp.sin(angle)
    across = jnp.broadcast_to(number, (half, 128)).T[0:1, :]
    _, other, _ = documents((1 - core) * half)
    bias[:half] = jnp.where(number == across, 0.0, MASKED_SCORE).astype(BF)
    bias[half:] = jnp.where(other == across, 0.0, MASKED_SCORE).astype(BF)

    for w in range(3):
        second(w)
    rows.start(Halves(cot_h), cot_o, es.at[1], er.at[1], el.at[4], True)
    first(3)
    first(0, copy_in)
    first(1, copy_in)
    third(0)
    rest(0)
    own(0).wait()
    for n in range(2):
        for i in range(8):
            gains_o[n : n + 1, i * 128 : i * 128 + 128] = gains_v[i, 0:1, n * 128 : n * 128 + 128].astype(F32)
    rows.wait(Halves(tok_h), tok_v, es.at[0], er.at[0], el.at[3], True)
    saved = []

    def save(src, dst):
        saved.append(pltpu.make_async_copy(src, dst, ws.at[len(saved)]))
        saved[-1].start()

    def share(src, dst, n, again):
        keep = pltpu.make_async_copy(mine, dst.at[:, own_rows], tl.at[n])
        give = remote(theirs, dst.at[:, sib_rows], ts.at[n], tr.at[n], sib)
        if again is not None:
            again[0].wait()
            again[1].wait_send()
        for i in range(4):
            mine[i * 128 : i * 128 + 128] = src[:, lanes((2 * i + core) * 128, 128)].T
            theirs[i * 128 : i * 128 + 128] = src[:, lanes((2 * i + 1 - core) * 128, 128)].T
        keep.start()
        give.start()
        return keep, give

    unit, _ = moments(tok_v[...].reshape(half, wide).astype(F32))
    normed[...] = (unit * gains_o[0:1]).astype(BF)
    save(tok_v, tok_o)
    save(bias, bias_o)
    shared = share(normed, nt_o, 0, None)
    third(1)
    rest(1)
    own(1).wait()
    save(qkv_v, qkv_o)

    def pair_send(n, i):
        ref = (k, v)[n]
        cols = pl.ds(i * 256, 256)
        return remote(ref.at[own_rows, cols], ref.at[sib_rows, cols], kvs.at[n, i], kvr.at[n, i], sib)

    for n, ref in ((1, k), (2, v), (0, q)):
        for i in range(4):
            product = nn(normed[...], qkv_v[:, :, n * wide + i * 256 : n * wide + i * 256 + 256].reshape(wide, 256))
            for j in range(2):
                cols = slice(i * 256 + j * 128, i * 256 + j * 128 + 128)
                value = product[:, j * 128 : j * 128 + 128]
                value = value if n == 2 else rope(value, cos_o[...], sin_o[...])
                ref[:half, cols] = value.astype(BF)
            if n:
                pair_send(n - 1, i).start()
    third(2)
    for n in range(2):
        for i in range(4):
            pair_send(n, i).wait()
    for ref, dst in ((q, q_o), (k, k_o), (v, v_o)):
        save(ref, dst)

    def attend(i, _):
        @pl.when(i == 4)
        def _():
            second(3)
            first(2, copy_in)

        @pl.when(i == 6)
        def _():
            second(0, copy_in)
            first(3, copy_in)

        cols = lanes(i * 128, 128)
        queries = q[:, cols] * jnp.asarray(0.125, BF)
        keys = k[:, cols]
        vt = v[:, cols].T
        outs = []
        for e in range(2):
            here = (lane < 64) if e == 0 else (lane >= 64)
            scores = nt(keys, jnp.where(here, queries, jnp.zeros_like(queries))) + bias[...].astype(F32)
            top = jnp.max(scores, axis=0, keepdims=True)
            p = jnp.exp(scores - top)
            total = jnp.sum(p, axis=0, keepdims=True)
            outs.append(nn(vt, p.astype(BF)) / total)
            lse_o[i, e : e + 1, :] = top + jnp.log(total)
        mix[:, cols] = jnp.concatenate([outs[0][:64], outs[1][64:]], axis=0).T.astype(BF)
        return 0

    lax.fori_loop(0, 8, attend, 0)
    second(1, copy_in)
    rest(2)
    own(2).wait()
    save(out_v, out_o)
    save(mix, mix_o)
    middle = tok_v[...].reshape(half, wide).astype(F32) + nn(mix[...], out_v[...].reshape(wide, wide))
    acc_f[...] = middle
    unit, _ = moments(middle)
    x2[...] = (unit * gains_o[1:2]).astype(BF)
    mid_save = pltpu.make_async_copy(acc_f, mid_o, ls.at[4])
    mid_save.start()
    third(3)
    third(0, copy_in)
    rows.wait(Halves(cot_h), cot_o, es.at[1], er.at[1], el.at[4], True)
    cot_load = [pltpu.make_async_copy(cot_o.at[i], gl.at[pl.ds(i * block, block)], el.at[i]) for i in range(2)]
    for c in cot_load:
        c.start()
    shared = share(x2, xt_o, 1, shared)
    shared = share(mix, mt_o, 2, shared)
    for c in cot_load:
        c.wait()
    glc_keep = pltpu.make_async_copy(gl.at[:, lanes(core * 512, 512)], glc_o.at[own_rows], tl.at[3])
    glc_give = remote(gl.at[:, lanes((1 - core) * 512, 512)], glc_o.at[sib_rows], ts.at[3], tr.at[3], sib)
    glc_keep.start()
    glc_give.start()
    mid_save.wait()
    rest(3)
    own(3).wait()

    def stage_copies(t):
        s = lax.rem(t, 2)
        r = lanes(t * GROUP, GROUP)
        return [
            pltpu.make_async_copy(gj.at[s], gj_o.at[t, own_rows], gw.at[s]),
            pltpu.make_async_copy(act.at[s], at_o.at[r, own_rows], aw.at[s]),
        ], [
            remote(gj.at[s], gj_o.at[t, sib_rows], gs_.at[s], gr_.at[t], sib),
            remote(act.at[s], at_o.at[r, sib_rows], as_.at[s], ar_.at[t], sib),
        ]

    def feed(t, _):
        s = lax.rem(t, 2)

        @pl.when(t + 2 < STEPS)
        def _():
            second(t + 2, copy_in)

        @pl.when(t + 4 < STEPS)
        def _():
            first(t + 4, copy_in)

        rest(t, copy_in)
        own_in(t).wait()
        wa = in_v[t, :, 0].reshape(wide, GROUP)
        wc = in_v[t, :, 1].reshape(wide, GROUP)
        wd = down_v[lanes(t * GROUP, GROUP)]
        a, c = nn(x2[...], wa), nn(x2[...], wc)
        grad_active = nt(gl[...], wd)
        phi = 0.5 * (1.0 + lax.erf(a * SQRT_HALF))
        gate = a * phi
        slope = phi + a * (jnp.exp(-0.5 * a * a) * DENSITY)
        active = (gate * c).astype(BF)
        ga = (slope * c * grad_active).astype(BF)
        gc = (gate * grad_active).astype(BF)

        @pl.when(t >= 2)
        def _():
            keep, give = stage_copies(t - 2)
            for copied in keep:
                copied.wait()
            for sent in give:
                sent.wait_send()

        gj[s, :, :GROUP] = ga
        gj[s, :, GROUP:] = gc
        act[s] = active.T
        keep, give = stage_copies(t)
        for started in keep + give:
            started.start()

        @pl.when(t + 1 < STEPS)
        def _():
            third(t + 1, copy_in)

        acc_f[...] += nn(active, wd)
        back = nt(ga, wa) + nt(gc, wc)

        @pl.when(t == 0)
        def _():
            acc_g[...] = back

        @pl.when(t > 0)
        def _():
            acc_g[...] += back

        return 0

    lax.fori_loop(0, STEPS, feed, 0)
    rows_b[...] = acc_f[...].astype(BF).reshape(2, block, wide)
    save(rows_b, ffn_o)
    save(acc_g, gn_o)
    for t in (STEPS - 2, STEPS - 1):
        keep, give = stage_copies(t)
        for copied in keep:
            copied.wait()
        for sent in give:
            sent.wait_send()
    for t in range(STEPS):
        for received in stage_copies(t)[1]:
            received.wait_recv()
    shared[0].wait()
    shared[1].wait_send()
    for n, dst in enumerate((nt_o, xt_o, mt_o)):
        remote(theirs, dst.at[:, sib_rows], ts.at[n], tr.at[n], sib).wait_recv()
    glc_keep.wait()
    glc_give.wait()
    for w in range(4):
        for kind in range(9):
            copy(w, kind).wait_send()
    for t in range(STEPS):
        for kind in range(9):
            copy_in(t, kind).wait_send()
    for c in saved:
        c.wait()


def front_all(attn_gain, ffn_gain, qkv, out, inw, down, tok, cot, starts, inverse):
    dma = pltpu.SemaphoreType.DMA
    block, wide = tok.shape[1:]
    half, hidden = 2 * block, STEPS * GROUP

    def shape(*s, kind=BF):
        return jax.ShapeDtypeStruct(s, kind)

    def buf(*s, kind=BF):
        return pltpu.VMEM(s, kind)

    whole = pl.BlockSpec(memory_space=pltpu.VMEM)
    return pl.pallas_call(
        front_kernel,
        out_shape=[
            shape(8, *qkv.shape), shape(8, *out.shape), shape(*cot.shape), shape(*tok.shape),
            shape(half, wide, kind=F32), shape(half, wide, kind=F32), shape(2, block, wide),
            shape(half, wide), shape(2 * half, wide), shape(2 * half, wide), shape(half, wide), shape(2 * half, half),
            shape(half, 2 * half), shape(half, 2 * half), shape(half, 2 * half), shape(2 * half, half),
            shape(STEPS, 2 * half, 2 * GROUP), shape(hidden, 2 * half),
            shape(2, wide, kind=F32), shape(half, 128, kind=F32), shape(half, 128, kind=F32), shape(8, 2, half, kind=F32),
        ],
        in_specs=[whole] * 2 + [ANY] * 6 + [whole] * 2,
        out_specs=[ANY] * 18 + [whole] * 4,
        scratch_shapes=[
            buf(8, 16, 256), buf(8, *qkv.shape), buf(8, *out.shape), buf(STEPS, 8, 2, 128, GROUP), buf(hidden, wide),
            buf(*tok.shape), buf(2, 8, 128, kind=jnp.int32), buf(half, wide, kind=F32), buf(half, wide, kind=F32),
            buf(half, wide), buf(half, wide), buf(half, wide), buf(half, wide), buf(2 * half, wide), buf(2 * half, wide),
            buf(half, wide), buf(2 * half, half),
            buf(16, 256), buf(8, 128, kind=jnp.int32), buf(half, wide), buf(half, wide),
            buf(2, half, 2 * GROUP), buf(2, GROUP, half), buf(half, half), buf(half, half), buf(2, block, wide),
            dma((4, 9)), dma((4, 9)), dma((STEPS, 9)), dma((STEPS, 9)), dma((5,)), dma((STEPS,)),
            dma((2, 2)), dma((2, 2)), dma((5,)), dma((1,)), dma((1,)), dma((2, 4)), dma((2, 4)), dma((10,)),
            dma((4,)), dma((4,)), dma((4,)), dma((2,)), dma((STEPS,)), dma((2,)), dma((2,)), dma((STEPS,)), dma((2,)),
        ],
        compiler_params=pltpu.CompilerParams(collective_id=1, has_side_effects=True, vmem_limit_bytes=VMEM_BYTES),
        name="gather_attention_feed_forward",
    )(attn_gain, ffn_gain, qkv, out, inw, down, tok, cot, starts, inverse)


def back_kernel(
    ffn_h, mid_h, gn_h, cot_h, qkv_h, out_h, q_h, k_h, v_h, mix_h, rows_h, bias_h, xt_h, mt_h, nt_h, glc_h, gj_h, at_h,
    gains, cosine, sine, lse,
    in_o, qkv_o, down_o, out_o, gain_o, outh_o, inh_o,
    acc_f, acc_g, win, xt, mt, gj, gq, at, glc, gm, dout, q, k, v, bias, kept, dx_kv, kvl, centres, terms, gs, gr,
    ld, gld, wsem, ps, pr, kvs, kvr, gqs, gqr, dxs, dxr, fo, es, er, el,
    *sum_refs,
):
    h = Here()
    rows = Rows(h.z, h.f, h.core)
    order = [op[1][1] for op in PLAN if op[0] in "fb" and op[1][0] == "w"]
    wide = Sums(h, sum_refs[0:7], {t: n % WIDE_SLOTS for n, t in enumerate(order)})
    down = Sums(h, sum_refs[7:14], {0: 0, 1: 1})
    outs = Sums(h, sum_refs[14:21], {0: 0})
    gain = Sums(h, sum_refs[21:28], {0: 0})
    groups = {"w": wide, "d": down, "o": outs, "g": gain}
    sib = (h.z, h.fc)
    half, width = dout.shape
    block = half // 2
    own_rows, sib_rows = pl.ds(0, half), pl.ds(half, half)
    lane = lax.broadcasted_iota(jnp.int32, (1, 128), 1)

    def load(src, dst, n):
        return pltpu.make_async_copy(src, dst, ld.at[n])

    def gj_load(t):
        return pltpu.make_async_copy(gj_h.at[t], gj, gld.at[0])

    def qkv_weights(u):
        return [
            pltpu.make_async_copy(qkv_h.at[:, :, lanes(n * 1024 + u * 256, 256)], win.at[:, :, pl.ds(n * 256, 256)], wsem.at[n])
            for n in range(3)
        ]

    loads = {
        "xt": load(xt_h, xt, 0), "mid": load(mid_h, acc_f, 1), "gn": load(gn_h, acc_g, 2),
        "c0": load(cot_h.at[0], dout.at[pl.ds(0, block)], 3), "c1": load(cot_h.at[1], dout.at[pl.ds(block, block)], 4),
        "w": load(out_h, k, 5), "mix": load(mix_h, v.at[own_rows], 6), "mt": load(mt_h, mt, 7),
        "at": load(at_h, at, 8), "glc": load(glc_h, glc, 9), "bias": load(bias_h, bias, 10), "q": load(q_h, q, 11),
        "nt": load(nt_h, mt, 7), "k": load(k_h, k, 5), "v": load(v_h, v, 6),
        "r0": load(rows_h.at[0], k.at[pl.ds(0, block)], 3), "r1": load(rows_h.at[1], k.at[pl.ds(block, block)], 4),
    }

    def start(*names):
        for name in names:
            loads[name].start()

    def wait(*names):
        for name in names:
            loads[name].wait()

    start("xt")
    gj_load(0).start()
    start("mid", "gn", "c0", "c1")
    start("w", "mix", "at", "glc", "mt", "bias", "q")
    h.greet(pltpu.get_barrier_semaphore(), rows)

    def put(group, t, term, cut):
        s = group.slot[t]
        term = term.astype(BF)
        for o in range(4):
            for n in range(2):
                group.acc[s, n, o // 2, o % 2] = term[o * 128 : o * 128 + 128, n * cut : n * cut + cut]

    def in_term(t):
        if t == 0:
            wait("xt")
        gj_load(t).wait()
        put(wide, t, nn(xt[...], gj[...]), GROUP)
        if t + 1 < STEPS:
            gj_load(t + 1).start()

    def down_term(j):
        if j == DOWN_FIRST:
            wait("at", "glc")
        term = nn(at[...], glc[:, j * 256 : j * 256 + 256])
        for f in range(8):
            down.acc[j, f % 2, f // 4, f // 2 % 2] = term[f * SHARD : f * SHARD + SHARD].astype(BF)

    gm_send = remote(gm.at[own_rows], gm.at[sib_rows], ps.at[0], pr.at[0], sib)

    def second_norm():
        wait("mid", "gn", "c0", "c1")
        back, terms[1:2] = norm_back(acc_f[...], gains[1:2], acc_g[...])
        grad_mid = dout[...].astype(F32) + back
        acc_f[...] = grad_mid
        gm[:half] = grad_mid.astype(BF)
        gm_send.start()

    def mixture_grads():
        wait("w", "mix")
        dout[...] = nt(gm[:half], k[...]).astype(BF)
        start("k")
        for j in range(8):
            cols = slice(j * 128, j * 128 + 128)
            products = (v[:half, cols].astype(F32) * dout[:, cols].astype(F32)).T
            for e in range(2):
                centres[j, e : e + 1] = jnp.sum(products[64 * e : 64 * e + 64], axis=0, keepdims=True)
        start("v")

    def out_term():
        wait("mt")
        gm_send.wait()
        put(outs, 0, nn(mt[...], gm[...]), 512)
        start("nt")

    def kv_rows(s):
        return pl.ds(s * half if isinstance(s, int) else pl.multiple_of(s * half, half), half)

    def kv_send(u):
        s = lax.rem(u, 2)
        return remote(dx_kv, kvl.at[s], kvs.at[s], kvr.at[s], sib)

    def gq_send(u):
        s = lax.rem(u, 2)
        return remote(gq.at[s, own_rows], gq.at[s, sib_rows], gqs.at[s], gqr.at[s], sib)

    def stashed(b, n, j):
        return jnp.concatenate([kept[b, pl.ds(n * 128, 128), pl.ds(m * 256 + j * 128, 128)] for m in range(4)], axis=0)

    def heads_back(p):
        u, j = p // 2, lax.rem(p, 2)
        s = lax.rem(u, 2)
        col = lanes(p * 128, 128)
        queries = q[:, col] * jnp.asarray(0.125, BF)
        keys, values, do = k[:, col], v[:, col], dout[:, col]
        kt = keys.T
        none = jnp.zeros_like(queries)
        dqs, dks, dvs = [], [], []
        for e in range(2):
            part = (lane < 64) if e == 0 else (lane >= 64)
            prob = jnp.exp(nt(keys, jnp.where(part, queries, none)) + bias[...].astype(F32) - lse[p, e : e + 1, :])
            dvs.append(nn(prob.astype(BF), do))
            ds = (prob * (nt(values, jnp.where(part, do, none)) - centres[p, e : e + 1, :])).astype(BF)
            dks.append(nn(ds, queries))
            dqs.append(nn(kt, ds))
        dq = jnp.concatenate([dqs[0][:64], dqs[1][64:]], axis=0).T
        dk = jnp.where(lane < 64, dks[0], dks[1]).astype(BF)
        dv = jnp.where(lane < 64, dvs[0], dvs[1]).astype(BF)
        for n, part in enumerate(((dq * 0.125).astype(BF), dk, dv)):
            for m in range(4):
                kept[s, pl.ds(n * 128, 128), lanes(m * 256 + j * 128, 128)] = part[m * 128 : m * 128 + 128]

        @pl.when((j == 0) & (u >= 1))
        def _():
            kv_send(u - 1).wait_send()

        dx_kv[:, lanes(j * 128, 128)] = dk[half:]
        dx_kv[:, lanes(256 + j * 128, 128)] = dv[half:]

    def heads_close(u):
        b = lax.rem(u, 2)

        @pl.when(u >= 2)
        def _():
            gq_send(u - 2).wait_send()

        kv_send(u).wait_recv()
        for j in range(2):
            c = slice(j * 128, j * 128 + 128)
            gq[b, :half, c] = rope_back(stashed(b, 0, j).astype(F32), cosine[...], sine[...]).astype(BF)
            g = added(stashed(b, 1, j), kvl[b, :, c]).astype(F32)
            gq[b, :half, 256 + j * 128 : 384 + j * 128] = rope_back(g, cosine[...], sine[...]).astype(BF)
            gq[b, :half, 512 + j * 128 : 640 + j * 128] = added(stashed(b, 2, j), kvl[b, :, 256 + j * 128 : 384 + j * 128])
        for c in qkv_weights(u):
            c.wait()
        back = nt(gq[b, :half], win[...].reshape(width, 768))

        @pl.when(u == 0)
        def _():
            acc_g[...] = back

        @pl.when(u > 0)
        def _():
            acc_g[...] += back

        @pl.when(u < 3)
        def _():
            for c in qkv_weights(u + 1):
                c.start()

    def qkv_term(u):
        gq_send(u).wait_recv()
        put(wide, STEPS + u, nn(mt[...], gq[u % 2]), GROUP)

    def first_norm():
        wait("r0", "r1")
        back, terms[0:1] = norm_back(k[:half].astype(F32), gains[0:1], acc_g[...])
        dout[...] = (acc_f[...] + back).astype(BF)

    gs_send = remote(gs, gr, ps.at[1], pr.at[1], sib)

    def gain_terms():
        for n in range(2):
            for o in range(4):
                for ref, part in ((gain.acc.at[0], h.core), (gs, 1 - h.core)):
                    low, high = terms[n : n + 1, 256 * o : 256 * o + 128], terms[n : n + 1, 256 * o + 128 : 256 * o + 256]
                    value = jnp.where(part == 0, low, high)
                    ref[n, o // 2, o % 2] = jnp.broadcast_to(value, (16, 128)).astype(BF)
        gs_send.start()
        gs_send.wait()
        for n in range(2):
            for o in range(4):
                gain.acc[0, n, o // 2, o % 2] = added(gain.acc[0, n, o // 2, o % 2], gr[n, o // 2, o % 2])

    def dx(j):
        return kvl.at[j, pl.ds(0, SHARD), pl.ds(0, 256)]

    def down_swap(j, act, ref):
        act(remote(ref.at[j, 1 - h.core], dx(j), dxs.at[j], dxr.at[j], sib))

    def to_end(j):
        return pltpu.make_async_copy(dx(j), down_o.at[:, lanes((1 - h.core) * 512 + j * 256, 256)], fo.at[2, 5 + j])

    def write(name, t, act, ref):
        if name == "w" and t < STEPS:
            for n in range(2):
                act(pltpu.make_async_copy(ref.at[t, n], in_o.at[n, :, pl.ds(t * GROUP, GROUP)], fo.at[0, 2 * t + n]))
        elif name == "w":
            parts = ((0, 0, 256, 0), (0, 256, 128, 1024), (1, 0, 128, 1152), (1, 128, 256, 2048))
            for n, (m, at_col, size, to) in enumerate(parts):
                dst = qkv_o.at[:, pl.ds(to + (t - STEPS) * 256, size)]
                act(pltpu.make_async_copy(ref.at[t, m, :, pl.ds(at_col, size)], dst, fo.at[1, 4 * (t - STEPS) + n]))
        elif name == "d":
            dst = down_o.at[:, lanes(h.core * 512 + t * 256, 256)]
            act(pltpu.make_async_copy(ref.at[t, h.core], dst, fo.at[2, 3 + t]))
        elif name == "o":
            for n in range(2):
                act(pltpu.make_async_copy(ref.at[0, n], out_o.at[:, pl.ds(n * 512, 512)], fo.at[2, n]))
        else:
            act(pltpu.make_async_copy(ref, gain_o, fo.at[2, 2]))

    sent = [0, 0]

    def piece(which):
        size = block // PIECES
        part = pl.ds(sent[which] * size, size)
        sent[which] += 1
        if which == 0:
            rows.start(ffn_h, outh_o, es.at[0], er.at[0], el.at[0], False, part)
        else:
            rows.start(Halves(dout), inh_o, es.at[1], er.at[1], el.at[1], False, part)

    work = {"ln2": second_norm, "do": mixture_grads, "og": out_term, "H": first_norm, "gains": gain_terms}

    def perform(ops):
        for op in ops:
            if op[0] == "c":
                if op[1] in work:
                    work[op[1]]()
            elif op[0] == "r":
                piece(op[1])
            else:
                (name, t), group = op[1], groups[op[1][0]]
                if op[0] == "s":
                    getattr(group, Sums.LATER[op[2]])(t)
                    if op[2] == 5:
                        group.total(functools.partial(write, name, t, lambda c: c.start()))
                        if name == "d":
                            down.total(functools.partial(down_swap, t, lambda c: c.start()))
                else:
                    if name == "w":
                        in_term(t) if t < STEPS else qkv_term(t - STEPS)
                    elif name == "d":
                        down_term(t)
                    group.begin(t)

    before, loop, after = split_plan()
    perform(before)
    wait("bias", "q", "k", "v", "nt")
    for c in qkv_weights(0):
        c.start()

    def each(p, _):
        pl.when(p < 8)(lambda: heads_back(p))
        pl.when(p == 8)(lambda: start("r0", "r1"))
        for n in range(10):
            if loop[n, 0]:
                pl.when(p == n)(functools.partial(perform, loop[n, 0]))

        @pl.when((lax.rem(p, 2) == 1) & (p >= 3))
        def _():
            heads_close((p - 3) // 2)

        for n in range(10):
            if loop[n, 1]:
                pl.when(p == n)(functools.partial(perform, loop[n, 1]))
            if loop[n, 2]:
                pl.when(p == n)(functools.partial(perform, loop[n, 2]))

        @pl.when((lax.rem(p, 2) == 1) & (p < 8))
        def _():
            kv_send(p // 2).start()

        @pl.when((lax.rem(p, 2) == 1) & (p >= 3))
        def _():
            gq_send((p - 3) // 2).start()

        return 0

    lax.fori_loop(0, 10, each, 0)
    perform(after)
    for j in range(2):
        down.total(functools.partial(down_swap, j, lambda c: c.wait()))
        to_end(j).start()
    kv_send(3).wait_send()
    gq_send(2).wait_send()
    gq_send(3).wait_send()

    for name, group in groups.items():
        for t in group.slot:
            group.total(functools.partial(write, name, t, lambda c: c.wait()))
    for j in range(2):
        to_end(j).wait()
    rows.wait(ffn_h, outh_o, es.at[0], er.at[0], el.at[0], False)
    rows.wait(Halves(dout), inh_o, es.at[1], er.at[1], el.at[1], False)


def back_all(ffn_rows, *args):
    dma = pltpu.SemaphoreType.DMA
    block, wide = ffn_rows.shape[1:]
    half = 2 * block

    def buf(*s, kind=BF):
        return pltpu.VMEM(s, kind)

    def shape(*s):
        return jax.ShapeDtypeStruct(s, BF)

    whole = pl.BlockSpec(memory_space=pltpu.VMEM)
    scratch = [
        buf(half, wide, kind=F32), buf(half, wide, kind=F32), buf(8, 128, 768),
        buf(half, 2 * half), buf(half, 2 * half), buf(2 * half, 768), buf(2, 2 * half, 768),
        buf(STEPS * GROUP, 2 * half), buf(2 * half, half), buf(2 * half, wide), buf(half, wide),
        buf(half, wide), buf(2 * half, wide), buf(2 * half, wide), buf(2 * half, half),
        buf(2, GROUP, wide), buf(half, 512), buf(2, half, 512), buf(8, 2, half, kind=F32), buf(2, wide, kind=F32),
        buf(2, 2, 2, 16, 128), buf(2, 2, 2, 16, 128),
        dma((13,)), dma((1,)), dma((3,)), dma((2,)), dma((2,)), dma((2,)), dma((2,)), dma((2,)), dma((2,)),
        dma((2,)), dma((2,)), dma((3, 16)), dma((2, 2)), dma((2, 2)), dma((2,)),
    ]
    for s in ((11, WIDE_SLOTS, 128, GROUP), (2, 2, SHARD, 256), (1, 1, 128, 512), (1, 1, 16, 128)):
        scratch += Sums.scratch(*s)
    return pl.pallas_call(
        back_kernel,
        out_shape=[
            shape(2, 128, STEPS * GROUP), shape(128, 3 * wide), shape(SHARD, wide), shape(128, wide), shape(1, 2, 16, 128),
            shape(2, block, wide), shape(2, block, wide),
        ],
        in_specs=[ANY] * 18 + [whole] * 4,
        out_specs=[ANY] * 7,
        scratch_shapes=scratch,
        compiler_params=pltpu.CompilerParams(collective_id=2, has_side_effects=True, vmem_limit_bytes=VMEM_BYTES),
        name="backward_and_sums",
    )(ffn_rows, *args)


def chip_streams(tokens, cotangent, doc_starts, qkv_weight, out_weight, in_weight, down_weight, attn_gain, ffn_gain):
    wide = tokens.shape[3]
    shard = down_weight.shape[0]
    spare = jnp.zeros((in_weight.shape[0], SHARD - shard), BF)
    pieces = [in_weight[:, n * shard : (n + 1) * shard] for n in range(16)]
    in_parts = jnp.stack([jnp.concatenate([p for n in range(8) for p in (pieces[8 * m + n], spare)], axis=1) for m in range(2)])
    down_rows = jnp.pad(down_weight, ((0, SHARD - shard), (0, 0)))
    inverse = ROPE_THETA ** (-jnp.arange(0, HEAD_DIM, 2, dtype=F32) / HEAD_DIM)
    (qkv_f, out_f, cot, rows_low, middle, gn, ffn_rows, q, k, v, mixture, bias, xt, mt, nt_rows, glc, gj, at,
     both_gains, cosine, sine, lse) = front_all(
        attn_gain[None], ffn_gain[None], qkv_weight, out_weight, in_parts, down_rows,
        tokens[:, 0], cotangent[:, 0], doc_starts[:, 0], jnp.tile(inverse, 4)[None],
    )
    in_t, qkv_t, down_t, out_t, gain_t, out_home, in_home = back_all(
        ffn_rows, middle, gn, cot, qkv_f, out_f.reshape(wide, wide), q, k, v, mixture, rows_low, bias, xt, mt, nt_rows, glc, gj, at,
        both_gains, cosine, sine, lse,
    )
    in_cols = [in_t[m, :, n * SHARD : n * SHARD + shard] for m in range(2) for n in range(8)]
    return (
        out_home[:, None].astype(F32),
        in_home[:, None].astype(F32),
        qkv_t.astype(F32),
        out_t.astype(F32),
        jnp.concatenate(in_cols, axis=1).astype(F32),
        down_t[:shard].astype(F32),
        gain_t[0, 0, 0].astype(F32),
        gain_t[0, 1, 0].astype(F32),
    )


def solution(mesh):
    whole_chips = dict(mesh.shape) == {"seq": 4, "fsdp": 8}
    return jax.shard_map(
        chip_streams if whole_chips else shards,
        mesh=mesh,
        in_specs=(
            P(None, "fsdp", "seq", None),
            P(None, "fsdp", "seq", None),
            P(None, "fsdp", None),
            P("fsdp", None),
            P("fsdp", None),
            P("fsdp", None),
            P("fsdp", None),
            P("fsdp"),
            P("fsdp"),
        ),
        out_specs=(
            P(None, "fsdp", "seq", None),
            P(None, "fsdp", "seq", None),
            P("fsdp", None),
            P("fsdp", None),
            P("fsdp", None),
            P("fsdp", None),
            P("fsdp"),
            P("fsdp"),
        ),
        check_vma=False,
    )
```

```python
import functools
from functools import partial

import jax
import jax.numpy as jnp
from jax import lax
from jax.experimental import pallas as pl
from jax.experimental.pallas import tpu as pltpu
from jax.sharding import PartitionSpec as P

HEADS = 16
HEAD_DIM = 64


EPSILON = 1e-05
ROPE_THETA = 160000.0
MASKED_SCORE = -1e30


def as_sent(x):

    def short(part):
        return part.astype(jnp.bfloat16) if part.dtype == jnp.float32 else part

    return jax.tree.map(short, x)


def layer_norm(values, norm_gain):
    average = jnp.mean(values, axis=-1, keepdims=True)
    centred = values - average
    spread = jnp.mean(centred * centred, axis=-1, keepdims=True)
    return centred * lax.rsqrt(spread + EPSILON) * norm_gain


def gated_gelu(joined):
    half_width = joined.shape[-1] // 2
    return jax.nn.gelu(joined[:, :half_width], approximate=False) * joined[:, half_width:]


def rotate(values, cosine_table, sine_table):
    half_width = values.shape[-1] // 2
    turned = jnp.concatenate([-values[..., half_width:], values[..., :half_width]], axis=-1)
    return values * cosine_table + turned * sine_table


def rope_tables(starts, places, head_width):
    preceding = starts[None, :] <= places[:, None]
    doc_begin = jnp.max(jnp.where(preceding, starts[None, :], 0), axis=-1)
    offsets = (places - doc_begin).astype(jnp.float32)
    inverse = ROPE_THETA ** (-jnp.arange(0, head_width, 2, dtype=jnp.float32) / head_width)
    angles = offsets[:, None] * inverse[None, :]
    angles = jnp.concatenate([angles, angles], axis=-1)
    return (jnp.cos(angles), jnp.sin(angles))


def segment_ids(starts, places):
    return jnp.sum((starts[None, :] <= places[:, None]).astype(jnp.int32), axis=-1) - 1


def turn_pair(pair, cosine_table, sine_table):
    shaped = pair.reshape(pair.shape[0], 2, HEADS, HEAD_DIM)
    turned = rotate(shaped, cosine_table[:, None, None, :], sine_table[:, None, None, :])
    return turned.reshape(pair.shape[0], 2 * HEADS * HEAD_DIM)


def attend_forward(queries, keys_in, values_in, segments, head_count):
    length = queries.shape[0]
    head_width = queries.shape[1] // head_count
    block_rows = min(512, length)
    blocks = length // block_rows
    keyset = keys_in.reshape(length, head_count, head_width)
    valueset = values_in.reshape(length, head_count, head_width)
    factor = head_width ** (-0.5)

    def one_block(pieces):
        query_rows, block_segs = pieces
        scores = (
            jnp.einsum("qhd,khd->hqk", query_rows, keyset, preferred_element_type=jnp.float32)
            * factor
        )
        scores = jnp.where((block_segs[:, None] == segments[None, :])[None], scores, MASKED_SCORE)
        row_max = jnp.max(scores, axis=-1, keepdims=True)
        totals = jnp.sum(jnp.exp(scores - row_max), axis=-1, keepdims=True)
        logsums = row_max + jnp.log(totals)
        weights = jnp.exp(scores - logsums).astype(jnp.bfloat16)
        mixture = jnp.einsum("hqk,khd->qhd", weights, valueset, preferred_element_type=jnp.float32)
        return (mixture, logsums)

    mixture, logsums = lax.map(
        one_block,
        (
            queries.reshape(blocks, block_rows, head_count, head_width),
            segments.reshape(blocks, block_rows),
        ),
    )
    return (mixture.reshape(length, head_count * head_width), logsums)


def attend_backward(queries, keys_in, values_in, grads_in, segments, logsums, head_count):
    length = queries.shape[0]
    head_width = queries.shape[1] // head_count
    block_rows = min(512, length)
    blocks = length // block_rows
    keyset = keys_in.reshape(length, head_count, head_width)
    valueset = values_in.reshape(length, head_count, head_width)
    factor = head_width ** (-0.5)

    def one_block(carry, pieces):
        key_grad, value_grad = carry
        query_rows, block_segs, grad_rows, block_lse = pieces
        scores = (
            jnp.einsum("qhd,khd->hqk", query_rows, keyset, preferred_element_type=jnp.float32)
            * factor
        )
        scores = jnp.where((block_segs[:, None] == segments[None, :])[None], scores, MASKED_SCORE)
        weights = jnp.exp(scores - block_lse)
        value_grad = value_grad + jnp.einsum(
            "hqk,qhd->khd",
            weights.astype(jnp.bfloat16),
            grad_rows,
            preferred_element_type=jnp.float32,
        )
        grad_weights = jnp.einsum(
            "qhd,khd->hqk", grad_rows, valueset, preferred_element_type=jnp.float32
        )
        centre = jnp.sum(weights * grad_weights, axis=-1, keepdims=True)
        grad_scores = (weights * (grad_weights - centre)).astype(jnp.bfloat16)
        query_grad = (
            jnp.einsum("hqk,khd->qhd", grad_scores, keyset, preferred_element_type=jnp.float32)
            * factor
        )
        key_grad = (
            key_grad
            + jnp.einsum(
                "hqk,qhd->khd", grad_scores, query_rows, preferred_element_type=jnp.float32
            )
            * factor
        )
        return ((key_grad, value_grad), query_grad)

    empty = jnp.zeros((length, head_count, head_width), jnp.float32)
    pieces = (
        queries.reshape(blocks, block_rows, head_count, head_width),
        segments.reshape(blocks, block_rows),
        grads_in.reshape(blocks, block_rows, head_count, head_width),
        logsums,
    )
    (key_grad, value_grad), query_grad = lax.scan(one_block, (empty, empty), pieces)
    flat_shape = (length, head_count * head_width)
    return (
        query_grad.reshape(flat_shape).astype(jnp.bfloat16),
        key_grad.reshape(flat_shape).astype(jnp.bfloat16),
        value_grad.reshape(flat_shape).astype(jnp.bfloat16),
    )


def shards(
    tokens,
    cotangent,
    doc_starts,
    qkv_weight,
    out_weight,
    in_weight,
    down_weight,
    attn_gain,
    ffn_gain,
):
    micro_count = tokens.shape[0]
    token_rows = tokens.shape[2]
    model_width = tokens.shape[3]
    seq_count = lax.axis_size("seq")
    head_count = HEADS // seq_count
    places = lax.axis_index("seq") * token_rows + jnp.arange(token_rows, dtype=jnp.int32)
    everywhere = jnp.arange(token_rows * seq_count, dtype=jnp.int32)
    outputs = []
    input_grads = []
    full_terms = None
    shard_terms = None
    for micro_step in range(micro_count):
        rows_in = tokens[micro_step, 0]
        starts = doc_starts[micro_step, 0]
        cosine_table, sine_table = rope_tables(starts, places, HEAD_DIM)
        segments = segment_ids(starts, everywhere)
        attn_set = (
            lax.all_gather(qkv_weight, "fsdp", axis=0, tiled=True),
            lax.all_gather(out_weight, "fsdp", axis=0, tiled=True),
            lax.all_gather(attn_gain, "fsdp", axis=0, tiled=True),
        )
        qkv_full, out_full, gain_one = attn_set
        normed, norm_back = jax.vjp(layer_norm, rows_in, gain_one.astype(jnp.float32))
        normed_low = normed.astype(jnp.bfloat16)
        qkv_rows = jnp.dot(normed_low, qkv_full, preferred_element_type=jnp.float32)
        turned, turn_back = jax.vjp(
            partial(turn_pair, cosine_table=cosine_table, sine_table=sine_table),
            qkv_rows[:, : 2 * model_width],
        )
        queries = turned[:, :model_width].astype(jnp.bfloat16)
        keyset = turned[:, model_width:].astype(jnp.bfloat16)
        valueset = qkv_rows[:, 2 * model_width :].astype(jnp.bfloat16)
        query_heads, key_heads, value_heads = (
            lax.all_to_all(queries, "seq", split_axis=1, concat_axis=0, tiled=True),
            lax.all_to_all(keyset, "seq", split_axis=1, concat_axis=0, tiled=True),
            lax.all_to_all(valueset, "seq", split_axis=1, concat_axis=0, tiled=True),
        )
        mixture, logsums = attend_forward(query_heads, key_heads, value_heads, segments, head_count)
        mixture_rows = lax.all_to_all(
            mixture.astype(jnp.bfloat16), "seq", split_axis=0, concat_axis=1, tiled=True
        )
        middle = rows_in + jnp.dot(mixture_rows, out_full, preferred_element_type=jnp.float32)
        ffn_set = (
            lax.all_gather(in_weight, "fsdp", axis=0, tiled=True),
            lax.all_gather(down_weight, "fsdp", axis=0, tiled=True),
            lax.all_gather(ffn_gain, "fsdp", axis=0, tiled=True),
        )
        in_full, down_full, gain_two = ffn_set
        normed_two, norm_back_two = jax.vjp(layer_norm, middle, gain_two.astype(jnp.float32))
        normed_two_low = normed_two.astype(jnp.bfloat16)
        joined = jnp.dot(normed_two_low, in_full, preferred_element_type=jnp.float32)
        active, gelu_back = jax.vjp(gated_gelu, joined)
        active_low = active.astype(jnp.bfloat16)
        outputs.append(middle + jnp.dot(active_low, down_full, preferred_element_type=jnp.float32))
        grad_out = cotangent[micro_step, 0]
        grad_low = grad_out.astype(jnp.bfloat16)
        ffn_set = (
            lax.all_gather(in_weight, "fsdp", axis=0, tiled=True),
            lax.all_gather(down_weight, "fsdp", axis=0, tiled=True),
            lax.all_gather(ffn_gain, "fsdp", axis=0, tiled=True),
        )
        in_full, down_full, gain_two = ffn_set
        down_term = jnp.dot(active_low.T, grad_low, preferred_element_type=jnp.float32)
        grad_active = jnp.dot(grad_low, down_full.T, preferred_element_type=jnp.float32)
        grad_joined = gelu_back(grad_active)[0].astype(jnp.bfloat16)
        in_term = jnp.dot(normed_two_low.T, grad_joined, preferred_element_type=jnp.float32)
        grad_normed_two = jnp.dot(grad_joined, in_full.T, preferred_element_type=jnp.float32)
        grad_middle_norm, gain_two_term = norm_back_two(grad_normed_two)
        grad_middle = grad_out + grad_middle_norm
        grad_mid_low = grad_middle.astype(jnp.bfloat16)
        attn_set = (
            lax.all_gather(qkv_weight, "fsdp", axis=0, tiled=True),
            lax.all_gather(out_weight, "fsdp", axis=0, tiled=True),
            lax.all_gather(attn_gain, "fsdp", axis=0, tiled=True),
        )
        qkv_full, out_full, gain_one = attn_set
        out_term = jnp.dot(mixture_rows.T, grad_mid_low, preferred_element_type=jnp.float32)
        grad_mixture = jnp.dot(grad_mid_low, out_full.T, preferred_element_type=jnp.float32).astype(
            jnp.bfloat16
        )
        grad_heads = lax.all_to_all(grad_mixture, "seq", split_axis=1, concat_axis=0, tiled=True)
        query_grad, key_grad, value_grad = attend_backward(
            query_heads, key_heads, value_heads, grad_heads, segments, logsums, head_count
        )
        query_back, key_back, value_back = (
            lax.all_to_all(query_grad, "seq", split_axis=0, concat_axis=1, tiled=True),
            lax.all_to_all(key_grad, "seq", split_axis=0, concat_axis=1, tiled=True),
            lax.all_to_all(value_grad, "seq", split_axis=0, concat_axis=1, tiled=True),
        )
        grad_pair = turn_back(jnp.concatenate([query_back, key_back], axis=1).astype(jnp.float32))[
            0
        ]
        grad_qkv = jnp.concatenate([grad_pair, value_back.astype(jnp.float32)], axis=1).astype(
            jnp.bfloat16
        )
        qkv_term = jnp.dot(normed_low.T, grad_qkv, preferred_element_type=jnp.float32)
        grad_normed = jnp.dot(grad_qkv, qkv_full.T, preferred_element_type=jnp.float32)
        grad_rows_norm, gain_one_term = norm_back(grad_normed)
        input_grads.append(grad_middle + grad_rows_norm)
        terms = (qkv_term, out_term, in_term, down_term, gain_one_term, gain_two_term)
        full_terms = terms if full_terms is None else jax.tree.map(jnp.add, full_terms, terms)
    shard_terms = jax.tree.map(
        lambda part: part.astype(jnp.float32),
        lax.psum_scatter(as_sent(full_terms), "fsdp", scatter_dimension=0, tiled=True),
    )
    totals = jax.tree.map(
        lambda part: part.astype(jnp.float32), lax.psum(as_sent(shard_terms), "seq")
    )
    return (
        jnp.stack(outputs)[:, None],
        jnp.stack(input_grads)[:, None],
        totals[0],
        totals[1],
        totals[2],
        totals[3],
        totals[4],
        totals[5],
    )


MESH = pl.DeviceIdType.MESH
ANY = pl.BlockSpec(memory_space=pl.ANY)
VMEM_BYTES = 127 * 2**19
BF = jnp.bfloat16
F32 = jnp.float32


def nn(a, b):
    return lax.dot_general(a, b, (((1,), (0,)), ((), ())), preferred_element_type=F32)


def nt(a, b):
    return lax.dot_general(a, b, (((1,), (1,)), ((), ())), preferred_element_type=F32)


def spot():
    z, f = lax.axis_index("seq"), lax.axis_index("fsdp")
    core = lax.rem(f, 2)
    x = lax.rem(f // 2, 2)
    y = f // 4
    return z, f, y, x, core


def remote(src, dst, send, recv, where):
    return pltpu.make_async_remote_copy(
        src_ref=src, dst_ref=dst, send_sem=send, recv_sem=recv, device_id=where, device_id_type=MESH
    )


class Rows:
    def __init__(self, z, f, core):
        base = f - core
        self.work, self.home = [], []
        for i in range(2):
            zw, cw = 2 * i + core, z // 2
            self.work.append((zw, base + cw, (zw == z) & (cw == core)))
            zh, ch = 2 * core + i, lax.rem(z, 2)
            self.home.append((zh, base + ch, (zh == z) & (ch == core)))
        self.z = z

    def greet(self, barrier):
        count = 0
        for zt, ft, same in self.work + self.home:

            @pl.when(jnp.logical_not(same))
            def _():
                pl.semaphore_signal(barrier, inc=1, device_id=(zt, ft), device_id_type=MESH)

            count = count + jnp.where(same, 0, 1)
        return count

    def start(self, src, dst, send, recv, local, out, piece=slice(None)):
        places = self.work if out else self.home
        slot = lax.rem(self.z, 2) if out else self.z // 2
        for i, (zt, ft, same) in enumerate(places):

            @pl.when(same)
            def _(i=i):
                pltpu.make_async_copy(src.at[i, piece], dst.at[slot, piece], local).start()

            @pl.when(jnp.logical_not(same))
            def _(i=i, zt=zt, ft=ft):
                remote(src.at[i, piece], dst.at[slot, piece], send.at[i], recv.at[slot], (zt, ft)).start()

    def wait(self, src, dst, send, recv, local, out):
        goes, comes = (self.work, self.home) if out else (self.home, self.work)
        for i, (zt, ft, same) in enumerate(goes):

            @pl.when(same)
            def _(i=i):
                pltpu.make_async_copy(src.at[i], dst.at[i], local).wait()

            @pl.when(jnp.logical_not(same))
            def _(i=i, zt=zt, ft=ft):
                remote(src.at[i], dst.at[i], send.at[i], recv.at[i], (zt, ft)).wait_send()

        for i, (zt, ft, same) in enumerate(comes):

            @pl.when(jnp.logical_not(same))
            def _(i=i, zt=zt, ft=ft):
                remote(src.at[i], dst.at[i], send.at[i], recv.at[i], (zt, ft)).wait_recv()


def halves(width):
    cut = (width // 128 // 2) * 128
    return pl.ds(0, cut), pl.ds(cut, width - cut)


SQRT_HALF = 0.7071067811865476
DENSITY = 0.3989422804014327
BY_Z = (2, 4)
SHARD = 336
GROUP = 384
STEPS = 7


def moments(values):
    average = jnp.mean(values, axis=-1, keepdims=True)
    centred = values - average
    spread = jnp.mean(centred * centred, axis=-1, keepdims=True)
    scale = lax.rsqrt(spread + EPSILON)
    return centred * scale, scale


def norm_back(values, gain, grads):
    unit, scale = moments(values)
    spread = grads * gain
    inner = spread - jnp.mean(spread, axis=-1, keepdims=True)
    inner = inner - unit * jnp.mean(spread * unit, axis=-1, keepdims=True)
    return inner * scale, jnp.sum(grads * unit, axis=0, keepdims=True)


def rope_back(grads, cosine, sine):
    lane = lax.broadcasted_iota(jnp.int32, (1, 128), 1)
    low = lax.rem(lane, 64) < 32
    u = grads * sine
    return grads * cosine + jnp.where(low, pltpu.roll(u, 96, 1), -pltpu.roll(u, 32, 1))


class Sums:
    KINDS = 9

    @staticmethod
    def scratch(count, slots, rows, wide):
        dma = pltpu.SemaphoreType.DMA((count, Sums.KINDS))
        shapes = [(slots, 2, 2, 2), (count, 2, 2), (count, 2), (count, 2), (count,)]
        return [pltpu.VMEM(s + (rows, wide), BF) for s in shapes] + [dma, dma]

    def __init__(self, here, refs, slot):
        self.here, self.slot = here, slot
        self.acc, self.rx, self.r2, self.zr, self.zr2, self.send, self.recv = refs

    def copy(self, t, kind):
        h = self.here
        acc = self.acc.at[self.slot[t]]
        plan = {
            0: lambda: (acc.at[0, :, 1 - h.x], self.rx.at[t, 0], (h.z, h.fx)),
            1: lambda: (acc.at[1, 1 - h.y], self.rx.at[t, 1], (h.z, h.fy)),
            2: lambda: (self.rx.at[t, 0, 1 - h.y], self.r2.at[t, 0], (h.z, h.fy)),
            3: lambda: (self.rx.at[t, 1, 1 - h.x], self.r2.at[t, 1], (h.z, h.fx)),
            4: lambda: (self.r2.at[t], self.zr.at[t], (h.near, h.f)),
            5: lambda: (self.zr.at[t, 1 - h.own], self.zr2.at[t], (h.across, h.f)),
            6: lambda: (self.r2.at[t, h.own], self.r2.at[t, h.own], (h.across, h.f)),
            7: lambda: (self.r2.at[t, h.own], self.zr.at[t, h.own], (h.near, h.f)),
            8: lambda: (self.r2.at[t, 1 - h.own], self.zr.at[t, 1 - h.own], (h.near, h.f)),
        }
        src, dst, where = plan[kind]()
        return remote(src, dst, self.send.at[t, kind], self.recv.at[t, kind], where)

    def begin(self, t):
        self.copy(t, 0).start()
        self.copy(t, 1).start()

    def cross(self, t):
        h, s = self.here, self.slot[t]
        self.copy(t, 0).wait()
        self.rx[t, 0, 1 - h.y] = added(self.rx[t, 0, 1 - h.y], self.acc[s, 0, 1 - h.y, h.x])
        self.copy(t, 2).start()
        self.copy(t, 1).wait()
        self.rx[t, 1, 1 - h.x] = added(self.rx[t, 1, 1 - h.x], self.acc[s, 1, h.y, 1 - h.x])
        self.copy(t, 3).start()

    def plane(self, t):
        h, s = self.here, self.slot[t]
        self.copy(t, 2).wait()
        self.r2[t, 0] = added(self.r2[t, 0], self.rx[t, 0, h.y], self.acc[s, 0, h.y, h.x])
        self.copy(t, 3).wait()
        self.r2[t, 1] = added(self.r2[t, 1], self.rx[t, 1, h.x], self.acc[s, 1, h.y, h.x])

        @pl.when(h.outer)
        def _():
            self.copy(t, 4).start()

    def meet(self, t):
        h = self.here

        @pl.when(jnp.logical_not(h.outer))
        def _():
            self.copy(t, 4).wait_recv()
            self.zr[t, 1 - h.own] = added(self.zr[t, 1 - h.own], self.r2[t, 1 - h.own])
            self.copy(t, 5).start()

    def sums(self, t):
        h = self.here

        @pl.when(jnp.logical_not(h.outer))
        def _():
            self.copy(t, 5).wait()
            self.r2[t, h.own] = added(self.r2[t, h.own], self.zr[t, h.own], self.zr2[t])
            self.copy(t, 6).start()
            self.copy(t, 7).start()

    def spread(self, t):
        @pl.when(jnp.logical_not(self.here.outer))
        def _():
            self.copy(t, 6).wait_recv()
            self.copy(t, 8).start()

    def finish(self, t):
        @pl.when(jnp.logical_not(self.here.outer))
        def _():
            self.copy(t, 6).wait_send()
            self.copy(t, 7).wait_send()
            self.copy(t, 8).wait_send()

        @pl.when(self.here.outer)
        def _():
            self.copy(t, 4).wait_send()
            self.copy(t, 7).wait_recv()
            self.copy(t, 8).wait_recv()

    def total(self, act):
        for ref, there in ((self.zr, self.here.outer), (self.r2, jnp.logical_not(self.here.outer))):
            pl.when(there)(functools.partial(act, ref))

    LATER = ("cross", "plane", "meet", "sums", "spread", "finish")


def added(*terms):
    total = terms[0].astype(F32)
    for term in terms[1:]:
        total = total + term.astype(F32)
    return total.astype(BF)


class Halves:
    def __init__(self, ref):
        self.ref, self.at, self.size = ref, self, ref.shape[0] // 2

    def __getitem__(self, index):
        i, piece = index if isinstance(index, tuple) else (index, slice(None))
        if isinstance(piece, slice):
            return self.ref.at[pl.ds(i * self.size, self.size)]
        return self.ref.at[pl.ds(i * self.size + piece.start, piece.size)]


class Here:
    def __init__(self):
        self.z, self.f, self.y, self.x, self.core = spot()
        self.fx = self.f + 2 - 4 * self.x
        self.fy = self.f + 4 - 8 * self.y
        self.fc = self.f + 1 - 2 * self.core
        z = self.z
        self.outer = (z == 0) | (z == 3)
        self.near = jnp.where(z < 2, 1 - z, 5 - z)
        self.across = jnp.where(self.outer, z, 3 - z)
        self.own = jnp.where(z < 2, 0, 1)

    def greet(self, barrier, rows, column=0):
        for n in range(column):
            pl.semaphore_signal(barrier, inc=1, device_id=(lax.rem(self.z + n + 1, 4), self.f), device_id_type=MESH)
        for t in (self.fx, self.fy, self.fc):
            pl.semaphore_signal(barrier, inc=1, device_id=(self.z, t), device_id_type=MESH)
        pl.semaphore_signal(barrier, inc=1, device_id=(self.near, self.f), device_id_type=MESH)

        @pl.when(jnp.logical_not(self.outer))
        def _():
            pl.semaphore_signal(barrier, inc=1, device_id=(self.across, self.f), device_id_type=MESH)

        pl.semaphore_wait(barrier, rows.greet(barrier) + 4 + column + jnp.where(self.outer, 0, 1))


def lanes(start, size):
    return pl.ds(start if isinstance(start, int) else pl.multiple_of(start, 128), size)


PIECES = 8
WIDE_SLOTS = 3
DOWN_FIRST = 0
PLAN = (
    ("r", 0),
    ("f", ("w", 0)),
    ("r", 0),
    ("f", ("w", 1)),
    ("c", "ln2"),
    ("r", 0),
    ("f", ("d", 0)),
    ("s", ("w", 0), 0),
    ("r", 0),
    ("c", "do"),
    ("s", ("w", 1), 0),
    ("r", 0),
    ("c", "og"),
    ("r", 0),
    ("b", ("o", 0)),
    ("c", "E0.0"),
    ("c", "E0.1"),
    ("s", ("d", 0), 0),
    ("r", 0),
    ("c", "E1.0"),
    ("s", ("w", 0), 1),
    ("s", ("w", 1), 1),
    ("r", 0),
    ("c", "E1.1"),
    ("f", ("w", 2)),
    ("c", "F0"),
    ("s", ("o", 0), 0),
    ("s", ("w", 0), 2),
    ("c", "E2.0"),
    ("s", ("d", 0), 1),
    ("s", ("w", 1), 2),
    ("f", ("w", 3)),
    ("s", ("w", 0), 3),
    ("c", "E2.1"),
    ("s", ("w", 2), 0),
    ("s", ("w", 1), 3),
    ("c", "F1"),
    ("s", ("o", 0), 1),
    ("s", ("w", 0), 4),
    ("f", ("d", 1)),
    ("s", ("w", 3), 0),
    ("s", ("w", 1), 4),
    ("s", ("d", 0), 2),
    ("c", "G0"),
    ("s", ("w", 2), 1),
    ("b", ("w", 7)),
    ("c", "E3.0"),
    ("s", ("o", 0), 2),
    ("c", "E3.1"),
    ("s", ("d", 0), 3),
    ("c", "F2"),
    ("s", ("d", 1), 0),
    ("s", ("o", 0), 3),
    ("s", ("w", 2), 2),
    ("c", "G1"),
    ("s", ("w", 3), 1),
    ("b", ("w", 8)),
    ("c", "F3"),
    ("s", ("d", 0), 4),
    ("c", "G2"),
    ("s", ("w", 7), 0),
    ("s", ("o", 0), 4),
    ("s", ("w", 3), 2),
    ("b", ("w", 9)),
    ("c", "H"),
    ("s", ("d", 1), 1),
    ("s", ("w", 2), 3),
    ("s", ("w", 3), 3),
    ("c", "gains"),
    ("b", ("g", 0)),
    ("c", "G3"),
    ("s", ("w", 8), 0),
    ("s", ("w", 2), 4),
    ("r", 1),
    ("s", ("w", 7), 1),
    ("f", ("w", 4)),
    ("s", ("w", 3), 4),
    ("r", 1),
    ("s", ("w", 9), 0),
    ("s", ("g", 0), 0),
    ("s", ("d", 1), 2),
    ("s", ("w", 8), 1),
    ("f", ("w", 5)),
    ("r", 1),
    ("s", ("w", 4), 0),
    ("s", ("d", 1), 3),
    ("s", ("w", 7), 2),
    ("s", ("w", 9), 1),
    ("s", ("g", 0), 1),
    ("f", ("w", 6)),
    ("s", ("w", 8), 2),
    ("s", ("w", 5), 0),
    ("s", ("d", 1), 4),
    ("s", ("w", 4), 1),
    ("s", ("w", 7), 3),
    ("b", ("w", 10)),
    ("s", ("w", 0), 5),
    ("s", ("w", 1), 5),
    ("s", ("d", 0), 5),
    ("s", ("o", 0), 5),
    ("s", ("w", 2), 5),
    ("s", ("w", 3), 5),
    ("r", 1),
    ("s", ("w", 8), 3),
    ("s", ("w", 9), 2),
    ("s", ("g", 0), 2),
    ("s", ("w", 7), 4),
    ("s", ("d", 1), 5),
    ("s", ("w", 6), 0),
    ("s", ("w", 5), 1),
    ("s", ("w", 4), 2),
    ("s", ("w", 8), 4),
    ("r", 1),
    ("s", ("w", 9), 3),
    ("s", ("g", 0), 3),
    ("s", ("w", 5), 2),
    ("s", ("w", 4), 3),
    ("s", ("w", 10), 0),
    ("s", ("w", 7), 5),
    ("s", ("w", 6), 1),
    ("s", ("w", 8), 5),
    ("s", ("w", 10), 1),
    ("s", ("w", 9), 4),
    ("s", ("g", 0), 4),
    ("s", ("w", 6), 2),
    ("s", ("w", 5), 3),
    ("s", ("w", 4), 4),
    ("s", ("w", 10), 2),
    ("s", ("w", 6), 3),
    ("s", ("w", 5), 4),
    ("r", 1),
    ("s", ("w", 10), 3),
    ("s", ("w", 6), 4),
    ("r", 1),
    ("s", ("w", 10), 4),
    ("r", 1),
    ("s", ("w", 9), 5),
    ("s", ("g", 0), 5),
    ("s", ("w", 4), 5),
    ("s", ("w", 5), 5),
    ("s", ("w", 6), 5),
    ("s", ("w", 10), 5),
)


def split_plan():
    before, loop, after = [], {(n, m): [] for n in range(10) for m in range(3)}, []
    place = before
    for op in PLAN:
        mark = op[1] if op[0] == "c" else ""
        if mark in ("H", "G3"):
            place = after
        elif mark[:1] == "E":
            place = loop[2 * int(mark[1]) + int(mark[3]), 0]
        elif mark[:1] == "F":
            place = loop[2 * int(mark[1]) + 3, 1]
        elif mark[:1] == "G":
            place = loop[2 * int(mark[1]) + 5, 2]
        if mark[:1] not in ("E", "F", "G") or mark == "G3":
            place.append(op)
    return before, loop, after


def rope(values, cosine, sine):
    lane = lax.broadcasted_iota(jnp.int32, (1, 128), 1)
    turned = jnp.where(lax.rem(lane, 64) < 32, -pltpu.roll(values, 96, 1), pltpu.roll(values, 32, 1))
    return values * cosine + turned * sine


def front_kernel(
    attn_h, ffn_h, qkv_h, out_h, in_h, down_h, tok_f, cot_f, starts_f, inverse,
    qkv_o, out_o, cot_o, tok_o, mid_o, gn_o, ffn_o, q_o, k_o, v_o, mix_o, bias_o, xt_o, mt_o, nt_o, glc_o, gj_o, at_o,
    gains_o, cos_o, sin_o, lse_o,
    gains_v, qkv_v, out_v, in_v, down_v, tok_v, starts_v, acc_f, acc_g, gl, normed, x2, q, k, v, mix, bias,
    gains_h, starts_h, tok_h, cot_h, gj, act, mine, theirs, rows_b,
    ss, rs, ssi, rsi, ls, lsi, es, er, el, ds_, dr, kvs, kvr, ws, ts, tr, tl, gs_, gr_, gw, as_, ar_, aw,
):
    h = Here()
    rows = Rows(h.z, h.f, h.core)
    z, f, core = h.z, h.f, h.core
    fx, fy, fc = h.fx, h.fy, h.fc
    fd = fx + 4 - 8 * h.y
    sib = (z, fc)
    half, wide = normed.shape
    block = half // 2
    own_rows, sib_rows = pl.ds(0, half), pl.ds(half, half)

    shards = (gains_h, qkv_h, out_h, down_h)
    wholes = (gains_v, qkv_v, out_v, down_v)
    targets = (fx, fy, fc, fy, fx, fc, fc, fc, fc)

    def part(w, i, cols=None):
        whole = wholes[w]
        if w < 3:
            return whole.at[i] if cols is None else whole.at[i, :, cols]
        r = pl.ds(pl.multiple_of(i * SHARD, 16), SHARD)
        return whole.at[r] if cols is None else whole.at[r, cols]

    def copy(w, k):
        a, b = halves(shards[w].shape[1])
        place = {3: (fx, a), 4: (fy, b), 5: (fx,), 6: (fy,), 7: (fd, a), 8: (fd, b)}
        dst = part(w, f) if k < 3 else part(w, *place[k])
        return remote(shards[w] if k < 3 else dst, dst, ss.at[w, k], rs.at[w, k], (z, targets[k]))

    quarter = pl.ds(pl.multiple_of(z * 32, 32), 32)

    def place_in(t, i, *more):
        return in_v.at[(t, i // 2, lax.rem(i, 2)) + more]

    def copy_in(t, k):
        cols = lanes(t * GROUP, GROUP)
        if t in BY_Z:
            if k in (0, 1):
                return remote(in_h.at[:, quarter, cols], place_in(t, f, slice(None), quarter), ssi.at[t, k], rsi.at[t, k], (z, targets[k]))
            if k in (3, 4):
                dst = place_in(t, (fx, fy)[k - 3], k - 3, quarter)
                return remote(dst, dst, ssi.at[t, k], rsi.at[t, k], (z, targets[k]))
            if k < 8:
                dst = in_v.at[t, :, core, :, quarter]
                return remote(dst, dst, ssi.at[t, k], rsi.at[t, k], (lax.rem(z + k - 4, 4), f))
            dst = in_v.at[t, :, core]
            return remote(dst, dst, ssi.at[t, k], rsi.at[t, k], sib)
        place = {3: (fx, 0), 4: (fy, 1), 5: (fx,), 6: (fy,), 7: (fd, 0), 8: (fd, 1)}
        dst = place_in(t, f) if k < 3 else place_in(t, *place[k])
        return remote(in_h.at[:, :, cols] if k < 3 else dst, dst, ssi.at[t, k], rsi.at[t, k], (z, targets[k]))

    def quarters(t, stage):
        waits, starts = (((), (0, 1)), ((0, 1), (3, 4)), ((3, 4), (5, 6, 7)), ((5, 6, 7), (8,)), ((8,), ()))[stage]
        for k in waits:
            copy_in(t, k).wait_recv()
        if stage == 2:
            own_in(t).wait()
        for k in starts:
            copy_in(t, k).start()

    def first(w, copy=copy):
        for k in range(3):
            copy(w, k).start()

    def second(w, copy=copy):
        for k in (0, 1):
            copy(w, k).wait_recv()
            copy(w, k + 3).start()
            copy(w, k + 5).start()

    def third(w, copy=copy):
        for k in (3, 4):
            copy(w, k).wait_recv()
            copy(w, k + 4).start()

    def rest(w, copy=copy):
        for k in (2, 5, 6, 7, 8):
            copy(w, k).wait_recv()

    def own(w):
        return pltpu.make_async_copy(shards[w], part(w, f), ls.at[w])

    def own_in(t):
        cols = lanes(t * GROUP, GROUP)
        if t in BY_Z:
            return pltpu.make_async_copy(in_h.at[:, quarter, cols], place_in(t, f, slice(None), quarter), lsi.at[t])
        return pltpu.make_async_copy(in_h.at[:, :, cols], place_in(t, f), lsi.at[t])

    wide_in = [
        [pltpu.make_async_copy(src.at[i], ref.at[pl.ds(i * block, block)], el.at[i]) for i in range(2)]
        for src, ref in ((tok_f, acc_f), (cot_f, acc_g))
    ]
    for c in wide_in[0]:
        c.start()
    gains_h[:, :128] = jnp.broadcast_to(attn_h[...].astype(F32), (16, 128)).astype(BF)
    gains_h[:, 128:] = jnp.broadcast_to(ffn_h[...].astype(F32), (16, 128)).astype(BF)
    starts_h[...] = jnp.zeros(starts_h.shape, jnp.int32)
    starts_h[:2, :8] = starts_f[...]
    for c in wide_in[0]:
        c.wait()
    tok_h[...] = acc_f[...].astype(BF)
    for c in wide_in[1]:
        c.start()
    for w in range(4):
        own(w).start()
    for t in range(STEPS):
        own_in(t).start()
    h.greet(pltpu.get_barrier_semaphore(), rows, 3)
    info = remote(starts_h, starts_v.at[core], ds_.at[0], dr.at[0], sib)
    own_info = pltpu.make_async_copy(starts_h, starts_v.at[core], el.at[2])
    info.start()
    own_info.start()
    rows.start(Halves(tok_h), tok_v, es.at[0], er.at[0], el.at[3], True)
    for t in BY_Z:
        quarters(t, 0)
    for w in range(3):
        first(w)
    for c in wide_in[1]:
        c.wait()
    cot_h[...] = acc_g[...].astype(BF)
    info.wait()
    own_info.wait()

    lane = lax.broadcasted_iota(jnp.int32, (1, 128), 1)
    begins = starts_v[lax.rem(z, 2), pl.ds(z // 2, 1), :]
    inside = lane < 8

    def documents(base):
        place = lax.broadcasted_iota(jnp.int32, (half, 128), 0) + base
        before = (begins <= place) & inside
        number = jnp.sum(jnp.where(before, 1.0, 0.0), axis=1, keepdims=True)
        begin = jnp.max(jnp.where(before, begins, 0).astype(F32), axis=1, keepdims=True)
        return place, number, begin

    place, number, begin = documents(core * half)
    angle = (place.astype(F32) - begin) * inverse[...]
    cos_o[...] = jnp.cos(angle)
    sin_o[...] = jnp.sin(angle)
    across = jnp.broadcast_to(number, (half, 128)).T[0:1, :]
    _, other, _ = documents((1 - core) * half)
    bias[:half] = jnp.where(number == across, 0.0, MASKED_SCORE).astype(BF)
    bias[half:] = jnp.where(other == across, 0.0, MASKED_SCORE).astype(BF)

    for t in BY_Z:
        quarters(t, 1)
    for w in range(3):
        second(w)
    rows.start(Halves(cot_h), cot_o, es.at[1], er.at[1], el.at[4], True)
    first(3)
    first(0, copy_in)
    first(1, copy_in)
    for t in BY_Z:
        quarters(t, 2)
    third(0)
    rest(0)
    own(0).wait()
    for n in range(2):
        for i in range(8):
            gains_o[n : n + 1, i * 128 : i * 128 + 128] = gains_v[i, 0:1, n * 128 : n * 128 + 128].astype(F32)
    rows.wait(Halves(tok_h), tok_v, es.at[0], er.at[0], el.at[3], True)
    saved = []

    def save(src, dst):
        saved.append(pltpu.make_async_copy(src, dst, ws.at[len(saved)]))
        saved[-1].start()

    def share(src, dst, n, again):
        keep = pltpu.make_async_copy(mine, dst.at[:, own_rows], tl.at[n])
        give = remote(theirs, dst.at[:, sib_rows], ts.at[n], tr.at[n], sib)
        if again is not None:
            again[0].wait()
            again[1].wait_send()
        for i in range(4):
            mine[i * 128 : i * 128 + 128] = src[:, lanes((2 * i + core) * 128, 128)].T
            theirs[i * 128 : i * 128 + 128] = src[:, lanes((2 * i + 1 - core) * 128, 128)].T
        keep.start()
        give.start()
        return keep, give

    unit, _ = moments(tok_v[...].reshape(half, wide).astype(F32))
    normed[...] = (unit * gains_o[0:1]).astype(BF)
    save(tok_v, tok_o)
    save(bias, bias_o)
    shared = share(normed, nt_o, 0, None)
    third(1)
    rest(1)
    own(1).wait()
    save(qkv_v, qkv_o)

    def pair_send(n, i):
        ref = (k, v)[n]
        cols = pl.ds(i * 256, 256)
        return remote(ref.at[own_rows, cols], ref.at[sib_rows, cols], kvs.at[n, i], kvr.at[n, i], sib)

    for n, ref in ((1, k), (2, v), (0, q)):
        for i in range(4):
            product = nn(normed[...], qkv_v[:, :, n * wide + i * 256 : n * wide + i * 256 + 256].reshape(wide, 256))
            for j in range(2):
                cols = slice(i * 256 + j * 128, i * 256 + j * 128 + 128)
                value = product[:, j * 128 : j * 128 + 128]
                value = value if n == 2 else rope(value, cos_o[...], sin_o[...])
                ref[:half, cols] = value.astype(BF)
            if n:
                pair_send(n - 1, i).start()
    third(2)
    for n in range(2):
        for i in range(4):
            pair_send(n, i).wait()
    for ref, dst in ((q, q_o), (k, k_o), (v, v_o)):
        save(ref, dst)

    def attend(i, _):
        @pl.when(i == 4)
        def _():
            second(3)

        @pl.when(i == 6)
        def _():
            second(0, copy_in)

        cols = lanes(i * 128, 128)
        queries = q[:, cols] * jnp.asarray(0.125, BF)
        keys = k[:, cols]
        vt = v[:, cols].T
        outs = []
        for e in range(2):
            here = (lane < 64) if e == 0 else (lane >= 64)
            scores = nt(keys, jnp.where(here, queries, jnp.zeros_like(queries))) + bias[...].astype(F32)
            top = jnp.max(scores, axis=0, keepdims=True)
            p = jnp.exp(scores - top)
            total = jnp.sum(p, axis=0, keepdims=True)
            outs.append(nn(vt, p.astype(BF)) / total)
            lse_o[i, e : e + 1, :] = top + jnp.log(total)
        mix[:, cols] = jnp.concatenate([outs[0][:64], outs[1][64:]], axis=0).T.astype(BF)
        return 0

    lax.fori_loop(0, 8, attend, 0)
    second(1, copy_in)
    first(3, copy_in)
    first(5, copy_in)
    rest(2)
    own(2).wait()
    save(out_v, out_o)
    save(mix, mix_o)
    middle = tok_v[...].reshape(half, wide).astype(F32) + nn(mix[...], out_v[...].reshape(wide, wide))
    acc_f[...] = middle
    unit, _ = moments(middle)
    x2[...] = (unit * gains_o[1:2]).astype(BF)
    mid_save = pltpu.make_async_copy(acc_f, mid_o, ls.at[4])
    mid_save.start()
    third(3)
    third(0, copy_in)
    rows.wait(Halves(cot_h), cot_o, es.at[1], er.at[1], el.at[4], True)
    cot_load = [pltpu.make_async_copy(cot_o.at[i], gl.at[pl.ds(i * block, block)], el.at[i]) for i in range(2)]
    for c in cot_load:
        c.start()
    shared = share(x2, xt_o, 1, shared)
    shared = share(mix, mt_o, 2, shared)
    for c in cot_load:
        c.wait()
    glc_keep = pltpu.make_async_copy(gl.at[:, lanes(core * 512, 512)], glc_o.at[own_rows], tl.at[3])
    glc_give = remote(gl.at[:, lanes((1 - core) * 512, 512)], glc_o.at[sib_rows], ts.at[3], tr.at[3], sib)
    glc_keep.start()
    glc_give.start()
    mid_save.wait()
    quarters(2, 3)
    rest(3)
    own(3).wait()

    def stage_copies(t):
        s = lax.rem(t, 2)
        r = lanes(t * GROUP, GROUP)
        return [
            pltpu.make_async_copy(gj.at[s], gj_o.at[t, own_rows], gw.at[s]),
            pltpu.make_async_copy(act.at[s], at_o.at[r, own_rows], aw.at[s]),
        ], [
            remote(gj.at[s], gj_o.at[t, sib_rows], gs_.at[s], gr_.at[t], sib),
            remote(act.at[s], at_o.at[r, sib_rows], as_.at[s], ar_.at[t], sib),
        ]

    def feed(t, _):
        s = lax.rem(t, 2)

        def at_step(events):
            for n, todo in events.items():

                @pl.when(t == n)
                def _(todo=todo):
                    for act, *args in todo:
                        act(*args)

        at_step({
            1: [(second, 3, copy_in), (first, 6, copy_in)],
            2: [(second, 5, copy_in), (quarters, 4, 3)],
            3: [(second, 6, copy_in)],
        })

        def ready(n):
            if n in BY_Z:
                quarters(n, 4)
            else:
                rest(n, copy_in)
                own_in(n).wait()

        at_step({n: [(ready, n)] for n in range(STEPS)})
        w = jnp.concatenate([in_v[t, :, :, m].reshape(wide, GROUP) for m in range(2)], axis=1)
        wd = down_v[lanes(t * GROUP, GROUP)]
        joined = nn(x2[...], w)
        a, c = joined[:, :GROUP], joined[:, GROUP:]
        grad_active = nt(gl[...], wd)
        phi = 0.5 * (1.0 + lax.erf(a * SQRT_HALF))
        gate = a * phi
        slope = phi + a * (jnp.exp(-0.5 * a * a) * DENSITY)
        active = (gate * c).astype(BF)
        ga = (slope * c * grad_active).astype(BF)
        gc = (gate * grad_active).astype(BF)

        @pl.when(t >= 2)
        def _():
            keep, give = stage_copies(t - 2)
            for copied in keep:
                copied.wait()
            for sent in give:
                sent.wait_send()

        gj[s, :, :GROUP] = ga
        gj[s, :, GROUP:] = gc
        act[s] = active.T
        keep, give = stage_copies(t)
        for started in keep + give:
            started.start()

        at_step({n: [(third, m, copy_in)] for n, m in ((0, 1), (2, 3), (3, 5), (4, 6))})
        acc_f[...] += nn(active, wd)
        back = nt(gj[s], w)

        @pl.when(t == 0)
        def _():
            acc_g[...] = back

        @pl.when(t > 0)
        def _():
            acc_g[...] += back

        return 0

    lax.fori_loop(0, STEPS, feed, 0)
    rows_b[...] = acc_f[...].astype(BF).reshape(2, block, wide)
    save(rows_b, ffn_o)
    save(acc_g, gn_o)
    for t in (STEPS - 2, STEPS - 1):
        keep, give = stage_copies(t)
        for copied in keep:
            copied.wait()
        for sent in give:
            sent.wait_send()
    for t in range(STEPS):
        for received in stage_copies(t)[1]:
            received.wait_recv()
    shared[0].wait()
    shared[1].wait_send()
    for n, dst in enumerate((nt_o, xt_o, mt_o)):
        remote(theirs, dst.at[:, sib_rows], ts.at[n], tr.at[n], sib).wait_recv()
    glc_keep.wait()
    glc_give.wait()
    for w in range(4):
        for kind in range(9):
            copy(w, kind).wait_send()
    for t in range(STEPS):
        for kind in range(9):
            if t not in BY_Z or kind != 2:
                copy_in(t, kind).wait_send()
    for c in saved:
        c.wait()


def front_all(attn_gain, ffn_gain, qkv, out, inw, down, tok, cot, starts, inverse):
    dma = pltpu.SemaphoreType.DMA
    block, wide = tok.shape[1:]
    half, hidden = 2 * block, STEPS * GROUP

    def shape(*s, kind=BF):
        return jax.ShapeDtypeStruct(s, kind)

    def buf(*s, kind=BF):
        return pltpu.VMEM(s, kind)

    whole = pl.BlockSpec(memory_space=pltpu.VMEM)
    return pl.pallas_call(
        front_kernel,
        out_shape=[
            shape(8, *qkv.shape), shape(8, *out.shape), shape(*cot.shape), shape(*tok.shape),
            shape(half, wide, kind=F32), shape(half, wide, kind=F32), shape(2, block, wide),
            shape(half, wide), shape(2 * half, wide), shape(2 * half, wide), shape(half, wide), shape(2 * half, half),
            shape(half, 2 * half), shape(half, 2 * half), shape(half, 2 * half), shape(2 * half, half),
            shape(STEPS, 2 * half, 2 * GROUP), shape(hidden, 2 * half),
            shape(2, wide, kind=F32), shape(half, 128, kind=F32), shape(half, 128, kind=F32), shape(8, 2, half, kind=F32),
        ],
        in_specs=[whole] * 2 + [ANY] * 6 + [whole] * 2,
        out_specs=[ANY] * 18 + [whole] * 4,
        scratch_shapes=[
            buf(8, 16, 256), buf(8, *qkv.shape), buf(8, *out.shape), buf(STEPS, 4, 2, 2, 128, GROUP), buf(hidden, wide),
            buf(*tok.shape), buf(2, 8, 128, kind=jnp.int32), buf(half, wide, kind=F32), buf(half, wide, kind=F32),
            buf(half, wide), buf(half, wide), buf(half, wide), buf(half, wide), buf(2 * half, wide), buf(2 * half, wide),
            buf(half, wide), buf(2 * half, half),
            buf(16, 256), buf(8, 128, kind=jnp.int32), buf(half, wide), buf(half, wide),
            buf(2, half, 2 * GROUP), buf(2, GROUP, half), buf(half, half), buf(half, half), buf(2, block, wide),
            dma((4, 9)), dma((4, 9)), dma((STEPS, 9)), dma((STEPS, 9)), dma((5,)), dma((STEPS,)),
            dma((2, 2)), dma((2, 2)), dma((5,)), dma((1,)), dma((1,)), dma((2, 4)), dma((2, 4)), dma((10,)),
            dma((4,)), dma((4,)), dma((4,)), dma((2,)), dma((STEPS,)), dma((2,)), dma((2,)), dma((STEPS,)), dma((2,)),
        ],
        compiler_params=pltpu.CompilerParams(collective_id=1, has_side_effects=True, vmem_limit_bytes=VMEM_BYTES),
        name="gather_attention_feed_forward",
    )(attn_gain, ffn_gain, qkv, out, inw, down, tok, cot, starts, inverse)


def back_kernel(
    ffn_h, mid_h, gn_h, cot_h, qkv_h, out_h, q_h, k_h, v_h, mix_h, rows_h, bias_h, xt_h, mt_h, nt_h, glc_h, gj_h, at_h,
    gains, cosine, sine, lse,
    in_o, qkv_o, down_o, out_o, gain_o, outh_o, inh_o,
    acc_f, acc_g, win, xt, mt, gj, gq, at, glc, gm, dout, q, k, v, bias, kept, dx_kv, kvl, centres, terms, gs, gr,
    ld, gld, wsem, ps, pr, kvs, kvr, gqs, gqr, dxs, dxr, fo, es, er, el,
    *sum_refs,
):
    h = Here()
    rows = Rows(h.z, h.f, h.core)
    order = [op[1][1] for op in PLAN if op[0] in "fb" and op[1][0] == "w"]
    wide = Sums(h, sum_refs[0:7], {t: n % WIDE_SLOTS for n, t in enumerate(order)})
    down = Sums(h, sum_refs[7:14], {0: 0, 1: 1})
    outs = Sums(h, sum_refs[14:21], {0: 0})
    gain = Sums(h, sum_refs[21:28], {0: 0})
    groups = {"w": wide, "d": down, "o": outs, "g": gain}
    sib = (h.z, h.fc)
    half, width = dout.shape
    block = half // 2
    own_rows, sib_rows = pl.ds(0, half), pl.ds(half, half)
    lane = lax.broadcasted_iota(jnp.int32, (1, 128), 1)

    def load(src, dst, n):
        return pltpu.make_async_copy(src, dst, ld.at[n])

    def gj_load(t):
        return pltpu.make_async_copy(gj_h.at[t], gj, gld.at[0])

    def qkv_weights(u):
        return [
            pltpu.make_async_copy(qkv_h.at[:, :, lanes(n * 1024 + u * 256, 256)], win.at[:, :, pl.ds(n * 256, 256)], wsem.at[n])
            for n in range(3)
        ]

    loads = {
        "xt": load(xt_h, xt, 0), "mid": load(mid_h, acc_f, 1), "gn": load(gn_h, acc_g, 2),
        "c0": load(cot_h.at[0], dout.at[pl.ds(0, block)], 3), "c1": load(cot_h.at[1], dout.at[pl.ds(block, block)], 4),
        "w": load(out_h, k, 5), "mix": load(mix_h, v.at[own_rows], 6), "mt": load(mt_h, mt, 7),
        "at": load(at_h, at, 8), "glc": load(glc_h, glc, 9), "bias": load(bias_h, bias, 10), "q": load(q_h, q, 11),
        "nt": load(nt_h, mt, 7), "k": load(k_h, k, 5), "v": load(v_h, v, 6),
        "r0": load(rows_h.at[0], k.at[pl.ds(0, block)], 3), "r1": load(rows_h.at[1], k.at[pl.ds(block, block)], 4),
    }

    def start(*names):
        for name in names:
            loads[name].start()

    def wait(*names):
        for name in names:
            loads[name].wait()

    start("xt")
    gj_load(0).start()
    start("mid", "gn", "c0", "c1")
    start("w", "mix", "at", "glc", "mt", "bias", "q")
    h.greet(pltpu.get_barrier_semaphore(), rows)

    def put(group, t, term, cut):
        s = group.slot[t]
        term = term.astype(BF)
        for o in range(4):
            for n in range(2):
                group.acc[s, n, o // 2, o % 2] = term[o * 128 : o * 128 + 128, n * cut : n * cut + cut]

    def in_term(t):
        if t == 0:
            wait("xt")
        gj_load(t).wait()
        put(wide, t, nn(xt[...], gj[...]), GROUP)
        if t + 1 < STEPS:
            gj_load(t + 1).start()

    def down_term(j):
        if j == DOWN_FIRST:
            wait("at", "glc")
        term = nn(at[...], glc[:, j * 256 : j * 256 + 256])
        for f in range(8):
            down.acc[j, f % 2, f // 4, f // 2 % 2] = term[f * SHARD : f * SHARD + SHARD].astype(BF)

    gm_send = remote(gm.at[own_rows], gm.at[sib_rows], ps.at[0], pr.at[0], sib)

    def second_norm():
        wait("mid", "gn", "c0", "c1")
        back, terms[1:2] = norm_back(acc_f[...], gains[1:2], acc_g[...])
        grad_mid = dout[...].astype(F32) + back
        acc_f[...] = grad_mid
        gm[:half] = grad_mid.astype(BF)
        gm_send.start()

    def mixture_grads():
        wait("w", "mix")
        dout[...] = nt(gm[:half], k[...]).astype(BF)
        start("k")
        for j in range(8):
            cols = slice(j * 128, j * 128 + 128)
            products = (v[:half, cols].astype(F32) * dout[:, cols].astype(F32)).T
            for e in range(2):
                centres[j, e : e + 1] = jnp.sum(products[64 * e : 64 * e + 64], axis=0, keepdims=True)
        start("v")

    def out_term():
        wait("mt")
        gm_send.wait()
        put(outs, 0, nn(mt[...], gm[...]), 512)
        start("nt")

    def kv_rows(s):
        return pl.ds(s * half if isinstance(s, int) else pl.multiple_of(s * half, half), half)

    def kv_send(u):
        s = lax.rem(u, 2)
        return remote(dx_kv, kvl.at[s], kvs.at[s], kvr.at[s], sib)

    def gq_send(u):
        s = lax.rem(u, 2)
        return remote(gq.at[s, own_rows], gq.at[s, sib_rows], gqs.at[s], gqr.at[s], sib)

    def stashed(b, n, j):
        return jnp.concatenate([kept[b, pl.ds(n * 128, 128), pl.ds(m * 256 + j * 128, 128)] for m in range(4)], axis=0)

    def heads_back(p):
        u, j = p // 2, lax.rem(p, 2)
        s = lax.rem(u, 2)
        col = lanes(p * 128, 128)
        queries = q[:, col] * jnp.asarray(0.125, BF)
        keys, values, do = k[:, col], v[:, col], dout[:, col]
        kt = keys.T
        none = jnp.zeros_like(queries)
        dqs, dks, dvs = [], [], []
        for e in range(2):
            part = (lane < 64) if e == 0 else (lane >= 64)
            prob = jnp.exp(nt(keys, jnp.where(part, queries, none)) + bias[...].astype(F32) - lse[p, e : e + 1, :])
            dvs.append(nn(prob.astype(BF), do))
            ds = (prob * (nt(values, jnp.where(part, do, none)) - centres[p, e : e + 1, :])).astype(BF)
            dks.append(nn(ds, queries))
            dqs.append(nn(kt, ds))
        dq = jnp.concatenate([dqs[0][:64], dqs[1][64:]], axis=0).T
        dk = jnp.where(lane < 64, dks[0], dks[1]).astype(BF)
        dv = jnp.where(lane < 64, dvs[0], dvs[1]).astype(BF)
        for n, part in enumerate(((dq * 0.125).astype(BF), dk, dv)):
            for m in range(4):
                kept[s, pl.ds(n * 128, 128), lanes(m * 256 + j * 128, 128)] = part[m * 128 : m * 128 + 128]

        @pl.when((j == 0) & (u >= 1))
        def _():
            kv_send(u - 1).wait_send()

        dx_kv[:, lanes(j * 128, 128)] = dk[half:]
        dx_kv[:, lanes(256 + j * 128, 128)] = dv[half:]

    def heads_close(u):
        b = lax.rem(u, 2)

        @pl.when(u >= 2)
        def _():
            gq_send(u - 2).wait_send()

        kv_send(u).wait_recv()
        for j in range(2):
            c = slice(j * 128, j * 128 + 128)
            gq[b, :half, c] = rope_back(stashed(b, 0, j).astype(F32), cosine[...], sine[...]).astype(BF)
            g = added(stashed(b, 1, j), kvl[b, :, c]).astype(F32)
            gq[b, :half, 256 + j * 128 : 384 + j * 128] = rope_back(g, cosine[...], sine[...]).astype(BF)
            gq[b, :half, 512 + j * 128 : 640 + j * 128] = added(stashed(b, 2, j), kvl[b, :, 256 + j * 128 : 384 + j * 128])
        for c in qkv_weights(u):
            c.wait()
        back = nt(gq[b, :half], win[...].reshape(width, 768))

        @pl.when(u == 0)
        def _():
            acc_g[...] = back

        @pl.when(u > 0)
        def _():
            acc_g[...] += back

        @pl.when(u < 3)
        def _():
            for c in qkv_weights(u + 1):
                c.start()

    def qkv_term(u):
        gq_send(u).wait_recv()
        put(wide, STEPS + u, nn(mt[...], gq[u % 2]), GROUP)

    def first_norm():
        wait("r0", "r1")
        back, terms[0:1] = norm_back(k[:half].astype(F32), gains[0:1], acc_g[...])
        dout[...] = (acc_f[...] + back).astype(BF)

    gs_send = remote(gs, gr, ps.at[1], pr.at[1], sib)

    def gain_terms():
        for n in range(2):
            for o in range(4):
                for ref, part in ((gain.acc.at[0], h.core), (gs, 1 - h.core)):
                    low, high = terms[n : n + 1, 256 * o : 256 * o + 128], terms[n : n + 1, 256 * o + 128 : 256 * o + 256]
                    value = jnp.where(part == 0, low, high)
                    ref[n, o // 2, o % 2] = jnp.broadcast_to(value, (16, 128)).astype(BF)
        gs_send.start()
        gs_send.wait()
        for n in range(2):
            for o in range(4):
                gain.acc[0, n, o // 2, o % 2] = added(gain.acc[0, n, o // 2, o % 2], gr[n, o // 2, o % 2])

    def dx(j):
        return kvl.at[j, pl.ds(0, SHARD), pl.ds(0, 256)]

    def down_swap(j, act, ref):
        act(remote(ref.at[j, 1 - h.core], dx(j), dxs.at[j], dxr.at[j], sib))

    def to_end(j):
        return pltpu.make_async_copy(dx(j), down_o.at[:, lanes((1 - h.core) * 512 + j * 256, 256)], fo.at[2, 5 + j])

    def write(name, t, act, ref):
        if name == "w" and t < STEPS:
            for n in range(2):
                act(pltpu.make_async_copy(ref.at[t, n], in_o.at[n, :, pl.ds(t * GROUP, GROUP)], fo.at[0, 2 * t + n]))
        elif name == "w":
            parts = ((0, 0, 256, 0), (0, 256, 128, 1024), (1, 0, 128, 1152), (1, 128, 256, 2048))
            for n, (m, at_col, size, to) in enumerate(parts):
                dst = qkv_o.at[:, pl.ds(to + (t - STEPS) * 256, size)]
                act(pltpu.make_async_copy(ref.at[t, m, :, pl.ds(at_col, size)], dst, fo.at[1, 4 * (t - STEPS) + n]))
        elif name == "d":
            dst = down_o.at[:, lanes(h.core * 512 + t * 256, 256)]
            act(pltpu.make_async_copy(ref.at[t, h.core], dst, fo.at[2, 3 + t]))
        elif name == "o":
            for n in range(2):
                act(pltpu.make_async_copy(ref.at[0, n], out_o.at[:, pl.ds(n * 512, 512)], fo.at[2, n]))
        else:
            act(pltpu.make_async_copy(ref, gain_o, fo.at[2, 2]))

    sent = [0, 0]

    def piece(which):
        size = block // PIECES
        part = pl.ds(sent[which] * size, size)
        sent[which] += 1
        if which == 0:
            rows.start(ffn_h, outh_o, es.at[0], er.at[0], el.at[0], False, part)
        else:
            rows.start(Halves(dout), inh_o, es.at[1], er.at[1], el.at[1], False, part)

    work = {"ln2": second_norm, "do": mixture_grads, "og": out_term, "H": first_norm, "gains": gain_terms}

    def perform(ops):
        for op in ops:
            if op[0] == "c":
                if op[1] in work:
                    work[op[1]]()
            elif op[0] == "r":
                piece(op[1])
            else:
                (name, t), group = op[1], groups[op[1][0]]
                if op[0] == "s":
                    getattr(group, Sums.LATER[op[2]])(t)
                    if op[2] == 5:
                        group.total(functools.partial(write, name, t, lambda c: c.start()))
                        if name == "d":
                            down.total(functools.partial(down_swap, t, lambda c: c.start()))
                else:
                    if name == "w":
                        in_term(t) if t < STEPS else qkv_term(t - STEPS)
                    elif name == "d":
                        down_term(t)
                    group.begin(t)

    before, loop, after = split_plan()
    perform(before)
    wait("bias", "q", "k", "v", "nt")
    for c in qkv_weights(0):
        c.start()

    def each(p, _):
        pl.when(p < 8)(lambda: heads_back(p))
        pl.when(p == 8)(lambda: start("r0", "r1"))
        for n in range(10):
            if loop[n, 0]:
                pl.when(p == n)(functools.partial(perform, loop[n, 0]))

        @pl.when((lax.rem(p, 2) == 1) & (p >= 3))
        def _():
            heads_close((p - 3) // 2)

        for n in range(10):
            if loop[n, 1]:
                pl.when(p == n)(functools.partial(perform, loop[n, 1]))
            if loop[n, 2]:
                pl.when(p == n)(functools.partial(perform, loop[n, 2]))

        @pl.when((lax.rem(p, 2) == 1) & (p < 8))
        def _():
            kv_send(p // 2).start()

        @pl.when((lax.rem(p, 2) == 1) & (p >= 3))
        def _():
            gq_send((p - 3) // 2).start()

        return 0

    lax.fori_loop(0, 10, each, 0)
    perform(after)
    for j in range(2):
        down.total(functools.partial(down_swap, j, lambda c: c.wait()))
        to_end(j).start()
    kv_send(3).wait_send()
    gq_send(2).wait_send()
    gq_send(3).wait_send()

    for name, group in groups.items():
        for t in group.slot:
            group.total(functools.partial(write, name, t, lambda c: c.wait()))
    for j in range(2):
        to_end(j).wait()
    rows.wait(ffn_h, outh_o, es.at[0], er.at[0], el.at[0], False)
    rows.wait(Halves(dout), inh_o, es.at[1], er.at[1], el.at[1], False)


def back_all(ffn_rows, *args):
    dma = pltpu.SemaphoreType.DMA
    block, wide = ffn_rows.shape[1:]
    half = 2 * block

    def buf(*s, kind=BF):
        return pltpu.VMEM(s, kind)

    def shape(*s):
        return jax.ShapeDtypeStruct(s, BF)

    whole = pl.BlockSpec(memory_space=pltpu.VMEM)
    scratch = [
        buf(half, wide, kind=F32), buf(half, wide, kind=F32), buf(8, 128, 768),
        buf(half, 2 * half), buf(half, 2 * half), buf(2 * half, 768), buf(2, 2 * half, 768),
        buf(STEPS * GROUP, 2 * half), buf(2 * half, half), buf(2 * half, wide), buf(half, wide),
        buf(half, wide), buf(2 * half, wide), buf(2 * half, wide), buf(2 * half, half),
        buf(2, GROUP, wide), buf(half, 512), buf(2, half, 512), buf(8, 2, half, kind=F32), buf(2, wide, kind=F32),
        buf(2, 2, 2, 16, 128), buf(2, 2, 2, 16, 128),
        dma((13,)), dma((1,)), dma((3,)), dma((2,)), dma((2,)), dma((2,)), dma((2,)), dma((2,)), dma((2,)),
        dma((2,)), dma((2,)), dma((3, 16)), dma((2, 2)), dma((2, 2)), dma((2,)),
    ]
    for s in ((11, WIDE_SLOTS, 128, GROUP), (2, 2, SHARD, 256), (1, 1, 128, 512), (1, 1, 16, 128)):
        scratch += Sums.scratch(*s)
    return pl.pallas_call(
        back_kernel,
        out_shape=[
            shape(2, 128, STEPS * GROUP), shape(128, 3 * wide), shape(SHARD, wide), shape(128, wide), shape(1, 2, 16, 128),
            shape(2, block, wide), shape(2, block, wide),
        ],
        in_specs=[ANY] * 18 + [whole] * 4,
        out_specs=[ANY] * 7,
        scratch_shapes=scratch,
        compiler_params=pltpu.CompilerParams(collective_id=2, has_side_effects=True, vmem_limit_bytes=VMEM_BYTES),
        name="backward_and_sums",
    )(ffn_rows, *args)


def chip_streams(tokens, cotangent, doc_starts, qkv_weight, out_weight, in_weight, down_weight, attn_gain, ffn_gain):
    wide = tokens.shape[3]
    shard = down_weight.shape[0]
    spare = jnp.zeros((in_weight.shape[0], SHARD - shard), BF)
    pieces = [in_weight[:, n * shard : (n + 1) * shard] for n in range(16)]
    in_parts = jnp.stack([jnp.concatenate([p for n in range(8) for p in (pieces[8 * m + n], spare)], axis=1) for m in range(2)])
    down_rows = jnp.pad(down_weight, ((0, SHARD - shard), (0, 0)))
    inverse = ROPE_THETA ** (-jnp.arange(0, HEAD_DIM, 2, dtype=F32) / HEAD_DIM)
    (qkv_f, out_f, cot, rows_low, middle, gn, ffn_rows, q, k, v, mixture, bias, xt, mt, nt_rows, glc, gj, at,
     both_gains, cosine, sine, lse) = front_all(
        attn_gain[None], ffn_gain[None], qkv_weight, out_weight, in_parts, down_rows,
        tokens[:, 0], cotangent[:, 0], doc_starts[:, 0], jnp.tile(inverse, 4)[None],
    )
    in_t, qkv_t, down_t, out_t, gain_t, out_home, in_home = back_all(
        ffn_rows, middle, gn, cot, qkv_f, out_f.reshape(wide, wide), q, k, v, mixture, rows_low, bias, xt, mt, nt_rows, glc, gj, at,
        both_gains, cosine, sine, lse,
    )
    in_cols = [in_t[m, :, n * SHARD : n * SHARD + shard] for m in range(2) for n in range(8)]
    return (
        out_home[:, None].astype(F32),
        in_home[:, None].astype(F32),
        qkv_t.astype(F32),
        out_t.astype(F32),
        jnp.concatenate(in_cols, axis=1).astype(F32),
        down_t[:shard].astype(F32),
        gain_t[0, 0, 0].astype(F32),
        gain_t[0, 1, 0].astype(F32),
    )


def solution(mesh):
    whole_chips = dict(mesh.shape) == {"seq": 4, "fsdp": 8}
    return jax.shard_map(
        chip_streams if whole_chips else shards,
        mesh=mesh,
        in_specs=(
            P(None, "fsdp", "seq", None),
            P(None, "fsdp", "seq", None),
            P(None, "fsdp", None),
            P("fsdp", None),
            P("fsdp", None),
            P("fsdp", None),
            P("fsdp", None),
            P("fsdp"),
            P("fsdp"),
        ),
        out_specs=(
            P(None, "fsdp", "seq", None),
            P(None, "fsdp", "seq", None),
            P("fsdp", None),
            P("fsdp", None),
            P("fsdp", None),
            P("fsdp", None),
            P("fsdp"),
            P("fsdp"),
        ),
        check_vma=False,
    )
```

```python
import functools
from functools import partial

import jax
import jax.numpy as jnp
import numpy as np
from jax import lax
from jax.experimental import pallas as pl
from jax.experimental.pallas import tpu as pltpu
from jax.sharding import PartitionSpec as P

HEADS = 16
HEAD_DIM = 64


EPSILON = 1e-05
ROPE_THETA = 160000.0
MASKED_SCORE = -1e30


def as_sent(x):

    def short(part):
        return part.astype(jnp.bfloat16) if part.dtype == jnp.float32 else part

    return jax.tree.map(short, x)


def layer_norm(values, norm_gain):
    average = jnp.mean(values, axis=-1, keepdims=True)
    centred = values - average
    spread = jnp.mean(centred * centred, axis=-1, keepdims=True)
    return centred * lax.rsqrt(spread + EPSILON) * norm_gain


def gated_gelu(joined):
    half_width = joined.shape[-1] // 2
    return jax.nn.gelu(joined[:, :half_width], approximate=False) * joined[:, half_width:]


def rotate(values, cosine_table, sine_table):
    half_width = values.shape[-1] // 2
    turned = jnp.concatenate([-values[..., half_width:], values[..., :half_width]], axis=-1)
    return values * cosine_table + turned * sine_table


def rope_tables(starts, places, head_width):
    preceding = starts[None, :] <= places[:, None]
    doc_begin = jnp.max(jnp.where(preceding, starts[None, :], 0), axis=-1)
    offsets = (places - doc_begin).astype(jnp.float32)
    inverse = ROPE_THETA ** (-jnp.arange(0, head_width, 2, dtype=jnp.float32) / head_width)
    angles = offsets[:, None] * inverse[None, :]
    angles = jnp.concatenate([angles, angles], axis=-1)
    return (jnp.cos(angles), jnp.sin(angles))


def segment_ids(starts, places):
    return jnp.sum((starts[None, :] <= places[:, None]).astype(jnp.int32), axis=-1) - 1


def turn_pair(pair, cosine_table, sine_table):
    shaped = pair.reshape(pair.shape[0], 2, HEADS, HEAD_DIM)
    turned = rotate(shaped, cosine_table[:, None, None, :], sine_table[:, None, None, :])
    return turned.reshape(pair.shape[0], 2 * HEADS * HEAD_DIM)


def attend_forward(queries, keys_in, values_in, segments, head_count):
    length = queries.shape[0]
    head_width = queries.shape[1] // head_count
    block_rows = min(512, length)
    blocks = length // block_rows
    keyset = keys_in.reshape(length, head_count, head_width)
    valueset = values_in.reshape(length, head_count, head_width)
    factor = head_width ** (-0.5)

    def one_block(pieces):
        query_rows, block_segs = pieces
        scores = (
            jnp.einsum("qhd,khd->hqk", query_rows, keyset, preferred_element_type=jnp.float32)
            * factor
        )
        scores = jnp.where((block_segs[:, None] == segments[None, :])[None], scores, MASKED_SCORE)
        row_max = jnp.max(scores, axis=-1, keepdims=True)
        totals = jnp.sum(jnp.exp(scores - row_max), axis=-1, keepdims=True)
        logsums = row_max + jnp.log(totals)
        weights = jnp.exp(scores - logsums).astype(jnp.bfloat16)
        mixture = jnp.einsum("hqk,khd->qhd", weights, valueset, preferred_element_type=jnp.float32)
        return (mixture, logsums)

    mixture, logsums = lax.map(
        one_block,
        (
            queries.reshape(blocks, block_rows, head_count, head_width),
            segments.reshape(blocks, block_rows),
        ),
    )
    return (mixture.reshape(length, head_count * head_width), logsums)


def attend_backward(queries, keys_in, values_in, grads_in, segments, logsums, head_count):
    length = queries.shape[0]
    head_width = queries.shape[1] // head_count
    block_rows = min(512, length)
    blocks = length // block_rows
    keyset = keys_in.reshape(length, head_count, head_width)
    valueset = values_in.reshape(length, head_count, head_width)
    factor = head_width ** (-0.5)

    def one_block(carry, pieces):
        key_grad, value_grad = carry
        query_rows, block_segs, grad_rows, block_lse = pieces
        scores = (
            jnp.einsum("qhd,khd->hqk", query_rows, keyset, preferred_element_type=jnp.float32)
            * factor
        )
        scores = jnp.where((block_segs[:, None] == segments[None, :])[None], scores, MASKED_SCORE)
        weights = jnp.exp(scores - block_lse)
        value_grad = value_grad + jnp.einsum(
            "hqk,qhd->khd",
            weights.astype(jnp.bfloat16),
            grad_rows,
            preferred_element_type=jnp.float32,
        )
        grad_weights = jnp.einsum(
            "qhd,khd->hqk", grad_rows, valueset, preferred_element_type=jnp.float32
        )
        centre = jnp.sum(weights * grad_weights, axis=-1, keepdims=True)
        grad_scores = (weights * (grad_weights - centre)).astype(jnp.bfloat16)
        query_grad = (
            jnp.einsum("hqk,khd->qhd", grad_scores, keyset, preferred_element_type=jnp.float32)
            * factor
        )
        key_grad = (
            key_grad
            + jnp.einsum(
                "hqk,qhd->khd", grad_scores, query_rows, preferred_element_type=jnp.float32
            )
            * factor
        )
        return ((key_grad, value_grad), query_grad)

    empty = jnp.zeros((length, head_count, head_width), jnp.float32)
    pieces = (
        queries.reshape(blocks, block_rows, head_count, head_width),
        segments.reshape(blocks, block_rows),
        grads_in.reshape(blocks, block_rows, head_count, head_width),
        logsums,
    )
    (key_grad, value_grad), query_grad = lax.scan(one_block, (empty, empty), pieces)
    flat_shape = (length, head_count * head_width)
    return (
        query_grad.reshape(flat_shape).astype(jnp.bfloat16),
        key_grad.reshape(flat_shape).astype(jnp.bfloat16),
        value_grad.reshape(flat_shape).astype(jnp.bfloat16),
    )


def shards(
    tokens,
    cotangent,
    doc_starts,
    qkv_weight,
    out_weight,
    in_weight,
    down_weight,
    attn_gain,
    ffn_gain,
):
    micro_count = tokens.shape[0]
    token_rows = tokens.shape[2]
    model_width = tokens.shape[3]
    seq_count = lax.axis_size("seq")
    head_count = HEADS // seq_count
    places = lax.axis_index("seq") * token_rows + jnp.arange(token_rows, dtype=jnp.int32)
    everywhere = jnp.arange(token_rows * seq_count, dtype=jnp.int32)
    outputs = []
    input_grads = []
    full_terms = None
    shard_terms = None
    for micro_step in range(micro_count):
        rows_in = tokens[micro_step, 0]
        starts = doc_starts[micro_step, 0]
        cosine_table, sine_table = rope_tables(starts, places, HEAD_DIM)
        segments = segment_ids(starts, everywhere)
        attn_set = (
            lax.all_gather(qkv_weight, "fsdp", axis=0, tiled=True),
            lax.all_gather(out_weight, "fsdp", axis=0, tiled=True),
            lax.all_gather(attn_gain, "fsdp", axis=0, tiled=True),
        )
        qkv_full, out_full, gain_one = attn_set
        normed, norm_back = jax.vjp(layer_norm, rows_in, gain_one.astype(jnp.float32))
        normed_low = normed.astype(jnp.bfloat16)
        qkv_rows = jnp.dot(normed_low, qkv_full, preferred_element_type=jnp.float32)
        turned, turn_back = jax.vjp(
            partial(turn_pair, cosine_table=cosine_table, sine_table=sine_table),
            qkv_rows[:, : 2 * model_width],
        )
        queries = turned[:, :model_width].astype(jnp.bfloat16)
        keyset = turned[:, model_width:].astype(jnp.bfloat16)
        valueset = qkv_rows[:, 2 * model_width :].astype(jnp.bfloat16)
        query_heads, key_heads, value_heads = (
            lax.all_to_all(queries, "seq", split_axis=1, concat_axis=0, tiled=True),
            lax.all_to_all(keyset, "seq", split_axis=1, concat_axis=0, tiled=True),
            lax.all_to_all(valueset, "seq", split_axis=1, concat_axis=0, tiled=True),
        )
        mixture, logsums = attend_forward(query_heads, key_heads, value_heads, segments, head_count)
        mixture_rows = lax.all_to_all(
            mixture.astype(jnp.bfloat16), "seq", split_axis=0, concat_axis=1, tiled=True
        )
        middle = rows_in + jnp.dot(mixture_rows, out_full, preferred_element_type=jnp.float32)
        ffn_set = (
            lax.all_gather(in_weight, "fsdp", axis=0, tiled=True),
            lax.all_gather(down_weight, "fsdp", axis=0, tiled=True),
            lax.all_gather(ffn_gain, "fsdp", axis=0, tiled=True),
        )
        in_full, down_full, gain_two = ffn_set
        normed_two, norm_back_two = jax.vjp(layer_norm, middle, gain_two.astype(jnp.float32))
        normed_two_low = normed_two.astype(jnp.bfloat16)
        joined = jnp.dot(normed_two_low, in_full, preferred_element_type=jnp.float32)
        active, gelu_back = jax.vjp(gated_gelu, joined)
        active_low = active.astype(jnp.bfloat16)
        outputs.append(middle + jnp.dot(active_low, down_full, preferred_element_type=jnp.float32))
        grad_out = cotangent[micro_step, 0]
        grad_low = grad_out.astype(jnp.bfloat16)
        ffn_set = (
            lax.all_gather(in_weight, "fsdp", axis=0, tiled=True),
            lax.all_gather(down_weight, "fsdp", axis=0, tiled=True),
            lax.all_gather(ffn_gain, "fsdp", axis=0, tiled=True),
        )
        in_full, down_full, gain_two = ffn_set
        down_term = jnp.dot(active_low.T, grad_low, preferred_element_type=jnp.float32)
        grad_active = jnp.dot(grad_low, down_full.T, preferred_element_type=jnp.float32)
        grad_joined = gelu_back(grad_active)[0].astype(jnp.bfloat16)
        in_term = jnp.dot(normed_two_low.T, grad_joined, preferred_element_type=jnp.float32)
        grad_normed_two = jnp.dot(grad_joined, in_full.T, preferred_element_type=jnp.float32)
        grad_middle_norm, gain_two_term = norm_back_two(grad_normed_two)
        grad_middle = grad_out + grad_middle_norm
        grad_mid_low = grad_middle.astype(jnp.bfloat16)
        attn_set = (
            lax.all_gather(qkv_weight, "fsdp", axis=0, tiled=True),
            lax.all_gather(out_weight, "fsdp", axis=0, tiled=True),
            lax.all_gather(attn_gain, "fsdp", axis=0, tiled=True),
        )
        qkv_full, out_full, gain_one = attn_set
        out_term = jnp.dot(mixture_rows.T, grad_mid_low, preferred_element_type=jnp.float32)
        grad_mixture = jnp.dot(grad_mid_low, out_full.T, preferred_element_type=jnp.float32).astype(
            jnp.bfloat16
        )
        grad_heads = lax.all_to_all(grad_mixture, "seq", split_axis=1, concat_axis=0, tiled=True)
        query_grad, key_grad, value_grad = attend_backward(
            query_heads, key_heads, value_heads, grad_heads, segments, logsums, head_count
        )
        query_back, key_back, value_back = (
            lax.all_to_all(query_grad, "seq", split_axis=0, concat_axis=1, tiled=True),
            lax.all_to_all(key_grad, "seq", split_axis=0, concat_axis=1, tiled=True),
            lax.all_to_all(value_grad, "seq", split_axis=0, concat_axis=1, tiled=True),
        )
        grad_pair = turn_back(jnp.concatenate([query_back, key_back], axis=1).astype(jnp.float32))[
            0
        ]
        grad_qkv = jnp.concatenate([grad_pair, value_back.astype(jnp.float32)], axis=1).astype(
            jnp.bfloat16
        )
        qkv_term = jnp.dot(normed_low.T, grad_qkv, preferred_element_type=jnp.float32)
        grad_normed = jnp.dot(grad_qkv, qkv_full.T, preferred_element_type=jnp.float32)
        grad_rows_norm, gain_one_term = norm_back(grad_normed)
        input_grads.append(grad_middle + grad_rows_norm)
        terms = (qkv_term, out_term, in_term, down_term, gain_one_term, gain_two_term)
        full_terms = terms if full_terms is None else jax.tree.map(jnp.add, full_terms, terms)
    shard_terms = jax.tree.map(
        lambda part: part.astype(jnp.float32),
        lax.psum_scatter(as_sent(full_terms), "fsdp", scatter_dimension=0, tiled=True),
    )
    totals = jax.tree.map(
        lambda part: part.astype(jnp.float32), lax.psum(as_sent(shard_terms), "seq")
    )
    return (
        jnp.stack(outputs)[:, None],
        jnp.stack(input_grads)[:, None],
        totals[0],
        totals[1],
        totals[2],
        totals[3],
        totals[4],
        totals[5],
    )


MESH = pl.DeviceIdType.MESH
ANY = pl.BlockSpec(memory_space=pl.ANY)
VMEM_BYTES = 127 * 2**19
BF = jnp.bfloat16
F32 = jnp.float32


def nn(a, b):
    return lax.dot_general(a, b, (((1,), (0,)), ((), ())), preferred_element_type=F32)


def nt(a, b):
    return lax.dot_general(a, b, (((1,), (1,)), ((), ())), preferred_element_type=F32)


def spot():
    z, f = lax.axis_index("seq"), lax.axis_index("fsdp")
    core = lax.rem(f, 2)
    x = lax.rem(f // 2, 2)
    y = f // 4
    return z, f, y, x, core


def remote(src, dst, send, recv, where):
    return pltpu.make_async_remote_copy(
        src_ref=src, dst_ref=dst, send_sem=send, recv_sem=recv, device_id=where, device_id_type=MESH
    )


class Rows:
    def __init__(self, z, f, core):
        base = f - core
        self.work, self.home = [], []
        for i in range(2):
            zw, cw = 2 * i + core, z // 2
            self.work.append((zw, base + cw, (zw == z) & (cw == core)))
            zh, ch = 2 * core + i, lax.rem(z, 2)
            self.home.append((zh, base + ch, (zh == z) & (ch == core)))
        self.z = z

    def greet(self, barrier):
        count = 0
        for zt, ft, same in self.work + self.home:

            @pl.when(jnp.logical_not(same))
            def _():
                pl.semaphore_signal(barrier, inc=1, device_id=(zt, ft), device_id_type=MESH)

            count = count + jnp.where(same, 0, 1)
        return count

    def start(self, src, dst, send, recv, local, out, piece=slice(None)):
        places = self.work if out else self.home
        slot = lax.rem(self.z, 2) if out else self.z // 2
        for i, (zt, ft, same) in enumerate(places):

            @pl.when(same)
            def _(i=i):
                pltpu.make_async_copy(src.at[i, piece], dst.at[slot, piece], local).start()

            @pl.when(jnp.logical_not(same))
            def _(i=i, zt=zt, ft=ft):
                remote(src.at[i, piece], dst.at[slot, piece], send.at[i], recv.at[slot], (zt, ft)).start()

    def wait(self, src, dst, send, recv, local, out):
        goes, comes = (self.work, self.home) if out else (self.home, self.work)
        for i, (zt, ft, same) in enumerate(goes):

            @pl.when(same)
            def _(i=i):
                pltpu.make_async_copy(src.at[i], dst.at[i], local).wait()

            @pl.when(jnp.logical_not(same))
            def _(i=i, zt=zt, ft=ft):
                remote(src.at[i], dst.at[i], send.at[i], recv.at[i], (zt, ft)).wait_send()

        for i, (zt, ft, same) in enumerate(comes):

            @pl.when(jnp.logical_not(same))
            def _(i=i, zt=zt, ft=ft):
                remote(src.at[i], dst.at[i], send.at[i], recv.at[i], (zt, ft)).wait_recv()


def halves(width):
    cut = (width // 128 // 2) * 128
    return pl.ds(0, cut), pl.ds(cut, width - cut)


SQRT_HALF = 0.7071067811865476
DENSITY = 0.3989422804014327
BY_Z = (2, 4)
SHARD = 336
GROUP = 384
STEPS = 7


def moments(values):
    average = jnp.mean(values, axis=-1, keepdims=True)
    centred = values - average
    spread = jnp.mean(centred * centred, axis=-1, keepdims=True)
    scale = lax.rsqrt(spread + EPSILON)
    return centred * scale, scale


def norm_back(values, gain, grads):
    unit, scale = moments(values)
    spread = grads * gain
    inner = spread - jnp.mean(spread, axis=-1, keepdims=True)
    inner = inner - unit * jnp.mean(spread * unit, axis=-1, keepdims=True)
    return inner * scale, jnp.sum(grads * unit, axis=0, keepdims=True)


def rope_back(grads, cosine, sine):
    lane = lax.broadcasted_iota(jnp.int32, (1, 128), 1)
    low = lax.rem(lane, 64) < 32
    u = grads * sine
    return grads * cosine + jnp.where(low, pltpu.roll(u, 96, 1), -pltpu.roll(u, 32, 1))


class Sums:
    KINDS = 9

    @staticmethod
    def scratch(count, slots, rows, wide):
        dma = pltpu.SemaphoreType.DMA((count, Sums.KINDS))
        shapes = [(slots, 2, 2, 2), (count, 2, 2), (count, 2), (count, 2), (count,)]
        return [pltpu.VMEM(s + (rows, wide), BF) for s in shapes] + [dma, dma]

    def __init__(self, here, refs, slot):
        self.here, self.slot = here, slot
        self.acc, self.rx, self.r2, self.zr, self.zr2, self.send, self.recv = refs

    def copy(self, t, kind):
        h = self.here
        acc = self.acc.at[self.slot[t]]
        plan = {
            0: lambda: (acc.at[0, :, 1 - h.x], self.rx.at[t, 0], (h.z, h.fx)),
            1: lambda: (acc.at[1, 1 - h.y], self.rx.at[t, 1], (h.z, h.fy)),
            2: lambda: (self.rx.at[t, 0, 1 - h.y], self.r2.at[t, 0], (h.z, h.fy)),
            3: lambda: (self.rx.at[t, 1, 1 - h.x], self.r2.at[t, 1], (h.z, h.fx)),
            4: lambda: (self.r2.at[t], self.zr.at[t], (h.near, h.f)),
            5: lambda: (self.zr.at[t, 1 - h.own], self.zr2.at[t], (h.across, h.f)),
            6: lambda: (self.r2.at[t, h.own], self.r2.at[t, h.own], (h.across, h.f)),
            7: lambda: (self.r2.at[t, h.own], self.zr.at[t, h.own], (h.near, h.f)),
            8: lambda: (self.r2.at[t, 1 - h.own], self.zr.at[t, 1 - h.own], (h.near, h.f)),
        }
        src, dst, where = plan[kind]()
        return remote(src, dst, self.send.at[t, kind], self.recv.at[t, kind], where)

    def begin(self, t):
        self.copy(t, 0).start()
        self.copy(t, 1).start()

    def cross(self, t):
        h, s = self.here, self.slot[t]
        self.copy(t, 0).wait()
        self.rx[t, 0, 1 - h.y] = added(self.rx[t, 0, 1 - h.y], self.acc[s, 0, 1 - h.y, h.x])
        self.copy(t, 2).start()
        self.copy(t, 1).wait()
        self.rx[t, 1, 1 - h.x] = added(self.rx[t, 1, 1 - h.x], self.acc[s, 1, h.y, 1 - h.x])
        self.copy(t, 3).start()

    def plane(self, t):
        h, s = self.here, self.slot[t]
        self.copy(t, 2).wait()
        self.r2[t, 0] = added(self.r2[t, 0], self.rx[t, 0, h.y], self.acc[s, 0, h.y, h.x])
        self.copy(t, 3).wait()
        self.r2[t, 1] = added(self.r2[t, 1], self.rx[t, 1, h.x], self.acc[s, 1, h.y, h.x])

        @pl.when(h.outer)
        def _():
            self.copy(t, 4).start()

    def meet(self, t):
        h = self.here

        @pl.when(jnp.logical_not(h.outer))
        def _():
            self.copy(t, 4).wait_recv()
            self.zr[t, 1 - h.own] = added(self.zr[t, 1 - h.own], self.r2[t, 1 - h.own])
            self.copy(t, 5).start()

    def sums(self, t):
        h = self.here

        @pl.when(jnp.logical_not(h.outer))
        def _():
            self.copy(t, 5).wait()
            self.r2[t, h.own] = added(self.r2[t, h.own], self.zr[t, h.own], self.zr2[t])
            self.copy(t, 6).start()
            self.copy(t, 7).start()

    def spread(self, t):
        @pl.when(jnp.logical_not(self.here.outer))
        def _():
            self.copy(t, 6).wait_recv()
            self.copy(t, 8).start()

    def finish(self, t):
        @pl.when(jnp.logical_not(self.here.outer))
        def _():
            self.copy(t, 6).wait_send()
            self.copy(t, 7).wait_send()
            self.copy(t, 8).wait_send()

        @pl.when(self.here.outer)
        def _():
            self.copy(t, 4).wait_send()
            self.copy(t, 7).wait_recv()
            self.copy(t, 8).wait_recv()

    def total(self, act):
        for ref, there in ((self.zr, self.here.outer), (self.r2, jnp.logical_not(self.here.outer))):
            pl.when(there)(functools.partial(act, ref))

    LATER = ("cross", "plane", "meet", "sums", "spread", "finish")


def added(*terms):
    total = terms[0].astype(F32)
    for term in terms[1:]:
        total = total + term.astype(F32)
    return total.astype(BF)


class Halves:
    def __init__(self, ref):
        self.ref, self.at, self.size = ref, self, ref.shape[0] // 2

    def __getitem__(self, index):
        i, piece = index if isinstance(index, tuple) else (index, slice(None))
        if isinstance(piece, slice):
            return self.ref.at[pl.ds(i * self.size, self.size)]
        return self.ref.at[pl.ds(i * self.size + piece.start, piece.size)]


class Here:
    def __init__(self):
        self.z, self.f, self.y, self.x, self.core = spot()
        self.fx = self.f + 2 - 4 * self.x
        self.fy = self.f + 4 - 8 * self.y
        self.fc = self.f + 1 - 2 * self.core
        z = self.z
        self.outer = (z == 0) | (z == 3)
        self.near = jnp.where(z < 2, 1 - z, 5 - z)
        self.across = jnp.where(self.outer, z, 3 - z)
        self.own = jnp.where(z < 2, 0, 1)

    def greet(self, barrier, rows, column=0):
        for n in range(column):
            pl.semaphore_signal(barrier, inc=1, device_id=(lax.rem(self.z + n + 1, 4), self.f), device_id_type=MESH)
        for t in (self.fx, self.fy, self.fc):
            pl.semaphore_signal(barrier, inc=1, device_id=(self.z, t), device_id_type=MESH)
        pl.semaphore_signal(barrier, inc=1, device_id=(self.near, self.f), device_id_type=MESH)

        @pl.when(jnp.logical_not(self.outer))
        def _():
            pl.semaphore_signal(barrier, inc=1, device_id=(self.across, self.f), device_id_type=MESH)

        pl.semaphore_wait(barrier, rows.greet(barrier) + 4 + column + jnp.where(self.outer, 0, 1))


def lanes(start, size):
    return pl.ds(start if isinstance(start, int) else pl.multiple_of(start, 128), size)


PIECES = 8
WIDE_SLOTS = 3
DOWN_FIRST = 0
PLAN = (
    ("r", 0),
    ("f", ("w", 0)),
    ("r", 0),
    ("f", ("w", 1)),
    ("c", "ln2"),
    ("r", 0),
    ("f", ("d", 0)),
    ("s", ("w", 0), 0),
    ("r", 0),
    ("c", "do"),
    ("s", ("w", 1), 0),
    ("r", 0),
    ("c", "og"),
    ("r", 0),
    ("b", ("o", 0)),
    ("c", "E0.0"),
    ("c", "E0.1"),
    ("s", ("d", 0), 0),
    ("r", 0),
    ("c", "E1.0"),
    ("s", ("w", 0), 1),
    ("s", ("w", 1), 1),
    ("r", 0),
    ("c", "E1.1"),
    ("f", ("w", 2)),
    ("c", "F0"),
    ("s", ("o", 0), 0),
    ("s", ("w", 0), 2),
    ("c", "E2.0"),
    ("s", ("d", 0), 1),
    ("s", ("w", 1), 2),
    ("f", ("w", 3)),
    ("s", ("w", 0), 3),
    ("c", "E2.1"),
    ("s", ("w", 2), 0),
    ("s", ("w", 1), 3),
    ("c", "F1"),
    ("s", ("o", 0), 1),
    ("s", ("w", 0), 4),
    ("f", ("d", 1)),
    ("s", ("w", 3), 0),
    ("s", ("w", 1), 4),
    ("s", ("d", 0), 2),
    ("c", "G0"),
    ("s", ("w", 2), 1),
    ("b", ("w", 7)),
    ("c", "E3.0"),
    ("s", ("o", 0), 2),
    ("c", "E3.1"),
    ("s", ("d", 0), 3),
    ("c", "F2"),
    ("s", ("d", 1), 0),
    ("s", ("o", 0), 3),
    ("s", ("w", 2), 2),
    ("c", "G1"),
    ("s", ("w", 3), 1),
    ("b", ("w", 8)),
    ("c", "F3"),
    ("s", ("d", 0), 4),
    ("c", "G2"),
    ("s", ("w", 7), 0),
    ("s", ("o", 0), 4),
    ("s", ("w", 3), 2),
    ("b", ("w", 9)),
    ("c", "H"),
    ("s", ("d", 1), 1),
    ("s", ("w", 2), 3),
    ("s", ("w", 3), 3),
    ("c", "gains"),
    ("b", ("g", 0)),
    ("c", "G3"),
    ("s", ("w", 8), 0),
    ("s", ("w", 2), 4),
    ("r", 1),
    ("s", ("w", 7), 1),
    ("f", ("w", 4)),
    ("s", ("w", 3), 4),
    ("r", 1),
    ("s", ("w", 9), 0),
    ("s", ("g", 0), 0),
    ("s", ("d", 1), 2),
    ("s", ("w", 8), 1),
    ("f", ("w", 5)),
    ("r", 1),
    ("s", ("w", 4), 0),
    ("s", ("d", 1), 3),
    ("s", ("w", 7), 2),
    ("s", ("w", 9), 1),
    ("s", ("g", 0), 1),
    ("f", ("w", 6)),
    ("s", ("w", 8), 2),
    ("s", ("w", 5), 0),
    ("s", ("d", 1), 4),
    ("s", ("w", 4), 1),
    ("s", ("w", 7), 3),
    ("b", ("w", 10)),
    ("s", ("w", 0), 5),
    ("s", ("w", 1), 5),
    ("s", ("d", 0), 5),
    ("s", ("o", 0), 5),
    ("s", ("w", 2), 5),
    ("s", ("w", 3), 5),
    ("r", 1),
    ("s", ("w", 8), 3),
    ("s", ("w", 9), 2),
    ("s", ("g", 0), 2),
    ("s", ("w", 7), 4),
    ("s", ("d", 1), 5),
    ("s", ("w", 6), 0),
    ("s", ("w", 5), 1),
    ("s", ("w", 4), 2),
    ("s", ("w", 8), 4),
    ("r", 1),
    ("s", ("w", 9), 3),
    ("s", ("g", 0), 3),
    ("s", ("w", 5), 2),
    ("s", ("w", 4), 3),
    ("s", ("w", 10), 0),
    ("s", ("w", 7), 5),
    ("s", ("w", 6), 1),
    ("s", ("w", 8), 5),
    ("s", ("w", 10), 1),
    ("s", ("w", 9), 4),
    ("s", ("g", 0), 4),
    ("s", ("w", 6), 2),
    ("s", ("w", 5), 3),
    ("s", ("w", 4), 4),
    ("s", ("w", 10), 2),
    ("s", ("w", 6), 3),
    ("s", ("w", 5), 4),
    ("r", 1),
    ("s", ("w", 10), 3),
    ("s", ("w", 6), 4),
    ("r", 1),
    ("s", ("w", 10), 4),
    ("r", 1),
    ("s", ("w", 9), 5),
    ("s", ("g", 0), 5),
    ("s", ("w", 4), 5),
    ("s", ("w", 5), 5),
    ("s", ("w", 6), 5),
    ("s", ("w", 10), 5),
)


def split_plan():
    before, loop, after = [], {(n, m): [] for n in range(10) for m in range(3)}, []
    place = before
    for op in PLAN:
        mark = op[1] if op[0] == "c" else ""
        if mark in ("H", "G3"):
            place = after
        elif mark[:1] == "E":
            place = loop[2 * int(mark[1]) + int(mark[3]), 0]
        elif mark[:1] == "F":
            place = loop[2 * int(mark[1]) + 3, 1]
        elif mark[:1] == "G":
            place = loop[2 * int(mark[1]) + 5, 2]
        if mark[:1] not in ("E", "F", "G") or mark == "G3":
            place.append(op)
    return before, loop, after


def rope(values, cosine, sine):
    lane = lax.broadcasted_iota(jnp.int32, (1, 128), 1)
    turned = jnp.where(lax.rem(lane, 64) < 32, -pltpu.roll(values, 96, 1), pltpu.roll(values, 32, 1))
    return values * cosine + turned * sine


def front_kernel(
    attn_h, ffn_h, qkv_h, out_h, in_h, down_h, tok_f, cot_f, starts_f, inverse,
    qkv_o, out_o, cot_o, tok_o, mid_o, gn_o, ffn_o, q_o, k_o, v_o, mix_o, bias_o, xt_o, mt_o, nt_o, glc_o, gj_o, at_o,
    gains_o, cos_o, sin_o, lse_o,
    gains_v, qkv_v, out_v, in_v, down_v, tok_v, starts_v, acc_f, acc_g, gl, normed, x2, q, k, v, mix, bias,
    gains_h, starts_h, tok_h, cot_h, gj, act, mine, theirs, rows_b,
    ss, rs, ssi, rsi, ls, lsi, es, er, el, ds_, dr, kvs, kvr, ws, ts, tr, tl, gs_, gr_, gw, as_, ar_, aw,
):
    h = Here()
    rows = Rows(h.z, h.f, h.core)
    z, f, core = h.z, h.f, h.core
    fx, fy, fc = h.fx, h.fy, h.fc
    fd = fx + 4 - 8 * h.y
    sib = (z, fc)
    half, wide = normed.shape
    block = half // 2
    own_rows, sib_rows = pl.ds(0, half), pl.ds(half, half)

    shards = (gains_h, qkv_h, out_h, down_h)
    wholes = (gains_v, qkv_v, out_v, down_v)
    targets = (fx, fy, fc, fy, fx, fc, fc, fc, fc)

    def part(w, i, cols=None):
        whole = wholes[w]
        if w < 3:
            return whole.at[i] if cols is None else whole.at[i, :, cols]
        r = pl.ds(pl.multiple_of(i * SHARD, 16), SHARD)
        return whole.at[r] if cols is None else whole.at[r, cols]

    def copy(w, k):
        a, b = halves(shards[w].shape[1])
        place = {3: (fx, a), 4: (fy, b), 5: (fx,), 6: (fy,), 7: (fd, a), 8: (fd, b)}
        dst = part(w, f) if k < 3 else part(w, *place[k])
        return remote(shards[w] if k < 3 else dst, dst, ss.at[w, k], rs.at[w, k], (z, targets[k]))

    quarter = pl.ds(pl.multiple_of(z * 32, 32), 32)

    def place_in(t, i, *more):
        return in_v.at[(t, i // 2, lax.rem(i, 2)) + more]

    def copy_in(t, k):
        cols = lanes(t * GROUP, GROUP)
        if t in BY_Z:
            if k in (0, 1):
                return remote(in_h.at[:, quarter, cols], place_in(t, f, slice(None), quarter), ssi.at[t, k], rsi.at[t, k], (z, targets[k]))
            if k in (3, 4):
                dst = place_in(t, (fx, fy)[k - 3], k - 3, quarter)
                return remote(dst, dst, ssi.at[t, k], rsi.at[t, k], (z, targets[k]))
            if k < 8:
                dst = in_v.at[t, :, core, :, quarter]
                return remote(dst, dst, ssi.at[t, k], rsi.at[t, k], (lax.rem(z + k - 4, 4), f))
            dst = in_v.at[t, :, core]
            return remote(dst, dst, ssi.at[t, k], rsi.at[t, k], sib)
        place = {3: (fx, 0), 4: (fy, 1), 5: (fx,), 6: (fy,), 7: (fd, 0), 8: (fd, 1)}
        dst = place_in(t, f) if k < 3 else place_in(t, *place[k])
        return remote(in_h.at[:, :, cols] if k < 3 else dst, dst, ssi.at[t, k], rsi.at[t, k], (z, targets[k]))

    def quarters(t, stage):
        waits, starts = (((), (0, 1)), ((0, 1), (3, 4)), ((3, 4), (5, 6, 7)), ((5, 6, 7), (8,)), ((8,), ()))[stage]
        for k in waits:
            copy_in(t, k).wait_recv()
        if stage == 2:
            own_in(t).wait()
        for k in starts:
            copy_in(t, k).start()

    def first(w, copy=copy):
        for k in range(3):
            copy(w, k).start()

    def second(w, copy=copy):
        for k in (0, 1):
            copy(w, k).wait_recv()
            copy(w, k + 3).start()
            copy(w, k + 5).start()

    def third(w, copy=copy):
        for k in (3, 4):
            copy(w, k).wait_recv()
            copy(w, k + 4).start()

    def rest(w, copy=copy):
        for k in (2, 5, 6, 7, 8):
            copy(w, k).wait_recv()

    def own(w):
        return pltpu.make_async_copy(shards[w], part(w, f), ls.at[w])

    def own_in(t):
        cols = lanes(t * GROUP, GROUP)
        if t in BY_Z:
            return pltpu.make_async_copy(in_h.at[:, quarter, cols], place_in(t, f, slice(None), quarter), lsi.at[t])
        return pltpu.make_async_copy(in_h.at[:, :, cols], place_in(t, f), lsi.at[t])

    wide_in = [
        [pltpu.make_async_copy(src.at[i], ref.at[pl.ds(i * block, block)], el.at[i]) for i in range(2)]
        for src, ref in ((tok_f, acc_f), (cot_f, acc_g))
    ]
    for c in wide_in[0]:
        c.start()
    gains_h[:, :128] = jnp.broadcast_to(attn_h[...].astype(F32), (16, 128)).astype(BF)
    gains_h[:, 128:] = jnp.broadcast_to(ffn_h[...].astype(F32), (16, 128)).astype(BF)
    starts_h[...] = jnp.zeros(starts_h.shape, jnp.int32)
    starts_h[:2, :8] = starts_f[...]
    for c in wide_in[0]:
        c.wait()
    tok_h[...] = acc_f[...].astype(BF)
    for c in wide_in[1]:
        c.start()
    for w in range(4):
        own(w).start()
    for t in range(STEPS):
        own_in(t).start()
    h.greet(pltpu.get_barrier_semaphore(), rows, 3)
    info = remote(starts_h, starts_v.at[core], ds_.at[0], dr.at[0], sib)
    own_info = pltpu.make_async_copy(starts_h, starts_v.at[core], el.at[2])
    info.start()
    own_info.start()
    rows.start(Halves(tok_h), tok_v, es.at[0], er.at[0], el.at[3], True)
    for t in BY_Z:
        quarters(t, 0)
    for w in range(3):
        first(w)
    for c in wide_in[1]:
        c.wait()
    cot_h[...] = acc_g[...].astype(BF)
    info.wait()
    own_info.wait()

    lane = lax.broadcasted_iota(jnp.int32, (1, 128), 1)
    begins = starts_v[lax.rem(z, 2), pl.ds(z // 2, 1), :]
    inside = lane < 8

    def documents(base):
        place = lax.broadcasted_iota(jnp.int32, (half, 128), 0) + base
        before = (begins <= place) & inside
        number = jnp.sum(jnp.where(before, 1.0, 0.0), axis=1, keepdims=True)
        begin = jnp.max(jnp.where(before, begins, 0).astype(F32), axis=1, keepdims=True)
        return place, number, begin

    place, number, begin = documents(core * half)
    angle = (place.astype(F32) - begin) * inverse[...]
    cos_o[...] = jnp.cos(angle)
    sin_o[...] = jnp.sin(angle)
    across = jnp.broadcast_to(number, (half, 128)).T[0:1, :]
    _, other, _ = documents((1 - core) * half)
    bias[:half] = jnp.where(number == across, 0.0, MASKED_SCORE).astype(BF)
    bias[half:] = jnp.where(other == across, 0.0, MASKED_SCORE).astype(BF)

    for t in BY_Z:
        quarters(t, 1)
    for w in range(3):
        second(w)
    rows.start(Halves(cot_h), cot_o, es.at[1], er.at[1], el.at[4], True)
    first(3)
    first(0, copy_in)
    first(1, copy_in)
    for t in BY_Z:
        quarters(t, 2)
    third(0)
    rest(0)
    own(0).wait()
    for n in range(2):
        for i in range(8):
            gains_o[n : n + 1, i * 128 : i * 128 + 128] = gains_v[i, 0:1, n * 128 : n * 128 + 128].astype(F32)
    rows.wait(Halves(tok_h), tok_v, es.at[0], er.at[0], el.at[3], True)
    saved = []

    def save(src, dst):
        saved.append(pltpu.make_async_copy(src, dst, ws.at[len(saved)]))
        saved[-1].start()

    def share(src, dst, n, again):
        keep = pltpu.make_async_copy(mine, dst.at[:, own_rows], tl.at[n])
        give = remote(theirs, dst.at[:, sib_rows], ts.at[n], tr.at[n], sib)
        if again is not None:
            again[0].wait()
            again[1].wait_send()
        for i in range(4):
            mine[i * 128 : i * 128 + 128] = src[:, lanes((2 * i + core) * 128, 128)].T
            theirs[i * 128 : i * 128 + 128] = src[:, lanes((2 * i + 1 - core) * 128, 128)].T
        keep.start()
        give.start()
        return keep, give

    unit, _ = moments(tok_v[...].reshape(half, wide).astype(F32))
    normed[...] = (unit * gains_o[0:1]).astype(BF)
    save(tok_v, tok_o)
    save(bias, bias_o)
    shared = share(normed, nt_o, 0, None)
    third(1)
    rest(1)
    own(1).wait()
    save(qkv_v, qkv_o)

    def pair_send(n, i):
        ref = (k, v)[n]
        cols = pl.ds(i * 256, 256)
        return remote(ref.at[own_rows, cols], ref.at[sib_rows, cols], kvs.at[n, i], kvr.at[n, i], sib)

    for n, ref in ((1, k), (2, v), (0, q)):
        for i in range(4):
            product = nn(normed[...], qkv_v[:, :, n * wide + i * 256 : n * wide + i * 256 + 256].reshape(wide, 256))
            for j in range(2):
                cols = slice(i * 256 + j * 128, i * 256 + j * 128 + 128)
                value = product[:, j * 128 : j * 128 + 128]
                value = value if n == 2 else rope(value, cos_o[...], sin_o[...])
                ref[:half, cols] = value.astype(BF)
            if n:
                pair_send(n - 1, i).start()
    third(2)
    for n in range(2):
        for i in range(4):
            pair_send(n, i).wait()
    for ref, dst in ((q, q_o), (k, k_o), (v, v_o)):
        save(ref, dst)

    def attend(i, _):
        @pl.when(i == 4)
        def _():
            second(3)

        @pl.when(i == 6)
        def _():
            second(0, copy_in)

        cols = lanes(i * 128, 128)
        queries = q[:, cols] * jnp.asarray(0.125, BF)
        keys = k[:, cols]
        vt = v[:, cols].T
        outs = []
        for e in range(2):
            here = (lane < 64) if e == 0 else (lane >= 64)
            scores = nt(keys, jnp.where(here, queries, jnp.zeros_like(queries))) + bias[...].astype(F32)
            top = jnp.max(scores, axis=0, keepdims=True)
            p = jnp.exp(scores - top)
            total = jnp.sum(p, axis=0, keepdims=True)
            outs.append(nn(vt, p.astype(BF)) / total)
            lse_o[i, e : e + 1, :] = top + jnp.log(total)
        mix[:, cols] = jnp.concatenate([outs[0][:64], outs[1][64:]], axis=0).T.astype(BF)
        return 0

    lax.fori_loop(0, 8, attend, 0)
    second(1, copy_in)
    first(3, copy_in)
    first(5, copy_in)
    rest(2)
    own(2).wait()
    save(out_v, out_o)
    save(mix, mix_o)
    middle = tok_v[...].reshape(half, wide).astype(F32) + nn(mix[...], out_v[...].reshape(wide, wide))
    acc_f[...] = middle
    unit, _ = moments(middle)
    x2[...] = (unit * gains_o[1:2]).astype(BF)
    mid_save = pltpu.make_async_copy(acc_f, mid_o, ls.at[4])
    mid_save.start()
    third(3)
    third(0, copy_in)
    rows.wait(Halves(cot_h), cot_o, es.at[1], er.at[1], el.at[4], True)
    cot_load = [pltpu.make_async_copy(cot_o.at[i], gl.at[pl.ds(i * block, block)], el.at[i]) for i in range(2)]
    for c in cot_load:
        c.start()
    shared = share(x2, xt_o, 1, shared)
    shared = share(mix, mt_o, 2, shared)
    for c in cot_load:
        c.wait()
    glc_keep = pltpu.make_async_copy(gl.at[:, lanes(core * 512, 512)], glc_o.at[own_rows], tl.at[3])
    glc_give = remote(gl.at[:, lanes((1 - core) * 512, 512)], glc_o.at[sib_rows], ts.at[3], tr.at[3], sib)
    glc_keep.start()
    glc_give.start()
    mid_save.wait()
    quarters(2, 3)
    rest(3)
    own(3).wait()

    def stage_copies(t):
        s = lax.rem(t, 2)
        r = lanes(t * GROUP, GROUP)
        return [
            pltpu.make_async_copy(gj.at[s], gj_o.at[t, own_rows], gw.at[s]),
            pltpu.make_async_copy(act.at[s], at_o.at[r, own_rows], aw.at[s]),
        ], [
            remote(gj.at[s], gj_o.at[t, sib_rows], gs_.at[s], gr_.at[t], sib),
            remote(act.at[s], at_o.at[r, sib_rows], as_.at[s], ar_.at[t], sib),
        ]

    def feed(t, _):
        s = lax.rem(t, 2)

        def at_step(events):
            for n, todo in events.items():

                @pl.when(t == n)
                def _(todo=todo):
                    for act, *args in todo:
                        act(*args)

        at_step({
            1: [(second, 3, copy_in), (first, 6, copy_in)],
            2: [(second, 5, copy_in), (quarters, 4, 3)],
            3: [(second, 6, copy_in)],
        })

        def ready(n):
            if n in BY_Z:
                quarters(n, 4)
            else:
                rest(n, copy_in)
                own_in(n).wait()

        at_step({n: [(ready, n)] for n in range(STEPS)})
        w = jnp.concatenate([in_v[t, :, :, m].reshape(wide, GROUP) for m in range(2)], axis=1)
        wd = down_v[lanes(t * GROUP, GROUP)]
        joined = nn(x2[...], w)
        a, c = joined[:, :GROUP], joined[:, GROUP:]
        grad_active = nt(gl[...], wd)
        phi = 0.5 * (1.0 + lax.erf(a * SQRT_HALF))
        gate = a * phi
        slope = phi + a * (jnp.exp(-0.5 * a * a) * DENSITY)
        active = (gate * c).astype(BF)
        ga = (slope * c * grad_active).astype(BF)
        gc = (gate * grad_active).astype(BF)

        @pl.when(t >= 2)
        def _():
            keep, give = stage_copies(t - 2)
            for copied in keep:
                copied.wait()
            for sent in give:
                sent.wait_send()

        gj[s, :, :GROUP] = ga
        gj[s, :, GROUP:] = gc
        act[s] = active.T
        keep, give = stage_copies(t)
        for started in keep + give:
            started.start()

        at_step({n: [(third, m, copy_in)] for n, m in ((0, 1), (2, 3), (3, 5), (4, 6))})
        acc_f[...] += nn(active, wd)
        back = nt(gj[s], w)

        @pl.when(t == 0)
        def _():
            acc_g[...] = back

        @pl.when(t > 0)
        def _():
            acc_g[...] += back

        return 0

    lax.fori_loop(0, STEPS, feed, 0)
    rows_b[...] = acc_f[...].astype(BF).reshape(2, block, wide)
    save(rows_b, ffn_o)
    save(acc_g, gn_o)
    for t in (STEPS - 2, STEPS - 1):
        keep, give = stage_copies(t)
        for copied in keep:
            copied.wait()
        for sent in give:
            sent.wait_send()
    for t in range(STEPS):
        for received in stage_copies(t)[1]:
            received.wait_recv()
    shared[0].wait()
    shared[1].wait_send()
    for n, dst in enumerate((nt_o, xt_o, mt_o)):
        remote(theirs, dst.at[:, sib_rows], ts.at[n], tr.at[n], sib).wait_recv()
    glc_keep.wait()
    glc_give.wait()
    for w in range(4):
        for kind in range(9):
            copy(w, kind).wait_send()
    for t in range(STEPS):
        for kind in range(9):
            if t not in BY_Z or kind != 2:
                copy_in(t, kind).wait_send()
    for c in saved:
        c.wait()


def front_all(attn_gain, ffn_gain, qkv, out, inw, down, tok, cot, starts, inverse):
    dma = pltpu.SemaphoreType.DMA
    block, wide = tok.shape[1:]
    half, hidden = 2 * block, STEPS * GROUP

    def shape(*s, kind=BF):
        return jax.ShapeDtypeStruct(s, kind)

    def buf(*s, kind=BF):
        return pltpu.VMEM(s, kind)

    whole = pl.BlockSpec(memory_space=pltpu.VMEM)
    return pl.pallas_call(
        front_kernel,
        out_shape=[
            shape(8, *qkv.shape), shape(8, *out.shape), shape(*cot.shape), shape(*tok.shape),
            shape(half, wide, kind=F32), shape(half, wide, kind=F32), shape(2, block, wide),
            shape(half, wide), shape(2 * half, wide), shape(2 * half, wide), shape(half, wide), shape(2 * half, half),
            shape(half, 2 * half), shape(half, 2 * half), shape(half, 2 * half), shape(2 * half, half),
            shape(STEPS, 2 * half, 2 * GROUP), shape(hidden, 2 * half),
            shape(2, wide, kind=F32), shape(half, 128, kind=F32), shape(half, 128, kind=F32), shape(8, 2, half, kind=F32),
        ],
        in_specs=[whole] * 2 + [ANY] * 6 + [whole] * 2,
        out_specs=[ANY] * 18 + [whole] * 4,
        scratch_shapes=[
            buf(8, 16, 256), buf(8, *qkv.shape), buf(8, *out.shape), buf(STEPS, 4, 2, 2, 128, GROUP), buf(hidden, wide),
            buf(*tok.shape), buf(2, 8, 128, kind=jnp.int32), buf(half, wide, kind=F32), buf(half, wide, kind=F32),
            buf(half, wide), buf(half, wide), buf(half, wide), buf(half, wide), buf(2 * half, wide), buf(2 * half, wide),
            buf(half, wide), buf(2 * half, half),
            buf(16, 256), buf(8, 128, kind=jnp.int32), buf(half, wide), buf(half, wide),
            buf(2, half, 2 * GROUP), buf(2, GROUP, half), buf(half, half), buf(half, half), buf(2, block, wide),
            dma((4, 9)), dma((4, 9)), dma((STEPS, 9)), dma((STEPS, 9)), dma((5,)), dma((STEPS,)),
            dma((2, 2)), dma((2, 2)), dma((5,)), dma((1,)), dma((1,)), dma((2, 4)), dma((2, 4)), dma((10,)),
            dma((4,)), dma((4,)), dma((4,)), dma((2,)), dma((STEPS,)), dma((2,)), dma((2,)), dma((STEPS,)), dma((2,)),
        ],
        compiler_params=pltpu.CompilerParams(collective_id=1, has_side_effects=True, vmem_limit_bytes=VMEM_BYTES),
        name="gather_attention_feed_forward",
    )(attn_gain, ffn_gain, qkv, out, inw, down, tok, cot, starts, inverse)


def back_kernel(
    ffn_h, mid_h, gn_h, cot_h, qkv_h, out_h, q_h, k_h, v_h, mix_h, rows_h, bias_h, xt_h, mt_h, nt_h, glc_h, gj_h, at_h,
    gains, cosine, sine, lse,
    in_o, qkv_o, down_o, out_o, gain_o, outh_o, inh_o,
    acc_f, acc_g, win, xt, mt, gj, gq, at, glc, gm, dout, q, k, v, bias, kept, dx_kv, kvl, centres, terms, gs, gr,
    ld, gld, wsem, ps, pr, kvs, kvr, gqs, gqr, dxs, dxr, fo, es, er, el,
    *sum_refs,
):
    h = Here()
    rows = Rows(h.z, h.f, h.core)
    order = [op[1][1] for op in PLAN if op[0] in "fb" and op[1][0] == "w"]
    wide = Sums(h, sum_refs[0:7], {t: n % WIDE_SLOTS for n, t in enumerate(order)})
    down = Sums(h, sum_refs[7:14], {0: 0, 1: 1})
    outs = Sums(h, sum_refs[14:21], {0: 0})
    gain = Sums(h, sum_refs[21:28], {0: 0})
    groups = {"w": wide, "d": down, "o": outs, "g": gain}
    sib = (h.z, h.fc)
    half, width = dout.shape
    block = half // 2
    own_rows, sib_rows = pl.ds(0, half), pl.ds(half, half)
    lane = lax.broadcasted_iota(jnp.int32, (1, 128), 1)

    def load(src, dst, n):
        return pltpu.make_async_copy(src, dst, ld.at[n])

    def gj_load(t):
        return pltpu.make_async_copy(gj_h.at[t], gj, gld.at[0])

    def qkv_weights(u):
        return [
            pltpu.make_async_copy(qkv_h.at[:, :, lanes(n * 1024 + u * 256, 256)], win.at[:, :, pl.ds(n * 256, 256)], wsem.at[n])
            for n in range(3)
        ]

    loads = {
        "xt": load(xt_h, xt, 0), "mid": load(mid_h, acc_f, 1), "gn": load(gn_h, acc_g, 2),
        "c0": load(cot_h.at[0], dout.at[pl.ds(0, block)], 3), "c1": load(cot_h.at[1], dout.at[pl.ds(block, block)], 4),
        "w": load(out_h, k, 5), "mix": load(mix_h, v.at[own_rows], 6), "mt": load(mt_h, mt, 7),
        "at": load(at_h, at, 8), "glc": load(glc_h, glc, 9), "bias": load(bias_h, bias, 10), "q": load(q_h, q, 11),
        "nt": load(nt_h, mt, 7), "k": load(k_h, k, 5), "v": load(v_h, v, 6),
        "r0": load(rows_h.at[0], k.at[pl.ds(0, block)], 3), "r1": load(rows_h.at[1], k.at[pl.ds(block, block)], 4),
    }

    def start(*names):
        for name in names:
            loads[name].start()

    def wait(*names):
        for name in names:
            loads[name].wait()

    start("xt")
    gj_load(0).start()
    start("mid", "gn", "c0", "c1")
    start("w", "mix", "at", "glc", "mt", "bias", "q")
    h.greet(pltpu.get_barrier_semaphore(), rows)

    def put(group, t, term, cut):
        s = group.slot[t]
        term = term.astype(BF)
        for o in range(4):
            for n in range(2):
                group.acc[s, n, o // 2, o % 2] = term[o * 128 : o * 128 + 128, n * cut : n * cut + cut]

    def in_term(t):
        if t == 0:
            wait("xt")
        gj_load(t).wait()
        put(wide, t, nn(xt[...], gj[...]), GROUP)
        if t + 1 < STEPS:
            gj_load(t + 1).start()

    def down_term(j):
        if j == DOWN_FIRST:
            wait("at", "glc")
        term = nn(at[...], glc[:, j * 256 : j * 256 + 256])
        for f in range(8):
            down.acc[j, f % 2, f // 4, f // 2 % 2] = term[f * SHARD : f * SHARD + SHARD].astype(BF)

    gm_send = remote(gm.at[own_rows], gm.at[sib_rows], ps.at[0], pr.at[0], sib)

    def second_norm():
        wait("mid", "gn", "c0", "c1")
        back, terms[1:2] = norm_back(acc_f[...], gains[1:2], acc_g[...])
        grad_mid = dout[...].astype(F32) + back
        acc_f[...] = grad_mid
        gm[:half] = grad_mid.astype(BF)
        gm_send.start()

    def mixture_grads():
        wait("w", "mix")
        dout[...] = nt(gm[:half], k[...]).astype(BF)
        start("k")
        for j in range(8):
            cols = slice(j * 128, j * 128 + 128)
            products = (v[:half, cols].astype(F32) * dout[:, cols].astype(F32)).T
            for e in range(2):
                centres[j, e : e + 1] = jnp.sum(products[64 * e : 64 * e + 64], axis=0, keepdims=True)
        start("v")

    def out_term():
        wait("mt")
        gm_send.wait()
        put(outs, 0, nn(mt[...], gm[...]), 512)
        start("nt")

    def kv_rows(s):
        return pl.ds(s * half if isinstance(s, int) else pl.multiple_of(s * half, half), half)

    def kv_send(u):
        s = lax.rem(u, 2)
        return remote(dx_kv, kvl.at[s], kvs.at[s], kvr.at[s], sib)

    def gq_send(u):
        s = lax.rem(u, 2)
        return remote(gq.at[s, own_rows], gq.at[s, sib_rows], gqs.at[s], gqr.at[s], sib)

    def stashed(b, n, j):
        return jnp.concatenate([kept[b, pl.ds(n * 128, 128), pl.ds(m * 256 + j * 128, 128)] for m in range(4)], axis=0)

    def heads_back(p):
        u, j = p // 2, lax.rem(p, 2)
        s = lax.rem(u, 2)
        col = lanes(p * 128, 128)
        queries = q[:, col] * jnp.asarray(0.125, BF)
        keys, values, do = k[:, col], v[:, col], dout[:, col]
        kt = keys.T
        none = jnp.zeros_like(queries)
        dqs, dks, dvs = [], [], []
        for e in range(2):
            part = (lane < 64) if e == 0 else (lane >= 64)
            prob = jnp.exp(nt(keys, jnp.where(part, queries, none)) + bias[...].astype(F32) - lse[p, e : e + 1, :])
            dvs.append(nn(prob.astype(BF), do))
            ds = (prob * (nt(values, jnp.where(part, do, none)) - centres[p, e : e + 1, :])).astype(BF)
            dks.append(nn(ds, queries))
            dqs.append(nn(kt, ds))
        dq = jnp.concatenate([dqs[0][:64], dqs[1][64:]], axis=0).T
        dk = jnp.where(lane < 64, dks[0], dks[1]).astype(BF)
        dv = jnp.where(lane < 64, dvs[0], dvs[1]).astype(BF)
        for n, part in enumerate(((dq * 0.125).astype(BF), dk, dv)):
            for m in range(4):
                kept[s, pl.ds(n * 128, 128), lanes(m * 256 + j * 128, 128)] = part[m * 128 : m * 128 + 128]

        @pl.when((j == 0) & (u >= 1))
        def _():
            kv_send(u - 1).wait_send()

        dx_kv[:, lanes(j * 128, 128)] = dk[half:]
        dx_kv[:, lanes(256 + j * 128, 128)] = dv[half:]

    def heads_close(u):
        b = lax.rem(u, 2)

        @pl.when(u >= 2)
        def _():
            gq_send(u - 2).wait_send()

        kv_send(u).wait_recv()
        for j in range(2):
            c = slice(j * 128, j * 128 + 128)
            gq[b, :half, c] = rope_back(stashed(b, 0, j).astype(F32), cosine[...], sine[...]).astype(BF)
            g = added(stashed(b, 1, j), kvl[b, :, c]).astype(F32)
            gq[b, :half, 256 + j * 128 : 384 + j * 128] = rope_back(g, cosine[...], sine[...]).astype(BF)
            gq[b, :half, 512 + j * 128 : 640 + j * 128] = added(stashed(b, 2, j), kvl[b, :, 256 + j * 128 : 384 + j * 128])
        for c in qkv_weights(u):
            c.wait()
        back = nt(gq[b, :half], win[...].reshape(width, 768))

        @pl.when(u == 0)
        def _():
            acc_g[...] = back

        @pl.when(u > 0)
        def _():
            acc_g[...] += back

        @pl.when(u < 3)
        def _():
            for c in qkv_weights(u + 1):
                c.start()

    def qkv_term(u):
        gq_send(u).wait_recv()
        put(wide, STEPS + u, nn(mt[...], gq[u % 2]), GROUP)

    def first_norm():
        wait("r0", "r1")
        back, terms[0:1] = norm_back(k[:half].astype(F32), gains[0:1], acc_g[...])
        dout[...] = (acc_f[...] + back).astype(BF)

    gs_send = remote(gs, gr, ps.at[1], pr.at[1], sib)

    def gain_terms():
        for n in range(2):
            for o in range(4):
                for ref, part in ((gain.acc.at[0], h.core), (gs, 1 - h.core)):
                    low, high = terms[n : n + 1, 256 * o : 256 * o + 128], terms[n : n + 1, 256 * o + 128 : 256 * o + 256]
                    value = jnp.where(part == 0, low, high)
                    ref[n, o // 2, o % 2] = jnp.broadcast_to(value, (16, 128)).astype(BF)
        gs_send.start()
        gs_send.wait()
        for n in range(2):
            for o in range(4):
                gain.acc[0, n, o // 2, o % 2] = added(gain.acc[0, n, o // 2, o % 2], gr[n, o // 2, o % 2])

    def dx(j):
        return kvl.at[j, pl.ds(0, SHARD), pl.ds(0, 256)]

    def down_swap(j, act, ref):
        act(remote(ref.at[j, 1 - h.core], dx(j), dxs.at[j], dxr.at[j], sib))

    def to_end(j):
        return pltpu.make_async_copy(dx(j), down_o.at[:, lanes((1 - h.core) * 512 + j * 256, 256)], fo.at[2, 5 + j])

    def write(name, t, act, ref):
        if name == "w" and t < STEPS:
            for n in range(2):
                act(pltpu.make_async_copy(ref.at[t, n], in_o.at[n, :, pl.ds(t * GROUP, GROUP)], fo.at[0, 2 * t + n]))
        elif name == "w":
            parts = ((0, 0, 256, 0), (0, 256, 128, 1024), (1, 0, 128, 1152), (1, 128, 256, 2048))
            for n, (m, at_col, size, to) in enumerate(parts):
                dst = qkv_o.at[:, pl.ds(to + (t - STEPS) * 256, size)]
                act(pltpu.make_async_copy(ref.at[t, m, :, pl.ds(at_col, size)], dst, fo.at[1, 4 * (t - STEPS) + n]))
        elif name == "d":
            dst = down_o.at[:, lanes(h.core * 512 + t * 256, 256)]
            act(pltpu.make_async_copy(ref.at[t, h.core], dst, fo.at[2, 3 + t]))
        elif name == "o":
            for n in range(2):
                act(pltpu.make_async_copy(ref.at[0, n], out_o.at[:, pl.ds(n * 512, 512)], fo.at[2, n]))
        else:
            act(pltpu.make_async_copy(ref, gain_o, fo.at[2, 2]))

    sent = [0, 0]

    def piece(which):
        size = block // PIECES
        part = pl.ds(sent[which] * size, size)
        sent[which] += 1
        if which == 0:
            rows.start(ffn_h, outh_o, es.at[0], er.at[0], el.at[0], False, part)
        else:
            rows.start(Halves(dout), inh_o, es.at[1], er.at[1], el.at[1], False, part)

    work = {"ln2": second_norm, "do": mixture_grads, "og": out_term, "H": first_norm, "gains": gain_terms}

    def perform(ops):
        for op in ops:
            if op[0] == "c":
                if op[1] in work:
                    work[op[1]]()
            elif op[0] == "r":
                piece(op[1])
            else:
                (name, t), group = op[1], groups[op[1][0]]
                if op[0] == "s":
                    getattr(group, Sums.LATER[op[2]])(t)
                    if op[2] == 5:
                        group.total(functools.partial(write, name, t, lambda c: c.start()))
                        if name == "d":
                            down.total(functools.partial(down_swap, t, lambda c: c.start()))
                else:
                    if name == "w":
                        in_term(t) if t < STEPS else qkv_term(t - STEPS)
                    elif name == "d":
                        down_term(t)
                    group.begin(t)

    before, loop, after = split_plan()
    perform(before)
    wait("bias", "q", "k", "v", "nt")
    for c in qkv_weights(0):
        c.start()

    def each(p, _):
        pl.when(p < 8)(lambda: heads_back(p))
        pl.when(p == 8)(lambda: start("r0", "r1"))
        for n in range(10):
            if loop[n, 0]:
                pl.when(p == n)(functools.partial(perform, loop[n, 0]))

        @pl.when((lax.rem(p, 2) == 1) & (p >= 3))
        def _():
            heads_close((p - 3) // 2)

        for n in range(10):
            if loop[n, 1]:
                pl.when(p == n)(functools.partial(perform, loop[n, 1]))
            if loop[n, 2]:
                pl.when(p == n)(functools.partial(perform, loop[n, 2]))

        @pl.when((lax.rem(p, 2) == 1) & (p < 8))
        def _():
            kv_send(p // 2).start()

        @pl.when((lax.rem(p, 2) == 1) & (p >= 3))
        def _():
            gq_send((p - 3) // 2).start()

        return 0

    lax.fori_loop(0, 10, each, 0)
    perform(after)
    for j in range(2):
        down.total(functools.partial(down_swap, j, lambda c: c.wait()))
        to_end(j).start()
    kv_send(3).wait_send()
    gq_send(2).wait_send()
    gq_send(3).wait_send()

    for name, group in groups.items():
        for t in group.slot:
            group.total(functools.partial(write, name, t, lambda c: c.wait()))
    for j in range(2):
        to_end(j).wait()
    rows.wait(ffn_h, outh_o, es.at[0], er.at[0], el.at[0], False)
    rows.wait(Halves(dout), inh_o, es.at[1], er.at[1], el.at[1], False)


def back_all(ffn_rows, *args):
    dma = pltpu.SemaphoreType.DMA
    block, wide = ffn_rows.shape[1:]
    half = 2 * block

    def buf(*s, kind=BF):
        return pltpu.VMEM(s, kind)

    def shape(*s):
        return jax.ShapeDtypeStruct(s, BF)

    whole = pl.BlockSpec(memory_space=pltpu.VMEM)
    scratch = [
        buf(half, wide, kind=F32), buf(half, wide, kind=F32), buf(8, 128, 768),
        buf(half, 2 * half), buf(half, 2 * half), buf(2 * half, 768), buf(2, 2 * half, 768),
        buf(STEPS * GROUP, 2 * half), buf(2 * half, half), buf(2 * half, wide), buf(half, wide),
        buf(half, wide), buf(2 * half, wide), buf(2 * half, wide), buf(2 * half, half),
        buf(2, GROUP, wide), buf(half, 512), buf(2, half, 512), buf(8, 2, half, kind=F32), buf(2, wide, kind=F32),
        buf(2, 2, 2, 16, 128), buf(2, 2, 2, 16, 128),
        dma((13,)), dma((1,)), dma((3,)), dma((2,)), dma((2,)), dma((2,)), dma((2,)), dma((2,)), dma((2,)),
        dma((2,)), dma((2,)), dma((3, 16)), dma((2, 2)), dma((2, 2)), dma((2,)),
    ]
    for s in ((11, WIDE_SLOTS, 128, GROUP), (2, 2, SHARD, 256), (1, 1, 128, 512), (1, 1, 16, 128)):
        scratch += Sums.scratch(*s)
    return pl.pallas_call(
        back_kernel,
        out_shape=[
            shape(2, 128, STEPS * GROUP), shape(128, 3 * wide), shape(SHARD, wide), shape(128, wide), shape(1, 2, 16, 128),
            shape(2, block, wide), shape(2, block, wide),
        ],
        in_specs=[ANY] * 18 + [whole] * 4,
        out_specs=[ANY] * 7,
        scratch_shapes=scratch,
        compiler_params=pltpu.CompilerParams(collective_id=2, has_side_effects=True, vmem_limit_bytes=VMEM_BYTES),
        name="backward_and_sums",
    )(ffn_rows, *args)


def lay_out_kernel(in_ref, down_ref, parts_ref, rows_ref):
    shard = in_ref.shape[1] // 16
    spare = jnp.zeros((in_ref.shape[0], SHARD - shard), F32)
    for m in range(2):
        pieces = []
        for n in range(8 * m, 8 * m + 8):
            pieces += [in_ref[:, n * shard : (n + 1) * shard].astype(F32), spare]
        parts_ref[m] = jnp.concatenate(pieces, axis=1).astype(BF)
    row = lax.broadcasted_iota(jnp.int32, down_ref.shape, 0) + pl.program_id(0) * down_ref.shape[0]
    rows_ref[...] = jnp.where(row < shard, down_ref[...].astype(F32), 0.0).astype(BF)


def lay_out(in_weight, down_weight):
    depth, wide = in_weight.shape[0], down_weight.shape[1]
    part = depth // 4
    return pl.pallas_call(
        lay_out_kernel,
        grid=(4,),
        in_specs=[pl.BlockSpec((part, in_weight.shape[1]), lambda i: (i, 0)), pl.BlockSpec((96, wide), lambda i: (i, 0))],
        out_specs=[pl.BlockSpec((2, part, 8 * SHARD), lambda i: (0, i, 0)), pl.BlockSpec((96, wide), lambda i: (i, 0))],
        out_shape=[jax.ShapeDtypeStruct((2, depth, 8 * SHARD), BF), jax.ShapeDtypeStruct((SHARD, wide), BF)],
        compiler_params=pltpu.CompilerParams(vmem_limit_bytes=VMEM_BYTES),
        name="lay_out_weights",
    )(in_weight, down_weight)


def results_kernel(out_b, grad_b, qkv_b, proj_b, in_b, down_b, out_r, grad_r, qkv_r, proj_r, in_r, down_r):
    for src, dst in ((out_b, out_r), (grad_b, grad_r), (qkv_b, qkv_r), (proj_b, proj_r), (down_b, down_r)):
        dst[...] = src[...].astype(F32)
    shard = in_r.shape[1] // 16
    pieces = []
    for m in range(2):
        whole = in_b[m].astype(F32)
        pieces += [whole[:, n * SHARD : n * SHARD + shard] for n in range(8)]
    in_r[...] = jnp.concatenate(pieces, axis=1)


def results(out_home, in_home, qkv_t, out_t, in_t, down_t, shard):
    block, wide = out_home.shape[1:]
    depth = qkv_t.shape[0]
    part = depth // 4

    def rows(size, width):
        return pl.BlockSpec((size, width), lambda i: (i, 0))

    home = pl.BlockSpec((2, block // 4, wide), lambda i: (0, i, 0))
    return pl.pallas_call(
        results_kernel,
        grid=(4,),
        in_specs=[home, home, rows(part, 3 * wide), rows(part, wide),
                  pl.BlockSpec((2, part, in_t.shape[2]), lambda i: (0, i, 0)), rows(96, wide)],
        out_specs=[home, home, rows(part, 3 * wide), rows(part, wide), rows(part, 16 * shard), rows(96, wide)],
        out_shape=[
            jax.ShapeDtypeStruct(out_home.shape, F32), jax.ShapeDtypeStruct(in_home.shape, F32),
            jax.ShapeDtypeStruct(qkv_t.shape, F32), jax.ShapeDtypeStruct(out_t.shape, F32),
            jax.ShapeDtypeStruct((depth, 16 * shard), F32), jax.ShapeDtypeStruct((shard, wide), F32),
        ],
        compiler_params=pltpu.CompilerParams(vmem_limit_bytes=VMEM_BYTES),
        name="results_to_float32",
    )(out_home, in_home, qkv_t, out_t, in_t, down_t)


def chip_streams(tokens, cotangent, doc_starts, qkv_weight, out_weight, in_weight, down_weight, attn_gain, ffn_gain):
    wide = tokens.shape[3]
    shard = down_weight.shape[0]
    in_parts, down_rows = lay_out(in_weight, down_weight)
    inverse = ROPE_THETA ** (-np.arange(0, HEAD_DIM, 2) / HEAD_DIM)
    (qkv_f, out_f, cot, rows_low, middle, gn, ffn_rows, q, k, v, mixture, bias, xt, mt, nt_rows, glc, gj, at,
     both_gains, cosine, sine, lse) = front_all(
        attn_gain[None], ffn_gain[None], qkv_weight, out_weight, in_parts, down_rows,
        tokens[:, 0], cotangent[:, 0], doc_starts[:, 0], np.tile(inverse, 4)[None].astype(np.float32),
    )
    in_t, qkv_t, down_t, out_t, gain_t, out_home, in_home = back_all(
        ffn_rows, middle, gn, cot, qkv_f, out_f.reshape(wide, wide), q, k, v, mixture, rows_low, bias, xt, mt, nt_rows, glc, gj, at,
        both_gains, cosine, sine, lse,
    )
    output, tokens_grad, qkv_grad, out_grad, in_grad, down_grad = results(out_home, in_home, qkv_t, out_t, in_t, down_t, shard)
    return (
        output[:, None],
        tokens_grad[:, None],
        qkv_grad,
        out_grad,
        in_grad,
        down_grad,
        gain_t[0, 0, 0].astype(F32),
        gain_t[0, 1, 0].astype(F32),
    )


def solution(mesh):
    whole_chips = dict(mesh.shape) == {"seq": 4, "fsdp": 8}
    return jax.shard_map(
        chip_streams if whole_chips else shards,
        mesh=mesh,
        in_specs=(
            P(None, "fsdp", "seq", None),
            P(None, "fsdp", "seq", None),
            P(None, "fsdp", None),
            P("fsdp", None),
            P("fsdp", None),
            P("fsdp", None),
            P("fsdp", None),
            P("fsdp"),
            P("fsdp"),
        ),
        out_specs=(
            P(None, "fsdp", "seq", None),
            P(None, "fsdp", "seq", None),
            P("fsdp", None),
            P("fsdp", None),
            P("fsdp", None),
            P("fsdp", None),
            P("fsdp"),
            P("fsdp"),
        ),
        check_vma=False,
    )
```

```python
import functools
from functools import partial

import jax
import jax.numpy as jnp
import numpy as np
from jax import lax
from jax.experimental import pallas as pl
from jax.experimental.pallas import tpu as pltpu
from jax.sharding import PartitionSpec as P

HEADS = 16
HEAD_DIM = 64


EPSILON = 1e-05
ROPE_THETA = 160000.0
MASKED_SCORE = -1e30


def as_sent(x):

    def short(part):
        return part.astype(jnp.bfloat16) if part.dtype == jnp.float32 else part

    return jax.tree.map(short, x)


def layer_norm(values, norm_gain):
    average = jnp.mean(values, axis=-1, keepdims=True)
    centred = values - average
    spread = jnp.mean(centred * centred, axis=-1, keepdims=True)
    return centred * lax.rsqrt(spread + EPSILON) * norm_gain


def gated_gelu(joined):
    half_width = joined.shape[-1] // 2
    return jax.nn.gelu(joined[:, :half_width], approximate=False) * joined[:, half_width:]


def rotate(values, cosine_table, sine_table):
    half_width = values.shape[-1] // 2
    turned = jnp.concatenate([-values[..., half_width:], values[..., :half_width]], axis=-1)
    return values * cosine_table + turned * sine_table


def rope_tables(starts, places, head_width):
    preceding = starts[None, :] <= places[:, None]
    doc_begin = jnp.max(jnp.where(preceding, starts[None, :], 0), axis=-1)
    offsets = (places - doc_begin).astype(jnp.float32)
    inverse = ROPE_THETA ** (-jnp.arange(0, head_width, 2, dtype=jnp.float32) / head_width)
    angles = offsets[:, None] * inverse[None, :]
    angles = jnp.concatenate([angles, angles], axis=-1)
    return (jnp.cos(angles), jnp.sin(angles))


def segment_ids(starts, places):
    return jnp.sum((starts[None, :] <= places[:, None]).astype(jnp.int32), axis=-1) - 1


def turn_pair(pair, cosine_table, sine_table):
    shaped = pair.reshape(pair.shape[0], 2, HEADS, HEAD_DIM)
    turned = rotate(shaped, cosine_table[:, None, None, :], sine_table[:, None, None, :])
    return turned.reshape(pair.shape[0], 2 * HEADS * HEAD_DIM)


def attend_forward(queries, keys_in, values_in, segments, head_count):
    length = queries.shape[0]
    head_width = queries.shape[1] // head_count
    block_rows = min(512, length)
    blocks = length // block_rows
    keyset = keys_in.reshape(length, head_count, head_width)
    valueset = values_in.reshape(length, head_count, head_width)
    factor = head_width ** (-0.5)

    def one_block(pieces):
        query_rows, block_segs = pieces
        scores = (
            jnp.einsum("qhd,khd->hqk", query_rows, keyset, preferred_element_type=jnp.float32)
            * factor
        )
        scores = jnp.where((block_segs[:, None] == segments[None, :])[None], scores, MASKED_SCORE)
        row_max = jnp.max(scores, axis=-1, keepdims=True)
        totals = jnp.sum(jnp.exp(scores - row_max), axis=-1, keepdims=True)
        logsums = row_max + jnp.log(totals)
        weights = jnp.exp(scores - logsums).astype(jnp.bfloat16)
        mixture = jnp.einsum("hqk,khd->qhd", weights, valueset, preferred_element_type=jnp.float32)
        return (mixture, logsums)

    mixture, logsums = lax.map(
        one_block,
        (
            queries.reshape(blocks, block_rows, head_count, head_width),
            segments.reshape(blocks, block_rows),
        ),
    )
    return (mixture.reshape(length, head_count * head_width), logsums)


def attend_backward(queries, keys_in, values_in, grads_in, segments, logsums, head_count):
    length = queries.shape[0]
    head_width = queries.shape[1] // head_count
    block_rows = min(512, length)
    blocks = length // block_rows
    keyset = keys_in.reshape(length, head_count, head_width)
    valueset = values_in.reshape(length, head_count, head_width)
    factor = head_width ** (-0.5)

    def one_block(carry, pieces):
        key_grad, value_grad = carry
        query_rows, block_segs, grad_rows, block_lse = pieces
        scores = (
            jnp.einsum("qhd,khd->hqk", query_rows, keyset, preferred_element_type=jnp.float32)
            * factor
        )
        scores = jnp.where((block_segs[:, None] == segments[None, :])[None], scores, MASKED_SCORE)
        weights = jnp.exp(scores - block_lse)
        value_grad = value_grad + jnp.einsum(
            "hqk,qhd->khd",
            weights.astype(jnp.bfloat16),
            grad_rows,
            preferred_element_type=jnp.float32,
        )
        grad_weights = jnp.einsum(
            "qhd,khd->hqk", grad_rows, valueset, preferred_element_type=jnp.float32
        )
        centre = jnp.sum(weights * grad_weights, axis=-1, keepdims=True)
        grad_scores = (weights * (grad_weights - centre)).astype(jnp.bfloat16)
        query_grad = (
            jnp.einsum("hqk,khd->qhd", grad_scores, keyset, preferred_element_type=jnp.float32)
            * factor
        )
        key_grad = (
            key_grad
            + jnp.einsum(
                "hqk,qhd->khd", grad_scores, query_rows, preferred_element_type=jnp.float32
            )
            * factor
        )
        return ((key_grad, value_grad), query_grad)

    empty = jnp.zeros((length, head_count, head_width), jnp.float32)
    pieces = (
        queries.reshape(blocks, block_rows, head_count, head_width),
        segments.reshape(blocks, block_rows),
        grads_in.reshape(blocks, block_rows, head_count, head_width),
        logsums,
    )
    (key_grad, value_grad), query_grad = lax.scan(one_block, (empty, empty), pieces)
    flat_shape = (length, head_count * head_width)
    return (
        query_grad.reshape(flat_shape).astype(jnp.bfloat16),
        key_grad.reshape(flat_shape).astype(jnp.bfloat16),
        value_grad.reshape(flat_shape).astype(jnp.bfloat16),
    )


def shards(
    tokens,
    cotangent,
    doc_starts,
    qkv_weight,
    out_weight,
    in_weight,
    down_weight,
    attn_gain,
    ffn_gain,
):
    micro_count = tokens.shape[0]
    token_rows = tokens.shape[2]
    model_width = tokens.shape[3]
    seq_count = lax.axis_size("seq")
    head_count = HEADS // seq_count
    places = lax.axis_index("seq") * token_rows + jnp.arange(token_rows, dtype=jnp.int32)
    everywhere = jnp.arange(token_rows * seq_count, dtype=jnp.int32)
    outputs = []
    input_grads = []
    full_terms = None
    shard_terms = None
    for micro_step in range(micro_count):
        rows_in = tokens[micro_step, 0]
        starts = doc_starts[micro_step, 0]
        cosine_table, sine_table = rope_tables(starts, places, HEAD_DIM)
        segments = segment_ids(starts, everywhere)
        attn_set = (
            lax.all_gather(qkv_weight, "fsdp", axis=0, tiled=True),
            lax.all_gather(out_weight, "fsdp", axis=0, tiled=True),
            lax.all_gather(attn_gain, "fsdp", axis=0, tiled=True),
        )
        qkv_full, out_full, gain_one = attn_set
        normed, norm_back = jax.vjp(layer_norm, rows_in, gain_one.astype(jnp.float32))
        normed_low = normed.astype(jnp.bfloat16)
        qkv_rows = jnp.dot(normed_low, qkv_full, preferred_element_type=jnp.float32)
        turned, turn_back = jax.vjp(
            partial(turn_pair, cosine_table=cosine_table, sine_table=sine_table),
            qkv_rows[:, : 2 * model_width],
        )
        queries = turned[:, :model_width].astype(jnp.bfloat16)
        keyset = turned[:, model_width:].astype(jnp.bfloat16)
        valueset = qkv_rows[:, 2 * model_width :].astype(jnp.bfloat16)
        query_heads, key_heads, value_heads = (
            lax.all_to_all(queries, "seq", split_axis=1, concat_axis=0, tiled=True),
            lax.all_to_all(keyset, "seq", split_axis=1, concat_axis=0, tiled=True),
            lax.all_to_all(valueset, "seq", split_axis=1, concat_axis=0, tiled=True),
        )
        mixture, logsums = attend_forward(query_heads, key_heads, value_heads, segments, head_count)
        mixture_rows = lax.all_to_all(
            mixture.astype(jnp.bfloat16), "seq", split_axis=0, concat_axis=1, tiled=True
        )
        middle = rows_in + jnp.dot(mixture_rows, out_full, preferred_element_type=jnp.float32)
        ffn_set = (
            lax.all_gather(in_weight, "fsdp", axis=0, tiled=True),
            lax.all_gather(down_weight, "fsdp", axis=0, tiled=True),
            lax.all_gather(ffn_gain, "fsdp", axis=0, tiled=True),
        )
        in_full, down_full, gain_two = ffn_set
        normed_two, norm_back_two = jax.vjp(layer_norm, middle, gain_two.astype(jnp.float32))
        normed_two_low = normed_two.astype(jnp.bfloat16)
        joined = jnp.dot(normed_two_low, in_full, preferred_element_type=jnp.float32)
        active, gelu_back = jax.vjp(gated_gelu, joined)
        active_low = active.astype(jnp.bfloat16)
        outputs.append(middle + jnp.dot(active_low, down_full, preferred_element_type=jnp.float32))
        grad_out = cotangent[micro_step, 0]
        grad_low = grad_out.astype(jnp.bfloat16)
        ffn_set = (
            lax.all_gather(in_weight, "fsdp", axis=0, tiled=True),
            lax.all_gather(down_weight, "fsdp", axis=0, tiled=True),
            lax.all_gather(ffn_gain, "fsdp", axis=0, tiled=True),
        )
        in_full, down_full, gain_two = ffn_set
        down_term = jnp.dot(active_low.T, grad_low, preferred_element_type=jnp.float32)
        grad_active = jnp.dot(grad_low, down_full.T, preferred_element_type=jnp.float32)
        grad_joined = gelu_back(grad_active)[0].astype(jnp.bfloat16)
        in_term = jnp.dot(normed_two_low.T, grad_joined, preferred_element_type=jnp.float32)
        grad_normed_two = jnp.dot(grad_joined, in_full.T, preferred_element_type=jnp.float32)
        grad_middle_norm, gain_two_term = norm_back_two(grad_normed_two)
        grad_middle = grad_out + grad_middle_norm
        grad_mid_low = grad_middle.astype(jnp.bfloat16)
        attn_set = (
            lax.all_gather(qkv_weight, "fsdp", axis=0, tiled=True),
            lax.all_gather(out_weight, "fsdp", axis=0, tiled=True),
            lax.all_gather(attn_gain, "fsdp", axis=0, tiled=True),
        )
        qkv_full, out_full, gain_one = attn_set
        out_term = jnp.dot(mixture_rows.T, grad_mid_low, preferred_element_type=jnp.float32)
        grad_mixture = jnp.dot(grad_mid_low, out_full.T, preferred_element_type=jnp.float32).astype(
            jnp.bfloat16
        )
        grad_heads = lax.all_to_all(grad_mixture, "seq", split_axis=1, concat_axis=0, tiled=True)
        query_grad, key_grad, value_grad = attend_backward(
            query_heads, key_heads, value_heads, grad_heads, segments, logsums, head_count
        )
        query_back, key_back, value_back = (
            lax.all_to_all(query_grad, "seq", split_axis=0, concat_axis=1, tiled=True),
            lax.all_to_all(key_grad, "seq", split_axis=0, concat_axis=1, tiled=True),
            lax.all_to_all(value_grad, "seq", split_axis=0, concat_axis=1, tiled=True),
        )
        grad_pair = turn_back(jnp.concatenate([query_back, key_back], axis=1).astype(jnp.float32))[
            0
        ]
        grad_qkv = jnp.concatenate([grad_pair, value_back.astype(jnp.float32)], axis=1).astype(
            jnp.bfloat16
        )
        qkv_term = jnp.dot(normed_low.T, grad_qkv, preferred_element_type=jnp.float32)
        grad_normed = jnp.dot(grad_qkv, qkv_full.T, preferred_element_type=jnp.float32)
        grad_rows_norm, gain_one_term = norm_back(grad_normed)
        input_grads.append(grad_middle + grad_rows_norm)
        terms = (qkv_term, out_term, in_term, down_term, gain_one_term, gain_two_term)
        full_terms = terms if full_terms is None else jax.tree.map(jnp.add, full_terms, terms)
    shard_terms = jax.tree.map(
        lambda part: part.astype(jnp.float32),
        lax.psum_scatter(as_sent(full_terms), "fsdp", scatter_dimension=0, tiled=True),
    )
    totals = jax.tree.map(
        lambda part: part.astype(jnp.float32), lax.psum(as_sent(shard_terms), "seq")
    )
    return (
        jnp.stack(outputs)[:, None],
        jnp.stack(input_grads)[:, None],
        totals[0],
        totals[1],
        totals[2],
        totals[3],
        totals[4],
        totals[5],
    )


MESH = pl.DeviceIdType.MESH
ANY = pl.BlockSpec(memory_space=pl.ANY)
VMEM_BYTES = 127 * 2**19
BF = jnp.bfloat16
F32 = jnp.float32


def nn(a, b):
    return lax.dot_general(a, b, (((1,), (0,)), ((), ())), preferred_element_type=F32)


def nt(a, b):
    return lax.dot_general(a, b, (((1,), (1,)), ((), ())), preferred_element_type=F32)


def spot():
    z, f = lax.axis_index("seq"), lax.axis_index("fsdp")
    core = lax.rem(f, 2)
    x = lax.rem(f // 2, 2)
    y = f // 4
    return z, f, y, x, core


def remote(src, dst, send, recv, where):
    return pltpu.make_async_remote_copy(
        src_ref=src, dst_ref=dst, send_sem=send, recv_sem=recv, device_id=where, device_id_type=MESH
    )


class Rows:
    def __init__(self, z, f, core):
        base = f - core
        self.work, self.home = [], []
        for i in range(2):
            zw, cw = 2 * i + core, z // 2
            self.work.append((zw, base + cw, (zw == z) & (cw == core)))
            zh, ch = 2 * core + i, lax.rem(z, 2)
            self.home.append((zh, base + ch, (zh == z) & (ch == core)))
        self.z = z

    def greet(self, barrier):
        count = 0
        for zt, ft, same in self.work + self.home:

            @pl.when(jnp.logical_not(same))
            def _():
                pl.semaphore_signal(barrier, inc=1, device_id=(zt, ft), device_id_type=MESH)

            count = count + jnp.where(same, 0, 1)
        return count

    def start(self, src, dst, send, recv, local, out, piece=slice(None)):
        places = self.work if out else self.home
        slot = lax.rem(self.z, 2) if out else self.z // 2
        for i, (zt, ft, same) in enumerate(places):

            @pl.when(same)
            def _(i=i):
                pltpu.make_async_copy(src.at[i, piece], dst.at[slot, piece], local).start()

            @pl.when(jnp.logical_not(same))
            def _(i=i, zt=zt, ft=ft):
                remote(src.at[i, piece], dst.at[slot, piece], send.at[i], recv.at[slot], (zt, ft)).start()

    def wait(self, src, dst, send, recv, local, out):
        goes, comes = (self.work, self.home) if out else (self.home, self.work)
        for i, (zt, ft, same) in enumerate(goes):

            @pl.when(same)
            def _(i=i):
                pltpu.make_async_copy(src.at[i], dst.at[i], local).wait()

            @pl.when(jnp.logical_not(same))
            def _(i=i, zt=zt, ft=ft):
                remote(src.at[i], dst.at[i], send.at[i], recv.at[i], (zt, ft)).wait_send()

        for i, (zt, ft, same) in enumerate(comes):

            @pl.when(jnp.logical_not(same))
            def _(i=i, zt=zt, ft=ft):
                remote(src.at[i], dst.at[i], send.at[i], recv.at[i], (zt, ft)).wait_recv()


def halves(width):
    cut = (width // 128 // 2) * 128
    return pl.ds(0, cut), pl.ds(cut, width - cut)


SQRT_HALF = 0.7071067811865476
DENSITY = 0.3989422804014327
BY_Z = (2, 4)
SHARD = 336
GROUP = 384
STEPS = 7


def moments(values):
    average = jnp.mean(values, axis=-1, keepdims=True)
    centred = values - average
    spread = jnp.mean(centred * centred, axis=-1, keepdims=True)
    scale = lax.rsqrt(spread + EPSILON)
    return centred * scale, scale


def norm_back(values, gain, grads):
    unit, scale = moments(values)
    spread = grads * gain
    inner = spread - jnp.mean(spread, axis=-1, keepdims=True)
    inner = inner - unit * jnp.mean(spread * unit, axis=-1, keepdims=True)
    return inner * scale, jnp.sum(grads * unit, axis=0, keepdims=True)


def rope_back(grads, cosine, sine):
    lane = lax.broadcasted_iota(jnp.int32, (1, 128), 1)
    low = lax.rem(lane, 64) < 32
    u = grads * sine
    return grads * cosine + jnp.where(low, pltpu.roll(u, 96, 1), -pltpu.roll(u, 32, 1))


class Sums:
    KINDS = 9

    @staticmethod
    def scratch(count, slots, rows, wide):
        dma = pltpu.SemaphoreType.DMA((count, Sums.KINDS))
        shapes = [(slots, 2, 2, 2), (count, 2, 2), (count, 2), (count, 2), (count,)]
        return [pltpu.VMEM(s + (rows, wide), BF) for s in shapes] + [dma, dma]

    def __init__(self, here, refs, slot):
        self.here, self.slot = here, slot
        self.acc, self.rx, self.r2, self.zr, self.zr2, self.send, self.recv = refs

    def copy(self, t, kind):
        h = self.here
        acc = self.acc.at[self.slot[t]]
        plan = {
            0: lambda: (acc.at[0, :, 1 - h.x], self.rx.at[t, 0], (h.z, h.fx)),
            1: lambda: (acc.at[1, 1 - h.y], self.rx.at[t, 1], (h.z, h.fy)),
            2: lambda: (self.rx.at[t, 0, 1 - h.y], self.r2.at[t, 0], (h.z, h.fy)),
            3: lambda: (self.rx.at[t, 1, 1 - h.x], self.r2.at[t, 1], (h.z, h.fx)),
            4: lambda: (self.r2.at[t], self.zr.at[t], (h.near, h.f)),
            5: lambda: (self.zr.at[t, 1 - h.own], self.zr2.at[t], (h.across, h.f)),
            6: lambda: (self.r2.at[t, h.own], self.r2.at[t, h.own], (h.across, h.f)),
            7: lambda: (self.r2.at[t, h.own], self.zr.at[t, h.own], (h.near, h.f)),
            8: lambda: (self.r2.at[t, 1 - h.own], self.zr.at[t, 1 - h.own], (h.near, h.f)),
        }
        src, dst, where = plan[kind]()
        return remote(src, dst, self.send.at[t, kind], self.recv.at[t, kind], where)

    def begin(self, t):
        self.copy(t, 0).start()
        self.copy(t, 1).start()

    def cross(self, t):
        h, s = self.here, self.slot[t]
        self.copy(t, 0).wait()
        self.rx[t, 0, 1 - h.y] = added(self.rx[t, 0, 1 - h.y], self.acc[s, 0, 1 - h.y, h.x])
        self.copy(t, 2).start()
        self.copy(t, 1).wait()
        self.rx[t, 1, 1 - h.x] = added(self.rx[t, 1, 1 - h.x], self.acc[s, 1, h.y, 1 - h.x])
        self.copy(t, 3).start()

    def plane(self, t):
        h, s = self.here, self.slot[t]
        self.copy(t, 2).wait()
        self.r2[t, 0] = added(self.r2[t, 0], self.rx[t, 0, h.y], self.acc[s, 0, h.y, h.x])
        self.copy(t, 3).wait()
        self.r2[t, 1] = added(self.r2[t, 1], self.rx[t, 1, h.x], self.acc[s, 1, h.y, h.x])

        @pl.when(h.outer)
        def _():
            self.copy(t, 4).start()

    def meet(self, t):
        h = self.here

        @pl.when(jnp.logical_not(h.outer))
        def _():
            self.copy(t, 4).wait_recv()
            self.zr[t, 1 - h.own] = added(self.zr[t, 1 - h.own], self.r2[t, 1 - h.own])
            self.copy(t, 5).start()

    def sums(self, t):
        h = self.here

        @pl.when(jnp.logical_not(h.outer))
        def _():
            self.copy(t, 5).wait()
            self.r2[t, h.own] = added(self.r2[t, h.own], self.zr[t, h.own], self.zr2[t])
            self.copy(t, 6).start()
            self.copy(t, 7).start()

    def spread(self, t):
        @pl.when(jnp.logical_not(self.here.outer))
        def _():
            self.copy(t, 6).wait_recv()
            self.copy(t, 8).start()

    def finish(self, t):
        @pl.when(jnp.logical_not(self.here.outer))
        def _():
            self.copy(t, 6).wait_send()
            self.copy(t, 7).wait_send()
            self.copy(t, 8).wait_send()

        @pl.when(self.here.outer)
        def _():
            self.copy(t, 4).wait_send()
            self.copy(t, 7).wait_recv()
            self.copy(t, 8).wait_recv()

    def total(self, act):
        for ref, there in ((self.zr, self.here.outer), (self.r2, jnp.logical_not(self.here.outer))):
            pl.when(there)(functools.partial(act, ref))

    LATER = ("cross", "plane", "meet", "sums", "spread", "finish")


def added(*terms):
    total = terms[0].astype(F32)
    for term in terms[1:]:
        total = total + term.astype(F32)
    return total.astype(BF)


class Halves:
    def __init__(self, ref):
        self.ref, self.at, self.size = ref, self, ref.shape[0] // 2

    def __getitem__(self, index):
        i, piece = index if isinstance(index, tuple) else (index, slice(None))
        if isinstance(piece, slice):
            return self.ref.at[pl.ds(i * self.size, self.size)]
        return self.ref.at[pl.ds(i * self.size + piece.start, piece.size)]


class Here:
    def __init__(self):
        self.z, self.f, self.y, self.x, self.core = spot()
        self.fx = self.f + 2 - 4 * self.x
        self.fy = self.f + 4 - 8 * self.y
        self.fc = self.f + 1 - 2 * self.core
        z = self.z
        self.outer = (z == 0) | (z == 3)
        self.near = jnp.where(z < 2, 1 - z, 5 - z)
        self.across = jnp.where(self.outer, z, 3 - z)
        self.own = jnp.where(z < 2, 0, 1)

    def greet(self, barrier, rows, column=0):
        for n in range(column):
            pl.semaphore_signal(barrier, inc=1, device_id=(lax.rem(self.z + n + 1, 4), self.f), device_id_type=MESH)
        for t in (self.fx, self.fy, self.fc):
            pl.semaphore_signal(barrier, inc=1, device_id=(self.z, t), device_id_type=MESH)
        pl.semaphore_signal(barrier, inc=1, device_id=(self.near, self.f), device_id_type=MESH)

        @pl.when(jnp.logical_not(self.outer))
        def _():
            pl.semaphore_signal(barrier, inc=1, device_id=(self.across, self.f), device_id_type=MESH)

        pl.semaphore_wait(barrier, rows.greet(barrier) + 4 + column + jnp.where(self.outer, 0, 1))


def lanes(start, size):
    return pl.ds(start if isinstance(start, int) else pl.multiple_of(start, 128), size)


PIECES = 8
WIDE_SLOTS = 3
DOWN_FIRST = 0
PLAN = (
    ("r", 0),
    ("f", ("w", 0)),
    ("r", 0),
    ("f", ("w", 1)),
    ("c", "ln2"),
    ("r", 0),
    ("f", ("d", 0)),
    ("s", ("w", 0), 0),
    ("r", 0),
    ("c", "do"),
    ("s", ("w", 1), 0),
    ("r", 0),
    ("c", "og"),
    ("r", 0),
    ("b", ("o", 0)),
    ("c", "E0.0"),
    ("c", "E0.1"),
    ("s", ("d", 0), 0),
    ("r", 0),
    ("c", "E1.0"),
    ("s", ("w", 0), 1),
    ("s", ("w", 1), 1),
    ("r", 0),
    ("c", "E1.1"),
    ("f", ("w", 2)),
    ("c", "F0"),
    ("s", ("o", 0), 0),
    ("s", ("w", 0), 2),
    ("c", "E2.0"),
    ("s", ("d", 0), 1),
    ("s", ("w", 1), 2),
    ("f", ("w", 3)),
    ("s", ("w", 0), 3),
    ("c", "E2.1"),
    ("s", ("w", 2), 0),
    ("s", ("w", 1), 3),
    ("c", "F1"),
    ("s", ("o", 0), 1),
    ("s", ("w", 0), 4),
    ("f", ("d", 1)),
    ("s", ("w", 3), 0),
    ("s", ("w", 1), 4),
    ("s", ("d", 0), 2),
    ("c", "G0"),
    ("s", ("w", 2), 1),
    ("b", ("w", 7)),
    ("c", "E3.0"),
    ("s", ("o", 0), 2),
    ("c", "E3.1"),
    ("s", ("d", 0), 3),
    ("c", "F2"),
    ("s", ("d", 1), 0),
    ("s", ("o", 0), 3),
    ("s", ("w", 2), 2),
    ("c", "G1"),
    ("s", ("w", 3), 1),
    ("b", ("w", 8)),
    ("c", "F3"),
    ("s", ("d", 0), 4),
    ("c", "G2"),
    ("s", ("w", 7), 0),
    ("s", ("o", 0), 4),
    ("s", ("w", 3), 2),
    ("b", ("w", 9)),
    ("c", "H"),
    ("s", ("d", 1), 1),
    ("s", ("w", 2), 3),
    ("s", ("w", 3), 3),
    ("c", "gains"),
    ("b", ("g", 0)),
    ("c", "G3"),
    ("s", ("w", 8), 0),
    ("s", ("w", 2), 4),
    ("r", 1),
    ("s", ("w", 7), 1),
    ("f", ("w", 4)),
    ("s", ("w", 3), 4),
    ("r", 1),
    ("s", ("w", 9), 0),
    ("s", ("g", 0), 0),
    ("s", ("d", 1), 2),
    ("s", ("w", 8), 1),
    ("f", ("w", 5)),
    ("r", 1),
    ("s", ("w", 4), 0),
    ("s", ("d", 1), 3),
    ("s", ("w", 7), 2),
    ("s", ("w", 9), 1),
    ("s", ("g", 0), 1),
    ("f", ("w", 6)),
    ("s", ("w", 8), 2),
    ("s", ("w", 5), 0),
    ("s", ("d", 1), 4),
    ("s", ("w", 4), 1),
    ("s", ("w", 7), 3),
    ("b", ("w", 10)),
    ("s", ("w", 0), 5),
    ("s", ("w", 1), 5),
    ("s", ("d", 0), 5),
    ("s", ("o", 0), 5),
    ("s", ("w", 2), 5),
    ("s", ("w", 3), 5),
    ("r", 1),
    ("s", ("w", 8), 3),
    ("s", ("w", 9), 2),
    ("s", ("g", 0), 2),
    ("s", ("w", 7), 4),
    ("s", ("d", 1), 5),
    ("s", ("w", 6), 0),
    ("s", ("w", 5), 1),
    ("s", ("w", 4), 2),
    ("s", ("w", 8), 4),
    ("r", 1),
    ("s", ("w", 9), 3),
    ("s", ("g", 0), 3),
    ("s", ("w", 5), 2),
    ("s", ("w", 4), 3),
    ("s", ("w", 10), 0),
    ("s", ("w", 7), 5),
    ("s", ("w", 6), 1),
    ("s", ("w", 8), 5),
    ("s", ("w", 10), 1),
    ("s", ("w", 9), 4),
    ("s", ("g", 0), 4),
    ("s", ("w", 6), 2),
    ("s", ("w", 5), 3),
    ("s", ("w", 4), 4),
    ("s", ("w", 10), 2),
    ("s", ("w", 6), 3),
    ("s", ("w", 5), 4),
    ("r", 1),
    ("s", ("w", 10), 3),
    ("s", ("w", 6), 4),
    ("r", 1),
    ("s", ("w", 10), 4),
    ("r", 1),
    ("s", ("w", 9), 5),
    ("s", ("g", 0), 5),
    ("s", ("w", 4), 5),
    ("s", ("w", 5), 5),
    ("s", ("w", 6), 5),
    ("s", ("w", 10), 5),
)


def split_plan():
    before, loop, after = [], {(n, m): [] for n in range(10) for m in range(3)}, []
    place = before
    for op in PLAN:
        mark = op[1] if op[0] == "c" else ""
        if mark in ("H", "G3"):
            place = after
        elif mark[:1] == "E":
            place = loop[2 * int(mark[1]) + int(mark[3]), 0]
        elif mark[:1] == "F":
            place = loop[2 * int(mark[1]) + 3, 1]
        elif mark[:1] == "G":
            place = loop[2 * int(mark[1]) + 5, 2]
        if mark[:1] not in ("E", "F", "G") or mark == "G3":
            place.append(op)
    return before, loop, after


def rope(values, cosine, sine):
    lane = lax.broadcasted_iota(jnp.int32, (1, 128), 1)
    turned = jnp.where(lax.rem(lane, 64) < 32, -pltpu.roll(values, 96, 1), pltpu.roll(values, 32, 1))
    return values * cosine + turned * sine


def front_kernel(
    attn_h, ffn_h, qkv_h, out_h, in_h, down_h, tok_f, cot_f, starts_f, inverse,
    qkv_o, out_o, cot_o, tok_o, mid_o, gn_o, ffn_o, q_o, k_o, v_o, mix_o, bias_o, xt_o, mt_o, nt_o, glc_o, gj_o, at_o,
    gains_o, cos_o, sin_o, lse_o,
    gains_v, qkv_v, out_v, in_v, down_v, tok_v, starts_v, acc_f, acc_g, gl, normed, x2, q, k, v, mix, bias,
    gains_h, starts_h, tok_h, cot_h, gj, act, mine, theirs, rows_b,
    ss, rs, ssi, rsi, ls, lsi, es, er, el, ds_, dr, kvs, kvr, ws, ts, tr, tl, gs_, gr_, gw, as_, ar_, aw,
):
    h = Here()
    rows = Rows(h.z, h.f, h.core)
    z, f, core = h.z, h.f, h.core
    fx, fy, fc = h.fx, h.fy, h.fc
    fd = fx + 4 - 8 * h.y
    sib = (z, fc)
    half, wide = normed.shape
    block = half // 2
    own_rows, sib_rows = pl.ds(0, half), pl.ds(half, half)

    shards = (gains_h, qkv_h, out_h, down_h)
    wholes = (gains_v, qkv_v, out_v, down_v)
    targets = (fx, fy, fc, fy, fx, fc, fc, fc, fc)

    def part(w, i, cols=None):
        whole = wholes[w]
        if w < 3:
            return whole.at[i] if cols is None else whole.at[i, :, cols]
        r = pl.ds(pl.multiple_of(i * SHARD, 16), SHARD)
        return whole.at[r] if cols is None else whole.at[r, cols]

    def copy(w, k):
        a, b = halves(shards[w].shape[1])
        place = {3: (fx, a), 4: (fy, b), 5: (fx,), 6: (fy,), 7: (fd, a), 8: (fd, b)}
        dst = part(w, f) if k < 3 else part(w, *place[k])
        return remote(shards[w] if k < 3 else dst, dst, ss.at[w, k], rs.at[w, k], (z, targets[k]))

    quarter = pl.ds(pl.multiple_of(z * 32, 32), 32)

    def place_in(t, i, *more):
        return in_v.at[(t, i // 2, lax.rem(i, 2)) + more]

    def copy_in(t, k):
        cols = lanes(t * GROUP, GROUP)
        if t in BY_Z:
            if k in (0, 1):
                return remote(in_h.at[:, quarter, cols], place_in(t, f, slice(None), quarter), ssi.at[t, k], rsi.at[t, k], (z, targets[k]))
            if k in (3, 4):
                dst = place_in(t, (fx, fy)[k - 3], k - 3, quarter)
                return remote(dst, dst, ssi.at[t, k], rsi.at[t, k], (z, targets[k]))
            if k < 8:
                dst = in_v.at[t, :, core, :, quarter]
                return remote(dst, dst, ssi.at[t, k], rsi.at[t, k], (lax.rem(z + k - 4, 4), f))
            dst = in_v.at[t, :, core]
            return remote(dst, dst, ssi.at[t, k], rsi.at[t, k], sib)
        place = {3: (fx, 0), 4: (fy, 1), 5: (fx,), 6: (fy,), 7: (fd, 0), 8: (fd, 1)}
        dst = place_in(t, f) if k < 3 else place_in(t, *place[k])
        return remote(in_h.at[:, :, cols] if k < 3 else dst, dst, ssi.at[t, k], rsi.at[t, k], (z, targets[k]))

    def quarters(t, stage):
        waits, starts = (((), (0, 1)), ((0, 1), (3, 4)), ((3, 4), (5, 6, 7)), ((5, 6, 7), (8,)), ((8,), ()))[stage]
        for k in waits:
            copy_in(t, k).wait_recv()
        if stage == 2:
            own_in(t).wait()
        for k in starts:
            copy_in(t, k).start()

    def first(w, copy=copy):
        for k in range(3):
            copy(w, k).start()

    def second(w, copy=copy):
        for k in (0, 1):
            copy(w, k).wait_recv()
            copy(w, k + 3).start()
            copy(w, k + 5).start()

    def third(w, copy=copy):
        for k in (3, 4):
            copy(w, k).wait_recv()
            copy(w, k + 4).start()

    def rest(w, copy=copy):
        for k in (2, 5, 6, 7, 8):
            copy(w, k).wait_recv()

    def own(w):
        return pltpu.make_async_copy(shards[w], part(w, f), ls.at[w])

    def own_in(t):
        cols = lanes(t * GROUP, GROUP)
        if t in BY_Z:
            return pltpu.make_async_copy(in_h.at[:, quarter, cols], place_in(t, f, slice(None), quarter), lsi.at[t])
        return pltpu.make_async_copy(in_h.at[:, :, cols], place_in(t, f), lsi.at[t])

    wide_in = [
        [pltpu.make_async_copy(src.at[i], ref.at[pl.ds(i * block, block)], el.at[i]) for i in range(2)]
        for src, ref in ((tok_f, acc_f), (cot_f, acc_g))
    ]
    for c in wide_in[0]:
        c.start()
    gains_h[:, :128] = jnp.broadcast_to(attn_h[...].astype(F32), (16, 128)).astype(BF)
    gains_h[:, 128:] = jnp.broadcast_to(ffn_h[...].astype(F32), (16, 128)).astype(BF)
    starts_h[...] = jnp.zeros(starts_h.shape, jnp.int32)
    starts_h[:2, :8] = starts_f[...]
    for w in range(4):
        own(w).start()
    for t in range(STEPS):
        own_in(t).start()
    h.greet(pltpu.get_barrier_semaphore(), rows, 3)
    info = remote(starts_h, starts_v.at[core], ds_.at[0], dr.at[0], sib)
    own_info = pltpu.make_async_copy(starts_h, starts_v.at[core], el.at[2])
    info.start()
    own_info.start()
    for t in BY_Z:
        quarters(t, 0)
    for w in range(3):
        first(w)
    for c in wide_in[0]:
        c.wait()
    tok_h[...] = acc_f[...].astype(BF)
    rows.start(Halves(tok_h), tok_v, es.at[0], er.at[0], el.at[3], True)
    for c in wide_in[1]:
        c.start()
    for c in wide_in[1]:
        c.wait()
    cot_h[...] = acc_g[...].astype(BF)
    info.wait()
    own_info.wait()

    lane = lax.broadcasted_iota(jnp.int32, (1, 128), 1)
    begins = starts_v[lax.rem(z, 2), pl.ds(z // 2, 1), :]
    inside = lane < 8

    def documents(base):
        place = lax.broadcasted_iota(jnp.int32, (half, 128), 0) + base
        before = (begins <= place) & inside
        number = jnp.sum(jnp.where(before, 1.0, 0.0), axis=1, keepdims=True)
        begin = jnp.max(jnp.where(before, begins, 0).astype(F32), axis=1, keepdims=True)
        return place, number, begin

    place, number, begin = documents(core * half)
    angle = (place.astype(F32) - begin) * inverse[...]
    cos_o[...] = jnp.cos(angle)
    sin_o[...] = jnp.sin(angle)
    across = jnp.broadcast_to(number, (half, 128)).T[0:1, :]
    _, other, _ = documents((1 - core) * half)
    bias[:half] = jnp.where(number == across, 0.0, MASKED_SCORE).astype(BF)
    bias[half:] = jnp.where(other == across, 0.0, MASKED_SCORE).astype(BF)

    for t in BY_Z:
        quarters(t, 1)
    for w in range(3):
        second(w)
    rows.start(Halves(cot_h), cot_o, es.at[1], er.at[1], el.at[4], True)
    first(3)
    first(0, copy_in)
    first(1, copy_in)
    for t in BY_Z:
        quarters(t, 2)
    third(0)
    rest(0)
    own(0).wait()
    for n in range(2):
        for i in range(8):
            gains_o[n : n + 1, i * 128 : i * 128 + 128] = gains_v[i, 0:1, n * 128 : n * 128 + 128].astype(F32)
    rows.wait(Halves(tok_h), tok_v, es.at[0], er.at[0], el.at[3], True)
    saved = []

    def save(src, dst):
        saved.append(pltpu.make_async_copy(src, dst, ws.at[len(saved)]))
        saved[-1].start()

    def share(src, dst, n, again):
        keep = pltpu.make_async_copy(mine, dst.at[:, own_rows], tl.at[n])
        give = remote(theirs, dst.at[:, sib_rows], ts.at[n], tr.at[n], sib)
        if again is not None:
            again[0].wait()
            again[1].wait_send()
        for i in range(4):
            mine[i * 128 : i * 128 + 128] = src[:, lanes((2 * i + core) * 128, 128)].T
            theirs[i * 128 : i * 128 + 128] = src[:, lanes((2 * i + 1 - core) * 128, 128)].T
        keep.start()
        give.start()
        return keep, give

    unit, _ = moments(tok_v[...].reshape(half, wide).astype(F32))
    normed[...] = (unit * gains_o[0:1]).astype(BF)
    save(tok_v, tok_o)
    save(bias, bias_o)
    shared = share(normed, nt_o, 0, None)
    third(1)
    rest(1)
    own(1).wait()
    save(qkv_v, qkv_o)

    def pair_send(n, i):
        ref = (k, v)[n]
        cols = pl.ds(i * 256, 256)
        return remote(ref.at[own_rows, cols], ref.at[sib_rows, cols], kvs.at[n, i], kvr.at[n, i], sib)

    for n, ref in ((1, k), (2, v), (0, q)):
        for i in range(4):
            product = nn(normed[...], qkv_v[:, :, n * wide + i * 256 : n * wide + i * 256 + 256].reshape(wide, 256))
            for j in range(2):
                cols = slice(i * 256 + j * 128, i * 256 + j * 128 + 128)
                value = product[:, j * 128 : j * 128 + 128]
                value = value if n == 2 else rope(value, cos_o[...], sin_o[...])
                ref[:half, cols] = value.astype(BF)
            if n:
                pair_send(n - 1, i).start()
    third(2)
    for n in range(2):
        for i in range(4):
            pair_send(n, i).wait()
    for ref, dst in ((q, q_o), (k, k_o), (v, v_o)):
        save(ref, dst)

    def attend(i, _):
        @pl.when(i == 4)
        def _():
            second(3)

        @pl.when(i == 6)
        def _():
            second(0, copy_in)

        cols = lanes(i * 128, 128)
        queries = q[:, cols] * jnp.asarray(0.125, BF)
        keys = k[:, cols]
        vt = v[:, cols].T
        outs = []
        for e in range(2):
            here = (lane < 64) if e == 0 else (lane >= 64)
            scores = nt(keys, jnp.where(here, queries, jnp.zeros_like(queries))) + bias[...].astype(F32)
            top = jnp.max(scores, axis=0, keepdims=True)
            p = jnp.exp(scores - top)
            total = jnp.sum(p, axis=0, keepdims=True)
            outs.append(nn(vt, p.astype(BF)) / total)
            lse_o[i, e : e + 1, :] = top + jnp.log(total)
        mix[:, cols] = jnp.concatenate([outs[0][:64], outs[1][64:]], axis=0).T.astype(BF)
        return 0

    lax.fori_loop(0, 8, attend, 0)
    second(1, copy_in)
    first(3, copy_in)
    first(5, copy_in)
    rest(2)
    own(2).wait()
    save(out_v, out_o)
    save(mix, mix_o)
    middle = tok_v[...].reshape(half, wide).astype(F32) + nn(mix[...], out_v[...].reshape(wide, wide))
    acc_f[...] = middle
    unit, _ = moments(middle)
    x2[...] = (unit * gains_o[1:2]).astype(BF)
    mid_save = pltpu.make_async_copy(acc_f, mid_o, ls.at[4])
    mid_save.start()
    third(3)
    third(0, copy_in)
    rows.wait(Halves(cot_h), cot_o, es.at[1], er.at[1], el.at[4], True)
    cot_load = [pltpu.make_async_copy(cot_o.at[i], gl.at[pl.ds(i * block, block)], el.at[i]) for i in range(2)]
    for c in cot_load:
        c.start()
    shared = share(x2, xt_o, 1, shared)
    shared = share(mix, mt_o, 2, shared)
    for c in cot_load:
        c.wait()
    glc_keep = pltpu.make_async_copy(gl.at[:, lanes(core * 512, 512)], glc_o.at[own_rows], tl.at[3])
    glc_give = remote(gl.at[:, lanes((1 - core) * 512, 512)], glc_o.at[sib_rows], ts.at[3], tr.at[3], sib)
    glc_keep.start()
    glc_give.start()
    mid_save.wait()
    quarters(2, 3)
    rest(3)
    own(3).wait()

    def stage_copies(t):
        s = lax.rem(t, 2)
        r = lanes(t * GROUP, GROUP)
        return [
            pltpu.make_async_copy(gj.at[s], gj_o.at[t, own_rows], gw.at[s]),
            pltpu.make_async_copy(act.at[s], at_o.at[r, own_rows], aw.at[s]),
        ], [
            remote(gj.at[s], gj_o.at[t, sib_rows], gs_.at[s], gr_.at[t], sib),
            remote(act.at[s], at_o.at[r, sib_rows], as_.at[s], ar_.at[t], sib),
        ]

    def feed(t, _):
        s = lax.rem(t, 2)

        def at_step(events):
            for n, todo in events.items():

                @pl.when(t == n)
                def _(todo=todo):
                    for act, *args in todo:
                        act(*args)

        at_step({
            1: [(second, 3, copy_in), (first, 6, copy_in)],
            2: [(second, 5, copy_in), (quarters, 4, 3)],
            3: [(second, 6, copy_in)],
        })

        def ready(n):
            if n in BY_Z:
                quarters(n, 4)
            else:
                rest(n, copy_in)
                own_in(n).wait()

        at_step({n: [(ready, n)] for n in range(STEPS)})
        w = jnp.concatenate([in_v[t, :, :, m].reshape(wide, GROUP) for m in range(2)], axis=1)
        wd = down_v[lanes(t * GROUP, GROUP)]
        joined = nn(x2[...], w)
        a, c = joined[:, :GROUP], joined[:, GROUP:]
        grad_active = nt(gl[...], wd)
        phi = 0.5 * (1.0 + lax.erf(a * SQRT_HALF))
        gate = a * phi
        slope = phi + a * (jnp.exp(-0.5 * a * a) * DENSITY)
        active = (gate * c).astype(BF)
        ga = (slope * c * grad_active).astype(BF)
        gc = (gate * grad_active).astype(BF)

        @pl.when(t >= 2)
        def _():
            keep, give = stage_copies(t - 2)
            for copied in keep:
                copied.wait()
            for sent in give:
                sent.wait_send()

        gj[s, :, :GROUP] = ga
        gj[s, :, GROUP:] = gc
        act[s] = active.T
        keep, give = stage_copies(t)
        for started in keep + give:
            started.start()

        at_step({n: [(third, m, copy_in)] for n, m in ((0, 1), (2, 3), (3, 5), (4, 6))})
        acc_f[...] += nn(active, wd)
        back = nt(gj[s], w)

        @pl.when(t == 0)
        def _():
            acc_g[...] = back

        @pl.when(t > 0)
        def _():
            acc_g[...] += back

        return 0

    lax.fori_loop(0, STEPS, feed, 0)
    rows_b[...] = acc_f[...].astype(BF).reshape(2, block, wide)
    save(rows_b, ffn_o)
    save(acc_g, gn_o)
    for t in (STEPS - 2, STEPS - 1):
        keep, give = stage_copies(t)
        for copied in keep:
            copied.wait()
        for sent in give:
            sent.wait_send()
    for t in range(STEPS):
        for received in stage_copies(t)[1]:
            received.wait_recv()
    shared[0].wait()
    shared[1].wait_send()
    for n, dst in enumerate((nt_o, xt_o, mt_o)):
        remote(theirs, dst.at[:, sib_rows], ts.at[n], tr.at[n], sib).wait_recv()
    glc_keep.wait()
    glc_give.wait()
    for w in range(4):
        for kind in range(9):
            copy(w, kind).wait_send()
    for t in range(STEPS):
        for kind in range(9):
            if t not in BY_Z or kind != 2:
                copy_in(t, kind).wait_send()
    for c in saved:
        c.wait()


def front_all(attn_gain, ffn_gain, qkv, out, inw, down, tok, cot, starts, inverse):
    dma = pltpu.SemaphoreType.DMA
    block, wide = tok.shape[1:]
    half, hidden = 2 * block, STEPS * GROUP

    def shape(*s, kind=BF):
        return jax.ShapeDtypeStruct(s, kind)

    def buf(*s, kind=BF):
        return pltpu.VMEM(s, kind)

    whole = pl.BlockSpec(memory_space=pltpu.VMEM)
    return pl.pallas_call(
        front_kernel,
        out_shape=[
            shape(8, *qkv.shape), shape(8, *out.shape), shape(*cot.shape), shape(*tok.shape),
            shape(half, wide, kind=F32), shape(half, wide, kind=F32), shape(2, block, wide),
            shape(half, wide), shape(2 * half, wide), shape(2 * half, wide), shape(half, wide), shape(2 * half, half),
            shape(half, 2 * half), shape(half, 2 * half), shape(half, 2 * half), shape(2 * half, half),
            shape(STEPS, 2 * half, 2 * GROUP), shape(hidden, 2 * half),
            shape(2, wide, kind=F32), shape(half, 128, kind=F32), shape(half, 128, kind=F32), shape(8, 2, half, kind=F32),
        ],
        in_specs=[whole] * 2 + [ANY] * 6 + [whole] * 2,
        out_specs=[ANY] * 18 + [whole] * 4,
        scratch_shapes=[
            buf(8, 16, 256), buf(8, *qkv.shape), buf(8, *out.shape), buf(STEPS, 4, 2, 2, 128, GROUP), buf(hidden, wide),
            buf(*tok.shape), buf(2, 8, 128, kind=jnp.int32), buf(half, wide, kind=F32), buf(half, wide, kind=F32),
            buf(half, wide), buf(half, wide), buf(half, wide), buf(half, wide), buf(2 * half, wide), buf(2 * half, wide),
            buf(half, wide), buf(2 * half, half),
            buf(16, 256), buf(8, 128, kind=jnp.int32), buf(half, wide), buf(half, wide),
            buf(2, half, 2 * GROUP), buf(2, GROUP, half), buf(half, half), buf(half, half), buf(2, block, wide),
            dma((4, 9)), dma((4, 9)), dma((STEPS, 9)), dma((STEPS, 9)), dma((5,)), dma((STEPS,)),
            dma((2, 2)), dma((2, 2)), dma((5,)), dma((1,)), dma((1,)), dma((2, 4)), dma((2, 4)), dma((10,)),
            dma((4,)), dma((4,)), dma((4,)), dma((2,)), dma((STEPS,)), dma((2,)), dma((2,)), dma((STEPS,)), dma((2,)),
        ],
        compiler_params=pltpu.CompilerParams(collective_id=1, has_side_effects=True, vmem_limit_bytes=VMEM_BYTES),
        name="gather_attention_feed_forward",
    )(attn_gain, ffn_gain, qkv, out, inw, down, tok, cot, starts, inverse)


def back_kernel(
    ffn_h, mid_h, gn_h, cot_h, qkv_h, out_h, q_h, k_h, v_h, mix_h, rows_h, bias_h, xt_h, mt_h, nt_h, glc_h, gj_h, at_h,
    gains, cosine, sine, lse,
    in_o, qkv_o, down_o, out_o, gain_o, outh_o, inh_o,
    acc_f, acc_g, win, xt, mt, gj, gq, at, glc, gm, dout, q, k, v, bias, kept, dx_kv, kvl, centres, terms, gs, gr,
    ld, gld, wsem, ps, pr, kvs, kvr, gqs, gqr, dxs, dxr, fo, es, er, el,
    *sum_refs,
):
    h = Here()
    rows = Rows(h.z, h.f, h.core)
    order = [op[1][1] for op in PLAN if op[0] in "fb" and op[1][0] == "w"]
    wide = Sums(h, sum_refs[0:7], {t: n % WIDE_SLOTS for n, t in enumerate(order)})
    down = Sums(h, sum_refs[7:14], {0: 0, 1: 1})
    outs = Sums(h, sum_refs[14:21], {0: 0})
    gain = Sums(h, sum_refs[21:28], {0: 0})
    groups = {"w": wide, "d": down, "o": outs, "g": gain}
    sib = (h.z, h.fc)
    half, width = dout.shape
    block = half // 2
    own_rows, sib_rows = pl.ds(0, half), pl.ds(half, half)
    lane = lax.broadcasted_iota(jnp.int32, (1, 128), 1)

    def load(src, dst, n):
        return pltpu.make_async_copy(src, dst, ld.at[n])

    def gj_load(t):
        return pltpu.make_async_copy(gj_h.at[t], gj, gld.at[0])

    def qkv_weights(u):
        return [
            pltpu.make_async_copy(qkv_h.at[:, :, lanes(n * 1024 + u * 256, 256)], win.at[:, :, pl.ds(n * 256, 256)], wsem.at[n])
            for n in range(3)
        ]

    loads = {
        "xt": load(xt_h, xt, 0), "mid": load(mid_h, acc_f, 1), "gn": load(gn_h, acc_g, 2),
        "c0": load(cot_h.at[0], dout.at[pl.ds(0, block)], 3), "c1": load(cot_h.at[1], dout.at[pl.ds(block, block)], 4),
        "w": load(out_h, k, 5), "mix": load(mix_h, v.at[own_rows], 6), "mt": load(mt_h, mt, 7),
        "at": load(at_h, at, 8), "glc": load(glc_h, glc, 9), "bias": load(bias_h, bias, 10), "q": load(q_h, q, 11),
        "nt": load(nt_h, mt, 7), "k": load(k_h, k, 5), "v": load(v_h, v, 6),
        "r0": load(rows_h.at[0], k.at[pl.ds(0, block)], 3), "r1": load(rows_h.at[1], k.at[pl.ds(block, block)], 4),
    }

    def start(*names):
        for name in names:
            loads[name].start()

    def wait(*names):
        for name in names:
            loads[name].wait()

    start("xt")
    gj_load(0).start()
    start("mid", "gn", "c0", "c1")
    start("w", "mix", "at", "glc", "mt", "bias", "q")
    h.greet(pltpu.get_barrier_semaphore(), rows)

    def put(group, t, term, cut):
        s = group.slot[t]
        term = term.astype(BF)
        for o in range(4):
            for n in range(2):
                group.acc[s, n, o // 2, o % 2] = term[o * 128 : o * 128 + 128, n * cut : n * cut + cut]

    def in_term(t):
        if t == 0:
            wait("xt")
        gj_load(t).wait()
        put(wide, t, nn(xt[...], gj[...]), GROUP)
        if t + 1 < STEPS:
            gj_load(t + 1).start()

    def down_term(j):
        if j == DOWN_FIRST:
            wait("at", "glc")
        term = nn(at[...], glc[:, j * 256 : j * 256 + 256])
        for f in range(8):
            down.acc[j, f % 2, f // 4, f // 2 % 2] = term[f * SHARD : f * SHARD + SHARD].astype(BF)

    gm_send = remote(gm.at[own_rows], gm.at[sib_rows], ps.at[0], pr.at[0], sib)

    def second_norm():
        wait("mid", "gn", "c0", "c1")
        back, terms[1:2] = norm_back(acc_f[...], gains[1:2], acc_g[...])
        grad_mid = dout[...].astype(F32) + back
        acc_f[...] = grad_mid
        gm[:half] = grad_mid.astype(BF)
        gm_send.start()

    def mixture_grads():
        wait("w", "mix")
        dout[...] = nt(gm[:half], k[...]).astype(BF)
        start("k")
        for j in range(8):
            cols = slice(j * 128, j * 128 + 128)
            products = (v[:half, cols].astype(F32) * dout[:, cols].astype(F32)).T
            for e in range(2):
                centres[j, e : e + 1] = jnp.sum(products[64 * e : 64 * e + 64], axis=0, keepdims=True)
        start("v")

    def out_term():
        wait("mt")
        gm_send.wait()
        put(outs, 0, nn(mt[...], gm[...]), 512)
        start("nt")

    def kv_rows(s):
        return pl.ds(s * half if isinstance(s, int) else pl.multiple_of(s * half, half), half)

    def kv_send(u):
        s = lax.rem(u, 2)
        return remote(dx_kv, kvl.at[s], kvs.at[s], kvr.at[s], sib)

    def gq_send(u):
        s = lax.rem(u, 2)
        return remote(gq.at[s, own_rows], gq.at[s, sib_rows], gqs.at[s], gqr.at[s], sib)

    def stashed(b, n, j):
        return jnp.concatenate([kept[b, pl.ds(n * 128, 128), pl.ds(m * 256 + j * 128, 128)] for m in range(4)], axis=0)

    def heads_back(p):
        u, j = p // 2, lax.rem(p, 2)
        s = lax.rem(u, 2)
        col = lanes(p * 128, 128)
        queries = q[:, col] * jnp.asarray(0.125, BF)
        keys, values, do = k[:, col], v[:, col], dout[:, col]
        kt = keys.T
        none = jnp.zeros_like(queries)
        dqs, dks, dvs = [], [], []
        for e in range(2):
            part = (lane < 64) if e == 0 else (lane >= 64)
            prob = jnp.exp(nt(keys, jnp.where(part, queries, none)) + bias[...].astype(F32) - lse[p, e : e + 1, :])
            dvs.append(nn(prob.astype(BF), do))
            ds = (prob * (nt(values, jnp.where(part, do, none)) - centres[p, e : e + 1, :])).astype(BF)
            dks.append(nn(ds, queries))
            dqs.append(nn(kt, ds))
        dq = jnp.concatenate([dqs[0][:64], dqs[1][64:]], axis=0).T
        dk = jnp.where(lane < 64, dks[0], dks[1]).astype(BF)
        dv = jnp.where(lane < 64, dvs[0], dvs[1]).astype(BF)
        for n, part in enumerate(((dq * 0.125).astype(BF), dk, dv)):
            for m in range(4):
                kept[s, pl.ds(n * 128, 128), lanes(m * 256 + j * 128, 128)] = part[m * 128 : m * 128 + 128]

        @pl.when((j == 0) & (u >= 1))
        def _():
            kv_send(u - 1).wait_send()

        dx_kv[:, lanes(j * 128, 128)] = dk[half:]
        dx_kv[:, lanes(256 + j * 128, 128)] = dv[half:]

    def heads_close(u):
        b = lax.rem(u, 2)

        @pl.when(u >= 2)
        def _():
            gq_send(u - 2).wait_send()

        kv_send(u).wait_recv()
        for j in range(2):
            c = slice(j * 128, j * 128 + 128)
            gq[b, :half, c] = rope_back(stashed(b, 0, j).astype(F32), cosine[...], sine[...]).astype(BF)
            g = added(stashed(b, 1, j), kvl[b, :, c]).astype(F32)
            gq[b, :half, 256 + j * 128 : 384 + j * 128] = rope_back(g, cosine[...], sine[...]).astype(BF)
            gq[b, :half, 512 + j * 128 : 640 + j * 128] = added(stashed(b, 2, j), kvl[b, :, 256 + j * 128 : 384 + j * 128])
        for c in qkv_weights(u):
            c.wait()
        back = nt(gq[b, :half], win[...].reshape(width, 768))

        @pl.when(u == 0)
        def _():
            acc_g[...] = back

        @pl.when(u > 0)
        def _():
            acc_g[...] += back

        @pl.when(u < 3)
        def _():
            for c in qkv_weights(u + 1):
                c.start()

    def qkv_term(u):
        gq_send(u).wait_recv()
        put(wide, STEPS + u, nn(mt[...], gq[u % 2]), GROUP)

    def first_norm():
        wait("r0", "r1")
        back, terms[0:1] = norm_back(k[:half].astype(F32), gains[0:1], acc_g[...])
        dout[...] = (acc_f[...] + back).astype(BF)

    gs_send = remote(gs, gr, ps.at[1], pr.at[1], sib)

    def gain_terms():
        for n in range(2):
            for o in range(4):
                for ref, part in ((gain.acc.at[0], h.core), (gs, 1 - h.core)):
                    low, high = terms[n : n + 1, 256 * o : 256 * o + 128], terms[n : n + 1, 256 * o + 128 : 256 * o + 256]
                    value = jnp.where(part == 0, low, high)
                    ref[n, o // 2, o % 2] = jnp.broadcast_to(value, (16, 128)).astype(BF)
        gs_send.start()
        gs_send.wait()
        for n in range(2):
            for o in range(4):
                gain.acc[0, n, o // 2, o % 2] = added(gain.acc[0, n, o // 2, o % 2], gr[n, o // 2, o % 2])

    def dx(j):
        return kvl.at[j, pl.ds(0, SHARD), pl.ds(0, 256)]

    def down_swap(j, act, ref):
        act(remote(ref.at[j, 1 - h.core], dx(j), dxs.at[j], dxr.at[j], sib))

    def to_end(j):
        return pltpu.make_async_copy(dx(j), down_o.at[:, lanes((1 - h.core) * 512 + j * 256, 256)], fo.at[2, 5 + j])

    def write(name, t, act, ref):
        if name == "w" and t < STEPS:
            for n in range(2):
                act(pltpu.make_async_copy(ref.at[t, n], in_o.at[n, :, pl.ds(t * GROUP, GROUP)], fo.at[0, 2 * t + n]))
        elif name == "w":
            parts = ((0, 0, 256, 0), (0, 256, 128, 1024), (1, 0, 128, 1152), (1, 128, 256, 2048))
            for n, (m, at_col, size, to) in enumerate(parts):
                dst = qkv_o.at[:, pl.ds(to + (t - STEPS) * 256, size)]
                act(pltpu.make_async_copy(ref.at[t, m, :, pl.ds(at_col, size)], dst, fo.at[1, 4 * (t - STEPS) + n]))
        elif name == "d":
            dst = down_o.at[:, lanes(h.core * 512 + t * 256, 256)]
            act(pltpu.make_async_copy(ref.at[t, h.core], dst, fo.at[2, 3 + t]))
        elif name == "o":
            for n in range(2):
                act(pltpu.make_async_copy(ref.at[0, n], out_o.at[:, pl.ds(n * 512, 512)], fo.at[2, n]))
        else:
            act(pltpu.make_async_copy(ref, gain_o, fo.at[2, 2]))

    sent = [0, 0]

    def piece(which):
        size = block // PIECES
        part = pl.ds(sent[which] * size, size)
        sent[which] += 1
        if which == 0:
            rows.start(ffn_h, outh_o, es.at[0], er.at[0], el.at[0], False, part)
        else:
            rows.start(Halves(dout), inh_o, es.at[1], er.at[1], el.at[1], False, part)

    work = {"ln2": second_norm, "do": mixture_grads, "og": out_term, "H": first_norm, "gains": gain_terms}

    def perform(ops):
        for op in ops:
            if op[0] == "c":
                if op[1] in work:
                    work[op[1]]()
            elif op[0] == "r":
                piece(op[1])
            else:
                (name, t), group = op[1], groups[op[1][0]]
                if op[0] == "s":
                    getattr(group, Sums.LATER[op[2]])(t)
                    if op[2] == 5:
                        group.total(functools.partial(write, name, t, lambda c: c.start()))
                        if name == "d":
                            down.total(functools.partial(down_swap, t, lambda c: c.start()))
                else:
                    if name == "w":
                        in_term(t) if t < STEPS else qkv_term(t - STEPS)
                    elif name == "d":
                        down_term(t)
                    group.begin(t)

    before, loop, after = split_plan()
    perform(before)
    wait("bias", "q", "k", "v", "nt")
    for c in qkv_weights(0):
        c.start()

    def each(p, _):
        pl.when(p < 8)(lambda: heads_back(p))
        pl.when(p == 8)(lambda: start("r0", "r1"))
        for n in range(10):
            if loop[n, 0]:
                pl.when(p == n)(functools.partial(perform, loop[n, 0]))

        @pl.when((lax.rem(p, 2) == 1) & (p >= 3))
        def _():
            heads_close((p - 3) // 2)

        for n in range(10):
            if loop[n, 1]:
                pl.when(p == n)(functools.partial(perform, loop[n, 1]))
            if loop[n, 2]:
                pl.when(p == n)(functools.partial(perform, loop[n, 2]))

        @pl.when((lax.rem(p, 2) == 1) & (p < 8))
        def _():
            kv_send(p // 2).start()

        @pl.when((lax.rem(p, 2) == 1) & (p >= 3))
        def _():
            gq_send((p - 3) // 2).start()

        return 0

    lax.fori_loop(0, 10, each, 0)
    perform(after)
    for j in range(2):
        down.total(functools.partial(down_swap, j, lambda c: c.wait()))
        to_end(j).start()
    kv_send(3).wait_send()
    gq_send(2).wait_send()
    gq_send(3).wait_send()

    for name, group in groups.items():
        for t in group.slot:
            group.total(functools.partial(write, name, t, lambda c: c.wait()))
    for j in range(2):
        to_end(j).wait()
    rows.wait(ffn_h, outh_o, es.at[0], er.at[0], el.at[0], False)
    rows.wait(Halves(dout), inh_o, es.at[1], er.at[1], el.at[1], False)


def back_all(ffn_rows, *args):
    dma = pltpu.SemaphoreType.DMA
    block, wide = ffn_rows.shape[1:]
    half = 2 * block

    def buf(*s, kind=BF):
        return pltpu.VMEM(s, kind)

    def shape(*s):
        return jax.ShapeDtypeStruct(s, BF)

    whole = pl.BlockSpec(memory_space=pltpu.VMEM)
    scratch = [
        buf(half, wide, kind=F32), buf(half, wide, kind=F32), buf(8, 128, 768),
        buf(half, 2 * half), buf(half, 2 * half), buf(2 * half, 768), buf(2, 2 * half, 768),
        buf(STEPS * GROUP, 2 * half), buf(2 * half, half), buf(2 * half, wide), buf(half, wide),
        buf(half, wide), buf(2 * half, wide), buf(2 * half, wide), buf(2 * half, half),
        buf(2, GROUP, wide), buf(half, 512), buf(2, half, 512), buf(8, 2, half, kind=F32), buf(2, wide, kind=F32),
        buf(2, 2, 2, 16, 128), buf(2, 2, 2, 16, 128),
        dma((13,)), dma((1,)), dma((3,)), dma((2,)), dma((2,)), dma((2,)), dma((2,)), dma((2,)), dma((2,)),
        dma((2,)), dma((2,)), dma((3, 16)), dma((2, 2)), dma((2, 2)), dma((2,)),
    ]
    for s in ((11, WIDE_SLOTS, 128, GROUP), (2, 2, SHARD, 256), (1, 1, 128, 512), (1, 1, 16, 128)):
        scratch += Sums.scratch(*s)
    return pl.pallas_call(
        back_kernel,
        out_shape=[
            shape(2, 128, STEPS * GROUP), shape(128, 3 * wide), shape(SHARD, wide), shape(128, wide), shape(1, 2, 16, 128),
            shape(2, block, wide), shape(2, block, wide),
        ],
        in_specs=[ANY] * 18 + [whole] * 4,
        out_specs=[ANY] * 7,
        scratch_shapes=scratch,
        compiler_params=pltpu.CompilerParams(collective_id=2, has_side_effects=True, vmem_limit_bytes=VMEM_BYTES),
        name="backward_and_sums",
    )(ffn_rows, *args)


def lay_out_kernel(in_ref, down_ref, parts_ref, rows_ref):
    shard = in_ref.shape[1] // 16
    spare = jnp.zeros((in_ref.shape[0], SHARD - shard), BF)
    for m in range(2):
        pieces = []
        for n in range(8 * m, 8 * m + 8):
            pieces += [in_ref[:, n * shard : (n + 1) * shard], spare]
        parts_ref[m] = jnp.concatenate(pieces, axis=1)
    row = lax.broadcasted_iota(jnp.int32, down_ref.shape, 0) + pl.program_id(0) * down_ref.shape[0]
    rows_ref[...] = jnp.where(row < shard, down_ref[...].astype(F32), 0.0).astype(BF)


def lay_out(in_weight, down_weight):
    depth, wide = in_weight.shape[0], down_weight.shape[1]
    part = depth // 4
    return pl.pallas_call(
        lay_out_kernel,
        grid=(4,),
        in_specs=[pl.BlockSpec((part, in_weight.shape[1]), lambda i: (i, 0)), pl.BlockSpec((96, wide), lambda i: (i, 0))],
        out_specs=[pl.BlockSpec((2, part, 8 * SHARD), lambda i: (0, i, 0)), pl.BlockSpec((96, wide), lambda i: (i, 0))],
        out_shape=[jax.ShapeDtypeStruct((2, depth, 8 * SHARD), BF), jax.ShapeDtypeStruct((SHARD, wide), BF)],
        compiler_params=pltpu.CompilerParams(vmem_limit_bytes=VMEM_BYTES),
        name="lay_out_weights",
    )(in_weight, down_weight)


def results_kernel(out_b, grad_b, qkv_b, proj_b, in_b, down_b, gain_b, out_r, grad_r, qkv_r, proj_r, in_r, down_r, attn_r, ffn_r):
    attn_r[...] = gain_b[0, 0].astype(F32)[0:1]
    ffn_r[...] = gain_b[0, 1].astype(F32)[0:1]
    for src, dst in ((out_b, out_r), (grad_b, grad_r), (qkv_b, qkv_r), (proj_b, proj_r), (down_b, down_r)):
        dst[...] = src[...].astype(F32)
    shard = in_r.shape[1] // 16
    pieces = []
    for m in range(2):
        whole = in_b[m].astype(F32)
        pieces += [whole[:, n * SHARD : n * SHARD + shard] for n in range(8)]
    in_r[...] = jnp.concatenate(pieces, axis=1)


def results(out_home, in_home, qkv_t, out_t, in_t, down_t, gain_t, shard):
    block, wide = out_home.shape[1:]
    depth = qkv_t.shape[0]
    part = depth // 4

    def rows(size, width):
        return pl.BlockSpec((size, width), lambda i: (i, 0))

    home = pl.BlockSpec((2, block // 4, wide), lambda i: (0, i, 0))
    return pl.pallas_call(
        results_kernel,
        grid=(4,),
        in_specs=[home, home, rows(part, 3 * wide), rows(part, wide),
                  pl.BlockSpec((2, part, in_t.shape[2]), lambda i: (0, i, 0)), rows(96, wide),
                  pl.BlockSpec(gain_t.shape, lambda i: (0, 0, 0, 0))],
        out_specs=[home, home, rows(part, 3 * wide), rows(part, wide), rows(part, 16 * shard), rows(96, wide)]
        + [pl.BlockSpec((1, part * 4), lambda i: (0, 0))] * 2,
        out_shape=[
            jax.ShapeDtypeStruct(out_home.shape, F32), jax.ShapeDtypeStruct(in_home.shape, F32),
            jax.ShapeDtypeStruct(qkv_t.shape, F32), jax.ShapeDtypeStruct(out_t.shape, F32),
            jax.ShapeDtypeStruct((depth, 16 * shard), F32), jax.ShapeDtypeStruct((shard, wide), F32),
        ]
        + [jax.ShapeDtypeStruct((1, depth), F32)] * 2,
        compiler_params=pltpu.CompilerParams(vmem_limit_bytes=VMEM_BYTES),
        name="results_to_float32",
    )(out_home, in_home, qkv_t, out_t, in_t, down_t, gain_t)


def chip_streams(tokens, cotangent, doc_starts, qkv_weight, out_weight, in_weight, down_weight, attn_gain, ffn_gain):
    wide = tokens.shape[3]
    shard = down_weight.shape[0]
    in_parts, down_rows = lay_out(in_weight, down_weight)
    inverse = ROPE_THETA ** (-np.arange(0, HEAD_DIM, 2) / HEAD_DIM)
    (qkv_f, out_f, cot, rows_low, middle, gn, ffn_rows, q, k, v, mixture, bias, xt, mt, nt_rows, glc, gj, at,
     both_gains, cosine, sine, lse) = front_all(
        attn_gain[None], ffn_gain[None], qkv_weight, out_weight, in_parts, down_rows,
        tokens[:, 0], cotangent[:, 0], doc_starts[:, 0], np.tile(inverse, 4)[None].astype(np.float32),
    )
    in_t, qkv_t, down_t, out_t, gain_t, out_home, in_home = back_all(
        ffn_rows, middle, gn, cot, qkv_f, out_f.reshape(wide, wide), q, k, v, mixture, rows_low, bias, xt, mt, nt_rows, glc, gj, at,
        both_gains, cosine, sine, lse,
    )
    output, tokens_grad, qkv_grad, out_grad, in_grad, down_grad, attn_grad, ffn_grad = results(
        out_home, in_home, qkv_t, out_t, in_t, down_t, gain_t, shard
    )
    return (
        output[:, None],
        tokens_grad[:, None],
        qkv_grad,
        out_grad,
        in_grad,
        down_grad,
        attn_grad[0],
        ffn_grad[0],
    )


def solution(mesh):
    whole_chips = dict(mesh.shape) == {"seq": 4, "fsdp": 8}
    return jax.shard_map(
        chip_streams if whole_chips else shards,
        mesh=mesh,
        in_specs=(
            P(None, "fsdp", "seq", None),
            P(None, "fsdp", "seq", None),
            P(None, "fsdp", None),
            P("fsdp", None),
            P("fsdp", None),
            P("fsdp", None),
            P("fsdp", None),
            P("fsdp"),
            P("fsdp"),
        ),
        out_specs=(
            P(None, "fsdp", "seq", None),
            P(None, "fsdp", "seq", None),
            P("fsdp", None),
            P("fsdp", None),
            P("fsdp", None),
            P("fsdp", None),
            P("fsdp"),
            P("fsdp"),
        ),
        check_vma=False,
    )
```

```python
import functools
from functools import partial

import jax
import jax.numpy as jnp
import numpy as np
from jax import lax
from jax.experimental import pallas as pl
from jax.experimental.pallas import tpu as pltpu
from jax.sharding import PartitionSpec as P

HEADS = 16
HEAD_DIM = 64


EPSILON = 1e-05
ROPE_THETA = 160000.0
MASKED_SCORE = -1e30


def as_sent(x):

    def short(part):
        return part.astype(jnp.bfloat16) if part.dtype == jnp.float32 else part

    return jax.tree.map(short, x)


def layer_norm(values, norm_gain):
    average = jnp.mean(values, axis=-1, keepdims=True)
    centred = values - average
    spread = jnp.mean(centred * centred, axis=-1, keepdims=True)
    return centred * lax.rsqrt(spread + EPSILON) * norm_gain


def gated_gelu(joined):
    half_width = joined.shape[-1] // 2
    return jax.nn.gelu(joined[:, :half_width], approximate=False) * joined[:, half_width:]


def rotate(values, cosine_table, sine_table):
    half_width = values.shape[-1] // 2
    turned = jnp.concatenate([-values[..., half_width:], values[..., :half_width]], axis=-1)
    return values * cosine_table + turned * sine_table


def rope_tables(starts, places, head_width):
    preceding = starts[None, :] <= places[:, None]
    doc_begin = jnp.max(jnp.where(preceding, starts[None, :], 0), axis=-1)
    offsets = (places - doc_begin).astype(jnp.float32)
    inverse = ROPE_THETA ** (-jnp.arange(0, head_width, 2, dtype=jnp.float32) / head_width)
    angles = offsets[:, None] * inverse[None, :]
    angles = jnp.concatenate([angles, angles], axis=-1)
    return (jnp.cos(angles), jnp.sin(angles))


def segment_ids(starts, places):
    return jnp.sum((starts[None, :] <= places[:, None]).astype(jnp.int32), axis=-1) - 1


def turn_pair(pair, cosine_table, sine_table):
    shaped = pair.reshape(pair.shape[0], 2, HEADS, HEAD_DIM)
    turned = rotate(shaped, cosine_table[:, None, None, :], sine_table[:, None, None, :])
    return turned.reshape(pair.shape[0], 2 * HEADS * HEAD_DIM)


def attend_forward(queries, keys_in, values_in, segments, head_count):
    length = queries.shape[0]
    head_width = queries.shape[1] // head_count
    block_rows = min(512, length)
    blocks = length // block_rows
    keyset = keys_in.reshape(length, head_count, head_width)
    valueset = values_in.reshape(length, head_count, head_width)
    factor = head_width ** (-0.5)

    def one_block(pieces):
        query_rows, block_segs = pieces
        scores = (
            jnp.einsum("qhd,khd->hqk", query_rows, keyset, preferred_element_type=jnp.float32)
            * factor
        )
        scores = jnp.where((block_segs[:, None] == segments[None, :])[None], scores, MASKED_SCORE)
        row_max = jnp.max(scores, axis=-1, keepdims=True)
        totals = jnp.sum(jnp.exp(scores - row_max), axis=-1, keepdims=True)
        logsums = row_max + jnp.log(totals)
        weights = jnp.exp(scores - logsums).astype(jnp.bfloat16)
        mixture = jnp.einsum("hqk,khd->qhd", weights, valueset, preferred_element_type=jnp.float32)
        return (mixture, logsums)

    mixture, logsums = lax.map(
        one_block,
        (
            queries.reshape(blocks, block_rows, head_count, head_width),
            segments.reshape(blocks, block_rows),
        ),
    )
    return (mixture.reshape(length, head_count * head_width), logsums)


def attend_backward(queries, keys_in, values_in, grads_in, segments, logsums, head_count):
    length = queries.shape[0]
    head_width = queries.shape[1] // head_count
    block_rows = min(512, length)
    blocks = length // block_rows
    keyset = keys_in.reshape(length, head_count, head_width)
    valueset = values_in.reshape(length, head_count, head_width)
    factor = head_width ** (-0.5)

    def one_block(carry, pieces):
        key_grad, value_grad = carry
        query_rows, block_segs, grad_rows, block_lse = pieces
        scores = (
            jnp.einsum("qhd,khd->hqk", query_rows, keyset, preferred_element_type=jnp.float32)
            * factor
        )
        scores = jnp.where((block_segs[:, None] == segments[None, :])[None], scores, MASKED_SCORE)
        weights = jnp.exp(scores - block_lse)
        value_grad = value_grad + jnp.einsum(
            "hqk,qhd->khd",
            weights.astype(jnp.bfloat16),
            grad_rows,
            preferred_element_type=jnp.float32,
        )
        grad_weights = jnp.einsum(
            "qhd,khd->hqk", grad_rows, valueset, preferred_element_type=jnp.float32
        )
        centre = jnp.sum(weights * grad_weights, axis=-1, keepdims=True)
        grad_scores = (weights * (grad_weights - centre)).astype(jnp.bfloat16)
        query_grad = (
            jnp.einsum("hqk,khd->qhd", grad_scores, keyset, preferred_element_type=jnp.float32)
            * factor
        )
        key_grad = (
            key_grad
            + jnp.einsum(
                "hqk,qhd->khd", grad_scores, query_rows, preferred_element_type=jnp.float32
            )
            * factor
        )
        return ((key_grad, value_grad), query_grad)

    empty = jnp.zeros((length, head_count, head_width), jnp.float32)
    pieces = (
        queries.reshape(blocks, block_rows, head_count, head_width),
        segments.reshape(blocks, block_rows),
        grads_in.reshape(blocks, block_rows, head_count, head_width),
        logsums,
    )
    (key_grad, value_grad), query_grad = lax.scan(one_block, (empty, empty), pieces)
    flat_shape = (length, head_count * head_width)
    return (
        query_grad.reshape(flat_shape).astype(jnp.bfloat16),
        key_grad.reshape(flat_shape).astype(jnp.bfloat16),
        value_grad.reshape(flat_shape).astype(jnp.bfloat16),
    )


def shards(
    tokens,
    cotangent,
    doc_starts,
    qkv_weight,
    out_weight,
    in_weight,
    down_weight,
    attn_gain,
    ffn_gain,
):
    micro_count = tokens.shape[0]
    token_rows = tokens.shape[2]
    model_width = tokens.shape[3]
    seq_count = lax.axis_size("seq")
    head_count = HEADS // seq_count
    places = lax.axis_index("seq") * token_rows + jnp.arange(token_rows, dtype=jnp.int32)
    everywhere = jnp.arange(token_rows * seq_count, dtype=jnp.int32)
    outputs = []
    input_grads = []
    full_terms = None
    shard_terms = None
    for micro_step in range(micro_count):
        rows_in = tokens[micro_step, 0]
        starts = doc_starts[micro_step, 0]
        cosine_table, sine_table = rope_tables(starts, places, HEAD_DIM)
        segments = segment_ids(starts, everywhere)
        attn_set = (
            lax.all_gather(qkv_weight, "fsdp", axis=0, tiled=True),
            lax.all_gather(out_weight, "fsdp", axis=0, tiled=True),
            lax.all_gather(attn_gain, "fsdp", axis=0, tiled=True),
        )
        qkv_full, out_full, gain_one = attn_set
        normed, norm_back = jax.vjp(layer_norm, rows_in, gain_one.astype(jnp.float32))
        normed_low = normed.astype(jnp.bfloat16)
        qkv_rows = jnp.dot(normed_low, qkv_full, preferred_element_type=jnp.float32)
        turned, turn_back = jax.vjp(
            partial(turn_pair, cosine_table=cosine_table, sine_table=sine_table),
            qkv_rows[:, : 2 * model_width],
        )
        queries = turned[:, :model_width].astype(jnp.bfloat16)
        keyset = turned[:, model_width:].astype(jnp.bfloat16)
        valueset = qkv_rows[:, 2 * model_width :].astype(jnp.bfloat16)
        query_heads, key_heads, value_heads = (
            lax.all_to_all(queries, "seq", split_axis=1, concat_axis=0, tiled=True),
            lax.all_to_all(keyset, "seq", split_axis=1, concat_axis=0, tiled=True),
            lax.all_to_all(valueset, "seq", split_axis=1, concat_axis=0, tiled=True),
        )
        mixture, logsums = attend_forward(query_heads, key_heads, value_heads, segments, head_count)
        mixture_rows = lax.all_to_all(
            mixture.astype(jnp.bfloat16), "seq", split_axis=0, concat_axis=1, tiled=True
        )
        middle = rows_in + jnp.dot(mixture_rows, out_full, preferred_element_type=jnp.float32)
        ffn_set = (
            lax.all_gather(in_weight, "fsdp", axis=0, tiled=True),
            lax.all_gather(down_weight, "fsdp", axis=0, tiled=True),
            lax.all_gather(ffn_gain, "fsdp", axis=0, tiled=True),
        )
        in_full, down_full, gain_two = ffn_set
        normed_two, norm_back_two = jax.vjp(layer_norm, middle, gain_two.astype(jnp.float32))
        normed_two_low = normed_two.astype(jnp.bfloat16)
        joined = jnp.dot(normed_two_low, in_full, preferred_element_type=jnp.float32)
        active, gelu_back = jax.vjp(gated_gelu, joined)
        active_low = active.astype(jnp.bfloat16)
        outputs.append(middle + jnp.dot(active_low, down_full, preferred_element_type=jnp.float32))
        grad_out = cotangent[micro_step, 0]
        grad_low = grad_out.astype(jnp.bfloat16)
        ffn_set = (
            lax.all_gather(in_weight, "fsdp", axis=0, tiled=True),
            lax.all_gather(down_weight, "fsdp", axis=0, tiled=True),
            lax.all_gather(ffn_gain, "fsdp", axis=0, tiled=True),
        )
        in_full, down_full, gain_two = ffn_set
        down_term = jnp.dot(active_low.T, grad_low, preferred_element_type=jnp.float32)
        grad_active = jnp.dot(grad_low, down_full.T, preferred_element_type=jnp.float32)
        grad_joined = gelu_back(grad_active)[0].astype(jnp.bfloat16)
        in_term = jnp.dot(normed_two_low.T, grad_joined, preferred_element_type=jnp.float32)
        grad_normed_two = jnp.dot(grad_joined, in_full.T, preferred_element_type=jnp.float32)
        grad_middle_norm, gain_two_term = norm_back_two(grad_normed_two)
        grad_middle = grad_out + grad_middle_norm
        grad_mid_low = grad_middle.astype(jnp.bfloat16)
        attn_set = (
            lax.all_gather(qkv_weight, "fsdp", axis=0, tiled=True),
            lax.all_gather(out_weight, "fsdp", axis=0, tiled=True),
            lax.all_gather(attn_gain, "fsdp", axis=0, tiled=True),
        )
        qkv_full, out_full, gain_one = attn_set
        out_term = jnp.dot(mixture_rows.T, grad_mid_low, preferred_element_type=jnp.float32)
        grad_mixture = jnp.dot(grad_mid_low, out_full.T, preferred_element_type=jnp.float32).astype(
            jnp.bfloat16
        )
        grad_heads = lax.all_to_all(grad_mixture, "seq", split_axis=1, concat_axis=0, tiled=True)
        query_grad, key_grad, value_grad = attend_backward(
            query_heads, key_heads, value_heads, grad_heads, segments, logsums, head_count
        )
        query_back, key_back, value_back = (
            lax.all_to_all(query_grad, "seq", split_axis=0, concat_axis=1, tiled=True),
            lax.all_to_all(key_grad, "seq", split_axis=0, concat_axis=1, tiled=True),
            lax.all_to_all(value_grad, "seq", split_axis=0, concat_axis=1, tiled=True),
        )
        grad_pair = turn_back(jnp.concatenate([query_back, key_back], axis=1).astype(jnp.float32))[
            0
        ]
        grad_qkv = jnp.concatenate([grad_pair, value_back.astype(jnp.float32)], axis=1).astype(
            jnp.bfloat16
        )
        qkv_term = jnp.dot(normed_low.T, grad_qkv, preferred_element_type=jnp.float32)
        grad_normed = jnp.dot(grad_qkv, qkv_full.T, preferred_element_type=jnp.float32)
        grad_rows_norm, gain_one_term = norm_back(grad_normed)
        input_grads.append(grad_middle + grad_rows_norm)
        terms = (qkv_term, out_term, in_term, down_term, gain_one_term, gain_two_term)
        full_terms = terms if full_terms is None else jax.tree.map(jnp.add, full_terms, terms)
    shard_terms = jax.tree.map(
        lambda part: part.astype(jnp.float32),
        lax.psum_scatter(as_sent(full_terms), "fsdp", scatter_dimension=0, tiled=True),
    )
    totals = jax.tree.map(
        lambda part: part.astype(jnp.float32), lax.psum(as_sent(shard_terms), "seq")
    )
    return (
        jnp.stack(outputs)[:, None],
        jnp.stack(input_grads)[:, None],
        totals[0],
        totals[1],
        totals[2],
        totals[3],
        totals[4],
        totals[5],
    )


MESH = pl.DeviceIdType.MESH
ANY = pl.BlockSpec(memory_space=pl.ANY)
VMEM_BYTES = 127 * 2**19
BF = jnp.bfloat16
F32 = jnp.float32


def nn(a, b):
    return lax.dot_general(a, b, (((1,), (0,)), ((), ())), preferred_element_type=F32)


def nt(a, b):
    return lax.dot_general(a, b, (((1,), (1,)), ((), ())), preferred_element_type=F32)


def spot():
    z, f = lax.axis_index("seq"), lax.axis_index("fsdp")
    core = lax.rem(f, 2)
    x = lax.rem(f // 2, 2)
    y = f // 4
    return z, f, y, x, core


def remote(src, dst, send, recv, where):
    return pltpu.make_async_remote_copy(
        src_ref=src, dst_ref=dst, send_sem=send, recv_sem=recv, device_id=where, device_id_type=MESH
    )


class Rows:
    def __init__(self, z, f, core):
        base = f - core
        self.work, self.home = [], []
        for i in range(2):
            zw, cw = 2 * i + core, z // 2
            self.work.append((zw, base + cw, (zw == z) & (cw == core)))
            zh, ch = 2 * core + i, lax.rem(z, 2)
            self.home.append((zh, base + ch, (zh == z) & (ch == core)))
        self.z = z

    def greet(self, barrier):
        count = 0
        for zt, ft, same in self.work + self.home:

            @pl.when(jnp.logical_not(same))
            def _():
                pl.semaphore_signal(barrier, inc=1, device_id=(zt, ft), device_id_type=MESH)

            count = count + jnp.where(same, 0, 1)
        return count

    def start(self, src, dst, send, recv, local, out, piece=slice(None)):
        places = self.work if out else self.home
        slot = lax.rem(self.z, 2) if out else self.z // 2
        for i, (zt, ft, same) in enumerate(places):

            @pl.when(same)
            def _(i=i):
                pltpu.make_async_copy(src.at[i, piece], dst.at[slot, piece], local).start()

            @pl.when(jnp.logical_not(same))
            def _(i=i, zt=zt, ft=ft):
                remote(src.at[i, piece], dst.at[slot, piece], send.at[i], recv.at[slot], (zt, ft)).start()

    def wait(self, src, dst, send, recv, local, out):
        goes, comes = (self.work, self.home) if out else (self.home, self.work)
        for i, (zt, ft, same) in enumerate(goes):

            @pl.when(same)
            def _(i=i):
                pltpu.make_async_copy(src.at[i], dst.at[i], local).wait()

            @pl.when(jnp.logical_not(same))
            def _(i=i, zt=zt, ft=ft):
                remote(src.at[i], dst.at[i], send.at[i], recv.at[i], (zt, ft)).wait_send()

        for i, (zt, ft, same) in enumerate(comes):

            @pl.when(jnp.logical_not(same))
            def _(i=i, zt=zt, ft=ft):
                remote(src.at[i], dst.at[i], send.at[i], recv.at[i], (zt, ft)).wait_recv()


def halves(width):
    cut = (width // 128 // 2) * 128
    return pl.ds(0, cut), pl.ds(cut, width - cut)


SQRT_HALF = 0.7071067811865476
DENSITY = 0.3989422804014327
BY_Z = (2, 4)
SHARD = 336
GROUP = 384
STEPS = 7


def moments(values):
    average = jnp.mean(values, axis=-1, keepdims=True)
    centred = values - average
    spread = jnp.mean(centred * centred, axis=-1, keepdims=True)
    scale = lax.rsqrt(spread + EPSILON)
    return centred * scale, scale


def norm_back(values, gain, grads):
    unit, scale = moments(values)
    spread = grads * gain
    inner = spread - jnp.mean(spread, axis=-1, keepdims=True)
    inner = inner - unit * jnp.mean(spread * unit, axis=-1, keepdims=True)
    return inner * scale, jnp.sum(grads * unit, axis=0, keepdims=True)


def rope_back(grads, cosine, sine):
    lane = lax.broadcasted_iota(jnp.int32, (1, 128), 1)
    low = lax.rem(lane, 64) < 32
    u = grads * sine
    return grads * cosine + jnp.where(low, pltpu.roll(u, 96, 1), -pltpu.roll(u, 32, 1))


class Sums:
    KINDS = 9

    @staticmethod
    def scratch(count, slots, rows, wide):
        dma = pltpu.SemaphoreType.DMA((count, Sums.KINDS))
        shapes = [(slots, 2, 2, 2), (count, 2, 2), (count, 2), (count, 2), (count,)]
        return [pltpu.VMEM(s + (rows, wide), BF) for s in shapes] + [dma, dma]

    def __init__(self, here, refs, slot):
        self.here, self.slot = here, slot
        self.acc, self.rx, self.r2, self.zr, self.zr2, self.send, self.recv = refs

    def copy(self, t, kind):
        h = self.here
        acc = self.acc.at[self.slot[t]]
        plan = {
            0: lambda: (acc.at[0, :, 1 - h.x], self.rx.at[t, 0], (h.z, h.fx)),
            1: lambda: (acc.at[1, 1 - h.y], self.rx.at[t, 1], (h.z, h.fy)),
            2: lambda: (self.rx.at[t, 0, 1 - h.y], self.r2.at[t, 0], (h.z, h.fy)),
            3: lambda: (self.rx.at[t, 1, 1 - h.x], self.r2.at[t, 1], (h.z, h.fx)),
            4: lambda: (self.r2.at[t], self.zr.at[t], (h.near, h.f)),
            5: lambda: (self.zr.at[t, 1 - h.own], self.zr2.at[t], (h.across, h.f)),
            6: lambda: (self.r2.at[t, h.own], self.r2.at[t, h.own], (h.across, h.f)),
            7: lambda: (self.r2.at[t, h.own], self.zr.at[t, h.own], (h.near, h.f)),
            8: lambda: (self.r2.at[t, 1 - h.own], self.zr.at[t, 1 - h.own], (h.near, h.f)),
        }
        src, dst, where = plan[kind]()
        return remote(src, dst, self.send.at[t, kind], self.recv.at[t, kind], where)

    def begin(self, t):
        self.copy(t, 0).start()
        self.copy(t, 1).start()

    def cross(self, t):
        h, s = self.here, self.slot[t]
        self.copy(t, 0).wait()
        self.rx[t, 0, 1 - h.y] = added(self.rx[t, 0, 1 - h.y], self.acc[s, 0, 1 - h.y, h.x])
        self.copy(t, 2).start()
        self.copy(t, 1).wait()
        self.rx[t, 1, 1 - h.x] = added(self.rx[t, 1, 1 - h.x], self.acc[s, 1, h.y, 1 - h.x])
        self.copy(t, 3).start()

    def plane(self, t):
        h, s = self.here, self.slot[t]
        self.copy(t, 2).wait()
        self.r2[t, 0] = added(self.r2[t, 0], self.rx[t, 0, h.y], self.acc[s, 0, h.y, h.x])
        self.copy(t, 3).wait()
        self.r2[t, 1] = added(self.r2[t, 1], self.rx[t, 1, h.x], self.acc[s, 1, h.y, h.x])

        @pl.when(h.outer)
        def _():
            self.copy(t, 4).start()

    def meet(self, t):
        h = self.here

        @pl.when(jnp.logical_not(h.outer))
        def _():
            self.copy(t, 4).wait_recv()
            self.zr[t, 1 - h.own] = added(self.zr[t, 1 - h.own], self.r2[t, 1 - h.own])
            self.copy(t, 5).start()

    def sums(self, t):
        h = self.here

        @pl.when(jnp.logical_not(h.outer))
        def _():
            self.copy(t, 5).wait()
            self.r2[t, h.own] = added(self.r2[t, h.own], self.zr[t, h.own], self.zr2[t])
            self.copy(t, 6).start()
            self.copy(t, 7).start()

    def spread(self, t):
        @pl.when(jnp.logical_not(self.here.outer))
        def _():
            self.copy(t, 6).wait_recv()
            self.copy(t, 8).start()

    def finish(self, t):
        @pl.when(jnp.logical_not(self.here.outer))
        def _():
            self.copy(t, 6).wait_send()
            self.copy(t, 7).wait_send()
            self.copy(t, 8).wait_send()

        @pl.when(self.here.outer)
        def _():
            self.copy(t, 4).wait_send()
            self.copy(t, 7).wait_recv()
            self.copy(t, 8).wait_recv()

    def total(self, act):
        for ref, there in ((self.zr, self.here.outer), (self.r2, jnp.logical_not(self.here.outer))):
            pl.when(there)(functools.partial(act, ref))

    LATER = ("cross", "plane", "meet", "sums", "spread", "finish")


def added(*terms):
    total = terms[0].astype(F32)
    for term in terms[1:]:
        total = total + term.astype(F32)
    return total.astype(BF)


class Halves:
    def __init__(self, ref):
        self.ref, self.at, self.size = ref, self, ref.shape[0] // 2

    def __getitem__(self, index):
        i, piece = index if isinstance(index, tuple) else (index, slice(None))
        if isinstance(piece, slice):
            return self.ref.at[pl.ds(i * self.size, self.size)]
        return self.ref.at[pl.ds(i * self.size + piece.start, piece.size)]


class Here:
    def __init__(self):
        self.z, self.f, self.y, self.x, self.core = spot()
        self.fx = self.f + 2 - 4 * self.x
        self.fy = self.f + 4 - 8 * self.y
        self.fc = self.f + 1 - 2 * self.core
        z = self.z
        self.outer = (z == 0) | (z == 3)
        self.near = jnp.where(z < 2, 1 - z, 5 - z)
        self.across = jnp.where(self.outer, z, 3 - z)
        self.own = jnp.where(z < 2, 0, 1)

    def greet(self, barrier, rows, column=0):
        for n in range(column):
            pl.semaphore_signal(barrier, inc=1, device_id=(lax.rem(self.z + n + 1, 4), self.f), device_id_type=MESH)
        for t in (self.fx, self.fy, self.fc):
            pl.semaphore_signal(barrier, inc=1, device_id=(self.z, t), device_id_type=MESH)
        pl.semaphore_signal(barrier, inc=1, device_id=(self.near, self.f), device_id_type=MESH)

        @pl.when(jnp.logical_not(self.outer))
        def _():
            pl.semaphore_signal(barrier, inc=1, device_id=(self.across, self.f), device_id_type=MESH)

        pl.semaphore_wait(barrier, rows.greet(barrier) + 4 + column + jnp.where(self.outer, 0, 1))


def lanes(start, size):
    return pl.ds(start if isinstance(start, int) else pl.multiple_of(start, 128), size)


PIECES = 8
WIDE_SLOTS = 3
DOWN_FIRST = 0
PLAN = (
    ("r", 0),
    ("f", ("w", 0)),
    ("r", 0),
    ("f", ("w", 1)),
    ("c", "ln2"),
    ("r", 0),
    ("f", ("d", 0)),
    ("s", ("w", 0), 0),
    ("r", 0),
    ("c", "do"),
    ("s", ("w", 1), 0),
    ("r", 0),
    ("c", "og"),
    ("r", 0),
    ("b", ("o", 0)),
    ("c", "E0.0"),
    ("c", "E0.1"),
    ("s", ("d", 0), 0),
    ("r", 0),
    ("c", "E1.0"),
    ("s", ("w", 0), 1),
    ("s", ("w", 1), 1),
    ("r", 0),
    ("c", "E1.1"),
    ("f", ("w", 2)),
    ("c", "F0"),
    ("s", ("o", 0), 0),
    ("s", ("w", 0), 2),
    ("c", "E2.0"),
    ("s", ("d", 0), 1),
    ("s", ("w", 1), 2),
    ("f", ("w", 3)),
    ("s", ("w", 0), 3),
    ("c", "E2.1"),
    ("s", ("w", 2), 0),
    ("s", ("w", 1), 3),
    ("c", "F1"),
    ("s", ("o", 0), 1),
    ("s", ("w", 0), 4),
    ("f", ("d", 1)),
    ("s", ("w", 3), 0),
    ("s", ("w", 1), 4),
    ("s", ("d", 0), 2),
    ("c", "G0"),
    ("s", ("w", 2), 1),
    ("b", ("w", 7)),
    ("c", "E3.0"),
    ("s", ("o", 0), 2),
    ("c", "E3.1"),
    ("s", ("d", 0), 3),
    ("c", "F2"),
    ("s", ("d", 1), 0),
    ("s", ("o", 0), 3),
    ("s", ("w", 2), 2),
    ("c", "G1"),
    ("s", ("w", 3), 1),
    ("b", ("w", 8)),
    ("c", "F3"),
    ("s", ("d", 0), 4),
    ("c", "G2"),
    ("s", ("w", 7), 0),
    ("s", ("o", 0), 4),
    ("s", ("w", 3), 2),
    ("b", ("w", 9)),
    ("c", "H"),
    ("s", ("d", 1), 1),
    ("s", ("w", 2), 3),
    ("s", ("w", 3), 3),
    ("c", "gains"),
    ("b", ("g", 0)),
    ("c", "G3"),
    ("s", ("w", 8), 0),
    ("s", ("w", 2), 4),
    ("r", 1),
    ("s", ("w", 7), 1),
    ("f", ("w", 4)),
    ("s", ("w", 3), 4),
    ("r", 1),
    ("s", ("w", 9), 0),
    ("s", ("g", 0), 0),
    ("s", ("d", 1), 2),
    ("s", ("w", 8), 1),
    ("f", ("w", 5)),
    ("r", 1),
    ("s", ("w", 4), 0),
    ("s", ("d", 1), 3),
    ("s", ("w", 7), 2),
    ("s", ("w", 9), 1),
    ("s", ("g", 0), 1),
    ("f", ("w", 6)),
    ("s", ("w", 8), 2),
    ("s", ("w", 5), 0),
    ("s", ("d", 1), 4),
    ("s", ("w", 4), 1),
    ("s", ("w", 7), 3),
    ("b", ("w", 10)),
    ("s", ("w", 0), 5),
    ("s", ("w", 1), 5),
    ("s", ("d", 0), 5),
    ("s", ("o", 0), 5),
    ("s", ("w", 2), 5),
    ("s", ("w", 3), 5),
    ("r", 1),
    ("s", ("w", 8), 3),
    ("s", ("w", 9), 2),
    ("s", ("g", 0), 2),
    ("s", ("w", 7), 4),
    ("s", ("d", 1), 5),
    ("s", ("w", 6), 0),
    ("s", ("w", 5), 1),
    ("s", ("w", 4), 2),
    ("s", ("w", 8), 4),
    ("r", 1),
    ("s", ("w", 9), 3),
    ("s", ("g", 0), 3),
    ("s", ("w", 5), 2),
    ("s", ("w", 4), 3),
    ("s", ("w", 10), 0),
    ("s", ("w", 7), 5),
    ("s", ("w", 6), 1),
    ("s", ("w", 8), 5),
    ("s", ("w", 10), 1),
    ("s", ("w", 9), 4),
    ("s", ("g", 0), 4),
    ("s", ("w", 6), 2),
    ("s", ("w", 5), 3),
    ("s", ("w", 4), 4),
    ("s", ("w", 10), 2),
    ("s", ("w", 6), 3),
    ("s", ("w", 5), 4),
    ("r", 1),
    ("s", ("w", 10), 3),
    ("s", ("w", 6), 4),
    ("r", 1),
    ("s", ("w", 10), 4),
    ("r", 1),
    ("s", ("w", 9), 5),
    ("s", ("g", 0), 5),
    ("s", ("w", 4), 5),
    ("s", ("w", 5), 5),
    ("s", ("w", 6), 5),
    ("s", ("w", 10), 5),
)


def split_plan():
    before, loop, after = [], {(n, m): [] for n in range(10) for m in range(3)}, []
    place = before
    for op in PLAN:
        mark = op[1] if op[0] == "c" else ""
        if mark in ("H", "G3"):
            place = after
        elif mark[:1] == "E":
            place = loop[2 * int(mark[1]) + int(mark[3]), 0]
        elif mark[:1] == "F":
            place = loop[2 * int(mark[1]) + 3, 1]
        elif mark[:1] == "G":
            place = loop[2 * int(mark[1]) + 5, 2]
        if mark[:1] not in ("E", "F", "G") or mark == "G3":
            place.append(op)
    return before, loop, after


def rope(values, cosine, sine):
    lane = lax.broadcasted_iota(jnp.int32, (1, 128), 1)
    turned = jnp.where(lax.rem(lane, 64) < 32, -pltpu.roll(values, 96, 1), pltpu.roll(values, 32, 1))
    return values * cosine + turned * sine


def front_kernel(
    attn_h, ffn_h, qkv_h, out_h, in_h, down_h, tok_f, cot_f, starts_f, inverse,
    qkv_o, out_o, cot_o, tok_o, mid_o, gn_o, ffn_o, q_o, k_o, v_o, mix_o, bias_o, xt_o, mt_o, nt_o, glc_o, gj_o, at_o,
    gains_o, cos_o, sin_o, lse_o,
    gains_v, qkv_v, out_v, in_v, down_v, tok_v, starts_v, acc_f, acc_g, gl, normed, x2, q, k, v, mix, bias,
    gains_h, starts_h, tok_h, cot_h, gj, act, mine, theirs, rows_b,
    ss, rs, ssi, rsi, ls, lsi, es, er, el, ds_, dr, kvs, kvr, ws, ts, tr, tl, gs_, gr_, gw, as_, ar_, aw,
):
    h = Here()
    rows = Rows(h.z, h.f, h.core)
    z, f, core = h.z, h.f, h.core
    fx, fy, fc = h.fx, h.fy, h.fc
    fd = fx + 4 - 8 * h.y
    sib = (z, fc)
    half, wide = normed.shape
    block = half // 2
    own_rows, sib_rows = pl.ds(0, half), pl.ds(half, half)

    shards = (gains_h, qkv_h, out_h, down_h)
    wholes = (gains_v, qkv_v, out_v, down_v)
    targets = (fx, fy, fc, fy, fx, fc, fc, fc, fc)

    def part(w, i, cols=None):
        whole = wholes[w]
        if w < 3:
            return whole.at[i] if cols is None else whole.at[i, :, cols]
        r = pl.ds(pl.multiple_of(i * SHARD, 16), SHARD)
        return whole.at[r] if cols is None else whole.at[r, cols]

    def copy(w, k):
        a, b = halves(shards[w].shape[1])
        place = {3: (fx, a), 4: (fy, b), 5: (fx,), 6: (fy,), 7: (fd, a), 8: (fd, b)}
        dst = part(w, f) if k < 3 else part(w, *place[k])
        return remote(shards[w] if k < 3 else dst, dst, ss.at[w, k], rs.at[w, k], (z, targets[k]))

    quarter = pl.ds(pl.multiple_of(z * 32, 32), 32)

    def place_in(t, i, *more):
        return in_v.at[(t, i // 2, lax.rem(i, 2)) + more]

    def copy_in(t, k):
        cols = lanes(t * GROUP, GROUP)
        if t in BY_Z:
            if k in (0, 1):
                return remote(in_h.at[:, quarter, cols], place_in(t, f, slice(None), quarter), ssi.at[t, k], rsi.at[t, k], (z, targets[k]))
            if k in (3, 4):
                dst = place_in(t, (fx, fy)[k - 3], k - 3, quarter)
                return remote(dst, dst, ssi.at[t, k], rsi.at[t, k], (z, targets[k]))
            if k < 8:
                dst = in_v.at[t, :, core, :, quarter]
                return remote(dst, dst, ssi.at[t, k], rsi.at[t, k], (lax.rem(z + k - 4, 4), f))
            dst = in_v.at[t, :, core]
            return remote(dst, dst, ssi.at[t, k], rsi.at[t, k], sib)
        place = {3: (fx, 0), 4: (fy, 1), 5: (fx,), 6: (fy,), 7: (fd, 0), 8: (fd, 1)}
        dst = place_in(t, f) if k < 3 else place_in(t, *place[k])
        return remote(in_h.at[:, :, cols] if k < 3 else dst, dst, ssi.at[t, k], rsi.at[t, k], (z, targets[k]))

    def quarters(t, stage):
        waits, starts = (((), (0, 1)), ((0, 1), (3, 4)), ((3, 4), (5, 6, 7)), ((5, 6, 7), (8,)), ((8,), ()))[stage]
        for k in waits:
            copy_in(t, k).wait_recv()
        if stage == 2:
            own_in(t).wait()
        for k in starts:
            copy_in(t, k).start()

    def first(w, copy=copy):
        for k in range(3):
            copy(w, k).start()

    def second(w, copy=copy):
        for k in (0, 1):
            copy(w, k).wait_recv()
            copy(w, k + 3).start()
            copy(w, k + 5).start()

    def third(w, copy=copy):
        for k in (3, 4):
            copy(w, k).wait_recv()
            copy(w, k + 4).start()

    def rest(w, copy=copy):
        for k in (2, 5, 6, 7, 8):
            copy(w, k).wait_recv()

    def own(w):
        return pltpu.make_async_copy(shards[w], part(w, f), ls.at[w])

    def own_in(t):
        cols = lanes(t * GROUP, GROUP)
        if t in BY_Z:
            return pltpu.make_async_copy(in_h.at[:, quarter, cols], place_in(t, f, slice(None), quarter), lsi.at[t])
        return pltpu.make_async_copy(in_h.at[:, :, cols], place_in(t, f), lsi.at[t])

    wide_in = [
        [pltpu.make_async_copy(src.at[i], ref.at[pl.ds(i * block, block)], el.at[i]) for i in range(2)]
        for src, ref in ((tok_f, acc_f), (cot_f, acc_g))
    ]
    for c in wide_in[0]:
        c.start()
    gains_h[:, :128] = jnp.broadcast_to(attn_h[...].astype(F32), (16, 128)).astype(BF)
    gains_h[:, 128:] = jnp.broadcast_to(ffn_h[...].astype(F32), (16, 128)).astype(BF)
    starts_h[...] = jnp.zeros(starts_h.shape, jnp.int32)
    starts_h[:2, :8] = starts_f[...]
    for w in range(4):
        own(w).start()
    for t in range(STEPS):
        own_in(t).start()
    h.greet(pltpu.get_barrier_semaphore(), rows, 3)
    info = remote(starts_h, starts_v.at[core], ds_.at[0], dr.at[0], sib)
    own_info = pltpu.make_async_copy(starts_h, starts_v.at[core], el.at[2])
    info.start()
    own_info.start()
    for t in BY_Z:
        quarters(t, 0)
    for w in range(3):
        first(w)
    for c in wide_in[0]:
        c.wait()
    tok_h[...] = acc_f[...].astype(BF)
    rows.start(Halves(tok_h), tok_v, es.at[0], er.at[0], el.at[3], True)
    for c in wide_in[1]:
        c.start()
    for c in wide_in[1]:
        c.wait()
    cot_h[...] = acc_g[...].astype(BF)
    info.wait()
    own_info.wait()

    lane = lax.broadcasted_iota(jnp.int32, (1, 128), 1)
    begins = starts_v[lax.rem(z, 2), pl.ds(z // 2, 1), :]
    inside = lane < 8

    def documents(base):
        place = lax.broadcasted_iota(jnp.int32, (half, 128), 0) + base
        before = (begins <= place) & inside
        number = jnp.sum(jnp.where(before, 1.0, 0.0), axis=1, keepdims=True)
        begin = jnp.max(jnp.where(before, begins, 0).astype(F32), axis=1, keepdims=True)
        return place, number, begin

    place, number, begin = documents(core * half)
    angle = (place.astype(F32) - begin) * inverse[...]
    cos_o[...] = jnp.cos(angle)
    sin_o[...] = jnp.sin(angle)
    across = jnp.broadcast_to(number, (half, 128)).T[0:1, :]
    _, other, _ = documents((1 - core) * half)
    bias[:half] = jnp.where(number == across, 0.0, MASKED_SCORE).astype(BF)
    bias[half:] = jnp.where(other == across, 0.0, MASKED_SCORE).astype(BF)

    for t in BY_Z:
        quarters(t, 1)
    for w in range(3):
        second(w)
    rows.start(Halves(cot_h), cot_o, es.at[1], er.at[1], el.at[4], True)
    first(3)
    first(0, copy_in)
    first(1, copy_in)
    for t in BY_Z:
        quarters(t, 2)
    third(0)
    rest(0)
    own(0).wait()
    for n in range(2):
        for i in range(8):
            gains_o[n : n + 1, i * 128 : i * 128 + 128] = gains_v[i, 0:1, n * 128 : n * 128 + 128].astype(F32)
    rows.wait(Halves(tok_h), tok_v, es.at[0], er.at[0], el.at[3], True)
    saved = []

    def save(src, dst):
        saved.append(pltpu.make_async_copy(src, dst, ws.at[len(saved)]))
        saved[-1].start()

    def share(src, dst, n, again):
        keep = pltpu.make_async_copy(mine, dst.at[:, own_rows], tl.at[n])
        give = remote(theirs, dst.at[:, sib_rows], ts.at[n], tr.at[n], sib)
        if again is not None:
            again[0].wait()
            again[1].wait_send()
        for i in range(4):
            mine[i * 128 : i * 128 + 128] = src[:, lanes((2 * i + core) * 128, 128)].T
            theirs[i * 128 : i * 128 + 128] = src[:, lanes((2 * i + 1 - core) * 128, 128)].T
        keep.start()
        give.start()
        return keep, give

    unit, _ = moments(tok_v[...].reshape(half, wide).astype(F32))
    normed[...] = (unit * gains_o[0:1]).astype(BF)
    save(tok_v, tok_o)
    save(bias, bias_o)
    shared = share(normed, nt_o, 0, None)
    third(1)
    rest(1)
    own(1).wait()
    save(qkv_v, qkv_o)

    def pair_send(n, i):
        ref = (k, v)[n]
        cols = pl.ds(i * 256, 256)
        return remote(ref.at[own_rows, cols], ref.at[sib_rows, cols], kvs.at[n, i], kvr.at[n, i], sib)

    for n, ref in ((1, k), (2, v), (0, q)):
        for i in range(4):
            product = nn(normed[...], qkv_v[:, :, n * wide + i * 256 : n * wide + i * 256 + 256].reshape(wide, 256))
            for j in range(2):
                cols = slice(i * 256 + j * 128, i * 256 + j * 128 + 128)
                value = product[:, j * 128 : j * 128 + 128]
                value = value if n == 2 else rope(value, cos_o[...], sin_o[...])
                ref[:half, cols] = value.astype(BF)
            if n:
                pair_send(n - 1, i).start()
    third(2)
    for n in range(2):
        for i in range(4):
            pair_send(n, i).wait()
    for ref, dst in ((q, q_o), (k, k_o), (v, v_o)):
        save(ref, dst)

    def attend(i, _):
        @pl.when(i == 4)
        def _():
            second(3)

        @pl.when(i == 6)
        def _():
            second(0, copy_in)

        cols = lanes(i * 128, 128)
        queries = q[:, cols] * jnp.asarray(0.125, BF)
        keys = k[:, cols]
        vt = v[:, cols].T
        outs = []
        for e in range(2):
            here = (lane < 64) if e == 0 else (lane >= 64)
            scores = nt(keys, jnp.where(here, queries, jnp.zeros_like(queries))) + bias[...].astype(F32)
            top = jnp.max(scores, axis=0, keepdims=True)
            p = jnp.exp(scores - top)
            total = jnp.sum(p, axis=0, keepdims=True)
            outs.append(nn(vt, p.astype(BF)) / total)
            lse_o[i, e : e + 1, :] = top + jnp.log(total)
        mix[:, cols] = jnp.concatenate([outs[0][:64], outs[1][64:]], axis=0).T.astype(BF)
        return 0

    lax.fori_loop(0, 8, attend, 0)
    second(1, copy_in)
    first(3, copy_in)
    first(5, copy_in)
    rest(2)
    own(2).wait()
    save(out_v, out_o)
    save(mix, mix_o)
    middle = tok_v[...].reshape(half, wide).astype(F32) + nn(mix[...], out_v[...].reshape(wide, wide))
    acc_f[...] = middle
    unit, _ = moments(middle)
    x2[...] = (unit * gains_o[1:2]).astype(BF)
    mid_save = pltpu.make_async_copy(acc_f, mid_o, ls.at[4])
    mid_save.start()
    third(3)
    third(0, copy_in)
    rows.wait(Halves(cot_h), cot_o, es.at[1], er.at[1], el.at[4], True)
    cot_load = [pltpu.make_async_copy(cot_o.at[i], gl.at[pl.ds(i * block, block)], el.at[i]) for i in range(2)]
    for c in cot_load:
        c.start()
    shared = share(x2, xt_o, 1, shared)
    shared = share(mix, mt_o, 2, shared)
    for c in cot_load:
        c.wait()
    glc_keep = pltpu.make_async_copy(gl.at[:, lanes(core * 512, 512)], glc_o.at[own_rows], tl.at[3])
    glc_give = remote(gl.at[:, lanes((1 - core) * 512, 512)], glc_o.at[sib_rows], ts.at[3], tr.at[3], sib)
    glc_keep.start()
    glc_give.start()
    mid_save.wait()
    quarters(2, 3)
    rest(3)
    own(3).wait()

    def stage_copies(t):
        s = lax.rem(t, 2)
        r = lanes(t * GROUP, GROUP)
        return [
            pltpu.make_async_copy(gj.at[s], gj_o.at[t, own_rows], gw.at[s]),
            pltpu.make_async_copy(act.at[s], at_o.at[r, own_rows], aw.at[s]),
        ], [
            remote(gj.at[s], gj_o.at[t, sib_rows], gs_.at[s], gr_.at[t], sib),
            remote(act.at[s], at_o.at[r, sib_rows], as_.at[s], ar_.at[t], sib),
        ]

    def feed(t, _):
        s = lax.rem(t, 2)

        def at_step(events):
            for n, todo in events.items():

                @pl.when(t == n)
                def _(todo=todo):
                    for act, *args in todo:
                        act(*args)

        at_step({
            1: [(second, 3, copy_in), (first, 6, copy_in)],
            2: [(second, 5, copy_in), (quarters, 4, 3)],
            3: [(second, 6, copy_in)],
        })

        def ready(n):
            if n in BY_Z:
                quarters(n, 4)
            else:
                rest(n, copy_in)
                own_in(n).wait()

        at_step({n: [(ready, n)] for n in range(STEPS)})
        w = jnp.concatenate([in_v[t, :, :, m].reshape(wide, GROUP) for m in range(2)], axis=1)
        wd = down_v[lanes(t * GROUP, GROUP)]
        joined = nn(x2[...], w)
        a, c = joined[:, :GROUP], joined[:, GROUP:]
        grad_active = nt(gl[...], wd)
        phi = 0.5 * (1.0 + lax.erf(a * SQRT_HALF))
        gate = a * phi
        slope = phi + a * (jnp.exp(-0.5 * a * a) * DENSITY)
        active = (gate * c).astype(BF)
        ga = (slope * c * grad_active).astype(BF)
        gc = (gate * grad_active).astype(BF)

        @pl.when(t >= 2)
        def _():
            keep, give = stage_copies(t - 2)
            for copied in keep:
                copied.wait()
            for sent in give:
                sent.wait_send()

        gj[s, :, :GROUP] = ga
        gj[s, :, GROUP:] = gc
        act[s] = active.T
        keep, give = stage_copies(t)
        for started in keep + give:
            started.start()

        at_step({n: [(third, m, copy_in)] for n, m in ((0, 1), (2, 3), (3, 5), (4, 6))})
        acc_f[...] += nn(active, wd)
        back = nt(gj[s], w)

        @pl.when(t == 0)
        def _():
            acc_g[...] = back

        @pl.when(t > 0)
        def _():
            acc_g[...] += back

        return 0

    lax.fori_loop(0, STEPS, feed, 0)
    rows_b[...] = acc_f[...].astype(BF).reshape(2, block, wide)
    save(rows_b, ffn_o)
    save(acc_g, gn_o)
    for t in (STEPS - 2, STEPS - 1):
        keep, give = stage_copies(t)
        for copied in keep:
            copied.wait()
        for sent in give:
            sent.wait_send()
    for t in range(STEPS):
        for received in stage_copies(t)[1]:
            received.wait_recv()
    shared[0].wait()
    shared[1].wait_send()
    for n, dst in enumerate((nt_o, xt_o, mt_o)):
        remote(theirs, dst.at[:, sib_rows], ts.at[n], tr.at[n], sib).wait_recv()
    glc_keep.wait()
    glc_give.wait()
    for w in range(4):
        for kind in range(9):
            copy(w, kind).wait_send()
    for t in range(STEPS):
        for kind in range(9):
            if t not in BY_Z or kind != 2:
                copy_in(t, kind).wait_send()
    for c in saved:
        c.wait()


def front_all(attn_gain, ffn_gain, qkv, out, inw, down, tok, cot, starts, inverse):
    dma = pltpu.SemaphoreType.DMA
    block, wide = tok.shape[1:]
    half, hidden = 2 * block, STEPS * GROUP

    def shape(*s, kind=BF):
        return jax.ShapeDtypeStruct(s, kind)

    def buf(*s, kind=BF):
        return pltpu.VMEM(s, kind)

    whole = pl.BlockSpec(memory_space=pltpu.VMEM)
    return pl.pallas_call(
        front_kernel,
        out_shape=[
            shape(8, *qkv.shape), shape(8, *out.shape), shape(*cot.shape), shape(*tok.shape),
            shape(half, wide, kind=F32), shape(half, wide, kind=F32), shape(2, block, wide),
            shape(half, wide), shape(2 * half, wide), shape(2 * half, wide), shape(half, wide), shape(2 * half, half),
            shape(half, 2 * half), shape(half, 2 * half), shape(half, 2 * half), shape(2 * half, half),
            shape(STEPS, 2 * half, 2 * GROUP), shape(hidden, 2 * half),
            shape(2, wide, kind=F32), shape(half, 128, kind=F32), shape(half, 128, kind=F32), shape(8, 2, half, kind=F32),
        ],
        in_specs=[whole] * 2 + [ANY] * 6 + [whole] * 2,
        out_specs=[ANY] * 18 + [whole] * 4,
        scratch_shapes=[
            buf(8, 16, 256), buf(8, *qkv.shape), buf(8, *out.shape), buf(STEPS, 4, 2, 2, 128, GROUP), buf(hidden, wide),
            buf(*tok.shape), buf(2, 8, 128, kind=jnp.int32), buf(half, wide, kind=F32), buf(half, wide, kind=F32),
            buf(half, wide), buf(half, wide), buf(half, wide), buf(half, wide), buf(2 * half, wide), buf(2 * half, wide),
            buf(half, wide), buf(2 * half, half),
            buf(16, 256), buf(8, 128, kind=jnp.int32), buf(half, wide), buf(half, wide),
            buf(2, half, 2 * GROUP), buf(2, GROUP, half), buf(half, half), buf(half, half), buf(2, block, wide),
            dma((4, 9)), dma((4, 9)), dma((STEPS, 9)), dma((STEPS, 9)), dma((5,)), dma((STEPS,)),
            dma((2, 2)), dma((2, 2)), dma((5,)), dma((1,)), dma((1,)), dma((2, 4)), dma((2, 4)), dma((10,)),
            dma((4,)), dma((4,)), dma((4,)), dma((2,)), dma((STEPS,)), dma((2,)), dma((2,)), dma((STEPS,)), dma((2,)),
        ],
        compiler_params=pltpu.CompilerParams(collective_id=1, has_side_effects=True, vmem_limit_bytes=VMEM_BYTES),
        name="gather_attention_feed_forward",
    )(attn_gain, ffn_gain, qkv, out, inw, down, tok, cot, starts, inverse)


def back_kernel(
    ffn_h, mid_h, gn_h, cot_h, qkv_h, out_h, q_h, k_h, v_h, mix_h, rows_h, bias_h, xt_h, mt_h, nt_h, glc_h, gj_h, at_h,
    gains, cosine, sine, lse,
    in_o, qkv_o, down_o, out_o, gain_o, outh_o, inh_o,
    acc_f, acc_g, win, xt, mt, gj, gq, at, glc, gm, dout, q, k, v, bias, kept, dx_kv, kvl, centres, terms, gs, gr,
    ld, gld, wsem, ps, pr, kvs, kvr, gqs, gqr, dxs, dxr, fo, es, er, el,
    *sum_refs,
):
    h = Here()
    rows = Rows(h.z, h.f, h.core)
    order = [op[1][1] for op in PLAN if op[0] in "fb" and op[1][0] == "w"]
    wide = Sums(h, sum_refs[0:7], {t: n % WIDE_SLOTS for n, t in enumerate(order)})
    down = Sums(h, sum_refs[7:14], {0: 0, 1: 1})
    outs = Sums(h, sum_refs[14:21], {0: 0})
    gain = Sums(h, sum_refs[21:28], {0: 0})
    groups = {"w": wide, "d": down, "o": outs, "g": gain}
    sib = (h.z, h.fc)
    half, width = dout.shape
    block = half // 2
    own_rows, sib_rows = pl.ds(0, half), pl.ds(half, half)
    lane = lax.broadcasted_iota(jnp.int32, (1, 128), 1)

    def load(src, dst, n):
        return pltpu.make_async_copy(src, dst, ld.at[n])

    def gj_load(t):
        return pltpu.make_async_copy(gj_h.at[t], gj, gld.at[0])

    def qkv_weights(u):
        return [
            pltpu.make_async_copy(qkv_h.at[:, :, lanes(n * 1024 + u * 256, 256)], win.at[:, :, pl.ds(n * 256, 256)], wsem.at[n])
            for n in range(3)
        ]

    loads = {
        "xt": load(xt_h, xt, 0), "mid": load(mid_h, acc_f, 1), "gn": load(gn_h, acc_g, 2),
        "c0": load(cot_h.at[0], dout.at[pl.ds(0, block)], 3), "c1": load(cot_h.at[1], dout.at[pl.ds(block, block)], 4),
        "w": load(out_h, k, 5), "mix": load(mix_h, v.at[own_rows], 6), "mt": load(mt_h, mt, 7),
        "at": load(at_h, at, 8), "glc": load(glc_h, glc, 9), "bias": load(bias_h, bias, 10), "q": load(q_h, q, 11),
        "nt": load(nt_h, mt, 7), "k": load(k_h, k, 5), "v": load(v_h, v, 6),
        "r0": load(rows_h.at[0], k.at[pl.ds(0, block)], 3), "r1": load(rows_h.at[1], k.at[pl.ds(block, block)], 4),
    }

    def start(*names):
        for name in names:
            loads[name].start()

    def wait(*names):
        for name in names:
            loads[name].wait()

    start("xt")
    gj_load(0).start()
    start("mid", "gn", "c0", "c1")
    start("w", "mix", "at", "glc", "mt", "bias", "q")
    h.greet(pltpu.get_barrier_semaphore(), rows)

    def put(group, t, term, cut):
        s = group.slot[t]
        term = term.astype(BF)
        for o in range(4):
            for n in range(2):
                group.acc[s, n, o // 2, o % 2] = term[o * 128 : o * 128 + 128, n * cut : n * cut + cut]

    def in_term(t):
        if t == 0:
            wait("xt")
        gj_load(t).wait()
        put(wide, t, nn(xt[...], gj[...]), GROUP)
        if t + 1 < STEPS:
            gj_load(t + 1).start()

    def down_term(j):
        if j == DOWN_FIRST:
            wait("at", "glc")
        term = nn(at[...], glc[:, j * 256 : j * 256 + 256])
        for f in range(8):
            down.acc[j, f % 2, f // 4, f // 2 % 2] = term[f * SHARD : f * SHARD + SHARD].astype(BF)

    gm_send = remote(gm.at[own_rows], gm.at[sib_rows], ps.at[0], pr.at[0], sib)

    def second_norm():
        wait("mid", "gn", "c0", "c1")
        back, terms[1:2] = norm_back(acc_f[...], gains[1:2], acc_g[...])
        grad_mid = dout[...].astype(F32) + back
        acc_f[...] = grad_mid
        gm[:half] = grad_mid.astype(BF)
        gm_send.start()

    def mixture_grads():
        wait("w", "mix")
        dout[...] = nt(gm[:half], k[...]).astype(BF)
        start("k")
        for j in range(8):
            cols = slice(j * 128, j * 128 + 128)
            products = (v[:half, cols].astype(F32) * dout[:, cols].astype(F32)).T
            for e in range(2):
                centres[j, e : e + 1] = jnp.sum(products[64 * e : 64 * e + 64], axis=0, keepdims=True)
        start("v")

    def out_term():
        wait("mt")
        gm_send.wait()
        put(outs, 0, nn(mt[...], gm[...]), 512)
        start("nt")

    def kv_rows(s):
        return pl.ds(s * half if isinstance(s, int) else pl.multiple_of(s * half, half), half)

    def kv_send(u):
        s = lax.rem(u, 2)
        return remote(dx_kv, kvl.at[s], kvs.at[s], kvr.at[s], sib)

    def gq_send(u):
        s = lax.rem(u, 2)
        return remote(gq.at[s, own_rows], gq.at[s, sib_rows], gqs.at[s], gqr.at[s], sib)

    def stashed(b, n, j):
        return jnp.concatenate([kept[b, pl.ds(n * 128, 128), pl.ds(m * 256 + j * 128, 128)] for m in range(4)], axis=0)

    def heads_back(p):
        u, j = p // 2, lax.rem(p, 2)
        s = lax.rem(u, 2)
        col = lanes(p * 128, 128)
        queries = q[:, col] * jnp.asarray(0.125, BF)
        keys, values, do = k[:, col], v[:, col], dout[:, col]
        kt = keys.T
        none = jnp.zeros_like(queries)
        dqs, dks, dvs = [], [], []
        for e in range(2):
            part = (lane < 64) if e == 0 else (lane >= 64)
            prob = jnp.exp(nt(keys, jnp.where(part, queries, none)) + bias[...].astype(F32) - lse[p, e : e + 1, :])
            dvs.append(nn(prob.astype(BF), do))
            ds = (prob * (nt(values, jnp.where(part, do, none)) - centres[p, e : e + 1, :])).astype(BF)
            dks.append(nn(ds, queries))
            dqs.append(nn(kt, ds))
        dq = jnp.concatenate([dqs[0][:64], dqs[1][64:]], axis=0).T
        dk = jnp.where(lane < 64, dks[0], dks[1]).astype(BF)
        dv = jnp.where(lane < 64, dvs[0], dvs[1]).astype(BF)
        for n, part in enumerate(((dq * 0.125).astype(BF), dk, dv)):
            for m in range(4):
                kept[s, pl.ds(n * 128, 128), lanes(m * 256 + j * 128, 128)] = part[m * 128 : m * 128 + 128]

        @pl.when((j == 0) & (u >= 1))
        def _():
            kv_send(u - 1).wait_send()

        dx_kv[:, lanes(j * 128, 128)] = dk[half:]
        dx_kv[:, lanes(256 + j * 128, 128)] = dv[half:]

    def heads_close(u):
        b = lax.rem(u, 2)

        @pl.when(u >= 2)
        def _():
            gq_send(u - 2).wait_send()

        kv_send(u).wait_recv()
        for j in range(2):
            c = slice(j * 128, j * 128 + 128)
            gq[b, :half, c] = rope_back(stashed(b, 0, j).astype(F32), cosine[...], sine[...]).astype(BF)
            g = added(stashed(b, 1, j), kvl[b, :, c]).astype(F32)
            gq[b, :half, 256 + j * 128 : 384 + j * 128] = rope_back(g, cosine[...], sine[...]).astype(BF)
            gq[b, :half, 512 + j * 128 : 640 + j * 128] = added(stashed(b, 2, j), kvl[b, :, 256 + j * 128 : 384 + j * 128])
        for c in qkv_weights(u):
            c.wait()
        back = nt(gq[b, :half], win[...].reshape(width, 768))

        @pl.when(u == 0)
        def _():
            acc_g[...] = back

        @pl.when(u > 0)
        def _():
            acc_g[...] += back

        @pl.when(u < 3)
        def _():
            for c in qkv_weights(u + 1):
                c.start()

    def qkv_term(u):
        gq_send(u).wait_recv()
        put(wide, STEPS + u, nn(mt[...], gq[u % 2]), GROUP)

    def first_norm():
        wait("r0", "r1")
        back, terms[0:1] = norm_back(k[:half].astype(F32), gains[0:1], acc_g[...])
        dout[...] = (acc_f[...] + back).astype(BF)

    gs_send = remote(gs, gr, ps.at[1], pr.at[1], sib)

    def gain_terms():
        for n in range(2):
            for o in range(4):
                for ref, part in ((gain.acc.at[0], h.core), (gs, 1 - h.core)):
                    low, high = terms[n : n + 1, 256 * o : 256 * o + 128], terms[n : n + 1, 256 * o + 128 : 256 * o + 256]
                    value = jnp.where(part == 0, low, high)
                    ref[n, o // 2, o % 2] = jnp.broadcast_to(value, (16, 128)).astype(BF)
        gs_send.start()
        gs_send.wait()
        for n in range(2):
            for o in range(4):
                gain.acc[0, n, o // 2, o % 2] = added(gain.acc[0, n, o // 2, o % 2], gr[n, o // 2, o % 2])

    def dx(j):
        return kvl.at[j, pl.ds(0, SHARD), pl.ds(0, 256)]

    def down_swap(j, act, ref):
        act(remote(ref.at[j, 1 - h.core], dx(j), dxs.at[j], dxr.at[j], sib))

    def to_end(j):
        return pltpu.make_async_copy(dx(j), down_o.at[:, lanes((1 - h.core) * 512 + j * 256, 256)], fo.at[2, 5 + j])

    def write(name, t, act, ref):
        if name == "w" and t < STEPS:
            for n in range(2):
                act(pltpu.make_async_copy(ref.at[t, n], in_o.at[n, :, pl.ds(t * GROUP, GROUP)], fo.at[0, 2 * t + n]))
        elif name == "w":
            parts = ((0, 0, 256, 0), (0, 256, 128, 1024), (1, 0, 128, 1152), (1, 128, 256, 2048))
            for n, (m, at_col, size, to) in enumerate(parts):
                dst = qkv_o.at[:, pl.ds(to + (t - STEPS) * 256, size)]
                act(pltpu.make_async_copy(ref.at[t, m, :, pl.ds(at_col, size)], dst, fo.at[1, 4 * (t - STEPS) + n]))
        elif name == "d":
            dst = down_o.at[:, lanes(h.core * 512 + t * 256, 256)]
            act(pltpu.make_async_copy(ref.at[t, h.core], dst, fo.at[2, 3 + t]))
        elif name == "o":
            for n in range(2):
                act(pltpu.make_async_copy(ref.at[0, n], out_o.at[:, pl.ds(n * 512, 512)], fo.at[2, n]))
        else:
            act(pltpu.make_async_copy(ref, gain_o, fo.at[2, 2]))

    sent = [0, 0]

    def piece(which):
        size = block // PIECES
        part = pl.ds(sent[which] * size, size)
        sent[which] += 1
        if which == 0:
            rows.start(ffn_h, outh_o, es.at[0], er.at[0], el.at[0], False, part)
        else:
            rows.start(Halves(dout), inh_o, es.at[1], er.at[1], el.at[1], False, part)

    work = {"ln2": second_norm, "do": mixture_grads, "og": out_term, "H": first_norm, "gains": gain_terms}

    def perform(ops):
        for op in ops:
            if op[0] == "c":
                if op[1] in work:
                    work[op[1]]()
            elif op[0] == "r":
                piece(op[1])
            else:
                (name, t), group = op[1], groups[op[1][0]]
                if op[0] == "s":
                    getattr(group, Sums.LATER[op[2]])(t)
                    if op[2] == 5:
                        group.total(functools.partial(write, name, t, lambda c: c.start()))
                        if name == "d":
                            down.total(functools.partial(down_swap, t, lambda c: c.start()))
                else:
                    if name == "w":
                        in_term(t) if t < STEPS else qkv_term(t - STEPS)
                    elif name == "d":
                        down_term(t)
                    group.begin(t)

    before, loop, after = split_plan()
    perform(before)
    wait("bias", "q", "k", "v", "nt")
    for c in qkv_weights(0):
        c.start()

    def each(p, _):
        pl.when(p < 8)(lambda: heads_back(p))
        pl.when(p == 8)(lambda: start("r0", "r1"))
        for n in range(10):
            if loop[n, 0]:
                pl.when(p == n)(functools.partial(perform, loop[n, 0]))

        @pl.when((lax.rem(p, 2) == 1) & (p >= 3))
        def _():
            heads_close((p - 3) // 2)

        for n in range(10):
            if loop[n, 1]:
                pl.when(p == n)(functools.partial(perform, loop[n, 1]))
            if loop[n, 2]:
                pl.when(p == n)(functools.partial(perform, loop[n, 2]))

        @pl.when((lax.rem(p, 2) == 1) & (p < 8))
        def _():
            kv_send(p // 2).start()

        @pl.when((lax.rem(p, 2) == 1) & (p >= 3))
        def _():
            gq_send((p - 3) // 2).start()

        return 0

    lax.fori_loop(0, 10, each, 0)
    perform(after)
    for j in range(2):
        down.total(functools.partial(down_swap, j, lambda c: c.wait()))
        to_end(j).start()
    kv_send(3).wait_send()
    gq_send(2).wait_send()
    gq_send(3).wait_send()

    for name, group in groups.items():
        for t in group.slot:
            group.total(functools.partial(write, name, t, lambda c: c.wait()))
    for j in range(2):
        to_end(j).wait()
    rows.wait(ffn_h, outh_o, es.at[0], er.at[0], el.at[0], False)
    rows.wait(Halves(dout), inh_o, es.at[1], er.at[1], el.at[1], False)


def back_all(ffn_rows, *args):
    dma = pltpu.SemaphoreType.DMA
    block, wide = ffn_rows.shape[1:]
    half = 2 * block

    def buf(*s, kind=BF):
        return pltpu.VMEM(s, kind)

    def shape(*s):
        return jax.ShapeDtypeStruct(s, BF)

    whole = pl.BlockSpec(memory_space=pltpu.VMEM)
    scratch = [
        buf(half, wide, kind=F32), buf(half, wide, kind=F32), buf(8, 128, 768),
        buf(half, 2 * half), buf(half, 2 * half), buf(2 * half, 768), buf(2, 2 * half, 768),
        buf(STEPS * GROUP, 2 * half), buf(2 * half, half), buf(2 * half, wide), buf(half, wide),
        buf(half, wide), buf(2 * half, wide), buf(2 * half, wide), buf(2 * half, half),
        buf(2, GROUP, wide), buf(half, 512), buf(2, half, 512), buf(8, 2, half, kind=F32), buf(2, wide, kind=F32),
        buf(2, 2, 2, 16, 128), buf(2, 2, 2, 16, 128),
        dma((13,)), dma((1,)), dma((3,)), dma((2,)), dma((2,)), dma((2,)), dma((2,)), dma((2,)), dma((2,)),
        dma((2,)), dma((2,)), dma((3, 16)), dma((2, 2)), dma((2, 2)), dma((2,)),
    ]
    for s in ((11, WIDE_SLOTS, 128, GROUP), (2, 2, SHARD, 256), (1, 1, 128, 512), (1, 1, 16, 128)):
        scratch += Sums.scratch(*s)
    return pl.pallas_call(
        back_kernel,
        out_shape=[
            shape(2, 128, STEPS * GROUP), shape(128, 3 * wide), shape(SHARD, wide), shape(128, wide), shape(1, 2, 16, 128),
            shape(2, block, wide), shape(2, block, wide),
        ],
        in_specs=[ANY] * 18 + [whole] * 4,
        out_specs=[ANY] * 7,
        scratch_shapes=scratch,
        compiler_params=pltpu.CompilerParams(collective_id=2, has_side_effects=True, vmem_limit_bytes=VMEM_BYTES),
        name="backward_and_sums",
    )(ffn_rows, *args)


def lay_out_kernel(in_ref, down_ref, parts_ref, rows_ref):
    shard = in_ref.shape[1] // 16
    spare = jnp.zeros((in_ref.shape[0], SHARD - shard), BF)
    for m in range(2):
        pieces = []
        for n in range(8 * m, 8 * m + 8):
            pieces += [in_ref[:, n * shard : (n + 1) * shard], spare]
        parts_ref[m] = jnp.concatenate(pieces, axis=1)

    @pl.when(pl.program_id(0) == 0)
    def _():
        under = jnp.zeros((SHARD - shard, down_ref.shape[1]), F32)
        rows_ref[...] = jnp.concatenate([down_ref[...].astype(F32), under], axis=0).astype(BF)


def lay_out(in_weight, down_weight):
    depth, wide = in_weight.shape[0], down_weight.shape[1]
    part = depth // 4
    return pl.pallas_call(
        lay_out_kernel,
        grid=(4,),
        in_specs=[pl.BlockSpec((part, in_weight.shape[1]), lambda i: (i, 0)), pl.BlockSpec(down_weight.shape, lambda i: (0, 0))],
        out_specs=[pl.BlockSpec((2, part, 8 * SHARD), lambda i: (0, i, 0)), pl.BlockSpec((SHARD, wide), lambda i: (0, 0))],
        out_shape=[jax.ShapeDtypeStruct((2, depth, 8 * SHARD), BF), jax.ShapeDtypeStruct((SHARD, wide), BF)],
        compiler_params=pltpu.CompilerParams(vmem_limit_bytes=VMEM_BYTES),
        name="lay_out_weights",
    )(in_weight, down_weight)


def results_kernel(out_b, grad_b, qkv_b, proj_b, in_b, down_b, gain_b, out_r, grad_r, qkv_r, proj_r, in_r, down_r, attn_r, ffn_r):
    attn_r[...] = gain_b[0, 0].astype(F32)[0:1]
    ffn_r[...] = gain_b[0, 1].astype(F32)[0:1]
    for src, dst in ((out_b, out_r), (grad_b, grad_r), (qkv_b, qkv_r), (proj_b, proj_r), (down_b, down_r)):
        dst[...] = src[...].astype(F32)
    shard = in_r.shape[1] // 16
    pieces = []
    for m in range(2):
        whole = in_b[m].astype(F32)
        pieces += [whole[:, n * SHARD : n * SHARD + shard] for n in range(8)]
    in_r[...] = jnp.concatenate(pieces, axis=1)


def results(out_home, in_home, qkv_t, out_t, in_t, down_t, gain_t, shard):
    block, wide = out_home.shape[1:]
    depth = qkv_t.shape[0]
    part = depth // 4

    def rows(size, width):
        return pl.BlockSpec((size, width), lambda i: (i, 0))

    home = pl.BlockSpec((2, block // 4, wide), lambda i: (0, i, 0))
    return pl.pallas_call(
        results_kernel,
        grid=(4,),
        in_specs=[home, home, rows(part, 3 * wide), rows(part, wide),
                  pl.BlockSpec((2, part, in_t.shape[2]), lambda i: (0, i, 0)), rows(96, wide),
                  pl.BlockSpec(gain_t.shape, lambda i: (0, 0, 0, 0))],
        out_specs=[home, home, rows(part, 3 * wide), rows(part, wide), rows(part, 16 * shard), rows(96, wide)]
        + [pl.BlockSpec((1, part * 4), lambda i: (0, 0))] * 2,
        out_shape=[
            jax.ShapeDtypeStruct(out_home.shape, F32), jax.ShapeDtypeStruct(in_home.shape, F32),
            jax.ShapeDtypeStruct(qkv_t.shape, F32), jax.ShapeDtypeStruct(out_t.shape, F32),
            jax.ShapeDtypeStruct((depth, 16 * shard), F32), jax.ShapeDtypeStruct((shard, wide), F32),
        ]
        + [jax.ShapeDtypeStruct((1, depth), F32)] * 2,
        compiler_params=pltpu.CompilerParams(vmem_limit_bytes=VMEM_BYTES),
        name="results_to_float32",
    )(out_home, in_home, qkv_t, out_t, in_t, down_t, gain_t)


def chip_streams(tokens, cotangent, doc_starts, qkv_weight, out_weight, in_weight, down_weight, attn_gain, ffn_gain):
    wide = tokens.shape[3]
    shard = down_weight.shape[0]
    in_parts, down_rows = lay_out(in_weight, down_weight)
    inverse = ROPE_THETA ** (-np.arange(0, HEAD_DIM, 2) / HEAD_DIM)
    (qkv_f, out_f, cot, rows_low, middle, gn, ffn_rows, q, k, v, mixture, bias, xt, mt, nt_rows, glc, gj, at,
     both_gains, cosine, sine, lse) = front_all(
        attn_gain[None], ffn_gain[None], qkv_weight, out_weight, in_parts, down_rows,
        tokens[:, 0], cotangent[:, 0], doc_starts[:, 0], np.tile(inverse, 4)[None].astype(np.float32),
    )
    in_t, qkv_t, down_t, out_t, gain_t, out_home, in_home = back_all(
        ffn_rows, middle, gn, cot, qkv_f, out_f.reshape(wide, wide), q, k, v, mixture, rows_low, bias, xt, mt, nt_rows, glc, gj, at,
        both_gains, cosine, sine, lse,
    )
    output, tokens_grad, qkv_grad, out_grad, in_grad, down_grad, attn_grad, ffn_grad = results(
        out_home, in_home, qkv_t, out_t, in_t, down_t, gain_t, shard
    )
    return (
        output[:, None],
        tokens_grad[:, None],
        qkv_grad,
        out_grad,
        in_grad,
        down_grad,
        attn_grad[0],
        ffn_grad[0],
    )


def solution(mesh):
    whole_chips = dict(mesh.shape) == {"seq": 4, "fsdp": 8}
    return jax.shard_map(
        chip_streams if whole_chips else shards,
        mesh=mesh,
        in_specs=(
            P(None, "fsdp", "seq", None),
            P(None, "fsdp", "seq", None),
            P(None, "fsdp", None),
            P("fsdp", None),
            P("fsdp", None),
            P("fsdp", None),
            P("fsdp", None),
            P("fsdp"),
            P("fsdp"),
        ),
        out_specs=(
            P(None, "fsdp", "seq", None),
            P(None, "fsdp", "seq", None),
            P("fsdp", None),
            P("fsdp", None),
            P("fsdp", None),
            P("fsdp", None),
            P("fsdp"),
            P("fsdp"),
        ),
        check_vma=False,
    )
```
